32 devices in a mesh: dp: 8 (over z, x), hst: 4 (over y, core).
Axes of the slice: x: 2, y: 2, z: 4, core: 2. Of those that a mesh axis runs over, the one named last changes fastest.
Arguments:
- pixels: bfloat16 [4, 128, 128, 2048], P(None, ('dp', 'hst')), may hold values from -6 to 6
- crop_map: int32 [4, 128, 128], P(None, ('dp', 'hst')), may hold values from 0 to 4, as said below
- queue_rows: bfloat16 [512, 128], P(('dp', 'hst')), may hold values from -0.5390625 to 0.5390625
- conv_in: bfloat16 [2048, 512], replicated, may hold values from -0.125 to 0.125
- gain_one: float32 [512], replicated, may hold values from 0.25 to 1.75
- shift_one: float32 [512], replicated, may hold values from -1.5 to 1.5
- conv_mid: bfloat16 [4608, 512], replicated, may hold values from -0.09375 to 0.09375
- gain_two: float32 [512], replicated, may hold values from 0.25 to 1.75
- shift_two: float32 [512], replicated, may hold values from -1.5 to 1.5
- conv_out: bfloat16 [512, 2048], replicated, may hold values from -0.25 to 0.25
- gain_three: float32 [2048], replicated, may hold values from 0.25 to 1.75
- shift_three: float32 [2048], replicated, may hold values from -1.5 to 1.5
- head_weight: bfloat16 [2048, 2048], replicated, may hold values from -0.125 to 0.125
- head_gain: float32 [2048], replicated, may hold values from 0.25 to 1.75
- head_shift: float32 [2048], replicated, may hold values from -1.5 to 1.5
- embed_weight: bfloat16 [2048, 128], replicated, may hold values from -0.125 to 0.125
- embed_bias: float32 [128], replicated, may hold values from -1.5 to 1.5
- prototypes: bfloat16 [128, 3000], replicated, may hold values from -0.75 to 0.75
Outputs:
- total_loss: float32 [], replicated
- grad_pixels: bfloat16 [4, 128, 128, 2048], P(None, ('dp', 'hst'))
- grad_conv_in: float32 [2048, 512], P('dp')
- grad_gain_one: float32 [512], P('dp')
- grad_shift_one: float32 [512], P('dp')
- grad_conv_mid: float32 [4608, 512], P('dp')
- grad_gain_two: float32 [512], P('dp')
- grad_shift_two: float32 [512], P('dp')
- grad_conv_out: float32 [512, 2048], P('dp')
- grad_gain_three: float32 [2048], P('dp')
- grad_shift_three: float32 [2048], P('dp')
- grad_head_weight: float32 [2048, 2048], P('dp')
- grad_head_gain: float32 [2048], P('dp')
- grad_head_shift: float32 [2048], P('dp')
- grad_embed_weight: float32 [2048, 128], P('dp')
- grad_embed_bias: float32 [128], P('dp')
- grad_prototypes: float32 [128, 3000], P('dp')
The draws below stay inside these ranges and needn't reach their ends.
Inputs may be any that keep to these rules, and one draw needn't show every extreme that they name: `crop_map`: canvas pixels are row-major over 8 rows and 16 columns. Crop k of a canvas covers its top 3 to 8 rows in 2 to 4 columns starting at column 4 * k (the last crop at most 3 columns); other pixels hold 4. Crops 2 * j and 2 * j + 1 of a canvas are two views of one image.
All inputs are finite; a program needn't handle non-finite values.
Results may differ from the reference program's by a relative error of at most 0.024.
Values sent between devices are 32-bit elements; how exact they have to be, the bound alone decides.
No kernel may reach another device: no remote copies, remote signals or barrier semaphores. Data moves between devices by JAX's collectives and lax.ppermute only.
A program may use at most 320 MiB of HBM per device.

```python
import jax
import jax.numpy as jnp
from jax import lax

C = 2048
MID = 512
HEAD = 2048
FEAT = 128
PROTOS = 3000
TAPS = 9
ROWS = 8
COLS = 16
SLOTS = 4
MICRO = 4
SINK_ITERS = 3
PIX = 128
CANVASES = 128
CROPS = 512
QUEUE = 512


def draw_crop_map(key, part):
    key = jax.random.fold_in(key, 17)
    width_key, height_key = jax.random.split(key)
    canvas_index = jnp.arange(CANVASES, dtype=jnp.int32)
    least_width = 2 + canvas_index * 3 // CANVASES
    least_height = 3 + canvas_index * (ROWS - 2) // CANVASES
    width_step = jax.random.randint(width_key, (MICRO, CANVASES, SLOTS), 0, 2)
    height_step = jax.random.randint(height_key, (MICRO, CANVASES, SLOTS), 0, 2)
    widths = jnp.minimum(least_width[None, :, None] + width_step, 4)
    widths = jnp.minimum(widths, jnp.array([4, 4, 4, 3], jnp.int32))
    heights = jnp.minimum(least_height[None, :, None] + height_step, ROWS)
    column = jnp.arange(COLS, dtype=jnp.int32)
    slot_index = column // 4
    offset = column - 4 * slot_index
    slot_onehot = (slot_index[:, None] == jnp.arange(SLOTS, dtype=jnp.int32)[None, :]).astype(jnp.int32)
    col_width = jnp.sum(widths[:, :, None, :] * slot_onehot[None, None, :, :], -1)
    col_height = jnp.sum(heights[:, :, None, :] * slot_onehot[None, None, :, :], -1)
    row_index = jnp.arange(ROWS, dtype=jnp.int32)
    inside = (offset[None, None, None, :] < col_width[:, :, None, :]) & (row_index[None, None, :, None] < col_height[:, :, None, :])
    crop_ids = jnp.where(inside, slot_index[None, None, None, :], SLOTS)
    return crop_ids.reshape(MICRO, CANVASES, ROWS * COLS).astype(jnp.int32)


def with_spikes(drawn, own_key, source, target, shards_of, factor):
    owner, partner = [(jnp.arange(drawn.shape[position]) // (drawn.shape[position] // shards_of)).reshape([-1 if axis == position else 1 for axis in range(drawn.ndim)]) for position in (source, target)]
    chosen = jax.random.permutation(own_key, shards_of)[partner]
    strong = (owner == chosen) | (owner == (partner + shards_of // 2) % shards_of)
    return jnp.where(strong, factor * drawn, drawn)


def block_scale(own_key, shape, shards, smallest, high):
    level = 1.0
    for dim, parts in shards:
        draws = jax.random.uniform(jax.random.fold_in(jax.random.fold_in(own_key, 6), dim), (parts,), jnp.float32, smallest / len(shards), high / len(shards))
        level = level * jnp.repeat(jnp.exp(draws), shape[dim] // parts).reshape((-1,) + (1,) * (len(shape) - 1 - dim))
    return level


def normal_values(rng, dims, spread, reach, cuts=(), kind=jnp.bfloat16):
    values = jax.random.normal(rng, dims, jnp.float32) * spread
    if len(cuts) > 0:
        values = block_scale(rng, dims, cuts, -0.22, 0.18) * values
    return jnp.clip(values, min=-reach, max=reach).astype(kind)


def heavy_noise(own_key, dims, deviation, limit, cuts, heavy, kind=jnp.bfloat16):
    values = deviation * jax.random.normal(own_key, dims, jnp.float32)
    if cuts:
        values = values * block_scale(own_key, dims, cuts, -0.22, 0.18)
    return jnp.clip(with_spikes(values, jax.random.fold_in(own_key, 3), *heavy), -limit, limit).astype(kind)


def setup_inputs(seed: int = 0) -> dict:
    keys = jax.random.split(jax.random.key(seed), 19)
    return {
        "pixels": heavy_noise(keys[0], (MICRO, CANVASES, PIX, C), 1.0, 6.0, ((1, 32),), (1, 3, 32, 2.75)),
        "crop_map": draw_crop_map(jax.random.fold_in(keys[18], 71), 0),
        "queue_rows": normal_values(keys[2], (QUEUE, FEAT), 0.09, 0.5390625, ((0, 32),)),
        "conv_in": normal_values(keys[3], (C, MID), C ** -0.5, 0.125),
        "gain_one": jnp.clip(1.0 + 0.15 * jax.random.normal(keys[4], (MID,), jnp.float32), 0.25, 1.75),
        "shift_one": normal_values(keys[5], (MID,), 0.3, 1.5, (), jnp.float32),
        "conv_mid": normal_values(keys[6], (TAPS * MID, MID), (TAPS * MID) ** -0.5, 0.09375),
        "gain_two": jnp.clip(1.0 + 0.15 * jax.random.normal(keys[7], (MID,), jnp.float32), 0.25, 1.75),
        "shift_two": normal_values(keys[8], (MID,), 0.3, 1.5, (), jnp.float32),
        "conv_out": normal_values(keys[9], (MID, C), MID ** -0.5, 0.25),
        "gain_three": jnp.clip(1.0 + 0.15 * jax.random.normal(keys[10], (C,), jnp.float32), 0.25, 1.75),
        "shift_three": normal_values(keys[11], (C,), 0.3, 1.5, (), jnp.float32),
        "head_weight": normal_values(keys[12], (C, HEAD), C ** -0.5, 0.125),
        "head_gain": jnp.clip(1.0 + 0.15 * jax.random.normal(keys[13], (HEAD,), jnp.float32), 0.25, 1.75),
        "head_shift": normal_values(keys[14], (HEAD,), 0.3, 1.5, (), jnp.float32),
        "embed_weight": normal_values(keys[15], (HEAD, FEAT), HEAD ** -0.5, 0.125),
        "embed_bias": normal_values(keys[16], (FEAT,), 0.3, 1.5, (), jnp.float32),
        "prototypes": normal_values(keys[17], (FEAT, PROTOS), 64 ** -0.5, 0.75),
    }


eps_norm = 1e-05
eps_unit = 1e-06
transport_epsilon = 0.05
softmax_sharpness = 0.1
highest = lax.Precision.HIGHEST
tap_offsets = ((-1, -1), (-1, 0), (-1, 1), (0, -1), (0, 0), (0, 1), (1, -1), (1, 0), (1, 1))

@jax.custom_vjp
def low(v):
    return lax.optimization_barrier(v.astype(jnp.bfloat16)).astype(jnp.float32)

@jax.custom_vjp
def low_back(v):
    return v

def low_keep(v):
    return (low(v), None)

def low_pass(kept, grad):
    return (grad,)

def back_keep(v):
    return (v, None)

def back_low(kept, grad):
    return (low(grad),)
low.defvjp(low_keep, low_pass)
low_back.defvjp(back_keep, back_low)

def matmul(left, right):
    return jnp.dot(left, right, precision=highest, preferred_element_type=jnp.float32)

def shift_map(field, row_step, col_step, fill):
    widths = [(0, 0), (1, 1), (1, 1)] + [(0, 0)] * (field.ndim - 3)
    padded = jnp.pad(field, widths, constant_values=fill)
    height = field.shape[1]
    breadth = field.shape[2]
    return padded[:, 1 + row_step:1 + row_step + height, 1 + col_step:1 + col_step + breadth]

def tap_masks(crop_ids):
    crop_grid = crop_ids.reshape(crop_ids.shape[0], ROWS, COLS)
    result = []
    for row_step, col_step in tap_offsets:
        nearby = shift_map(crop_grid, row_step, col_step, -1)
        result.append(((nearby == crop_grid) & (crop_grid < SLOTS)).reshape(-1, 1))
    return result

def batch_norm(values, valid_mask, total, gain, shift):
    mean_value = lax.optimization_barrier(jnp.sum(values * valid_mask, 0)) / total
    centered = values - mean_value
    variance = lax.optimization_barrier(jnp.sum(centered * centered * valid_mask, 0)) / total
    return centered * lax.rsqrt(variance + eps_norm) * gain + shift

def forward(flat_pixels, crop_ids, valid_mask, pixel_total, params):
    conv_in, gain_one, shift_one, conv_mid, gain_two, shift_two, conv_out, gain_three, shift_three, head_weight, head_gain, head_shift, embed_weight, embed_bias, prototypes = params
    canvas = crop_ids.shape[0]
    middle = conv_in.shape[1]
    pre_one = batch_norm(low_back(matmul(flat_pixels, conv_in)), valid_mask, pixel_total, gain_one, shift_one)
    act_one = low(jax.nn.silu(pre_one) * valid_mask)
    act_grid = act_one.reshape(canvas, ROWS, COLS, middle)
    mask_list = tap_masks(crop_ids)
    pieces = []
    for mask_now, offset in zip(mask_list, tap_offsets):
        moved = shift_map(act_grid, offset[0], offset[1], 0.0).reshape(-1, middle)
        pieces.append(jnp.where(mask_now, moved, 0.0))
    columns = jnp.concatenate(pieces, 1)
    pre_two = batch_norm(low_back(matmul(columns, conv_mid)), valid_mask, pixel_total, gain_two, shift_two)
    act_two = low(jax.nn.silu(pre_two) * valid_mask)
    pre_three = batch_norm(low_back(matmul(act_two, conv_out)), valid_mask, pixel_total, gain_three, shift_three) + flat_pixels
    block_out = low(jax.nn.silu(pre_three) * valid_mask)
    onehot = (crop_ids[:, None, :] == jnp.arange(SLOTS, dtype=jnp.int32)[None, :, None]).astype(jnp.float32)
    crop_sizes = lax.optimization_barrier(jnp.sum(onehot, 2))
    pooled = jnp.einsum('cqp,cpd->cqd', onehot, block_out.reshape(canvas, PIX, -1), precision=highest)
    features = low((pooled / crop_sizes[:, :, None]).reshape(canvas * SLOTS, -1))
    crop_rows = canvas * SLOTS
    all_rows = jnp.ones((crop_rows, 1), jnp.float32)
    pre_four = batch_norm(low_back(matmul(features, head_weight)), all_rows, crop_rows * 1.0, head_gain, head_shift)
    act_four = low(jax.nn.silu(pre_four))
    embedded = matmul(act_four, embed_weight) + embed_bias
    unit_rows = low(embedded * lax.rsqrt(lax.optimization_barrier(jnp.sum(embedded * embedded, 1, keepdims=True)) + eps_unit))
    return matmul(unit_rows, prototypes)

def balanced_transport(prototype_logits):
    marginal_weight = jnp.exp(prototype_logits / transport_epsilon)
    for sweep in range(SINK_ITERS):
        marginal_weight = marginal_weight / lax.optimization_barrier(jnp.sum(marginal_weight, 0, keepdims=True))
        marginal_weight = marginal_weight / lax.optimization_barrier(jnp.sum(marginal_weight, 1, keepdims=True))
    return marginal_weight

def swapped_loss(prototype_logits, cluster_codes):
    log_likelihoods = jax.nn.log_softmax(prototype_logits / softmax_sharpness, -1)
    canvas = prototype_logits.shape[0] // SLOTS
    partner = cluster_codes.reshape(canvas, 2, 2, -1)[:, :, ::-1].reshape(prototype_logits.shape[0], -1)
    return -jnp.sum(partner * log_likelihoods)

def reference(pixels, crop_map, queue_rows, conv_in, gain_one, shift_one, conv_mid, gain_two, shift_two, conv_out, gain_three, shift_three, head_weight, head_gain, head_shift, embed_weight, embed_bias, prototypes):
    params = tuple((weight.astype(jnp.float32) for weight in (conv_in, gain_one, shift_one, conv_mid, gain_two, shift_two, conv_out, gain_three, shift_three, head_weight, head_gain, head_shift, embed_weight, embed_bias, prototypes)))
    queued_logits = matmul(queue_rows.astype(jnp.float32), params[14])
    loss_scale = 1.0 / (MICRO * CROPS)
    totals = None
    total_loss = jnp.zeros((), jnp.float32)
    grad_list = []
    for micro_index in range(MICRO):
        crop_ids = crop_map[micro_index]
        valid_mask = (crop_ids < SLOTS).astype(jnp.float32).reshape(-1, 1)
        pixel_total = jnp.sum(valid_mask)
        flat_pixels = pixels[micro_index].astype(jnp.float32).reshape(-1, C)

        def network(flat_in, weights):
            return forward(flat_in, crop_ids, valid_mask, pixel_total, weights)
        prototype_logits, pull_back = jax.vjp(network, flat_pixels, params)
        cluster_codes = balanced_transport(jnp.concatenate([prototype_logits, queued_logits], 0))[:prototype_logits.shape[0]]

        def objective(score_in):
            return swapped_loss(score_in, cluster_codes) * loss_scale
        part_loss, loss_back = jax.vjp(objective, prototype_logits)
        grad_scores, = loss_back(jnp.ones((), jnp.float32))
        grad_flat, grad_weights = pull_back(grad_scores)
        total_loss = total_loss + part_loss
        grad_list.append(grad_flat.astype(jnp.bfloat16).reshape(CANVASES, PIX, C))
        totals = grad_weights if totals is None else jax.tree.map(jnp.add, totals, grad_weights)
    return (total_loss, jnp.stack(grad_list), totals[0], totals[1], totals[2], totals[3], totals[4], totals[5], totals[6], totals[7], totals[8], totals[9], totals[10], totals[11], totals[12], totals[13], totals[14])
```

```python
import functools

import jax
import jax.numpy as jnp
from jax import lax
from jax.experimental import pallas as pl
from jax.experimental.pallas import tpu as pltpu
from jax.sharding import PartitionSpec as P

ROWS = 8
COLS = 16
SLOTS = 4
CELL = COLS // SLOTS
PIX = ROWS * COLS
SINK_ITERS = 3
TAPS = 9

eps_norm = 1e-05
eps_unit = 1e-06
transport_epsilon = 0.05
softmax_sharpness = 0.1
highest = lax.Precision.HIGHEST
F32 = jnp.float32
BF16 = jnp.bfloat16
AXES = ("dp", "hst")
MIB = 1 << 20


def swap(value, mask):
    count = lax.axis_size("dp") * lax.axis_size("hst")
    return lax.ppermute(value, AXES, [(i, i ^ mask) for i in range(count)])


def sync_groups():
    bits = (lax.axis_size("dp") * lax.axis_size("hst")).bit_length() - 1
    groups = [(1,)]
    bit = 1
    while bit < bits:
        if bit + 1 < bits:
            groups.append((1 << bit, 2 << bit, 3 << bit))
            bit += 2
        else:
            groups.append((1 << bit,))
            bit += 1
    return groups


def tree(parts):
    while len(parts) > 1:
        parts = [parts[i] + parts[i + 1] for i in range(0, len(parts), 2)]
    return parts[0]


def total_sum(value):
    for group in sync_groups():
        value = tree([value] + [swap(value, mask) for mask in group])
    return value


def merge_moments(moments, counts):
    for group, members in zip(sync_groups(), counts):
        parts = [moments] + [swap(moments, mask) for mask in group]
        whole = tree(list(members))
        mean = tree([n * part[:, 0] for n, part in zip(members, parts)]) / whole
        spread = tree(
            [part[:, 1] + n * (part[:, 0] - mean) ** 2 for n, part in zip(members, parts)]
        )
        moments = jnp.stack([mean, spread], 1)
    return moments[:, 0], moments[:, 1]


def first_merge(moments):
    counts = []
    for group in sync_groups():
        parts = [moments] + [swap(moments, mask) for mask in group]
        members = [part[:, 2] for part in parts]
        whole = tree(members)
        mean = tree([n * part[:, 0] for n, part in zip(members, parts)]) / whole
        spread = tree(
            [part[:, 1] + n * (part[:, 0] - mean) ** 2 for n, part in zip(members, parts)]
        )
        counts.append([n[:, :1] for n in members])
        moments = jnp.stack([mean, spread, whole], 1)
    return moments[:, 0], moments[:, 1], moments[:, 2, :1], counts


def bit_of(mask):
    index = lax.axis_index("dp") * lax.axis_size("hst") + lax.axis_index("hst")
    return (index // mask) % 2


def halve(value, axis, mask):
    bit = bit_of(mask)
    keep = lax.dynamic_index_in_dim(value, bit, axis, keepdims=False)
    send = lax.dynamic_index_in_dim(value, 1 - bit, axis, keepdims=False)
    return keep + swap(send, mask)


def joined(value, axis, mask):
    other = swap(value, mask)
    low = bit_of(mask) == 0
    return jnp.concatenate([jnp.where(low, value, other), jnp.where(low, other, value)], axis)


def split_rows(value, order):
    devices = lax.axis_size("dp")
    dp_bits = devices.bit_length() - 1
    base = lax.axis_size("hst")
    inner = 2 in order
    dims = [("dp", j) for j in reversed(range(dp_bits))] + ([("row", 0)] if inner else [])
    rest = value.shape[0] // (devices * (2 if inner else 1))
    value = value.reshape((2,) * len(dims) + (rest, value.shape[1]))
    for mask in order:
        key = ("row", 0) if mask == 2 else ("dp", (mask // base).bit_length() - 1)
        place = dims.index(key)
        value = halve(value, place, mask)
        dims.pop(place)
    return value


def dp_masks():
    base = lax.axis_size("hst")
    return [base << j for j in range(lax.axis_size("dp").bit_length() - 1)]


def reduce_weight(keep, send):
    value = keep + swap(send, 1)
    width = value.shape[1]
    masks = dp_masks()
    if width % 256 == 0:
        half = width // 2
        left = split_rows(value[:, :half], [2] + masks)
        right = split_rows(value[:, half:], masks[:1] + [2] + masks[1:])
        value = jnp.concatenate([left, right], 1)
    else:
        value = split_rows(value, [2] + masks)
    value = joined(value, 0, 2)
    return joined(value, 1, 1)


def own_shard(vector):
    piece_size = vector.shape[0] // lax.axis_size("dp")
    return lax.dynamic_slice_in_dim(vector, lax.axis_index("dp") * piece_size, piece_size, 0)


def run(body, grid, in_specs, out_specs, out_shape, scratch=(), flops=0, bytes_accessed=0, prefetch=0):
    return pl.pallas_call(
        body,
        grid_spec=pltpu.PrefetchScalarGridSpec(
            num_scalar_prefetch=prefetch,
            grid=grid,
            in_specs=in_specs,
            out_specs=out_specs,
            scratch_shapes=list(scratch),
        ),
        out_shape=out_shape,
        compiler_params=pltpu.CompilerParams(
            vmem_limit_bytes=56 * MIB, dimension_semantics=("arbitrary",) * len(grid)
        ),
        cost_estimate=pl.CostEstimate(
            flops=flops, bytes_accessed=bytes_accessed, transcendentals=0
        ),
    )


def shape(dims, dtype=F32):
    return jax.ShapeDtypeStruct(tuple(dims), dtype)


def sigmoid(u):
    return 0.5 * jnp.tanh(0.5 * u) + 0.5


def slope_of(u):
    s = sigmoid(u)
    return s * (1.0 + u * (1.0 - s))


def nt_dot(left, right):
    return lax.dot_general(left, right, (((1,), (1,)), ((), ())), preferred_element_type=F32)


def tn_dot(left, right):
    return lax.dot_general(left, right, (((0,), (0,)), ((), ())), preferred_element_type=F32)


def put_moments(stats_ref, h_ref, v, chunk, with_count):
    rows = h_ref.shape[0]
    count = jnp.sum(v, axis=0, keepdims=True)
    total = jnp.zeros((1, h_ref.shape[1]), F32)
    for i in range(0, rows, chunk):
        total += jnp.sum(h_ref[i : i + chunk] * v[i : i + chunk], axis=0, keepdims=True)
    mean = total / count
    spread = jnp.zeros((1, h_ref.shape[1]), F32)
    for i in range(0, rows, chunk):
        off = (h_ref[i : i + chunk] - mean) * v[i : i + chunk]
        spread += jnp.sum(off * off, axis=0, keepdims=True)
    stats_ref[0, 0:1, :] = mean
    stats_ref[0, 1:2, :] = spread
    if with_count:
        stats_ref[0, 2:3, :] = jnp.broadcast_to(count, mean.shape)


def first_body(x_ref, w_ref, v_ref, h_ref, stats_ref):
    h_ref[...] = jnp.dot(x_ref[...], w_ref[...], preferred_element_type=F32)
    put_moments(stats_ref, h_ref, v_ref[...], 64, True)


def first_product(x, weight, valid, micro):
    rows = x.shape[0] // micro
    depth, width = weight.shape
    return run(
        first_body,
        (micro,),
        [
            pl.BlockSpec((rows, depth), lambda m: (m, 0)),
            pl.BlockSpec((depth, width), lambda m: (0, 0)),
            pl.BlockSpec((rows, 1), lambda m: (m, 0)),
        ],
        [
            pl.BlockSpec((rows, width), lambda m: (m, 0)),
            pl.BlockSpec((1, 3, width), lambda m: (m, 0, 0)),
        ],
        [shape((micro * rows, width)), shape((micro, 3, width))],
        flops=2 * micro * rows * depth * width,
        bytes_accessed=2 * x.size,
    )(x, weight, valid)


def cell_column(rows):
    return lax.broadcasted_iota(jnp.int32, (rows, 1), 0) % CELL


def second_body(h_ref, v_ref, coef_ref, w_ref, a_ref, h2_ref, stats_ref, cols_ref):
    rows, width = h_ref.shape
    v = v_ref[...]
    mean = coef_ref[0, 0:1, :]
    factor = coef_ref[0, 1:2, :]
    shift = coef_ref[0, 2:3, :]
    pre = (h_ref[...] - mean) * factor + shift
    act = (pre * sigmoid(pre) * v).astype(BF16)
    a_ref[...] = act
    wide = act.astype(F32)
    place = cell_column(rows)
    sides = (
        jnp.where(place >= 1, pltpu.roll(wide, 1, 0), 0.0).astype(BF16),
        act,
        jnp.where(place <= CELL - 2, pltpu.roll(wide, rows - 1, 0), 0.0).astype(BF16),
    )
    blank = jnp.zeros((COLS, width), BF16)
    for c in range(3):
        side = sides[c]
        cols_ref[:, pl.ds((3 + c) * width, width)] = side
        for k in range(0, rows, PIX):
            cols_ref[k : k + COLS, pl.ds(c * width, width)] = blank
            cols_ref[k + COLS : k + PIX, pl.ds(c * width, width)] = side[k : k + PIX - COLS]
            cols_ref[k : k + PIX - COLS, pl.ds((6 + c) * width, width)] = side[k + COLS : k + PIX]
            cols_ref[k + PIX - COLS : k + PIX, pl.ds((6 + c) * width, width)] = blank
    h2_ref[...] = jnp.dot(cols_ref[...], w_ref[...], preferred_element_type=F32)
    put_moments(stats_ref, h2_ref, v, 64, False)


def second_product(h1, valid, coef, weight, micro):
    rows, width = h1.shape[0] // micro, h1.shape[1]
    return run(
        second_body,
        (micro,),
        [
            pl.BlockSpec((rows, width), lambda m: (m, 0)),
            pl.BlockSpec((rows, 1), lambda m: (m, 0)),
            pl.BlockSpec((1, 3, width), lambda m: (m, 0, 0)),
            pl.BlockSpec(weight.shape, lambda m: (0, 0)),
        ],
        [
            pl.BlockSpec((rows, width), lambda m: (m, 0)),
            pl.BlockSpec((rows, width), lambda m: (m, 0)),
            pl.BlockSpec((1, 2, width), lambda m: (m, 0, 0)),
        ],
        [
            shape((micro * rows, width), BF16),
            shape((micro * rows, width)),
            shape((micro, 2, width)),
        ],
        [pltpu.VMEM((rows, weight.shape[0]), BF16)],
        flops=2 * micro * rows * weight.size,
        bytes_accessed=10 * h1.size,
    )(h1, valid, coef, weight)


def third_body(h_ref, v_ref, coef_ref, w_ref, a_ref, h3_ref, stats_ref):
    v = v_ref[...]
    pre = (h_ref[...] - coef_ref[0, 0:1, :]) * coef_ref[0, 1:2, :] + coef_ref[0, 2:3, :]
    act = (pre * sigmoid(pre) * v).astype(BF16)
    a_ref[...] = act
    h3_ref[...] = jnp.dot(act, w_ref[...], preferred_element_type=F32)
    put_moments(stats_ref, h3_ref, v, 16, False)


def third_product(h2, valid, coef, weight, micro):
    rows, depth = h2.shape[0] // micro, h2.shape[1]
    width = weight.shape[1]
    return run(
        third_body,
        (micro,),
        [
            pl.BlockSpec((rows, depth), lambda m: (m, 0)),
            pl.BlockSpec((rows, 1), lambda m: (m, 0)),
            pl.BlockSpec((1, 3, depth), lambda m: (m, 0, 0)),
            pl.BlockSpec(weight.shape, lambda m: (0, 0)),
        ],
        [
            pl.BlockSpec((rows, depth), lambda m: (m, 0)),
            pl.BlockSpec((rows, width), lambda m: (m, 0)),
            pl.BlockSpec((1, 2, width), lambda m: (m, 0, 0)),
        ],
        [
            shape((micro * rows, depth), BF16),
            shape((micro * rows, width)),
            shape((micro, 2, width)),
        ],
        flops=2 * micro * rows * weight.size,
        bytes_accessed=4 * micro * rows * width,
    )(h2, valid, coef, weight)


def pool_body(h_ref, x_ref, v_ref, coef_ref, size_ref, feat_ref, first_ref, second_ref, slope_ref, norm_ref, sums_ref):
    rows, width = h_ref.shape
    mean = coef_ref[0, 0:1, :]
    scaled = coef_ref[0, 1:2, :]
    gain = coef_ref[0, 2:3, :]
    shift = coef_ref[0, 3:4, :]
    for k in range(rows // PIX):
        acc_out = jnp.zeros((COLS, width), F32)
        acc_first = jnp.zeros((COLS, width), F32)
        acc_second = jnp.zeros((COLS, width), F32)
        for r in range(ROWS):
            at = pl.ds(k * PIX + r * COLS, COLS)
            v = v_ref[at, :]
            normal = (h_ref[at, :] - mean) * scaled
            resid = normal * gain + shift + x_ref[at, :].astype(F32)
            sig = sigmoid(resid)
            kept = sig * v
            out = (resid * kept).astype(BF16).astype(F32)
            slope = kept * (1.0 + resid * (1.0 - sig))
            acc_out += out
            acc_first += slope
            acc_second += slope * normal
            slope_ref[at, :] = slope.astype(BF16)
            norm_ref[at, :] = normal.astype(BF16)
        place = pl.ds(k * COLS, COLS)
        sums_ref[0, place, :] = acc_out
        sums_ref[1, place, :] = acc_first
        sums_ref[2, place, :] = acc_second
    crops = size_ref.shape[0]
    lines = sums_ref.shape[1]
    pick = (
        lax.broadcasted_iota(jnp.int32, (crops, lines), 1) // CELL
        == lax.broadcasted_iota(jnp.int32, (crops, lines), 0)
    ).astype(F32)
    gather = functools.partial(jnp.dot, precision=highest, preferred_element_type=F32)
    feat_ref[...] = (gather(pick, sums_ref[0]) / size_ref[...]).astype(BF16).astype(F32)
    first_ref[...] = gather(pick, sums_ref[1])
    second_ref[...] = gather(pick, sums_ref[2])


def pool(h3, x, valid, coef, sizes, micro):
    rows, channels = h3.shape[0] // micro, h3.shape[1]
    crops = sizes.shape[0] // micro
    width = 512
    tile = pl.BlockSpec((rows, width), lambda m, c: (m, c))
    small = pl.BlockSpec((crops, width), lambda m, c: (m, c))
    return run(
        pool_body,
        (micro, channels // width),
        [
            tile,
            tile,
            pl.BlockSpec((rows, 1), lambda m, c: (m, 0)),
            pl.BlockSpec((1, 4, width), lambda m, c: (m, 0, c)),
            pl.BlockSpec((crops, 1), lambda m, c: (m, 0)),
        ],
        [small, small, small, tile, tile],
        [shape((micro * crops, channels))] * 3 + [shape(h3.shape, BF16)] * 2,
        [pltpu.VMEM((3, rows // ROWS, width), F32)],
        flops=40 * h3.size,
        bytes_accessed=10 * h3.size,
    )(h3, x, valid, coef, sizes)


def head_body(feat_ref, w_ref, g_ref, stats_ref):
    g = jnp.dot(feat_ref[...].astype(BF16), w_ref[...], preferred_element_type=F32)
    g_ref[...] = g
    micro = stats_ref.shape[0]
    crops = g.shape[0] // micro
    for m in range(micro):
        part = g[m * crops : (m + 1) * crops]
        mean = jnp.sum(part, axis=0, keepdims=True) / crops
        stats_ref[m, 0:1, :] = mean
        stats_ref[m, 1:2, :] = jnp.sum((part - mean) ** 2, axis=0, keepdims=True)


def head_product(feat, weight, micro):
    lines = feat.shape[0]
    depth, width = weight.shape
    tile = 512
    return run(
        head_body,
        (width // tile,),
        [
            pl.BlockSpec((lines, depth), lambda c: (0, 0)),
            pl.BlockSpec((depth, tile), lambda c: (0, c)),
        ],
        [
            pl.BlockSpec((lines, tile), lambda c: (0, c)),
            pl.BlockSpec((micro, 2, tile), lambda c: (0, 0, c)),
        ],
        [shape((lines, width)), shape((micro, 2, width))],
        flops=2 * lines * weight.size,
        bytes_accessed=2 * weight.size,
    )(feat, weight)


def head_back_body(dy_ref, g_ref, coef_ref, w_ref, size_ref, first_ref, second_ref, dg_ref, wide_ref, stats_ref, low_ref):
    micro = stats_ref.shape[0]
    lines = dy_ref.shape[0]
    crops = lines // micro

    @pl.when(pl.program_id(0) == 0)
    def _():
        for m in range(micro):
            at = pl.ds(m * crops, crops)
            normal = (g_ref[at, :] - coef_ref[m, 0:1, :]) * coef_ref[m, 1:2, :]
            dg = coef_ref[m, 2:3, :] * (
                dy_ref[at, :] - (coef_ref[m, 3:4, :] + normal * coef_ref[m, 4:5, :])
            )
            low = dg.astype(BF16)
            low_ref[at, :] = low
            dg_ref[at, :] = low.astype(F32)

    per_crop = nt_dot(low_ref[...], w_ref[...]) / size_ref[...]
    lift = (
        lax.broadcasted_iota(jnp.int32, (lines * CELL, lines), 0) // CELL
        == lax.broadcasted_iota(jnp.int32, (lines * CELL, lines), 1)
    ).astype(F32)
    wide_ref[...] = jnp.dot(lift, per_crop, precision=highest, preferred_element_type=F32)
    one = per_crop * first_ref[...]
    two = per_crop * second_ref[...]
    for m in range(micro):
        at = slice(m * crops, (m + 1) * crops)
        stats_ref[m, 0:1, :] = jnp.sum(one[at], axis=0, keepdims=True)
        stats_ref[m, 1:2, :] = jnp.sum(two[at], axis=0, keepdims=True)


def head_back(dy, g, coef, weight, sizes, first, second, micro):
    lines, width = dy.shape
    channels = weight.shape[0]
    tile = 512
    full = pl.BlockSpec((lines, width), lambda c: (0, 0))
    part = pl.BlockSpec((lines, tile), lambda c: (0, c))
    return run(
        head_back_body,
        (channels // tile,),
        [
            full,
            full,
            pl.BlockSpec((micro, 5, width), lambda c: (0, 0, 0)),
            pl.BlockSpec((tile, width), lambda c: (c, 0)),
            pl.BlockSpec((lines, 1), lambda c: (0, 0)),
            part,
            part,
        ],
        [
            full,
            pl.BlockSpec((lines * CELL, tile), lambda c: (0, c)),
            pl.BlockSpec((micro, 2, tile), lambda c: (0, 0, c)),
        ],
        [shape((lines, width)), shape((lines * CELL, channels)), shape((micro, 2, channels))],
        [pltpu.VMEM((lines, width), BF16)],
        flops=2 * lines * weight.size,
        bytes_accessed=2 * weight.size,
    )(dy, g, coef, weight, sizes, first, second)


def third_back_body(wide_ref, slope_ref, norm_ref, v_ref, coef_ref, w_ref, h2_ref, coef2_ref, d_ref, dy_ref, stats_ref):
    rows, channels = slope_ref.shape
    factor = coef_ref[0, 0:1, :]
    one = coef_ref[0, 1:2, :]
    two = coef_ref[0, 2:3, :]
    for k in range(rows // PIX):
        for r in range(ROWS):
            at = pl.ds(k * PIX + r * COLS, COLS)
            v = v_ref[at, :]
            dy = wide_ref[pl.ds(k * COLS, COLS), :] * slope_ref[at, :].astype(F32)
            d = factor * (dy - v * (one + norm_ref[at, :].astype(F32) * two))
            d_ref[at, :] = d.astype(BF16)
    d_act = nt_dot(d_ref[...], w_ref[...])
    normal = (h2_ref[...] - coef2_ref[0, 0:1, :]) * coef2_ref[0, 1:2, :]
    pre = normal * coef2_ref[0, 2:3, :] + coef2_ref[0, 3:4, :]
    dy = d_act * v_ref[...] * slope_of(pre)
    dy_ref[...] = dy
    stats_ref[0, 0:1, :] = jnp.sum(dy, axis=0, keepdims=True)
    stats_ref[0, 1:2, :] = jnp.sum(dy * normal, axis=0, keepdims=True)


def third_back(wide, slope, norm, valid, coef, weight, h2, coef2, micro):
    rows, channels = slope.shape[0] // micro, slope.shape[1]
    middle = weight.shape[0]
    lines = wide.shape[0] // micro
    big = pl.BlockSpec((rows, channels), lambda m: (m, 0))
    mid = pl.BlockSpec((rows, middle), lambda m: (m, 0))
    return run(
        third_back_body,
        (micro,),
        [
            pl.BlockSpec((lines, channels), lambda m: (m, 0)),
            big,
            big,
            pl.BlockSpec((rows, 1), lambda m: (m, 0)),
            pl.BlockSpec((1, 3, channels), lambda m: (m, 0, 0)),
            pl.BlockSpec(weight.shape, lambda m: (0, 0)),
            mid,
            pl.BlockSpec((1, 4, middle), lambda m: (m, 0, 0)),
        ],
        [big, mid, pl.BlockSpec((1, 2, middle), lambda m: (m, 0, 0))],
        [shape(slope.shape, BF16), shape(h2.shape), shape((micro, 2, middle))],
        flops=2 * slope.shape[0] * weight.size,
        bytes_accessed=6 * slope.size,
    )(wide, slope, norm, valid, coef, weight, h2, coef2)


def grad_body(which_ref, left_ref, right_ref, out_ref):
    out_ref[...] = tn_dot(left_ref[...], right_ref[...])


def half_grad(which, left, right, tile):
    rows, depth = left.shape
    half = right.shape[1] // 2
    return run(
        grad_body,
        (depth // tile,),
        [
            pl.BlockSpec((rows, tile), lambda c, w: (0, c)),
            pl.BlockSpec((rows, half), lambda c, w: (0, w[0])),
        ],
        pl.BlockSpec((tile, half), lambda c, w: (c, 0)),
        shape((depth, half)),
        flops=2 * rows * depth * half,
        bytes_accessed=2 * left.size + right.size + 4 * depth * half,
        prefetch=1,
    )(which, left, right)


def norm_back_body(dy_ref, h_ref, v_ref, coef_ref, d_ref):
    normal = (h_ref[...] - coef_ref[0, 0:1, :]) * coef_ref[0, 1:2, :]
    d = coef_ref[0, 2:3, :] * (
        dy_ref[...] - v_ref[...] * (coef_ref[0, 3:4, :] + normal * coef_ref[0, 4:5, :])
    )
    d_ref[...] = d.astype(BF16)


def norm_back(dy, h, valid, coef, micro):
    rows, width = dy.shape[0] // micro, dy.shape[1]
    mid = pl.BlockSpec((rows, width), lambda m: (m, 0))
    return run(
        norm_back_body,
        (micro,),
        [
            mid,
            mid,
            pl.BlockSpec((rows, 1), lambda m: (m, 0)),
            pl.BlockSpec((1, 5, width), lambda m: (m, 0, 0)),
        ],
        mid,
        shape(dy.shape, BF16),
        bytes_accessed=10 * dy.size,
    )(dy, h, valid, coef)


def taps_body(which_ref, a_ref, d_ref, out_ref, sides_ref, left_ref):
    rows, width = a_ref.shape
    tap = pl.program_id(0)

    @pl.when(tap == 0)
    def _():
        blank = jnp.zeros((COLS, width), BF16)
        place = cell_column(PIX)
        for k in range(rows // PIX):
            act = a_ref[k * PIX : (k + 1) * PIX, :]
            wide = act.astype(F32)
            sides = (
                jnp.where(place >= 1, pltpu.roll(wide, 1, 0), 0.0).astype(BF16),
                act,
                jnp.where(place <= CELL - 2, pltpu.roll(wide, PIX - 1, 0), 0.0).astype(BF16),
            )
            for c in range(3):
                sides_ref[c, k, 0:COLS, :] = blank
                sides_ref[c, k, COLS : COLS + PIX, :] = sides[c]
                sides_ref[c, k, COLS + PIX :, :] = blank

    row = tap // 3
    col = tap % 3
    start = pl.multiple_of(row * COLS, COLS)
    for k in range(rows // PIX):
        left_ref[k * PIX : (k + 1) * PIX, :] = sides_ref[col, k, pl.ds(start, PIX), :]
    out_ref[...] = tn_dot(left_ref[...], d_ref[...])


def taps_grad(which, act, d, tile=None):
    rows, width = act.shape
    half = d.shape[1] // 2
    return run(
        taps_body,
        (TAPS,),
        [
            pl.BlockSpec((rows, width), lambda t, w: (0, 0)),
            pl.BlockSpec((rows, half), lambda t, w: (0, w[0])),
        ],
        pl.BlockSpec((width, half), lambda t, w: (t, 0)),
        shape((TAPS * width, half)),
        [
            pltpu.VMEM((3, rows // PIX, PIX + 2 * COLS, width), BF16),
            pltpu.VMEM((rows, width), BF16),
        ],
        flops=2 * rows * TAPS * width * half,
        bytes_accessed=4 * TAPS * width * half,
        prefetch=1,
    )(which, act, d)


def second_back_body(d_ref, w_ref, v_ref, h1_ref, coef_ref, dy_ref, stats_ref, moved_ref):
    rows, width = d_ref.shape
    blank = jnp.zeros((COLS, width), BF16)
    for k in range(0, rows, PIX):
        moved_ref[0, k : k + PIX - COLS, :] = d_ref[k + COLS : k + PIX, :]
        moved_ref[0, k + PIX - COLS : k + PIX, :] = blank
        moved_ref[1, k : k + COLS, :] = blank
        moved_ref[1, k + COLS : k + PIX, :] = d_ref[k : k + PIX - COLS, :]
    sources = (moved_ref[0], d_ref[...], moved_ref[1])
    parts = []
    for c in range(3):
        part = None
        for r in range(3):
            tap = 3 * r + c
            term = nt_dot(sources[r], w_ref[tap * width : (tap + 1) * width, :])
            part = term if part is None else part + term
        parts.append(part)
    place = cell_column(rows)
    d_act = (
        parts[1]
        + jnp.where(place >= 1, pltpu.roll(parts[2], 1, 0), 0.0)
        + jnp.where(place <= CELL - 2, pltpu.roll(parts[0], rows - 1, 0), 0.0)
    )
    normal = (h1_ref[...] - coef_ref[0, 0:1, :]) * coef_ref[0, 1:2, :]
    pre = normal * coef_ref[0, 2:3, :] + coef_ref[0, 3:4, :]
    dy = d_act * v_ref[...] * slope_of(pre)
    dy_ref[...] = dy
    stats_ref[0, 0:1, :] = jnp.sum(dy, axis=0, keepdims=True)
    stats_ref[0, 1:2, :] = jnp.sum(dy * normal, axis=0, keepdims=True)


def second_back(d, weight, valid, h1, coef, micro):
    rows, width = d.shape[0] // micro, d.shape[1]
    mid = pl.BlockSpec((rows, width), lambda m: (m, 0))
    return run(
        second_back_body,
        (micro,),
        [
            mid,
            pl.BlockSpec(weight.shape, lambda m: (0, 0)),
            pl.BlockSpec((rows, 1), lambda m: (m, 0)),
            mid,
            pl.BlockSpec((1, 4, width), lambda m: (m, 0, 0)),
        ],
        [mid, pl.BlockSpec((1, 2, width), lambda m: (m, 0, 0))],
        [shape(d.shape), shape((micro, 2, width))],
        [pltpu.VMEM((2, rows, width), BF16)],
        flops=2 * micro * rows * weight.size,
        bytes_accessed=10 * d.size,
    )(d, weight, valid, h1, coef)


def pixels_body(d_ref, w_ref, wide_ref, slope_ref, out_ref):
    rows, channels = out_ref.shape
    width = 512
    for j in range(0, channels, width):
        lane = pl.ds(j, width)
        grad = nt_dot(d_ref[...], w_ref[lane, :])
        for k in range(rows // PIX):
            wide = wide_ref[pl.ds(k * COLS, COLS), lane]
            for r in range(ROWS):
                first = k * PIX + r * COLS
                at = pl.ds(first, COLS)
                out_ref[at, lane] = (
                    grad[first : first + COLS] + wide * slope_ref[at, lane].astype(F32)
                ).astype(BF16)


def pixels_grad(d, weight, wide, slope, micro):
    rows, channels = slope.shape[0] // micro, slope.shape[1]
    lines = wide.shape[0] // micro
    big = pl.BlockSpec((rows, channels), lambda m: (m, 0))
    return run(
        pixels_body,
        (micro,),
        [
            pl.BlockSpec((rows, d.shape[1]), lambda m: (m, 0)),
            pl.BlockSpec(weight.shape, lambda m: (0, 0)),
            pl.BlockSpec((lines, channels), lambda m: (m, 0)),
            big,
        ],
        big,
        shape(slope.shape, BF16),
        flops=2 * slope.shape[0] * weight.size,
        bytes_accessed=4 * slope.size,
    )(d, weight, wide, slope)


def factor_body(which_ref, *refs):
    lefts, rights, out_ref = refs[:-1][0::2], refs[:-1][1::2], refs[-1]
    left = jnp.concatenate([ref[...] for ref in lefts], 0).astype(BF16)
    right = jnp.concatenate([ref[...] for ref in rights], 0).astype(BF16)
    out_ref[...] = tn_dot(left, right)


def factor_grad(which, pairs):
    lines, depth = pairs[0][0].shape
    width = pairs[0][1].shape[1]
    quarter = width // 4
    tile = 512
    specs = []
    for _ in pairs:
        specs.append(pl.BlockSpec((lines, tile), lambda c, w: (0, c)))
        specs.append(pl.BlockSpec((lines, quarter), lambda c, w: (0, w[0])))
    return run(
        factor_body,
        (depth // tile,),
        specs,
        pl.BlockSpec((tile, quarter), lambda c, w: (c, 0)),
        shape((depth, quarter)),
        flops=2 * lines * len(pairs) * depth * quarter,
        bytes_accessed=4 * depth * quarter,
        prefetch=1,
    )(which, *[array for pair in pairs for array in pair])


def on_device(
    pixels,
    crop_map,
    queue_rows,
    conv_in,
    gain_one,
    shift_one,
    conv_mid,
    gain_two,
    shift_two,
    conv_out,
    gain_three,
    shift_three,
    head_weight,
    head_gain,
    head_shift,
    embed_weight,
    embed_bias,
    prototypes,
):
    micro, canvas, pixel_count, channels = pixels.shape
    devices = lax.axis_size("dp") * lax.axis_size("hst")
    crops = canvas * SLOTS
    total_crops = crops * devices * 1.0
    loss_scale = 1.0 / (micro * total_crops)
    half = lax.axis_index("hst") % 2
    keep_half = half.astype(jnp.int32).reshape(1)
    send_half = 1 - keep_half
    quarter = lax.axis_index("hst").astype(jnp.int32).reshape(1)

    x = pixels.reshape(micro * canvas * pixel_count, channels)
    valid = (crop_map < SLOTS).astype(F32).reshape(-1, 1)
    sizes = jnp.sum(
        (crop_map[:, :, None, :] == jnp.arange(SLOTS, dtype=jnp.int32)[:, None]).astype(F32), 3
    ).reshape(-1, 1)

    def across(vector):
        return jnp.broadcast_to(vector, (micro,) + vector.shape)

    h1, stats = first_product(x, conv_in, valid, micro)
    mean_one, spread, count, counts = first_merge(stats)
    scaled_one = lax.rsqrt(spread / count + eps_norm)
    coef = jnp.stack([mean_one, scaled_one * gain_one, across(shift_one)], 1)
    act_one, h2, stats = second_product(h1, valid, coef, conv_mid, micro)
    mean_two, spread = merge_moments(stats, counts)
    scaled_two = lax.rsqrt(spread / count + eps_norm)
    coef = jnp.stack([mean_two, scaled_two * gain_two, across(shift_two)], 1)
    act_two, h3, stats = third_product(h2, valid, coef, conv_out, micro)
    mean_three, spread = merge_moments(stats, counts)
    scaled_three = lax.rsqrt(spread / count + eps_norm)
    coef = jnp.stack([mean_three, scaled_three, across(gain_three), across(shift_three)], 1)
    feat, slope_first, slope_second, slope, norm_three = pool(h3, x, valid, coef, sizes, micro)
    g, stats = head_product(feat, head_weight, micro)
    crop_counts = []
    members = crops * 1.0
    for group in sync_groups():
        crop_counts.append([members] * (len(group) + 1))
        members = members * (len(group) + 1)
    mean_four, spread = merge_moments(stats, crop_counts)
    scaled_four = lax.rsqrt(spread / total_crops + eps_norm)

    shaped = g.reshape(micro, crops, -1)
    norm_four = (shaped - mean_four[:, None]) * scaled_four[:, None]
    pre_four = norm_four * head_gain + head_shift
    act_four = jax.nn.silu(pre_four).astype(BF16).reshape(micro * crops, -1)
    embedded = jnp.dot(act_four, embed_weight, preferred_element_type=F32) + embed_bias
    inverse = lax.rsqrt(jnp.sum(embedded * embedded, 1, keepdims=True) + eps_unit)
    unit_rows = (embedded * inverse).astype(BF16)
    logits = jnp.dot(unit_rows, prototypes, preferred_element_type=F32)
    queued = jnp.dot(queue_rows, prototypes, preferred_element_type=F32)
    batch = jnp.exp(logits / transport_epsilon).reshape(micro, crops, -1)
    queue = jnp.broadcast_to(
        jnp.exp(queued / transport_epsilon)[None], (micro,) + queued.shape
    )
    for sweep in range(SINK_ITERS):
        column = total_sum(jnp.sum(batch, 1) + jnp.sum(queue, 1))[:, None]
        batch = batch / column
        batch = batch / jnp.sum(batch, 2, keepdims=True)
        if sweep + 1 < SINK_ITERS:
            queue = queue / column
            queue = queue / jnp.sum(queue, 2, keepdims=True)
    pairs = batch.reshape(micro * crops // 2, 2, -1)
    partner = jnp.stack([pairs[:, 1], pairs[:, 0]], 1).reshape(micro * crops, -1)
    log_likelihoods = jax.nn.log_softmax(logits / softmax_sharpness, -1)
    loss_local = -jnp.sum(partner * log_likelihoods) * loss_scale
    grad_scores = (
        loss_scale
        * (jnp.sum(partner, 1, keepdims=True) * jnp.exp(log_likelihoods) - partner)
        / softmax_sharpness
    )
    grad_protos = jnp.dot(
        unit_rows.astype(F32).T, grad_scores, precision=highest, preferred_element_type=F32
    )
    grad_unit = jnp.dot(
        grad_scores, prototypes.astype(F32).T, precision=highest, preferred_element_type=F32
    )
    grad_embedded = inverse * grad_unit - embedded * inverse * inverse * inverse * jnp.sum(
        embedded * grad_unit, 1, keepdims=True
    )
    grad_embed = jnp.dot(
        act_four.astype(F32).T, grad_embedded, precision=highest, preferred_element_type=F32
    )
    grad_act_four = jnp.dot(
        grad_embedded, embed_weight.astype(F32).T, precision=highest, preferred_element_type=F32
    )
    dy_four = grad_act_four.reshape(micro, crops, -1) * slope_of(pre_four)
    width = dy_four.shape[-1]
    tail = jnp.zeros((1, width), F32)
    tail = tail.at[0, : embed_bias.shape[0]].set(jnp.sum(grad_embedded, 0))
    tail = tail.at[0, embed_bias.shape[0]].set(loss_local)
    payload = jnp.concatenate(
        [jnp.sum(dy_four, 1), jnp.sum(dy_four * norm_four, 1), tail], 0
    )
    payload = total_sum(payload)
    first_four, second_four = payload[:micro], payload[micro : 2 * micro]
    grad_bias = payload[2 * micro, : embed_bias.shape[0]]
    total_loss = payload[2 * micro, embed_bias.shape[0]]

    coef = jnp.stack(
        [
            mean_four,
            scaled_four,
            head_gain * scaled_four,
            first_four / total_crops,
            second_four / total_crops,
        ],
        1,
    )
    dg, wide, sums = head_back(
        dy_four.reshape(micro * crops, -1),
        g,
        coef,
        head_weight,
        sizes,
        slope_first,
        slope_second,
        micro,
    )
    sums = total_sum(sums)
    first_three, second_three = sums[:, 0], sums[:, 1]
    coef = jnp.stack(
        [gain_three * scaled_three, first_three / count, second_three / count], 1
    )
    coef2 = jnp.stack([mean_two, scaled_two, across(gain_two), across(shift_two)], 1)
    d_three, dy, sums = third_back(
        wide, slope, norm_three, valid, coef, conv_out, h2, coef2, micro
    )

    mine = jnp.concatenate([feat, dg], 0)
    across_y = swap(mine, 2)
    both = jnp.concatenate([mine, across_y], 0)
    other = swap(both, 1)
    lines = feat.shape[0]
    sets = [both[:2 * lines], both[2 * lines :], other[: 2 * lines], other[2 * lines :]]
    partial = factor_grad(quarter, [(s[:lines], s[lines:]) for s in sets])

    sums = total_sum(sums)
    first_two, second_two = sums[:, 0], sums[:, 1]
    coef = jnp.stack(
        [mean_two, scaled_two, gain_two * scaled_two, first_two / count, second_two / count], 1
    )
    d_two = norm_back(dy, h2, valid, coef, micro)
    coef1 = jnp.stack([mean_one, scaled_one, across(gain_one), across(shift_one)], 1)
    send_mid = taps_grad(send_half, act_one, d_two)
    keep_mid = taps_grad(keep_half, act_one, d_two)
    dy, sums = second_back(d_two, conv_mid, valid, h1, coef1, micro)
    sums = total_sum(sums)
    first_one, second_one = sums[:, 0], sums[:, 1]
    coef = jnp.stack(
        [mean_one, scaled_one, gain_one * scaled_one, first_one / count, second_one / count], 1
    )
    d_one = norm_back(dy, h1, valid, coef, micro)
    send_in = half_grad(send_half, x, d_one, 512)
    keep_in = half_grad(keep_half, x, d_one, 512)
    grad_x = pixels_grad(d_one, conv_in, wide, slope, micro)

    send_out = half_grad(send_half, act_two, d_three, 256)
    keep_out = half_grad(keep_half, act_two, d_three, 256)

    masks = dp_masks()
    grad_head = joined(joined(split_rows(partial, masks), 1, 1), 1, 2)
    grad_conv_out = reduce_weight(keep_out, send_out)
    grad_conv_mid = reduce_weight(keep_mid, send_mid)
    grad_conv_in = reduce_weight(keep_in, send_in)
    shards = lax.axis_size("dp")
    embed_rows = grad_embed.reshape(shards, 2, -1, grad_embed.shape[1])
    embed_part = halve(embed_rows, 1, 1).reshape(-1, grad_embed.shape[1])
    embed_part = joined(split_rows(embed_part, [2] + masks), 0, 2)
    grad_embed = joined(embed_part, 0, 1)
    protos = grad_protos.shape[1]
    padded = jnp.pad(grad_protos, ((0, 0), (0, -protos % 256)))
    folded = padded.reshape(padded.shape[0], 2, -1).swapaxes(0, 1)
    protos_part = joined(split_rows(halve(folded, 0, 1), [2] + masks), 0, 2)
    grad_protos = joined(protos_part, 1, 1)[:, :protos]

    return (
        total_loss,
        grad_x.reshape(pixels.shape),
        grad_conv_in,
        own_shard(jnp.sum(second_one, 0)),
        own_shard(jnp.sum(first_one, 0)),
        grad_conv_mid,
        own_shard(jnp.sum(second_two, 0)),
        own_shard(jnp.sum(first_two, 0)),
        grad_conv_out,
        own_shard(jnp.sum(second_three, 0)),
        own_shard(jnp.sum(first_three, 0)),
        grad_head,
        own_shard(jnp.sum(second_four, 0)),
        own_shard(jnp.sum(first_four, 0)),
        grad_embed,
        own_shard(grad_bias),
        grad_protos,
    )


def solution(mesh):
    placed = (
        P(None, ("dp", "hst"), None, None),
        P(None, ("dp", "hst"), None),
        P(("dp", "hst"), None),
    ) + (P(),) * 15
    return jax.shard_map(
        on_device,
        mesh=mesh,
        in_specs=placed,
        out_specs=(
            P(),
            P(None, ("dp", "hst"), None, None),
            P("dp", None),
            P("dp"),
            P("dp"),
            P("dp", None),
            P("dp"),
            P("dp"),
            P("dp", None),
            P("dp"),
            P("dp"),
            P("dp", None),
            P("dp"),
            P("dp"),
            P("dp", None),
            P("dp"),
            P("dp", None),
        ),
        check_vma=False,
    )
```

```python
import functools

import jax
import jax.numpy as jnp
from jax import lax
from jax.experimental import pallas as pl
from jax.experimental.pallas import tpu as pltpu
from jax.sharding import PartitionSpec as P

ROWS = 8
COLS = 16
SLOTS = 4
CELL = COLS // SLOTS
PIX = ROWS * COLS
SINK_ITERS = 3
TAPS = 9

eps_norm = 1e-05
eps_unit = 1e-06
transport_epsilon = 0.05
softmax_sharpness = 0.1
highest = lax.Precision.HIGHEST
F32 = jnp.float32
BF16 = jnp.bfloat16
AXES = ("dp", "hst")
MIB = 1 << 20


def swap(value, mask):
    count = lax.axis_size("dp") * lax.axis_size("hst")
    return lax.ppermute(value, AXES, [(i, i ^ mask) for i in range(count)])


def sync_groups():
    bits = (lax.axis_size("dp") * lax.axis_size("hst")).bit_length() - 1
    groups = [(1,)]
    bit = 1
    while bit < bits:
        if bit + 1 < bits:
            groups.append((1 << bit, 2 << bit, 3 << bit))
            bit += 2
        else:
            groups.append((1 << bit,))
            bit += 1
    return groups


def tree(parts):
    while len(parts) > 1:
        parts = [parts[i] + parts[i + 1] for i in range(0, len(parts), 2)]
    return parts[0]


def between(parts, gate, fillers):
    for filler in fillers:
        parts = list(tie(*parts, *filler(gate)))[: len(parts)]
    return parts


def pick(fillers, step):
    return fillers[step] if step < len(fillers) else ()


def sum_parts(value, fillers=()):
    groups = sync_groups()
    for step, group in enumerate(groups):
        parts = [value] + [swap(value, mask) for mask in group]
        parts = between(parts, value, pick(fillers, step))
        value = tree(parts)
    return parts


def merge(parts, members):
    whole = tree(list(members))
    mean = tree([n * part[:, 0] for n, part in zip(members, parts)]) / whole
    spread = tree(
        [part[:, 1] + n * (part[:, 0] - mean) ** 2 for n, part in zip(members, parts)]
    )
    return mean, spread, whole


def moment_parts(moments, counts, fillers=()):
    groups = sync_groups()
    for step, group in enumerate(groups):
        parts = [moments] + [swap(moments, mask) for mask in group]
        parts = between(parts, moments, pick(fillers, step))
        if step + 1 < len(groups):
            moments = jnp.stack(merge(parts, counts[step])[:2], 1)
    return parts


def first_parts(moments):
    groups = sync_groups()
    counts = []
    for step, group in enumerate(groups):
        parts = [moments] + [swap(moments, mask) for mask in group]
        if step + 1 < len(groups):
            members = [part[:, 2] for part in parts]
            moments = jnp.stack(merge(parts, members), 1)
            counts.append([n[:, :1] for n in members])
    return parts, counts


def bit_of(mask):
    index = lax.axis_index("dp") * lax.axis_size("hst") + lax.axis_index("hst")
    return (index // mask) % 2


def dp_masks():
    base = lax.axis_size("hst")
    return [base << j for j in range(lax.axis_size("dp").bit_length() - 1)]


def tie(first, *others):
    return lax.optimization_barrier((first,) + others)


def at(view, place, axis):
    return lax.dynamic_index_in_dim(view, place, axis, keepdims=False)


def core_swap(value, low, high):
    count = lax.axis_size("dp") * lax.axis_size("hst")
    pairs = [(i, i ^ (high if i % 2 else low)) for i in range(count)]
    return lax.ppermute(value, AXES, pairs)


def dp_halves(addends, mask, axis):
    bit = bit_of(mask)
    send = sum(at(array, 1 - bit, axis) for array in addends)
    return [at(array, bit, axis) for array in addends] + [swap(send, mask)]


def run(body, grid, in_specs, out_specs, out_shape, scratch=(), flops=0, bytes_accessed=0, prefetch=0, aliases=None):
    return pl.pallas_call(
        body,
        grid_spec=pltpu.PrefetchScalarGridSpec(
            num_scalar_prefetch=prefetch,
            grid=grid,
            in_specs=in_specs,
            out_specs=out_specs,
            scratch_shapes=list(scratch),
        ),
        out_shape=out_shape,
        name=body.__name__,
        input_output_aliases=aliases or {},
        compiler_params=pltpu.CompilerParams(
            vmem_limit_bytes=56 * MIB, dimension_semantics=("arbitrary",) * len(grid)
        ),
        cost_estimate=pl.CostEstimate(
            flops=flops, bytes_accessed=bytes_accessed, transcendentals=0
        ),
    )


def shape(dims, dtype=F32):
    return jax.ShapeDtypeStruct(tuple(dims), dtype)


def sigmoid(u):
    return 0.5 * jnp.tanh(0.5 * u) + 0.5


def norm_of(part_refs, members, m=0, lane=slice(None)):
    whole = tree(list(members))
    means = [ref[m, 0:1, lane] for ref in part_refs]
    mean = tree([n * one for n, one in zip(members, means)]) / whole
    spread = tree(
        [ref[m, 1:2, lane] + n * (one - mean) ** 2 for n, ref, one in zip(members, part_refs, means)]
    )
    return mean, lax.rsqrt(spread / whole + eps_norm)


def sums_of(part_refs, first, second, m=0):
    return (
        tree([ref[m, first : first + 1, :] for ref in part_refs]),
        tree([ref[m, second : second + 1, :] for ref in part_refs]),
    )


def counts_of(count_refs, m=0):
    return [ref[m, 2:3, 0:1] for ref in count_refs]


def whole(array):
    return pl.BlockSpec(array.shape, lambda *_: (0,) * len(array.shape))


def per_micro(array):
    return pl.BlockSpec((1,) + array.shape[1:], lambda m, *_: (m,) + (0,) * (array.ndim - 1))


def slope_of(u):
    s = sigmoid(u)
    return s * (1.0 + u * (1.0 - s))


def nt_dot(left, right):
    return lax.dot_general(left, right, (((1,), (1,)), ((), ())), preferred_element_type=F32)


def tn_dot(left, right):
    return lax.dot_general(left, right, (((0,), (0,)), ((), ())), preferred_element_type=F32)


def fold(y):
    return jnp.sum(y.reshape(y.shape[0] // 8, 8, y.shape[1]), 0)


def put_moments(stats_ref, h_ref, v_ref, with_count):
    rows, width = h_ref.shape
    chunk = 32
    lanes = 512
    v = v_ref[...]
    count = jnp.sum(v, axis=0, keepdims=True)
    first = jnp.sum(v[:PIX], axis=0, keepdims=True)
    for j in range(0, width, lanes):
        lane = slice(j, j + lanes)
        acc = jnp.zeros((8, lanes), F32)
        for i in range(0, PIX, chunk):
            acc += fold(h_ref[i : i + chunk, lane].astype(F32) * v_ref[i : i + chunk, :])
        pivot = jnp.sum(acc, axis=0, keepdims=True) / first
        line = jnp.zeros((8, lanes), F32)
        square = jnp.zeros((8, lanes), F32)
        for i in range(0, rows, chunk):
            off = (h_ref[i : i + chunk, lane].astype(F32) - pivot) * v_ref[i : i + chunk, :]
            line += fold(off)
            square += fold(off * off)
        total = jnp.sum(line, axis=0, keepdims=True)
        stats_ref[0, 0:1, lane] = pivot + total / count
        stats_ref[0, 1:2, lane] = (
            jnp.sum(square, axis=0, keepdims=True) - total * total / count
        )
        if with_count:
            stats_ref[0, 2:3, lane] = jnp.broadcast_to(count, (1, lanes))


def first_body(x_ref, w_ref, v_ref, h_ref, stats_ref):
    h_ref[...] = jnp.dot(x_ref[...], w_ref[...], preferred_element_type=F32)
    put_moments(stats_ref, h_ref, v_ref, True)


def first_product(x, weight, valid, micro):
    rows = x.shape[0] // micro
    depth, width = weight.shape
    return run(
        first_body,
        (micro,),
        [
            pl.BlockSpec((rows, depth), lambda m: (m, 0)),
            pl.BlockSpec((depth, width), lambda m: (0, 0)),
            pl.BlockSpec((rows, 1), lambda m: (m, 0)),
        ],
        [
            pl.BlockSpec((rows, width), lambda m: (m, 0)),
            pl.BlockSpec((1, 3, width), lambda m: (m, 0, 0)),
        ],
        [shape((micro * rows, width)), shape((micro, 3, width))],
        flops=2 * micro * rows * depth * width,
        bytes_accessed=2 * x.size,
    )(x, weight, valid)


def cell_column(rows):
    return lax.broadcasted_iota(jnp.int32, (rows, 1), 0) % CELL


def second_body(counts, refs):
    part_refs, (h_ref, v_ref, gain_ref, shift_ref, w_ref, a_ref, h2_ref, stats_ref, info_ref, cols_ref) = refs[:counts], refs[counts:]
    rows, width = h_ref.shape
    members = counts_of(part_refs)
    mean, scaled = norm_of(part_refs, members)
    info_ref[0, 0:1, :] = mean
    info_ref[0, 1:2, :] = scaled
    info_ref[0, 2:3, :] = jnp.broadcast_to(tree(list(members)), mean.shape)
    factor = scaled * gain_ref[...]
    shift = shift_ref[...]
    place = cell_column(COLS)
    has_left = (place >= 1).astype(F32)
    has_right = (place <= CELL - 2).astype(F32)
    blank = jnp.zeros((COLS, width), BF16)
    for i in range(0, rows, COLS):
        at = slice(i, i + COLS)
        pre = (h_ref[at, :] - mean) * factor + shift
        act = (pre * sigmoid(pre) * v_ref[at, :]).astype(BF16)
        a_ref[at, :] = act
        wide = act.astype(F32)
        sides = (
            (pltpu.roll(wide, 1, 0) * has_left).astype(BF16),
            act,
            (pltpu.roll(wide, COLS - 1, 0) * has_right).astype(BF16),
        )
        for c in range(3):
            cols_ref[at, (3 + c) * width : (4 + c) * width] = sides[c]
            if i % PIX < PIX - COLS:
                cols_ref[i + COLS : i + 2 * COLS, c * width : (c + 1) * width] = sides[c]
            else:
                cols_ref[at, (6 + c) * width : (7 + c) * width] = blank
            if i % PIX > 0:
                cols_ref[i - COLS : i, (6 + c) * width : (7 + c) * width] = sides[c]
            else:
                cols_ref[at, c * width : (c + 1) * width] = blank
    h2_ref[...] = jnp.dot(cols_ref[...], w_ref[...], preferred_element_type=F32)
    put_moments(stats_ref, h2_ref, v_ref, False)


def named(name, body, *fixed):
    def kernel(*refs):
        body(*fixed, refs)

    kernel.__name__ = name
    return kernel


def second_product(parts, h1, valid, gain, shift, weight, micro):
    rows, width = h1.shape[0] // micro, h1.shape[1]
    mid = pl.BlockSpec((rows, width), lambda m: (m, 0))
    return run(
        named("second_product", second_body, len(parts)),
        (micro,),
        [per_micro(part) for part in parts]
        + [
            mid,
            pl.BlockSpec((rows, 1), lambda m: (m, 0)),
            whole(gain),
            whole(shift),
            whole(weight),
        ],
        [
            mid,
            mid,
            pl.BlockSpec((1, 2, width), lambda m: (m, 0, 0)),
            pl.BlockSpec((1, 3, width), lambda m: (m, 0, 0)),
        ],
        [
            shape((micro * rows, width), BF16),
            shape((micro * rows, width)),
            shape((micro, 2, width)),
            shape((micro, 3, width)),
        ],
        [pltpu.VMEM((rows, weight.shape[0]), BF16)],
        flops=2 * micro * rows * weight.size,
        bytes_accessed=10 * h1.size,
    )(*parts, h1, valid, gain, shift, weight)


def third_body(counts, refs):
    part_refs, count_refs = refs[:counts], refs[counts : 2 * counts]
    h_ref, v_ref, gain_ref, shift_ref, w_ref, a_ref, h3_ref, stats_ref, info_ref, wide_ref = refs[2 * counts :]
    rows = h_ref.shape[0]
    mean, scaled = norm_of(part_refs, counts_of(count_refs))
    info_ref[0, 0:1, :] = mean
    info_ref[0, 1:2, :] = scaled
    factor = scaled * gain_ref[...]
    shift = shift_ref[...]
    for i in range(0, rows, 32):
        at = slice(i, i + 32)
        pre = (h_ref[at, :] - mean) * factor + shift
        a_ref[at, :] = (pre * sigmoid(pre) * v_ref[at, :]).astype(BF16)
    wide_ref[...] = jnp.dot(a_ref[...], w_ref[...], preferred_element_type=F32)
    h3_ref[...] = wide_ref[...].astype(BF16)
    put_moments(stats_ref, wide_ref, v_ref, False)


def third_product(parts, members, h2, valid, gain, shift, weight, micro):
    rows, depth = h2.shape[0] // micro, h2.shape[1]
    width = weight.shape[1]
    mid = pl.BlockSpec((rows, depth), lambda m: (m, 0))
    return run(
        named("third_product", third_body, len(parts)),
        (micro,),
        [per_micro(part) for part in parts + members]
        + [
            mid,
            pl.BlockSpec((rows, 1), lambda m: (m, 0)),
            whole(gain),
            whole(shift),
            whole(weight),
        ],
        [
            mid,
            pl.BlockSpec((rows, width), lambda m: (m, 0)),
            pl.BlockSpec((1, 2, width), lambda m: (m, 0, 0)),
            pl.BlockSpec((1, 2, depth), lambda m: (m, 0, 0)),
        ],
        [
            shape((micro * rows, depth), BF16),
            shape((micro * rows, width), BF16),
            shape((micro, 2, width)),
            shape((micro, 2, depth)),
        ],
        [pltpu.VMEM((rows, width), F32)],
        flops=2 * micro * rows * weight.size,
        bytes_accessed=4 * micro * rows * width,
    )(*parts, *members, h2, valid, gain, shift, weight)


def crop_sums(lines):
    crops = lines.shape[0] // CELL
    chosen = (
        lax.broadcasted_iota(jnp.int32, (crops, lines.shape[0]), 1) // CELL
        == lax.broadcasted_iota(jnp.int32, (crops, lines.shape[0]), 0)
    ).astype(F32)
    return jnp.dot(chosen, lines, precision=highest, preferred_element_type=F32)


def pool_body(counts, refs):
    part_refs, count_refs = refs[:counts], refs[counts : 2 * counts]
    h_ref, x_ref, v_ref, gain_ref, shift_ref, size_ref, feat_ref, info_ref, sums_ref = refs[2 * counts :]
    rows, width = h_ref.shape
    mean, scaled = norm_of(part_refs, counts_of(count_refs))
    info_ref[0, 0:1, :] = mean
    info_ref[0, 1:2, :] = scaled
    factor = scaled * gain_ref[...]
    shift = shift_ref[...]
    for j in range(0, width, 512):
        lane = slice(j, j + 512)
        for k in range(rows // PIX):
            acc = jnp.zeros((COLS, 512), F32)
            for r in range(ROWS):
                at = pl.ds(k * PIX + r * COLS, COLS)
                resid = (
                    (h_ref[at, lane].astype(F32) - mean[:, lane]) * factor[:, lane]
                    + shift[:, lane]
                    + x_ref[at, lane].astype(F32)
                )
                out = resid * (sigmoid(resid) * v_ref[at, :])
                acc += out.astype(BF16).astype(F32)
            sums_ref[pl.ds(k * COLS, COLS), lane] = acc
    feat_ref[...] = (crop_sums(sums_ref[...]) / size_ref[...]).astype(BF16).astype(F32)


def pool(parts, members, h3, x, valid, gain, shift, sizes, micro):
    rows, channels = h3.shape[0] // micro, h3.shape[1]
    crops = sizes.shape[0] // micro
    width = 1024
    tile = pl.BlockSpec((rows, width), lambda m, c: (m, c))
    line = pl.BlockSpec((1, width), lambda m, c: (0, c))
    pair = pl.BlockSpec((1, 2, width), lambda m, c: (m, 0, c))
    return run(
        named("pool", pool_body, len(parts)),
        (micro, channels // width),
        [pair] * len(parts)
        + [per_micro(part) for part in members]
        + [
            tile,
            tile,
            pl.BlockSpec((rows, 1), lambda m, c: (m, 0)),
            line,
            line,
            pl.BlockSpec((crops, 1), lambda m, c: (m, 0)),
        ],
        [pl.BlockSpec((crops, width), lambda m, c: (m, c)), pair],
        [shape((micro * crops, channels)), shape((micro, 2, channels))],
        [pltpu.VMEM((rows // ROWS, width), F32)],
        flops=20 * h3.size,
        bytes_accessed=4 * h3.size,
    )(*parts, *members, h3, x, valid, gain, shift, sizes)


def slope_body(*refs):
    h_ref, x_ref, v_ref, info_ref, gain_ref, shift_ref = refs[:6]
    slope_ref, first_ref, second_ref, sums_ref = refs[-4:]
    rows, width = h_ref.shape
    mean = info_ref[0, 0:1, :]
    scaled = info_ref[0, 1:2, :]
    factor = scaled * gain_ref[...]
    shift = shift_ref[...]
    for j in range(0, width, 512):
        lane = slice(j, j + 512)
        for k in range(rows // PIX):
            acc_first = jnp.zeros((COLS, 512), F32)
            acc_second = jnp.zeros((COLS, 512), F32)
            for r in range(ROWS):
                at = pl.ds(k * PIX + r * COLS, COLS)
                centred = h_ref[at, lane].astype(F32) - mean[:, lane]
                resid = centred * factor[:, lane] + shift[:, lane] + x_ref[at, lane].astype(F32)
                sig = sigmoid(resid)
                kept = sig * v_ref[at, :]
                slope = kept + resid * kept * (1.0 - sig)
                acc_first += slope
                acc_second += slope * centred
                slope_ref[at, lane] = slope.astype(BF16)
            place = pl.ds(k * COLS, COLS)
            sums_ref[0, place, lane] = acc_first
            sums_ref[1, place, lane] = acc_second * scaled[:, lane]
    first_ref[...] = crop_sums(sums_ref[0])
    second_ref[...] = crop_sums(sums_ref[1])


def slope_part(h3, x, valid, info, gain, shift, micro, index, earlier):
    rows, channels = h3.shape[0] // micro, h3.shape[1]
    crops = rows // PIX * SLOTS
    width = 1024
    tile = pl.BlockSpec((rows, width), lambda c: (index, c))
    small = pl.BlockSpec((crops, width), lambda c: (index, c))
    return run(
        slope_body,
        (channels // width,),
        [
            tile,
            tile,
            pl.BlockSpec((rows, 1), lambda c: (index, 0)),
            pl.BlockSpec((1, 2, width), lambda c: (index, 0, c)),
            pl.BlockSpec((1, width), lambda c: (0, c)),
            pl.BlockSpec((1, width), lambda c: (0, c)),
        ]
        + [pl.BlockSpec(memory_space=pl.ANY)] * len(earlier),
        [tile, small, small],
        [
            shape(h3.shape, BF16),
            shape((micro * crops, channels)),
            shape((micro * crops, channels)),
        ],
        [pltpu.VMEM((2, rows // ROWS, width), F32)],
        flops=30 * rows * channels,
        bytes_accessed=6 * rows * channels,
        aliases={6 + i: i for i in range(len(earlier))},
    )(h3, x, valid, info, gain, shift, *earlier)


def head_body(feat_ref, w_ref, g_ref, stats_ref):
    g = jnp.dot(feat_ref[...].astype(BF16), w_ref[...], preferred_element_type=F32)
    g_ref[...] = g
    micro = stats_ref.shape[0]
    crops = g.shape[0] // micro
    for m in range(micro):
        part = g[m * crops : (m + 1) * crops]
        mean = jnp.sum(part, axis=0, keepdims=True) / crops
        stats_ref[m, 0:1, :] = mean
        stats_ref[m, 1:2, :] = jnp.sum((part - mean) ** 2, axis=0, keepdims=True)


def head_product(feat, weight, micro):
    lines = feat.shape[0]
    depth, width = weight.shape
    tile = 512
    return run(
        head_body,
        (width // tile,),
        [
            pl.BlockSpec((lines, depth), lambda c: (0, 0)),
            pl.BlockSpec((depth, tile), lambda c: (0, c)),
        ],
        [
            pl.BlockSpec((lines, tile), lambda c: (0, c)),
            pl.BlockSpec((micro, 2, tile), lambda c: (0, 0, c)),
        ],
        [shape((lines, width)), shape((micro, 2, width))],
        flops=2 * lines * weight.size,
        bytes_accessed=2 * weight.size,
    )(feat, weight)


def head_back_body(total_crops, counts, refs):
    part_refs = refs[:counts]
    dy_ref, g_ref, info_ref, gain_ref, w_ref, size_ref, first_ref, second_ref, dg_ref, wide_ref, stats_ref, low_ref = refs[counts:]
    micro = stats_ref.shape[0]
    lines = dy_ref.shape[0]
    crops = lines // micro

    @pl.when(pl.program_id(0) == 0)
    def _():
        for m in range(micro):
            at = pl.ds(m * crops, crops)
            one = tree([ref[m : m + 1, :] for ref in part_refs]) / total_crops
            two = tree([ref[micro + m : micro + m + 1, :] for ref in part_refs]) / total_crops
            scaled = info_ref[m, 1:2, :]
            normal = (g_ref[at, :] - info_ref[m, 0:1, :]) * scaled
            dg = gain_ref[...] * scaled * (dy_ref[at, :] - (one + normal * two))
            low = dg.astype(BF16)
            low_ref[at, :] = low
            dg_ref[at, :] = low.astype(F32)

    per_crop = nt_dot(low_ref[...], w_ref[...]) / size_ref[...]
    lift = (
        lax.broadcasted_iota(jnp.int32, (lines * CELL, lines), 0) // CELL
        == lax.broadcasted_iota(jnp.int32, (lines * CELL, lines), 1)
    ).astype(F32)
    wide_ref[...] = jnp.dot(lift, per_crop, precision=highest, preferred_element_type=F32)
    one = per_crop * first_ref[...]
    two = per_crop * second_ref[...]
    for m in range(micro):
        at = slice(m * crops, (m + 1) * crops)
        stats_ref[m, 0:1, :] = jnp.sum(one[at], axis=0, keepdims=True)
        stats_ref[m, 1:2, :] = jnp.sum(two[at], axis=0, keepdims=True)


def head_back(parts, dy, g, info, gain, weight, sizes, first, second, total_crops):
    lines, width = dy.shape
    channels = weight.shape[0]
    micro = info.shape[0]
    tile = 512
    part = pl.BlockSpec((lines, tile), lambda c: (0, c))
    return run(
        named("head_back", head_back_body, total_crops, len(parts)),
        (channels // tile,),
        [whole(a) for a in parts]
        + [
            whole(dy),
            whole(g),
            whole(info),
            whole(gain),
            pl.BlockSpec((tile, width), lambda c: (c, 0)),
            whole(sizes),
            part,
            part,
        ],
        [
            whole(dy),
            pl.BlockSpec((lines * CELL, tile), lambda c: (0, c)),
            pl.BlockSpec((micro, 2, tile), lambda c: (0, 0, c)),
        ],
        [shape((lines, width)), shape((lines * CELL, channels)), shape((micro, 2, channels))],
        [pltpu.VMEM((lines, width), BF16)],
        flops=2 * lines * weight.size,
        bytes_accessed=2 * weight.size,
    )(*parts, dy, g, info, gain, weight, sizes, first, second)


def third_back_body(counts, refs):
    part_refs = refs[:counts]
    wide_ref, slope_ref, h3_ref, v_ref, info3_ref, gain3_ref, info1_ref, w_ref, h2_ref, info2_ref, gain2_ref, shift2_ref, d_ref, dy_ref, stats_ref = refs[counts:]
    rows, channels = slope_ref.shape
    number = info1_ref[0, 2:3, 0:1]
    first, second = sums_of(part_refs, 0, 1)
    mean = info3_ref[0, 0:1, :]
    scaled = info3_ref[0, 1:2, :]
    factor = gain3_ref[...] * scaled
    one = factor * first / number
    two = factor * scaled * second / number
    for j in range(0, channels, 512):
        lane = slice(j, j + 512)
        for k in range(rows // PIX):
            wide = wide_ref[pl.ds(k * COLS, COLS), lane] * factor[:, lane]
            for r in range(ROWS):
                at = pl.ds(k * PIX + r * COLS, COLS)
                back = one[:, lane] + (h3_ref[at, lane].astype(F32) - mean[:, lane]) * two[:, lane]
                d = wide * slope_ref[at, lane].astype(F32) - v_ref[at, :] * back
                d_ref[at, lane] = d.astype(BF16)
    dy_ref[...] = nt_dot(d_ref[...], w_ref[...])
    put_back(dy_ref, h2_ref, v_ref, info2_ref, gain2_ref, shift2_ref, stats_ref)


def put_back(dy_ref, h_ref, v_ref, info_ref, gain_ref, shift_ref, stats_ref):
    rows, width = dy_ref.shape
    first = jnp.zeros((8, width), F32)
    second = jnp.zeros((8, width), F32)
    for i in range(0, rows, 32):
        at = slice(i, i + 32)
        normal = (h_ref[at, :] - info_ref[0, 0:1, :]) * info_ref[0, 1:2, :]
        pre = normal * gain_ref[...] + shift_ref[...]
        dy = dy_ref[at, :] * v_ref[at, :] * slope_of(pre)
        dy_ref[at, :] = dy
        first += fold(dy)
        second += fold(dy * normal)
    stats_ref[0, 0:1, :] = jnp.sum(first, axis=0, keepdims=True)
    stats_ref[0, 1:2, :] = jnp.sum(second, axis=0, keepdims=True)


def third_back(parts, wide, slope, h3, valid, info3, gain3, info1, weight, h2, info2, gain2, shift2, micro):
    rows, channels = slope.shape[0] // micro, slope.shape[1]
    middle = weight.shape[0]
    lines = wide.shape[0] // micro
    big = pl.BlockSpec((rows, channels), lambda m: (m, 0))
    mid = pl.BlockSpec((rows, middle), lambda m: (m, 0))
    return run(
        named("third_back", third_back_body, len(parts)),
        (micro,),
        [per_micro(part) for part in parts]
        + [
            pl.BlockSpec((lines, channels), lambda m: (m, 0)),
            big,
            big,
            pl.BlockSpec((rows, 1), lambda m: (m, 0)),
            per_micro(info3),
            whole(gain3),
            per_micro(info1),
            whole(weight),
            mid,
            per_micro(info2),
            whole(gain2),
            whole(shift2),
        ],
        [big, mid, pl.BlockSpec((1, 2, middle), lambda m: (m, 0, 0))],
        [shape(slope.shape, BF16), shape(h2.shape), shape((micro, 2, middle))],
        flops=2 * slope.shape[0] * weight.size,
        bytes_accessed=6 * slope.size,
    )(*parts, wide, slope, h3, valid, info3, gain3, info1, weight, h2, info2, gain2, shift2)


def out_grad_body(which_ref, left_ref, right_ref, out_ref, turned_ref):
    @pl.when(pl.program_id(0) == 0)
    def _():
        turned_ref[...] = left_ref[...].T

    grad = jnp.dot(turned_ref[...], right_ref[...], preferred_element_type=F32)
    out_ref[0] = grad.reshape(out_ref.shape[1:])


def out_grad(which, left, right, shards):
    rows, depth = left.shape
    half = right.shape[1] // 2
    tile = 512
    steps = half // tile
    lines = depth // shards

    def column(c, w):
        return jnp.where(c // steps == 0, w[0], 1 - w[0]) * steps + c % steps

    return run(
        out_grad_body,
        (2 * steps,),
        [
            pl.BlockSpec(left.shape, lambda c, w: (0, 0)),
            pl.BlockSpec((rows, tile), lambda c, w: (0, column(c, w))),
        ],
        pl.BlockSpec((1, shards, lines, tile), lambda c, w: (c // steps, 0, c % steps, 0)),
        shape((2, shards, steps * lines, tile)),
        [pltpu.VMEM((depth, rows), BF16)],
        flops=2 * rows * depth * right.shape[1],
        bytes_accessed=2 * left.size + 2 * right.size + 8 * depth * half,
        prefetch=1,
    )(which, left, right)


def put_norm_back(part_refs, dy_ref, h_ref, v_ref, info_ref, number_ref, gain_ref, d_ref):
    micro = info_ref.shape[0]
    rows = dy_ref.shape[0] // micro
    for m in range(micro):
        number = number_ref[m, 2:3, 0:1]
        first, second = sums_of(part_refs, 0, 1, m)
        scaled = info_ref[m, 1:2, :]
        factor = gain_ref[...] * scaled
        one = factor * first / number
        two = factor * scaled * second / number
        mean = info_ref[m, 0:1, :]
        for i in range(m * rows, (m + 1) * rows, 32):
            at = slice(i, i + 32)
            back = one + (h_ref[at, :] - mean) * two
            d_ref[at, :] = (factor * dy_ref[at, :] - v_ref[at, :] * back).astype(BF16)


def put_sides(a_ref, sides_ref):
    rows, width = a_ref.shape
    blank = jnp.zeros((COLS, width), BF16)
    place = cell_column(COLS)
    has_left = (place >= 1).astype(F32)
    has_right = (place <= CELL - 2).astype(F32)
    for k in range(rows // PIX):
        for c in range(3):
            sides_ref[c, k, 0:COLS, :] = blank
            sides_ref[c, k, COLS + PIX :, :] = blank
        for r in range(ROWS):
            act = a_ref[k * PIX + r * COLS : k * PIX + (r + 1) * COLS, :]
            wide = act.astype(F32)
            at = slice((r + 1) * COLS, (r + 2) * COLS)
            sides_ref[0, k, at, :] = (pltpu.roll(wide, 1, 0) * has_left).astype(BF16)
            sides_ref[1, k, at, :] = act
            sides_ref[2, k, at, :] = (pltpu.roll(wide, COLS - 1, 0) * has_right).astype(BF16)


def put_tap(out_ref, sides_ref, turned_ref):
    tap = pl.program_id(0)
    _, canvases, _, width = sides_ref.shape
    start = pl.multiple_of(tap // 3 * COLS, COLS)
    left = sides_ref[tap % 3, :, pl.ds(start, PIX), :].reshape(canvases * PIX, width)
    out_ref[...] = jnp.dot(turned_ref[...], left, preferred_element_type=F32).T


def half_of(which_ref, d_ref):
    half = d_ref.shape[1] // 2
    return d_ref[:, pl.ds(pl.multiple_of(which_ref[0] * half, half), half)]


def mid_first_body(counts, refs):
    which_ref, part_refs = refs[0], refs[1 : 1 + counts]
    dy_ref, h_ref, v_ref, info_ref, number_ref, gain_ref, a_ref, d_ref, out_ref, sides_ref, turned_ref = refs[1 + counts :]

    @pl.when(pl.program_id(0) == 0)
    def _():
        put_norm_back(part_refs, dy_ref, h_ref, v_ref, info_ref, number_ref, gain_ref, d_ref)
        turned_ref[...] = half_of(which_ref, d_ref).T
        put_sides(a_ref, sides_ref)

    put_tap(out_ref, sides_ref, turned_ref)


def mid_second_body(refs):
    which_ref, d_ref, a_ref, out_ref, sides_ref, turned_ref = refs

    @pl.when(pl.program_id(0) == 0)
    def _():
        turned_ref[...] = half_of(which_ref, d_ref).T
        put_sides(a_ref, sides_ref)

    put_tap(out_ref, sides_ref, turned_ref)


def mid_grad(name, body, which, ins, act, with_d):
    rows, width = act.shape
    half = width // 2
    grad = pl.BlockSpec((width, half), lambda t, w: (t, 0))
    return run(
        named(name, body, *([len(ins) - 7] if with_d else [])),
        (TAPS,),
        [whole(a) for a in ins],
        [whole(act), grad] if with_d else grad,
        [shape(act.shape, BF16), shape((TAPS * width, half))]
        if with_d
        else shape((TAPS * width, half)),
        [
            pltpu.VMEM((3, rows // PIX, PIX + 2 * COLS, width), BF16),
            pltpu.VMEM((half, rows), BF16),
        ],
        flops=2 * rows * TAPS * width * half,
        bytes_accessed=4 * TAPS * width * half,
        prefetch=1,
    )(which, *ins)


def in_grad_body(counts, refs):
    which_ref, part_refs = refs[0], refs[1 : 1 + counts]
    dy_ref, h_ref, v_ref, info_ref, number_ref, gain_ref, x_ref, d_ref, send_ref, keep_ref, turned_ref = refs[1 + counts :]

    @pl.when(pl.program_id(0) == 0)
    def _():
        put_norm_back(part_refs, dy_ref, h_ref, v_ref, info_ref, number_ref, gain_ref, d_ref)
        turned_ref[...] = d_ref[...].T

    grad = jnp.dot(turned_ref[...], x_ref[...], preferred_element_type=F32).T
    half = grad.shape[1] // 2
    low = which_ref[0] == 0
    left, right = grad[:, :half], grad[:, half:]
    send_ref[...] = jnp.where(low, left, right)
    keep_ref[...] = jnp.where(low, right, left)


def in_grad(which, parts, dy, h, valid, info, number, gain, x):
    rows, width = dy.shape
    depth = x.shape[1]
    half = width // 2
    tile = 512
    ins = [*parts, dy, h, valid, info, number, gain]
    grad = pl.BlockSpec((tile, half), lambda c, w: (c, 0))
    return run(
        named("in_grad", in_grad_body, len(parts)),
        (depth // tile,),
        [whole(a) for a in ins] + [pl.BlockSpec((rows, tile), lambda c, w: (0, c))],
        [whole(dy), grad, grad],
        [shape(dy.shape, BF16), shape((depth, half)), shape((depth, half))],
        [pltpu.VMEM((width, rows), BF16)],
        flops=2 * rows * depth * width,
        bytes_accessed=2 * x.size + 4 * depth * width + 10 * dy.size,
        prefetch=1,
    )(which, *ins, x)


def second_back_body(d_ref, w_ref, v_ref, h1_ref, info_ref, gain_ref, shift_ref, dy_ref, stats_ref, moved_ref, packed_ref):
    rows, width = d_ref.shape

    @pl.when(pl.program_id(0) == 0)
    def _():
        for r in range(3):
            for c in range(3):
                tap = 3 * r + c
                packed_ref[c, :, r * width : (r + 1) * width] = w_ref[
                    tap * width : (tap + 1) * width, :
                ]

    blank = jnp.zeros((COLS, width), BF16)
    for k in range(0, rows, PIX):
        moved_ref[k : k + PIX - COLS, 0:width] = d_ref[k + COLS : k + PIX, :]
        moved_ref[k + PIX - COLS : k + PIX, 0:width] = blank
        moved_ref[k : k + COLS, 2 * width :] = blank
        moved_ref[k + COLS : k + PIX, 2 * width :] = d_ref[k : k + PIX - COLS, :]
    moved_ref[:, width : 2 * width] = d_ref[...]
    parts = [nt_dot(moved_ref[...], packed_ref[c]) for c in range(3)]
    place = cell_column(rows)
    dy_ref[...] = (
        parts[1]
        + pltpu.roll(parts[2], 1, 0) * (place >= 1).astype(F32)
        + pltpu.roll(parts[0], rows - 1, 0) * (place <= CELL - 2).astype(F32)
    )
    put_back(dy_ref, h1_ref, v_ref, info_ref, gain_ref, shift_ref, stats_ref)


def second_back(d, weight, valid, h1, info, gain, shift, micro):
    rows, width = d.shape[0] // micro, d.shape[1]
    mid = pl.BlockSpec((rows, width), lambda m: (m, 0))
    return run(
        second_back_body,
        (micro,),
        [
            mid,
            whole(weight),
            pl.BlockSpec((rows, 1), lambda m: (m, 0)),
            mid,
            per_micro(info),
            whole(gain),
            whole(shift),
        ],
        [mid, pl.BlockSpec((1, 2, width), lambda m: (m, 0, 0))],
        [shape(d.shape), shape((micro, 2, width))],
        [pltpu.VMEM((rows, 3 * width), BF16), pltpu.VMEM((3, width, 3 * width), BF16)],
        flops=2 * micro * rows * weight.size,
        bytes_accessed=10 * d.size,
    )(d, weight, valid, h1, info, gain, shift)


def pixels_body(d_ref, w_ref, wide_ref, slope_ref, out_ref):
    rows, channels = out_ref.shape
    width = 512
    for j in range(0, channels, width):
        lane = pl.ds(j, width)
        grad = nt_dot(d_ref[...], w_ref[lane, :])
        for k in range(rows // PIX):
            wide = wide_ref[pl.ds(k * COLS, COLS), lane]
            for r in range(ROWS):
                first = k * PIX + r * COLS
                at = pl.ds(first, COLS)
                out_ref[at, lane] = (
                    grad[first : first + COLS] + wide * slope_ref[at, lane].astype(F32)
                ).astype(BF16)


def pixels_grad(d, weight, wide, slope, micro):
    rows, channels = slope.shape[0] // micro, slope.shape[1]
    lines = wide.shape[0] // micro
    big = pl.BlockSpec((rows, channels), lambda m: (m, 0))
    return run(
        pixels_body,
        (micro,),
        [
            pl.BlockSpec((rows, d.shape[1]), lambda m: (m, 0)),
            pl.BlockSpec(weight.shape, lambda m: (0, 0)),
            pl.BlockSpec((lines, channels), lambda m: (m, 0)),
            big,
        ],
        big,
        shape(slope.shape, BF16),
        flops=2 * slope.shape[0] * weight.size,
        bytes_accessed=4 * slope.size,
    )(d, weight, wide, slope)


def factor_body(feat_ref, other_feat_ref, dg_ref, far_ref, near_ref, both_ref, out_ref):
    left = jnp.concatenate([feat_ref[...], other_feat_ref[...]], 0).astype(BF16)
    lines = dg_ref.shape[0] // 2
    right = jnp.concatenate(
        [
            ref[c * lines : (c + 1) * lines, :]
            for c in range(2)
            for ref in (dg_ref, near_ref, far_ref, both_ref)
        ],
        0,
    ).astype(BF16)
    out_ref[...] = tn_dot(left, right)


def factor_grad(feat, other_feat, dg, far, near, both):
    lines, depth = feat.shape
    width = dg.shape[1]
    tile = 512
    left = pl.BlockSpec((lines, tile), lambda c: (0, c))
    return run(
        factor_body,
        (depth // tile,),
        [left, left] + [whole(dg)] * 4,
        pl.BlockSpec((tile, width), lambda c: (c, 0)),
        shape((depth, width)),
        flops=4 * lines * depth * width,
        bytes_accessed=4 * depth * width,
    )(feat, other_feat, dg, far, near, both)


def embed_body(protos, counts, members, refs):
    part_refs = refs[:counts]
    g_ref, gain_ref, shift_ref, w_ref, bias_ref, table_ref, queue_ref, act_ref, z_ref, inverse_ref, unit_ref, logits_ref, batch_ref, line_ref, sums_ref, info_ref = refs[counts:]
    micro = info_ref.shape[0]
    crops = g_ref.shape[0] // micro
    for m in range(micro):
        at = slice(m * crops, (m + 1) * crops)
        mean, scaled = norm_of(part_refs, members, m)
        info_ref[m, 0:1, :] = mean
        info_ref[m, 1:2, :] = scaled
        pre = (g_ref[at, :] - mean) * scaled * gain_ref[...] + shift_ref[...]
        act_ref[at, :] = (pre * sigmoid(pre)).astype(BF16)
    z = jnp.dot(act_ref[...], w_ref[...], preferred_element_type=F32) + bias_ref[...]
    inverse = lax.rsqrt(jnp.sum(z * z, 1, keepdims=True) + eps_unit)
    unit = (z * inverse).astype(BF16)
    z_ref[...] = z
    inverse_ref[...] = inverse
    unit_ref[...] = unit
    logits = jnp.dot(unit, table_ref[...], preferred_element_type=F32)
    logits_ref[...] = logits
    real = lax.broadcasted_iota(jnp.int32, (1, logits.shape[1]), 1) < protos
    batch = jnp.where(real, jnp.exp(logits / transport_epsilon), 0.0)
    batch_ref[...] = batch
    queued = jnp.dot(queue_ref[...], table_ref[...], preferred_element_type=F32)
    line = jnp.where(real, jnp.exp(queued / transport_epsilon), 0.0)
    line_ref[...] = line
    queue_sum = jnp.sum(line, axis=0, keepdims=True)
    for m in range(micro):
        at = slice(m * crops, (m + 1) * crops)
        sums_ref[m : m + 1, :] = jnp.sum(batch[at], axis=0, keepdims=True) + queue_sum


def embed_product(parts, members, protos, g, gain, shift, weight, bias, table, queue):
    lines = g.shape[0]
    micro = parts[0].shape[0]
    feat = weight.shape[1]
    wide = table.shape[1]
    outs = [
        shape(g.shape, BF16),
        shape((lines, feat)),
        shape((lines, 1)),
        shape((lines, feat), BF16),
        shape((lines, wide)),
        shape((lines, wide)),
        shape((queue.shape[0], wide)),
        shape((micro, wide)),
        shape((micro, 2, g.shape[1])),
    ]
    ins = [*parts, g, gain, shift, weight, bias, table, queue]
    return run(
        named("embed", embed_body, protos, len(parts), members),
        (1,),
        [whole(a) for a in ins],
        [whole(a) for a in outs],
        outs,
        flops=2 * lines * table.size,
        bytes_accessed=8 * lines * wide,
    )(*ins)


def sweep_body(protos, counts, refs):
    part_refs = refs[:counts]
    batch_ref, queue_ref, new_batch_ref, new_queue_ref, sums_ref = refs[counts:]
    micro, wide = sums_ref.shape
    crops = batch_ref.shape[0] // micro
    lines = new_queue_ref.shape[0] // micro
    shared = queue_ref.shape[0] == lines
    real = lax.broadcasted_iota(jnp.int32, (1, wide), 1) < protos
    for m in range(micro):
        column = jnp.where(real, tree([ref[m : m + 1, :] for ref in part_refs]), 1.0)
        at = slice(m * crops, (m + 1) * crops)
        batch = batch_ref[at, :] / column
        batch = batch / jnp.sum(batch, 1, keepdims=True)
        new_batch_ref[at, :] = batch
        own = slice(m * lines, (m + 1) * lines)
        queue = queue_ref[slice(0, lines) if shared else own, :] / column
        queue = queue / jnp.sum(queue, 1, keepdims=True)
        new_queue_ref[own, :] = queue
        sums_ref[m : m + 1, :] = jnp.sum(batch, axis=0, keepdims=True) + jnp.sum(
            queue, axis=0, keepdims=True
        )


def sweep(parts, protos, batch, queue, lines):
    micro, wide = parts[0].shape
    outs = [shape(batch.shape), shape((micro * lines, wide)), shape(parts[0].shape)]
    ins = [*parts, batch, queue]
    return run(
        named("sweep", sweep_body, protos, len(parts)),
        (1,),
        [whole(a) for a in ins],
        [whole(a) for a in outs],
        outs,
        flops=20 * batch.size,
        bytes_accessed=16 * batch.size,
    )(*ins)


def split_dot(dot, left, right, wide_left):
    value = left if wide_left else right
    high = value.astype(BF16)
    low = (value - high.astype(F32)).astype(BF16)
    if wide_left:
        return dot(high, right) + dot(low, right)
    return dot(left, high) + dot(left, low)


def pack_small(packed_ref, protos, embed):
    _, shards, _, lines, width = packed_ref.shape
    rows = protos.shape[0] // shards // 2
    half = protos.shape[1] // 2
    groups = half // width
    lane = embed.shape[1]
    below = lines - groups * rows
    for c in range(2):
        for d in range(shards):
            for y in range(2):
                first = (2 * d + y) * rows
                for q in range(groups):
                    packed_ref[c, d, y, q * rows : (q + 1) * rows, :] = protos[
                        first : first + rows, c * half + q * width : c * half + (q + 1) * width
                    ]
                for q in range(width // lane):
                    first = (((2 * d + c) * 2 + y) * (width // lane) + q) * below
                    packed_ref[c, d, y, groups * rows :, q * lane : (q + 1) * lane] = embed[
                        first : first + below
                    ]


def unpack_small(packed, protos, embed):
    _, shards, _, lines, width = packed.shape
    rows = protos[0] // shards // 2
    groups = protos[1] // 2 // width
    lane = embed[1]
    above = packed[:, :, :, : groups * rows].reshape(2, shards, 2, groups, rows, width)
    below = packed[:, :, :, groups * rows :]
    below = below.reshape(2, shards, 2, lines - groups * rows, width // lane, lane)
    return (
        above.transpose(1, 2, 4, 0, 3, 5).reshape(protos),
        below.transpose(1, 0, 2, 4, 3, 5).reshape(embed),
    )


def packed_shape(protos, embed, shards):
    width = 512
    lines = protos[0] // shards // 2 * (protos[1] // 2 // width)
    return (2, shards, 2, lines + embed[0] * embed[1] // shards // 4 // width, width)


def loss_body(protos, scale, counts, refs):
    part_refs = refs[:counts]
    batch_ref, logits_ref, unit_ref, z_ref, inverse_ref, act_ref, g_ref, info_ref, gain_ref, shift_ref, w_ref, table_ref, packed_ref, dy_ref, sums_ref = refs[counts:]
    micro, wide = part_refs[0].shape
    lines = batch_ref.shape[0]
    crops = lines // micro
    real = lax.broadcasted_iota(jnp.int32, (1, wide), 1) < protos
    odd = lax.broadcasted_iota(jnp.int32, (crops, 1), 0) % 2 == 1
    parts = []
    loss = jnp.zeros((1, 1), F32)
    for m in range(micro):
        at = slice(m * crops, (m + 1) * crops)
        codes = batch_ref[at, :] / jnp.where(
            real, tree([ref[m : m + 1, :] for ref in part_refs]), 1.0
        )
        codes = codes / jnp.sum(codes, 1, keepdims=True)
        partner = jnp.where(odd, pltpu.roll(codes, 1, 0), pltpu.roll(codes, crops - 1, 0))
        sharp = logits_ref[at, :] / softmax_sharpness
        top = jnp.max(jnp.where(real, sharp, -jnp.inf), 1, keepdims=True)
        shifted = sharp - top
        mass = jnp.where(real, jnp.exp(shifted), 0.0)
        total = jnp.sum(mass, 1, keepdims=True)
        chance = shifted - jnp.log(total)
        loss += jnp.sum(jnp.sum(partner * chance, 1, keepdims=True), 0, keepdims=True)
        weight = jnp.sum(partner, 1, keepdims=True)
        parts.append((scale / softmax_sharpness) * (weight * (mass / total) - partner))
    d_scores = jnp.concatenate(parts, 0)
    unit = unit_ref[...]
    grad_protos = split_dot(tn_dot, unit, d_scores, False)
    d_unit = split_dot(nt_dot, d_scores, table_ref[...], True)
    z = z_ref[...]
    inverse = inverse_ref[...]
    dz = inverse * d_unit - z * (inverse * inverse * inverse) * jnp.sum(
        z * d_unit, 1, keepdims=True
    )
    grad_embed = split_dot(tn_dot, act_ref[...], dz, False)
    pack_small(packed_ref, grad_protos, grad_embed)
    d_act = split_dot(nt_dot, dz, w_ref[...], True)
    for m in range(micro):
        at = slice(m * crops, (m + 1) * crops)
        normal = (g_ref[at, :] - info_ref[m, 0:1, :]) * info_ref[m, 1:2, :]
        pre = normal * gain_ref[...] + shift_ref[...]
        dy = d_act[at] * slope_of(pre)
        dy_ref[at, :] = dy
        sums_ref[m : m + 1, :] = jnp.sum(dy, axis=0, keepdims=True)
        sums_ref[micro + m : micro + m + 1, :] = jnp.sum(dy * normal, axis=0, keepdims=True)
    feat = z.shape[1]
    sums_ref[2 * micro : 2 * micro + 1, :] = jnp.zeros((1, sums_ref.shape[1]), F32)
    sums_ref[2 * micro : 2 * micro + 1, 0:feat] = jnp.sum(dz, axis=0, keepdims=True)
    sums_ref[2 * micro : 2 * micro + 1, feat : 2 * feat] = jnp.broadcast_to(
        -scale * loss, (1, feat)
    )


def loss_grads(parts, protos, scale, batch, logits, unit, z, inverse, act, g, info, gain, shift, weight, table, shards):
    ins = [*parts, batch, logits, unit, z, inverse, act, g, info, gain, shift, weight, table]
    micro = info.shape[0]
    outs = [
        shape(packed_shape(table.shape, weight.shape, shards)),
        shape(g.shape),
        shape((2 * micro + 1, g.shape[1])),
    ]
    return run(
        named("loss", loss_body, protos, scale, len(parts)),
        (1,),
        [whole(a) for a in ins],
        [whole(a) for a in outs],
        outs,
        flops=8 * table.size * batch.shape[0],
        bytes_accessed=16 * batch.size,
    )(*ins)


def pick_block(rows, width, cell):
    return pl.BlockSpec((1, rows, width), lambda g, w: cell(g, w[0], w[1], w[2]) + (0,))


def sent_first(g, core, x, y):
    z, b = g // 2, g % 2
    return (2 * z + (1 - core) * (1 - x) + core * b, (1 - core) * b + core * (1 - y))


def kept_second(g, core, x, y):
    return (2 * g + x, y)


def sent_second(g, core, x, y):
    return (2 * g + (1 - core) * x + core * (1 - x), (1 - core) * (1 - y) + core * y)


def add_groups(refs, sizes, out_ref, extra=None):
    start = 0
    place = 0
    for count, rows in sizes:
        value = refs[place][0]
        for ref in refs[place + 1 : place + count]:
            value = value + ref[0]
        if extra is not None:
            value = value + extra[0, start : start + rows, :]
        out_ref[0, start : start + rows, :] = value
        place += count
        start += rows


def first_send(scalars, groups):
    sizes = [(len(addends), addends[0].shape[1] // 2) for addends in groups]
    shards, _, width = groups[0][0].shape
    lines = sum(rows for _, rows in sizes)
    specs = []
    for (count, rows), addends in zip(sizes, groups):
        specs += [pick_block(rows, width, sent_first)] * count
    flat = [array for addends in groups for array in addends]

    def body(refs):
        add_groups(refs[1:-1], sizes, refs[-1])

    return run(
        named("first_send", body),
        (shards,),
        specs,
        pl.BlockSpec((1, lines, width), lambda g, w: (g, 0, 0)),
        shape((shards, lines, width)),
        bytes_accessed=4 * lines * width * shards * 3,
        prefetch=1,
    )(scalars, *flat)


def second_send(scalars, groups, came):
    sizes = [(len(addends), addends[0].shape[1] // 2) for addends in groups]
    shards, _, width = groups[0][0].shape
    lines = sum(rows for _, rows in sizes)
    flat = [array for addends in groups for array in addends]
    specs = []
    for cell in (sent_second, kept_second):
        for (count, rows), addends in zip(sizes, groups):
            specs += [pick_block(rows, width, cell)] * count

    def bit(w):
        return (1 - w[0]) * w[2] + w[0] * w[1]

    specs.append(pl.BlockSpec((1, lines, width), lambda g, w: (2 * g + 1 - bit(w), 0, 0)))
    specs.append(pl.BlockSpec((1, lines, width), lambda g, w: (2 * g + bit(w), 0, 0)))
    out = pl.BlockSpec((1, lines, width), lambda g, w: (g, 0, 0))

    def body(refs):
        refs = refs[1:]
        add_groups(refs[: len(flat)], sizes, refs[-2], refs[2 * len(flat)])
        add_groups(refs[len(flat) : 2 * len(flat)], sizes, refs[-1], refs[2 * len(flat) + 1])

    return run(
        named("second_send", body),
        (shards // 2,),
        specs,
        [out, out],
        [shape((shards // 2, lines, width))] * 2,
        bytes_accessed=4 * lines * width * shards * 4,
        prefetch=1,
    )(scalars, *flat, *flat, came, came)


def place_early_body(scalars_ref, mine_ref, far_ref, mine_core_ref, far_core_ref, out_ref, embed_ref, protos_ref, head_ref):
    lines = out_ref.shape[0]
    rows = protos_ref.shape[0] // 2
    wide = 512
    groups = protos_ref.shape[1] // 2 // wide
    lane = embed_ref.shape[1]
    below = embed_ref.shape[0] // 4 // (wide // lane)
    start = lines + groups * rows + below
    for c, y, ref in ((0, 0, mine_ref), (0, 1, far_ref), (1, 0, mine_core_ref), (1, 1, far_core_ref)):
        c = scalars_ref[0] if c == 0 else 1 - scalars_ref[0]
        y = scalars_ref[2] if y == 0 else 1 - scalars_ref[2]
        column = pl.multiple_of((2 * c + y) * wide, wide)
        out_ref[:, pl.ds(column, wide)] = ref[0:lines, :]
        head_ref[:, pl.ds(column, wide)] = ref[start:, :]
        at = pl.ds(pl.multiple_of(y * rows, rows), rows)
        for q in range(groups):
            column = pl.multiple_of((c * groups + q) * wide, wide)
            protos_ref[at, pl.ds(column, wide)] = ref[lines + q * rows : lines + (q + 1) * rows, :]
        for q in range(wide // lane):
            first = pl.multiple_of(((2 * c + y) * (wide // lane) + q) * below, below)
            embed_ref[pl.ds(first, below), :] = ref[
                lines + groups * rows : start, q * lane : (q + 1) * lane
            ]


def place_late_body(scalars_ref, mine_ref, far_ref, mine_core_ref, far_core_ref, *out_refs):
    for c, y, ref in ((0, 0, mine_ref), (0, 1, far_ref), (1, 0, mine_core_ref), (1, 1, far_core_ref)):
        c = scalars_ref[0] if c == 0 else 1 - scalars_ref[0]
        y = scalars_ref[2] if y == 0 else 1 - scalars_ref[2]
        start = 0
        for out_ref in out_refs:
            rows, width = out_ref.shape[0] // 2, out_ref.shape[1] // 2
            out_ref[
                pl.ds(pl.multiple_of(y * rows, rows), rows),
                pl.ds(pl.multiple_of(c * width, width), width),
            ] = ref[start : start + rows, :]
            start += rows


def placed_pieces(body, scalars, pieces, outs):
    return run(
        body,
        (1,),
        [whole(a) for a in pieces],
        [whole(a) for a in outs],
        outs,
        prefetch=1,
    )(scalars, *pieces)


def gathered(mine):
    far = swap(mine, 2)
    return [mine, far, swap(mine, 1), swap(far, 1)]


def on_device(
    pixels,
    crop_map,
    queue_rows,
    conv_in,
    gain_one,
    shift_one,
    conv_mid,
    gain_two,
    shift_two,
    conv_out,
    gain_three,
    shift_three,
    head_weight,
    head_gain,
    head_shift,
    embed_weight,
    embed_bias,
    prototypes,
):
    micro, canvas, pixel_count, channels = pixels.shape
    devices = lax.axis_size("dp") * lax.axis_size("hst")
    crops = canvas * SLOTS
    total_crops = crops * devices * 1.0
    loss_scale = 1.0 / (micro * total_crops)
    x = pixels.reshape(micro * canvas * pixel_count, channels)
    valid = (crop_map < SLOTS).astype(F32).reshape(-1, 1)
    sizes = jnp.sum(
        (crop_map[:, :, None, :] == jnp.arange(SLOTS, dtype=jnp.int32)[:, None]).astype(F32), 3
    ).reshape(-1, 1)

    shards = lax.axis_size("dp")
    quick = shards == 8 and lax.axis_size("hst") == 4
    packs = 8
    protos = prototypes.shape[1]
    table = jnp.pad(prototypes, ((0, 0), (0, -protos % 1024)))

    def row(vector):
        return vector.reshape(1, -1)

    masks = dp_masks()
    near, far = masks[0], masks[1:]
    core = bit_of(1)
    side = bit_of(2)
    scalars = jnp.stack([core, bit_of(near), side]).astype(jnp.int32)
    keep_half = core.astype(jnp.int32).reshape(1)
    send_half = 1 - keep_half

    h1, stats = first_product(x, conv_in, valid, micro)
    members, counts = first_parts(stats)
    act_one, h2, stats, info_one = second_product(
        members, h1, valid, row(gain_one), row(shift_one), conv_mid, micro
    )
    parts = moment_parts(stats, counts)
    act_two, h3, stats, info_two = third_product(
        parts, members, h2, valid, row(gain_two), row(shift_two), conv_out, micro
    )
    parts = moment_parts(stats, counts)
    feat, info_three = pool(
        parts, members, h3, x, valid, row(gain_three), row(shift_three), sizes, micro
    )

    lines = feat.shape[0]
    if quick:
        by_bit = feat.reshape(lines, shards // 2, 2, -1)
        bit = bit_of(near)
        feat_keep = at(by_bit, bit, 2).reshape(lines, -1)
        feat_send = at(by_bit, 1 - bit, 2).reshape(lines, -1)
        feat_near = swap(feat_send, near)
    g, stats = head_product(feat, head_weight, micro)
    if quick:
        stats, feat_near = tie(stats, feat_near)

    crop_counts = []
    crop_members = []
    number = crops * 1.0
    for group in sync_groups():
        crop_members = [number] * (len(group) + 1)
        crop_counts.append(crop_members)
        number = number * (len(group) + 1)
    slopes = []

    def slope_filler(index):
        def fill(gate):
            source = tie(h3, gate)[0]
            slopes[:] = slope_part(
                source, x, valid, info_three, row(gain_three), row(shift_three), micro, index, slopes
            )
            return slopes

        return fill

    parts = moment_parts(stats, crop_counts, ((), (slope_filler(0),), (slope_filler(1),)))

    act_four, embedded, inverse, unit_rows, logits, batch, queue, column, info_four = embed_product(
        parts,
        crop_members,
        protos,
        g,
        row(head_gain),
        row(head_shift),
        embed_weight,
        row(embed_bias),
        table,
        queue_rows,
    )
    fillers = ((), (slope_filler(2),), (slope_filler(3),))
    for _ in range(SINK_ITERS - 1):
        parts = sum_parts(column, fillers)
        fillers = ()
        batch, queue, column = sweep(parts, protos, batch, queue, queue_rows.shape[0])
    parts = sum_parts(column, fillers)
    slope, slope_first, slope_second = slopes
    packed, dy_four, payload = loss_grads(
        parts,
        protos,
        loss_scale,
        batch,
        logits,
        unit_rows,
        embedded,
        inverse,
        act_four,
        g,
        info_four,
        row(head_gain),
        row(head_shift),
        embed_weight,
        table,
        packs,
    )
    if quick:
        small_recv = swap(at(packed, 1 - core, 0), 1)
    parts = sum_parts(payload)
    if quick:
        *parts, small_recv = tie(*parts, small_recv)
        small = [at(packed, core, 0), small_recv]
    payload = tree(list(parts))
    first_four, second_four = payload[:micro], payload[micro : 2 * micro]
    grad_bias = payload[2 * micro, : embed_bias.shape[0]]
    total_loss = payload[2 * micro, embed_bias.shape[0]]

    if quick:
        feat_keep, feat_near, *parts = tie(feat_keep, feat_near, *parts)
        feat_near = jnp.concatenate([feat_keep, feat_near], 0)
        feat_far = swap(feat_near, 2)
    dg, wide, sums = head_back(
        parts,
        dy_four,
        g,
        info_four,
        row(head_gain),
        head_weight,
        sizes,
        slope_first,
        slope_second,
        total_crops,
    )
    first_norm = (h1, valid, info_one, info_one, row(gain_one))
    second_norm = (h2, valid, info_two, info_one, row(gain_two))

    def from_third(parts):
        return third_back(
            parts,
            wide,
            slope,
            h3,
            valid,
            info_three,
            row(gain_three),
            info_one,
            conv_out,
            h2,
            info_two,
            row(gain_two),
            row(shift_two),
            micro,
        )

    def from_second(d):
        return second_back(
            d, conv_mid, valid, h1, info_one, row(gain_one), row(shift_one), micro
        )

    if quick:
        sums, dg, feat_far = tie(sums, dg, feat_far)
        feat_both = jnp.concatenate([feat_near, feat_far], 0)
        feat_other = swap(feat_both, 1)
        split = dg.reshape(lines, 2, -1)
        dg_other = swap(at(split, 1 - core, 1), 1)
        parts_three = sum_parts(sums)
        *parts_three, dg_other, feat_other = tie(*parts_three, dg_other, feat_other)
        split = jnp.concatenate([at(split, core, 1), dg_other], 0).reshape(2 * lines, 2, -1)
        dg_here, dg_there = at(split, side, 1), at(split, 1 - side, 1)
        *parts_three, dg_here, dg_there = tie(*parts_three, dg_here, dg_there)
        dg_far, dg_near, dg_both = swap(dg_there, 2), swap(dg_here, near), swap(dg_there, 2 + near)
        d_three, dy, sums = from_third(parts_three)
        sums, dy, d_three, dg_far, dg_near, dg_both = tie(sums, dy, d_three, dg_far, dg_near, dg_both)
        grads = {}

        def out_filler(gate):
            source = tie(d_three, gate)[0]
            grads["out"] = out_grad(send_half, act_two, source, shards)
            return [grads["out"]]

        def head_filler(gate):
            grads["out_recv"] = swap(grads["out"][0], 1)
            source = tie(dg_near, gate)[0]
            grads["head"] = factor_grad(feat_both, feat_other, dg_here, dg_far, source, dg_both)
            return [grads["head"], grads["out_recv"]]

        parts_two = sum_parts(sums, ((), (out_filler,), (head_filler,)))

        small = [array.reshape(shards, -1, array.shape[-1]) for array in small]
        early = [[grads["out"][1], grads["out_recv"]], small]
        early_out = first_send(scalars, early)
        *parts_two, early_out, partial = tie(*parts_two, early_out, grads["head"])
        came = core_swap(early_out, near, 2)
        partial = partial.reshape(2, 2, -1, partial.shape[1])
        head = dp_halves([partial], far[0], 1)
        d_two, mid_send = mid_grad(
            "mid_first",
            mid_first_body,
            send_half,
            [*parts_two, dy, *second_norm, act_one],
            act_one,
            True,
        )
        d_two, mid_send, early_came, head[-1] = tie(d_two, mid_send, came, head[-1])
        mid_recv = swap(mid_send, 1)
        early_send, early_keep = second_send(scalars, early, early_came)
        early_came = core_swap(early_send, 2, near)
        mid_keep = mid_grad(
            "mid_second", mid_second_body, keep_half, [d_two, act_one], act_one, False
        )
        mid_keep, mid_recv, early_came = tie(mid_keep, mid_recv, early_came)

        def sharded(array):
            return array.reshape(shards, -1, array.shape[-1])

        def by_bits(array):
            return array.reshape((2, 2) + array.shape[1:])

        late = [[sharded(mid_keep), sharded(mid_recv)]]
        mid_came = core_swap(first_send(scalars, late), near, 2)
        early = dp_halves([by_bits(early_keep), by_bits(early_came)], far[0], 1)
        d_two = tie(d_two, mid_keep)[0]
        dy, sums = from_second(d_two)
        dy, sums, mid_came, early[-1] = tie(dy, sums, mid_came, early[-1])
        parts_one = sum_parts(sums)
        mid_out, mid_keep = second_send(scalars, late, mid_came)
        *parts_one, mid_out = tie(*parts_one, mid_out)
        mid_came = core_swap(mid_out, 2, near)
        head = dp_halves(head, far[1], 0)
        d_one, in_send, in_keep = in_grad(send_half, parts_one, dy, *first_norm, x)
        d_one, in_send, in_keep, mid_came, head[-1] = tie(d_one, in_send, in_keep, mid_came, head[-1])
        in_recv = swap(in_send, 1)
        mid = dp_halves([by_bits(mid_keep), by_bits(mid_came)], far[0], 1)
        early = dp_halves(early, far[1], 0)
        inner = [[sharded(in_keep), sharded(in_recv)]]
        in_out = first_send(scalars, inner)
        in_came = core_swap(in_out, near, 2)
        d_one = tie(d_one, in_out)[0]
        grad_x = pixels_grad(d_one, conv_in, wide, slope, micro)
        grad_x, in_came, mid[-1], early[-1] = tie(grad_x, in_came, mid[-1], early[-1])
        in_out, in_keep = second_send(scalars, inner, in_came)
        in_came = core_swap(in_out, 2, near)
        mid = dp_halves(mid, far[1], 0)
        early_pieces = gathered(jnp.concatenate([sum(early), sum(head)], 0))
        inner = dp_halves([by_bits(in_keep), by_bits(in_came)], far[0], 1)
        inner = dp_halves(inner, far[1], 0)
        late_pieces = gathered(jnp.concatenate([sum(mid), sum(inner)], 0))

        channel = channels // shards
        grad_conv_out, grad_embed, grad_protos, grad_head = placed_pieces(
            place_early_body,
            scalars,
            early_pieces,
            [
                shape((conv_out.shape[0] // shards, channels)),
                shape((embed_weight.shape[0] // shards, embed_weight.shape[1])),
                shape((table.shape[0] // shards, table.shape[1])),
                shape((channel, head_weight.shape[1])),
            ],
        )
        grad_protos = grad_protos[:, :protos]
        grad_conv_mid, grad_conv_in = placed_pieces(
            place_late_body,
            scalars,
            late_pieces,
            [
                shape((conv_mid.shape[0] // shards, conv_mid.shape[1])),
                shape((channel, conv_in.shape[1])),
            ],
        )
    else:
        low, high = jnp.zeros((1,), jnp.int32), jnp.ones((1,), jnp.int32)

        def reduced(array):
            return lax.psum(lax.psum_scatter(array, "dp", scatter_dimension=0, tiled=True), "hst")

        parts_three = sum_parts(sums)
        d_three, dy, sums = from_third(parts_three)
        parts_two = sum_parts(sums)
        ins = [*parts_two, dy, *second_norm, act_one]
        d_two, mid_low = mid_grad("mid_first", mid_first_body, low, ins, act_one, True)
        mid_high = mid_grad("mid_second", mid_second_body, high, [d_two, act_one], act_one, False)
        dy, sums = from_second(d_two)
        parts_one = sum_parts(sums)
        d_one, in_low, in_high = in_grad(low, parts_one, dy, *first_norm, x)
        grad_x = pixels_grad(d_one, conv_in, wide, slope, micro)
        out = out_grad(low, act_two, d_three, shards)
        out = out.reshape(2, shards, -1, conv_out.shape[0] // shards, out.shape[-1])
        small_protos, small_embed = unpack_small(packed, table.shape, embed_weight.shape)
        grad_conv_out = reduced(out.transpose(1, 3, 0, 2, 4).reshape(conv_out.shape))
        grad_conv_mid = reduced(jnp.concatenate([mid_low, mid_high], 1))
        grad_conv_in = reduced(jnp.concatenate([in_low, in_high], 1))
        grad_head = reduced(
            jnp.dot(feat.astype(BF16).T, dg.astype(BF16), preferred_element_type=F32)
        )
        grad_embed = reduced(small_embed)
        grad_protos = reduced(small_protos)[:, :protos]

    def own_rows(vectors):
        sums = [jnp.sum(vector, 0) for vector in vectors]
        piece = sums[0].shape[0] // shards
        stacked = jnp.stack(sums)
        found = lax.dynamic_slice_in_dim(stacked, lax.axis_index("dp") * piece, piece, 1)
        return [found[i] for i in range(len(vectors))]

    def both_sums(parts):
        total = tree(list(parts))
        return [total[:, 1], total[:, 0]]

    small_ones = own_rows(both_sums(parts_one) + both_sums(parts_two))
    large_ones = own_rows(both_sums(parts_three) + [second_four, first_four])

    return (
        total_loss,
        grad_x.reshape(pixels.shape),
        grad_conv_in,
        small_ones[0],
        small_ones[1],
        grad_conv_mid,
        small_ones[2],
        small_ones[3],
        grad_conv_out,
        large_ones[0],
        large_ones[1],
        grad_head,
        large_ones[2],
        large_ones[3],
        grad_embed,
        lax.dynamic_slice_in_dim(
            grad_bias,
            lax.axis_index("dp") * (grad_bias.shape[0] // shards),
            grad_bias.shape[0] // shards,
            0,
        ),
        grad_protos,
    )


def solution(mesh):
    placed = (
        P(None, ("dp", "hst"), None, None),
        P(None, ("dp", "hst"), None),
        P(("dp", "hst"), None),
    ) + (P(),) * 15
    return jax.shard_map(
        on_device,
        mesh=mesh,
        in_specs=placed,
        out_specs=(
            P(),
            P(None, ("dp", "hst"), None, None),
            P("dp", None),
            P("dp"),
            P("dp"),
            P("dp", None),
            P("dp"),
            P("dp"),
            P("dp", None),
            P("dp"),
            P("dp"),
            P("dp", None),
            P("dp"),
            P("dp"),
            P("dp", None),
            P("dp"),
            P("dp", None),
        ),
        check_vma=False,
    )
```

```python
import functools

import jax
import jax.numpy as jnp
from jax import lax
from jax.experimental import pallas as pl
from jax.experimental.pallas import tpu as pltpu
from jax.sharding import PartitionSpec as P

ROWS = 8
COLS = 16
SLOTS = 4
CELL = COLS // SLOTS
PIX = ROWS * COLS
SINK_ITERS = 3
TAPS = 9

eps_norm = 1e-05
eps_unit = 1e-06
transport_epsilon = 0.05
softmax_sharpness = 0.1
highest = lax.Precision.HIGHEST
F32 = jnp.float32
BF16 = jnp.bfloat16
AXES = ("dp", "hst")
MIB = 1 << 20
LANES = 128


def swap(value, mask):
    count = lax.axis_size("dp") * lax.axis_size("hst")
    return lax.ppermute(value, AXES, [(i, i ^ mask) for i in range(count)])


def sync_groups():
    bits = (lax.axis_size("dp") * lax.axis_size("hst")).bit_length() - 1
    groups = [(1,)]
    bit = 1
    while bit < bits:
        if bit + 1 < bits:
            groups.append((1 << bit, 2 << bit, 3 << bit))
            bit += 2
        else:
            groups.append((1 << bit,))
            bit += 1
    return groups


def tree(parts):
    while len(parts) > 1:
        parts = [parts[i] + parts[i + 1] for i in range(0, len(parts), 2)]
    return parts[0]


def between(parts, gate, fillers):
    for filler in fillers:
        parts = list(tie(*parts, *filler(gate)))[: len(parts)]
    return parts


def pick(fillers, step):
    return fillers[step] if step < len(fillers) else ()


def sum_parts(value, fillers=()):
    groups = sync_groups()
    for step, group in enumerate(groups):
        parts = [value] + [swap(value, mask) for mask in group]
        parts = between(parts, value, pick(fillers, step))
        value = tree(parts)
    return parts


def merge(parts, members):
    whole = tree(list(members))
    mean = tree([n * part[:, 0] for n, part in zip(members, parts)]) / whole
    spread = tree(
        [part[:, 1] + n * (part[:, 0] - mean) ** 2 for n, part in zip(members, parts)]
    )
    return mean, spread, whole


def moment_parts(moments, counts, fillers=()):
    groups = sync_groups()
    for step, group in enumerate(groups):
        parts = [moments] + [swap(moments, mask) for mask in group]
        parts = between(parts, moments, pick(fillers, step))
        if step + 1 < len(groups):
            moments = jnp.stack(merge(parts, counts[step])[:2], 1)
    return parts


def first_parts(moments):
    groups = sync_groups()
    counts = []
    for step, group in enumerate(groups):
        parts = [moments] + [swap(moments, mask) for mask in group]
        if step + 1 < len(groups):
            members = [part[:, 2] for part in parts]
            moments = jnp.stack(merge(parts, members), 1)
            counts.append([n[:, :1] for n in members])
    return parts, counts


def bit_of(mask):
    index = lax.axis_index("dp") * lax.axis_size("hst") + lax.axis_index("hst")
    return (index // mask) % 2


def dp_masks():
    base = lax.axis_size("hst")
    return [base << j for j in range(lax.axis_size("dp").bit_length() - 1)]


def tie(first, *others):
    return lax.optimization_barrier((first,) + others)


def at(view, place, axis):
    return lax.dynamic_index_in_dim(view, place, axis, keepdims=False)


def core_swap(value, low, high):
    count = lax.axis_size("dp") * lax.axis_size("hst")
    pairs = [(i, i ^ (high if i % 2 else low)) for i in range(count)]
    return lax.ppermute(value, AXES, pairs)


def dp_halves(addends, mask, axis):
    bit = bit_of(mask)
    send = sum(at(array, 1 - bit, axis) for array in addends)
    return [at(array, bit, axis) for array in addends] + [swap(send, mask)]


def run(body, grid, in_specs, out_specs, out_shape, scratch=(), flops=0, bytes_accessed=0, prefetch=0, aliases=None):
    return pl.pallas_call(
        body,
        grid_spec=pltpu.PrefetchScalarGridSpec(
            num_scalar_prefetch=prefetch,
            grid=grid,
            in_specs=in_specs,
            out_specs=out_specs,
            scratch_shapes=list(scratch),
        ),
        out_shape=out_shape,
        name=body.__name__,
        input_output_aliases=aliases or {},
        compiler_params=pltpu.CompilerParams(
            vmem_limit_bytes=56 * MIB, dimension_semantics=("arbitrary",) * len(grid)
        ),
        cost_estimate=pl.CostEstimate(
            flops=flops, bytes_accessed=bytes_accessed, transcendentals=0
        ),
    )


def shape(dims, dtype=F32):
    return jax.ShapeDtypeStruct(tuple(dims), dtype)


def sigmoid(u):
    return 0.5 * jnp.tanh(0.5 * u) + 0.5


def norm_of(part_refs, members, m=0, lane=slice(None)):
    whole = tree(list(members))
    means = [ref[m, 0:1, lane] for ref in part_refs]
    mean = tree([n * one for n, one in zip(members, means)]) / whole
    spread = tree(
        [ref[m, 1:2, lane] + n * (one - mean) ** 2 for n, ref, one in zip(members, part_refs, means)]
    )
    return mean, lax.rsqrt(spread / whole + eps_norm)


def sums_of(part_refs, first, second, m=0):
    return (
        tree([ref[m, first : first + 1, :] for ref in part_refs]),
        tree([ref[m, second : second + 1, :] for ref in part_refs]),
    )


def counts_of(count_refs, m=0):
    return [ref[m, 2:3, 0:1] for ref in count_refs]


def whole(array):
    return pl.BlockSpec(array.shape, lambda *_: (0,) * len(array.shape))


def per_micro(array):
    return pl.BlockSpec((1,) + array.shape[1:], lambda m, *_: (m,) + (0,) * (array.ndim - 1))


def slope_of(u):
    s = sigmoid(u)
    return s * (1.0 + u * (1.0 - s))


def nt_dot(left, right):
    return lax.dot_general(left, right, (((1,), (1,)), ((), ())), preferred_element_type=F32)


def tn_dot(left, right):
    return lax.dot_general(left, right, (((0,), (0,)), ((), ())), preferred_element_type=F32)


def fold(y):
    return jnp.sum(y.reshape(y.shape[0] // 8, 8, y.shape[1]), 0)


def put_moments(stats_ref, h_ref, v_ref, with_count):
    rows, width = h_ref.shape
    chunk = 32
    lanes = 512
    v = v_ref[...]
    count = jnp.sum(v, axis=0, keepdims=True)
    first = jnp.sum(v[:PIX], axis=0, keepdims=True)
    for j in range(0, width, lanes):
        lane = slice(j, j + lanes)
        acc = jnp.zeros((8, lanes), F32)
        for i in range(0, PIX, chunk):
            acc += fold(h_ref[i : i + chunk, lane].astype(F32) * v_ref[i : i + chunk, :])
        pivot = jnp.sum(acc, axis=0, keepdims=True) / first
        line = jnp.zeros((8, lanes), F32)
        square = jnp.zeros((8, lanes), F32)
        for i in range(0, rows, chunk):
            off = (h_ref[i : i + chunk, lane].astype(F32) - pivot) * v_ref[i : i + chunk, :]
            line += fold(off)
            square += fold(off * off)
        total = jnp.sum(line, axis=0, keepdims=True)
        stats_ref[0, 0:1, lane] = pivot + total / count
        stats_ref[0, 1:2, lane] = (
            jnp.sum(square, axis=0, keepdims=True) - total * total / count
        )
        if with_count:
            stats_ref[0, 2:3, lane] = jnp.broadcast_to(count, (1, lanes))


def first_body(x_ref, w_ref, v_ref, h_ref, stats_ref):
    h_ref[...] = jnp.dot(x_ref[...], w_ref[...], preferred_element_type=F32)
    put_moments(stats_ref, h_ref, v_ref, True)


def first_product(x, weight, valid, micro):
    rows = x.shape[0] // micro
    depth, width = weight.shape
    return run(
        first_body,
        (micro,),
        [
            pl.BlockSpec((rows, depth), lambda m: (m, 0)),
            pl.BlockSpec((depth, width), lambda m: (0, 0)),
            pl.BlockSpec((rows, 1), lambda m: (m, 0)),
        ],
        [
            pl.BlockSpec((rows, width), lambda m: (m, 0)),
            pl.BlockSpec((1, 3, width), lambda m: (m, 0, 0)),
        ],
        [shape((micro * rows, width)), shape((micro, 3, width))],
        flops=2 * micro * rows * depth * width,
        bytes_accessed=2 * x.size,
    )(x, weight, valid)


def cell_column(rows):
    return lax.broadcasted_iota(jnp.int32, (rows, 1), 0) % CELL


def second_body(counts, refs):
    part_refs, (h_ref, v_ref, gain_ref, shift_ref, w_ref, a_ref, h2_ref, stats_ref, info_ref, cols_ref) = refs[:counts], refs[counts:]
    rows, width = h_ref.shape
    members = counts_of(part_refs)
    mean, scaled = norm_of(part_refs, members)
    info_ref[0, 0:1, :] = mean
    info_ref[0, 1:2, :] = scaled
    info_ref[0, 2:3, :] = jnp.broadcast_to(tree(list(members)), mean.shape)
    factor = scaled * gain_ref[...]
    shift = shift_ref[...]
    place = cell_column(COLS)
    has_left = (place >= 1).astype(F32)
    has_right = (place <= CELL - 2).astype(F32)
    blank = jnp.zeros((COLS, width), BF16)
    for i in range(0, rows, COLS):
        at = slice(i, i + COLS)
        pre = (h_ref[at, :] - mean) * factor + shift
        act = (pre * sigmoid(pre) * v_ref[at, :]).astype(BF16)
        a_ref[at, :] = act
        wide = act.astype(F32)
        sides = (
            (pltpu.roll(wide, 1, 0) * has_left).astype(BF16),
            act,
            (pltpu.roll(wide, COLS - 1, 0) * has_right).astype(BF16),
        )
        for c in range(3):
            cols_ref[at, (3 + c) * width : (4 + c) * width] = sides[c]
            if i % PIX < PIX - COLS:
                cols_ref[i + COLS : i + 2 * COLS, c * width : (c + 1) * width] = sides[c]
            else:
                cols_ref[at, (6 + c) * width : (7 + c) * width] = blank
            if i % PIX > 0:
                cols_ref[i - COLS : i, (6 + c) * width : (7 + c) * width] = sides[c]
            else:
                cols_ref[at, c * width : (c + 1) * width] = blank
    h2_ref[...] = jnp.dot(cols_ref[...], w_ref[...], preferred_element_type=F32)
    put_moments(stats_ref, h2_ref, v_ref, False)


def named(name, body, *fixed):
    def kernel(*refs):
        body(*fixed, refs)

    kernel.__name__ = name
    return kernel


def second_product(parts, h1, valid, gain, shift, weight, micro):
    rows, width = h1.shape[0] // micro, h1.shape[1]
    mid = pl.BlockSpec((rows, width), lambda m: (m, 0))
    return run(
        named("second_product", second_body, len(parts)),
        (micro,),
        [per_micro(part) for part in parts]
        + [
            mid,
            pl.BlockSpec((rows, 1), lambda m: (m, 0)),
            whole(gain),
            whole(shift),
            whole(weight),
        ],
        [
            mid,
            mid,
            pl.BlockSpec((1, 2, width), lambda m: (m, 0, 0)),
            pl.BlockSpec((1, 3, width), lambda m: (m, 0, 0)),
        ],
        [
            shape((micro * rows, width), BF16),
            shape((micro * rows, width)),
            shape((micro, 2, width)),
            shape((micro, 3, width)),
        ],
        [pltpu.VMEM((rows, weight.shape[0]), BF16)],
        flops=2 * micro * rows * weight.size,
        bytes_accessed=10 * h1.size,
    )(*parts, h1, valid, gain, shift, weight)


def third_body(counts, refs):
    part_refs, count_refs = refs[:counts], refs[counts : 2 * counts]
    h_ref, v_ref, gain_ref, shift_ref, w_ref, a_ref, h3_ref, stats_ref, info_ref, wide_ref = refs[2 * counts :]
    rows = h_ref.shape[0]
    mean, scaled = norm_of(part_refs, counts_of(count_refs))
    info_ref[0, 0:1, :] = mean
    info_ref[0, 1:2, :] = scaled
    factor = scaled * gain_ref[...]
    shift = shift_ref[...]
    for i in range(0, rows, 32):
        at = slice(i, i + 32)
        pre = (h_ref[at, :] - mean) * factor + shift
        a_ref[at, :] = (pre * sigmoid(pre) * v_ref[at, :]).astype(BF16)
    wide_ref[...] = jnp.dot(a_ref[...], w_ref[...], preferred_element_type=F32)
    h3_ref[...] = wide_ref[...].astype(BF16)
    put_moments(stats_ref, wide_ref, v_ref, False)


def third_product(parts, members, h2, valid, gain, shift, weight, micro):
    rows, depth = h2.shape[0] // micro, h2.shape[1]
    width = weight.shape[1]
    mid = pl.BlockSpec((rows, depth), lambda m: (m, 0))
    return run(
        named("third_product", third_body, len(parts)),
        (micro,),
        [per_micro(part) for part in parts + members]
        + [
            mid,
            pl.BlockSpec((rows, 1), lambda m: (m, 0)),
            whole(gain),
            whole(shift),
            whole(weight),
        ],
        [
            mid,
            pl.BlockSpec((rows, width), lambda m: (m, 0)),
            pl.BlockSpec((1, 2, width), lambda m: (m, 0, 0)),
            pl.BlockSpec((1, 2, depth), lambda m: (m, 0, 0)),
        ],
        [
            shape((micro * rows, depth), BF16),
            shape((micro * rows, width), BF16),
            shape((micro, 2, width)),
            shape((micro, 2, depth)),
        ],
        [pltpu.VMEM((rows, width), F32)],
        flops=2 * micro * rows * weight.size,
        bytes_accessed=4 * micro * rows * width,
    )(*parts, *members, h2, valid, gain, shift, weight)


def crop_sums(ref, *index):
    crops = ref.shape[-2] // CELL
    slabs = [
        tree([ref[(*index, j, pl.ds(i, crops, CELL), slice(None))] for i in range(CELL)])
        for j in range(ref.shape[-3])
    ]
    return jnp.concatenate(slabs, 1)


def put_lanes(ref, place, first, value, *index):
    for j in range(0, value.shape[1], LANES):
        ref[(*index, (first + j) // LANES, place, slice(None))] = value[:, j : j + LANES]


def pool_body(counts, refs):
    part_refs, count_refs = refs[:counts], refs[counts : 2 * counts]
    h_ref, x_ref, v_ref, gain_ref, shift_ref, size_ref, feat_ref, info_ref, sums_ref = refs[2 * counts :]
    rows, width = h_ref.shape
    mean, scaled = norm_of(part_refs, counts_of(count_refs))
    info_ref[0, 0:1, :] = mean
    info_ref[0, 1:2, :] = scaled
    factor = scaled * gain_ref[...]
    shift = shift_ref[...]
    for j in range(0, width, 512):
        lane = slice(j, j + 512)
        for k in range(rows // PIX):
            acc = jnp.zeros((COLS, 512), F32)
            for r in range(ROWS):
                at = pl.ds(k * PIX + r * COLS, COLS)
                resid = (
                    (h_ref[at, lane].astype(F32) - mean[:, lane]) * factor[:, lane]
                    + shift[:, lane]
                    + x_ref[at, lane].astype(F32)
                )
                out = resid * (sigmoid(resid) * v_ref[at, :])
                acc += out.astype(BF16).astype(F32)
            put_lanes(sums_ref, pl.ds(k * COLS, COLS), j, acc)
    feat_ref[...] = (crop_sums(sums_ref) / size_ref[...]).astype(BF16).astype(F32)


def pool(parts, members, h3, x, valid, gain, shift, sizes, micro):
    rows, channels = h3.shape[0] // micro, h3.shape[1]
    crops = sizes.shape[0] // micro
    width = 1024
    tile = pl.BlockSpec((rows, width), lambda m, c: (m, c))
    line = pl.BlockSpec((1, width), lambda m, c: (0, c))
    pair = pl.BlockSpec((1, 2, width), lambda m, c: (m, 0, c))
    return run(
        named("pool", pool_body, len(parts)),
        (micro, channels // width),
        [pair] * len(parts)
        + [per_micro(part) for part in members]
        + [
            tile,
            tile,
            pl.BlockSpec((rows, 1), lambda m, c: (m, 0)),
            line,
            line,
            pl.BlockSpec((crops, 1), lambda m, c: (m, 0)),
        ],
        [pl.BlockSpec((crops, width), lambda m, c: (m, c)), pair],
        [shape((micro * crops, channels)), shape((micro, 2, channels))],
        [pltpu.VMEM((width // LANES, rows // ROWS, LANES), F32)],
        flops=20 * h3.size,
        bytes_accessed=4 * h3.size,
    )(*parts, *members, h3, x, valid, gain, shift, sizes)


def slope_body(*refs):
    h_ref, x_ref, v_ref, info_ref, gain_ref, shift_ref = refs[:6]
    slope_ref, first_ref, second_ref, sums_ref = refs[-4:]
    rows, width = h_ref.shape
    mean = info_ref[0, 0:1, :]
    scaled = info_ref[0, 1:2, :]
    factor = scaled * gain_ref[...]
    shift = shift_ref[...]
    for j in range(0, width, 512):
        lane = slice(j, j + 512)
        for k in range(rows // PIX):
            acc_first = jnp.zeros((COLS, 512), F32)
            acc_second = jnp.zeros((COLS, 512), F32)
            for r in range(ROWS):
                at = pl.ds(k * PIX + r * COLS, COLS)
                centred = h_ref[at, lane].astype(F32) - mean[:, lane]
                resid = centred * factor[:, lane] + shift[:, lane] + x_ref[at, lane].astype(F32)
                sig = sigmoid(resid)
                kept = sig * v_ref[at, :]
                slope = kept + resid * kept * (1.0 - sig)
                acc_first += slope
                acc_second += slope * centred
                slope_ref[at, lane] = slope.astype(BF16)
            place = pl.ds(k * COLS, COLS)
            put_lanes(sums_ref, place, j, acc_first, 0)
            put_lanes(sums_ref, place, j, acc_second * scaled[:, lane], 1)
    first_ref[...] = crop_sums(sums_ref, 0)
    second_ref[...] = crop_sums(sums_ref, 1)


def slope_part(h3, x, valid, info, gain, shift, micro, index, earlier):
    rows, channels = h3.shape[0] // micro, h3.shape[1]
    crops = rows // PIX * SLOTS
    width = 1024
    tile = pl.BlockSpec((rows, width), lambda c: (index, c))
    small = pl.BlockSpec((crops, width), lambda c: (index, c))
    return run(
        slope_body,
        (channels // width,),
        [
            tile,
            tile,
            pl.BlockSpec((rows, 1), lambda c: (index, 0)),
            pl.BlockSpec((1, 2, width), lambda c: (index, 0, c)),
            pl.BlockSpec((1, width), lambda c: (0, c)),
            pl.BlockSpec((1, width), lambda c: (0, c)),
        ]
        + [pl.BlockSpec(memory_space=pl.ANY)] * len(earlier),
        [tile, small, small],
        [
            shape(h3.shape, BF16),
            shape((micro * crops, channels)),
            shape((micro * crops, channels)),
        ],
        [pltpu.VMEM((2, width // LANES, rows // ROWS, LANES), F32)],
        flops=30 * rows * channels,
        bytes_accessed=6 * rows * channels,
        aliases={6 + i: i for i in range(len(earlier))},
    )(h3, x, valid, info, gain, shift, *earlier)


def head_body(feat_ref, w_ref, g_ref, stats_ref):
    g = jnp.dot(feat_ref[...].astype(BF16), w_ref[...], preferred_element_type=F32)
    g_ref[...] = g
    micro = stats_ref.shape[0]
    crops = g.shape[0] // micro
    for m in range(micro):
        part = g[m * crops : (m + 1) * crops]
        mean = jnp.sum(part, axis=0, keepdims=True) / crops
        stats_ref[m, 0:1, :] = mean
        stats_ref[m, 1:2, :] = jnp.sum((part - mean) ** 2, axis=0, keepdims=True)


def head_product(feat, weight, micro):
    lines = feat.shape[0]
    depth, width = weight.shape
    tile = 512
    return run(
        head_body,
        (width // tile,),
        [
            pl.BlockSpec((lines, depth), lambda c: (0, 0)),
            pl.BlockSpec((depth, tile), lambda c: (0, c)),
        ],
        [
            pl.BlockSpec((lines, tile), lambda c: (0, c)),
            pl.BlockSpec((micro, 2, tile), lambda c: (0, 0, c)),
        ],
        [shape((lines, width)), shape((micro, 2, width))],
        flops=2 * lines * weight.size,
        bytes_accessed=2 * weight.size,
    )(feat, weight)


def head_back_body(total_crops, counts, refs):
    part_refs = refs[:counts]
    dy_ref, g_ref, info_ref, gain_ref, w_ref, size_ref, first_ref, second_ref, dg_ref, wide_ref, stats_ref, low_ref, spread_ref = refs[counts:]
    micro = stats_ref.shape[0]
    lines, width = dy_ref.shape
    crops = lines // micro

    @pl.when(pl.program_id(0) == 0)
    def _():
        for m in range(micro):
            at = pl.ds(m * crops, crops)
            one = tree([ref[m : m + 1, :width] for ref in part_refs]) / total_crops
            two = tree([ref[micro + m : micro + m + 1, :width] for ref in part_refs]) / total_crops
            scaled = info_ref[m, 1:2, :]
            normal = (g_ref[at, :] - info_ref[m, 0:1, :]) * scaled
            dg = gain_ref[...] * scaled * (dy_ref[at, :] - (one + normal * two))
            low = dg.astype(BF16)
            low_ref[at, :] = low
            dg_ref[at, :] = low.astype(F32)

    per_crop = nt_dot(low_ref[...], w_ref[...]) / size_ref[...]
    for j in range(wide_ref.shape[1] // LANES):
        lane = slice(j * LANES, (j + 1) * LANES)
        for i in range(CELL):
            spread_ref[j, pl.ds(i, lines, CELL), :] = per_crop[:, lane]
        wide_ref[:, lane] = spread_ref[j]
    one = per_crop * first_ref[...]
    two = per_crop * second_ref[...]
    for m in range(micro):
        at = slice(m * crops, (m + 1) * crops)
        stats_ref[m, 0:1, :] = jnp.sum(one[at], axis=0, keepdims=True)
        stats_ref[m, 1:2, :] = jnp.sum(two[at], axis=0, keepdims=True)


def head_back(parts, dy, g, info, gain, weight, sizes, first, second, total_crops):
    lines, width = dy.shape
    channels = weight.shape[0]
    micro = info.shape[0]
    tile = 512
    part = pl.BlockSpec((lines, tile), lambda c: (0, c))
    return run(
        named("head_back", head_back_body, total_crops, len(parts)),
        (channels // tile,),
        [whole(a) for a in parts]
        + [
            whole(dy),
            whole(g),
            whole(info),
            whole(gain),
            pl.BlockSpec((tile, width), lambda c: (c, 0)),
            whole(sizes),
            part,
            part,
        ],
        [
            whole(dy),
            pl.BlockSpec((lines * CELL, tile), lambda c: (0, c)),
            pl.BlockSpec((micro, 2, tile), lambda c: (0, 0, c)),
        ],
        [shape((lines, width)), shape((lines * CELL, channels)), shape((micro, 2, channels))],
        [
            pltpu.VMEM((lines, width), BF16),
            pltpu.VMEM((tile // LANES, lines * CELL, LANES), F32),
        ],
        flops=2 * lines * weight.size,
        bytes_accessed=2 * weight.size,
    )(*parts, dy, g, info, gain, weight, sizes, first, second)


def third_back_body(counts, refs):
    which_ref, part_refs = refs[0], refs[1 : 1 + counts]
    wide_ref, slope_ref, h3_ref, v_ref, info3_ref, gain3_ref, info1_ref, w_ref, act_ref, h2_ref, info2_ref, gain2_ref, shift2_ref, dy_ref, stats_ref, send_ref, keep_ref, d_ref, sum_ref = refs[1 + counts :]
    rows, channels = slope_ref.shape
    step = pl.program_id(0)
    number = info1_ref[0, 2:3, 0:1]
    first, second = sums_of(part_refs, 0, 1)
    mean = info3_ref[0, 0:1, :]
    scaled = info3_ref[0, 1:2, :]
    factor = gain3_ref[...] * scaled
    one = factor * first / number
    two = factor * scaled * second / number
    act = act_ref[...].T

    @pl.when(step == 0)
    def _():
        sum_ref[...] = jnp.zeros(sum_ref.shape, F32)

    tile = sum_ref.shape[2]
    for j in range(0, channels, tile):
        lane = slice(j, j + tile)
        for k in range(rows // PIX):
            wide = wide_ref[pl.ds(k * COLS, COLS), lane] * factor[:, lane]
            for r in range(ROWS):
                at = pl.ds(k * PIX + r * COLS, COLS)
                back = one[:, lane] + (h3_ref[at, lane].astype(F32) - mean[:, lane]) * two[:, lane]
                d = wide * slope_ref[at, lane].astype(F32) - v_ref[at, :] * back
                d_ref[at, lane] = d.astype(BF16)
        part = nt_dot(d_ref[:, lane], w_ref[:, lane])
        if j == 0:
            dy_ref[...] = part
        else:
            dy_ref[...] += part
        sum_ref[j // tile] += jnp.dot(act, d_ref[:, lane], preferred_element_type=F32)
    put_back(dy_ref, h2_ref, v_ref, info2_ref, gain2_ref, shift2_ref, stats_ref)

    @pl.when(step == pl.num_programs(0) - 1)
    def _():
        low = which_ref[0] == 0
        steps = sum_ref.shape[0] // 2
        lines = send_ref.shape[1] // steps
        for q in range(steps):
            place = slice(q * lines, (q + 1) * lines)
            left = sum_ref[q].reshape(-1, lines, tile)
            right = sum_ref[steps + q].reshape(-1, lines, tile)
            send_ref[:, place, :] = jnp.where(low, left, right)
            keep_ref[:, place, :] = jnp.where(low, right, left)


def put_back(dy_ref, h_ref, v_ref, info_ref, gain_ref, shift_ref, stats_ref):
    rows, width = dy_ref.shape
    first = jnp.zeros((8, width), F32)
    second = jnp.zeros((8, width), F32)
    for i in range(0, rows, 32):
        at = slice(i, i + 32)
        normal = (h_ref[at, :] - info_ref[0, 0:1, :]) * info_ref[0, 1:2, :]
        pre = normal * gain_ref[...] + shift_ref[...]
        dy = dy_ref[at, :] * v_ref[at, :] * slope_of(pre)
        dy_ref[at, :] = dy
        first += fold(dy)
        second += fold(dy * normal)
    stats_ref[0, 0:1, :] = jnp.sum(first, axis=0, keepdims=True)
    stats_ref[0, 1:2, :] = jnp.sum(second, axis=0, keepdims=True)


def third_back(which, parts, wide, slope, h3, valid, info3, gain3, info1, weight, act, h2, info2, gain2, shift2, micro, shards):
    rows, channels = slope.shape[0] // micro, slope.shape[1]
    middle = weight.shape[0]
    lines = wide.shape[0] // micro
    tile = 512
    big = pl.BlockSpec((rows, channels), lambda m, w: (m, 0))
    mid = pl.BlockSpec((rows, middle), lambda m, w: (m, 0))
    half = shape((shards, middle // shards * (channels // tile // 2), tile))
    return run(
        named("third_back", third_back_body, len(parts)),
        (micro,),
        [per_micro(part) for part in parts]
        + [
            pl.BlockSpec((lines, channels), lambda m, w: (m, 0)),
            big,
            big,
            pl.BlockSpec((rows, 1), lambda m, w: (m, 0)),
            per_micro(info3),
            whole(gain3),
            per_micro(info1),
            whole(weight),
            mid,
            mid,
            per_micro(info2),
            whole(gain2),
            whole(shift2),
        ],
        [
            mid,
            pl.BlockSpec((1, 2, middle), lambda m, w: (m, 0, 0)),
            whole(half),
            whole(half),
        ],
        [shape(h2.shape), shape((micro, 2, middle)), half, half],
        [
            pltpu.VMEM((rows, channels), BF16),
            pltpu.VMEM((channels // tile, middle, tile), F32),
        ],
        flops=4 * slope.shape[0] * weight.size,
        bytes_accessed=6 * slope.size,
        prefetch=1,
    )(which, *parts, wide, slope, h3, valid, info3, gain3, info1, weight, act, h2, info2, gain2, shift2)


def put_norm_back(part_refs, dy_ref, h_ref, v_ref, info_ref, number_ref, gain_ref, d_ref):
    micro = info_ref.shape[0]
    rows = dy_ref.shape[0] // micro
    for m in range(micro):
        number = number_ref[m, 2:3, 0:1]
        first, second = sums_of(part_refs, 0, 1, m)
        scaled = info_ref[m, 1:2, :]
        factor = gain_ref[...] * scaled
        one = factor * first / number
        two = factor * scaled * second / number
        mean = info_ref[m, 0:1, :]
        for i in range(m * rows, (m + 1) * rows, 32):
            at = slice(i, i + 32)
            back = one + (h_ref[at, :] - mean) * two
            d_ref[at, :] = (factor * dy_ref[at, :] - v_ref[at, :] * back).astype(BF16)


def put_sides(a_ref, sides_ref):
    rows, width = a_ref.shape
    blank = jnp.zeros((COLS, width), BF16)
    place = cell_column(COLS)
    has_left = (place >= 1).astype(F32)
    has_right = (place <= CELL - 2).astype(F32)
    for k in range(rows // PIX):
        for c in range(3):
            sides_ref[c, k, 0:COLS, :] = blank
            sides_ref[c, k, COLS + PIX :, :] = blank
        for r in range(ROWS):
            act = a_ref[k * PIX + r * COLS : k * PIX + (r + 1) * COLS, :]
            wide = act.astype(F32)
            at = slice((r + 1) * COLS, (r + 2) * COLS)
            sides_ref[0, k, at, :] = (pltpu.roll(wide, 1, 0) * has_left).astype(BF16)
            sides_ref[1, k, at, :] = act
            sides_ref[2, k, at, :] = (pltpu.roll(wide, COLS - 1, 0) * has_right).astype(BF16)


def put_tap(out_ref, sides_ref, half_ref):
    tap = pl.program_id(0)
    _, canvases, _, width = sides_ref.shape
    start = pl.multiple_of(tap // 3 * COLS, COLS)
    left = sides_ref[tap % 3, :, pl.ds(start, PIX), :].reshape(canvases * PIX, width)
    out_ref[...] = tn_dot(left, half_ref[...])


def half_of(which_ref, d_ref):
    half = d_ref.shape[1] // 2
    return d_ref[:, pl.ds(pl.multiple_of(which_ref[0] * half, half), half)]


def mid_first_body(counts, refs):
    which_ref, part_refs = refs[0], refs[1 : 1 + counts]
    dy_ref, h_ref, v_ref, info_ref, number_ref, gain_ref, a_ref, d_ref, out_ref, sides_ref, half_ref = refs[1 + counts :]

    @pl.when(pl.program_id(0) == 0)
    def _():
        put_norm_back(part_refs, dy_ref, h_ref, v_ref, info_ref, number_ref, gain_ref, d_ref)
        half_ref[...] = half_of(which_ref, d_ref)
        put_sides(a_ref, sides_ref)

    put_tap(out_ref, sides_ref, half_ref)


def mid_second_body(refs):
    which_ref, d_ref, a_ref, out_ref, sides_ref, half_ref = refs

    @pl.when(pl.program_id(0) == 0)
    def _():
        half_ref[...] = half_of(which_ref, d_ref)
        put_sides(a_ref, sides_ref)

    put_tap(out_ref, sides_ref, half_ref)


def mid_grad(name, body, which, ins, act, with_d):
    rows, width = act.shape
    half = width // 2
    grad = pl.BlockSpec((width, half), lambda t, w: (t, 0))
    return run(
        named(name, body, *([len(ins) - 7] if with_d else [])),
        (TAPS,),
        [whole(a) for a in ins],
        [whole(act), grad] if with_d else grad,
        [shape(act.shape, BF16), shape((TAPS * width, half))]
        if with_d
        else shape((TAPS * width, half)),
        [
            pltpu.VMEM((3, rows // PIX, PIX + 2 * COLS, width), BF16),
            pltpu.VMEM((rows, half), BF16),
        ],
        flops=2 * rows * TAPS * width * half,
        bytes_accessed=4 * TAPS * width * half,
        prefetch=1,
    )(which, *ins)


def in_grad_body(counts, refs):
    which_ref, part_refs = refs[0], refs[1 : 1 + counts]
    dy_ref, h_ref, v_ref, info_ref, number_ref, gain_ref, x_ref, d_ref, send_ref, keep_ref = refs[1 + counts :]

    @pl.when(pl.program_id(0) == 0)
    def _():
        put_norm_back(part_refs, dy_ref, h_ref, v_ref, info_ref, number_ref, gain_ref, d_ref)

    grad = tn_dot(x_ref[...], d_ref[...])
    half = grad.shape[1] // 2
    low = which_ref[0] == 0
    left, right = grad[:, :half], grad[:, half:]
    send_ref[...] = jnp.where(low, left, right)
    keep_ref[...] = jnp.where(low, right, left)


def in_grad(which, parts, dy, h, valid, info, number, gain, x):
    rows, width = dy.shape
    depth = x.shape[1]
    half = width // 2
    tile = 512
    ins = [*parts, dy, h, valid, info, number, gain]
    grad = pl.BlockSpec((tile, half), lambda c, w: (c, 0))
    return run(
        named("in_grad", in_grad_body, len(parts)),
        (depth // tile,),
        [whole(a) for a in ins] + [pl.BlockSpec((rows, tile), lambda c, w: (0, c))],
        [whole(dy), grad, grad],
        [shape(dy.shape, BF16), shape((depth, half)), shape((depth, half))],
        flops=2 * rows * depth * width,
        bytes_accessed=2 * x.size + 4 * depth * width + 10 * dy.size,
        prefetch=1,
    )(which, *ins, x)


def second_back_body(d_ref, w_ref, v_ref, h1_ref, info_ref, gain_ref, shift_ref, dy_ref, stats_ref, moved_ref, packed_ref):
    rows, width = d_ref.shape

    @pl.when(pl.program_id(0) == 0)
    def _():
        for r in range(3):
            for c in range(3):
                tap = 3 * r + c
                packed_ref[c, :, r * width : (r + 1) * width] = w_ref[
                    tap * width : (tap + 1) * width, :
                ]

    blank = jnp.zeros((COLS, width), BF16)
    for k in range(0, rows, PIX):
        moved_ref[k : k + PIX - COLS, 0:width] = d_ref[k + COLS : k + PIX, :]
        moved_ref[k + PIX - COLS : k + PIX, 0:width] = blank
        moved_ref[k : k + COLS, 2 * width :] = blank
        moved_ref[k + COLS : k + PIX, 2 * width :] = d_ref[k : k + PIX - COLS, :]
    moved_ref[:, width : 2 * width] = d_ref[...]
    parts = [nt_dot(moved_ref[...], packed_ref[c]) for c in range(3)]
    place = cell_column(rows)
    dy_ref[...] = (
        parts[1]
        + pltpu.roll(parts[2], 1, 0) * (place >= 1).astype(F32)
        + pltpu.roll(parts[0], rows - 1, 0) * (place <= CELL - 2).astype(F32)
    )
    put_back(dy_ref, h1_ref, v_ref, info_ref, gain_ref, shift_ref, stats_ref)


def second_back(d, weight, valid, h1, info, gain, shift, micro):
    rows, width = d.shape[0] // micro, d.shape[1]
    mid = pl.BlockSpec((rows, width), lambda m: (m, 0))
    return run(
        second_back_body,
        (micro,),
        [
            mid,
            whole(weight),
            pl.BlockSpec((rows, 1), lambda m: (m, 0)),
            mid,
            per_micro(info),
            whole(gain),
            whole(shift),
        ],
        [mid, pl.BlockSpec((1, 2, width), lambda m: (m, 0, 0))],
        [shape(d.shape), shape((micro, 2, width))],
        [pltpu.VMEM((rows, 3 * width), BF16), pltpu.VMEM((3, width, 3 * width), BF16)],
        flops=2 * micro * rows * weight.size,
        bytes_accessed=10 * d.size,
    )(d, weight, valid, h1, info, gain, shift)


def pixels_body(d_ref, w_ref, wide_ref, slope_ref, out_ref):
    rows, channels = out_ref.shape
    width = 512
    for j in range(0, channels, width):
        lane = pl.ds(j, width)
        grad = nt_dot(d_ref[...], w_ref[lane, :])
        for k in range(rows // PIX):
            wide = wide_ref[pl.ds(k * COLS, COLS), lane]
            for r in range(ROWS):
                first = k * PIX + r * COLS
                at = pl.ds(first, COLS)
                out_ref[at, lane] = (
                    grad[first : first + COLS] + wide * slope_ref[at, lane].astype(F32)
                ).astype(BF16)


def pixels_grad(d, weight, wide, slope, micro):
    rows, channels = slope.shape[0] // micro, slope.shape[1]
    lines = wide.shape[0] // micro
    big = pl.BlockSpec((rows, channels), lambda m: (m, 0))
    return run(
        pixels_body,
        (micro,),
        [
            pl.BlockSpec((rows, d.shape[1]), lambda m: (m, 0)),
            pl.BlockSpec(weight.shape, lambda m: (0, 0)),
            pl.BlockSpec((lines, channels), lambda m: (m, 0)),
            big,
        ],
        big,
        shape(slope.shape, BF16),
        flops=2 * slope.shape[0] * weight.size,
        bytes_accessed=4 * slope.size,
    )(d, weight, wide, slope)


def factor_body(feat_ref, other_feat_ref, dg_ref, far_ref, near_ref, both_ref, out_ref):
    left = jnp.concatenate([feat_ref[...], other_feat_ref[...]], 0).astype(BF16)
    lines = dg_ref.shape[0] // 2
    right = jnp.concatenate(
        [
            ref[c * lines : (c + 1) * lines, :]
            for c in range(2)
            for ref in (dg_ref, near_ref, far_ref, both_ref)
        ],
        0,
    ).astype(BF16)
    out_ref[...] = tn_dot(left, right)


def factor_grad(feat, other_feat, dg, far, near, both):
    lines, depth = feat.shape
    width = dg.shape[1]
    tile = 512
    left = pl.BlockSpec((lines, tile), lambda c: (0, c))
    return run(
        factor_body,
        (depth // tile,),
        [left, left] + [whole(dg)] * 4,
        pl.BlockSpec((tile, width), lambda c: (c, 0)),
        shape((depth, width)),
        flops=4 * lines * depth * width,
        bytes_accessed=4 * depth * width,
    )(feat, other_feat, dg, far, near, both)


def embed_body(protos, counts, members, refs):
    part_refs = refs[:counts]
    g_ref, gain_ref, shift_ref, w_ref, bias_ref, table_ref, queue_ref, act_ref, z_ref, inverse_ref, unit_ref, logits_ref, batch_ref, line_ref, sums_ref, info_ref = refs[counts:]
    micro = info_ref.shape[0]
    crops = g_ref.shape[0] // micro
    for m in range(micro):
        at = slice(m * crops, (m + 1) * crops)
        mean, scaled = norm_of(part_refs, members, m)
        info_ref[m, 0:1, :] = mean
        info_ref[m, 1:2, :] = scaled
        pre = (g_ref[at, :] - mean) * scaled * gain_ref[...] + shift_ref[...]
        act_ref[at, :] = (pre * sigmoid(pre)).astype(BF16)
    z = jnp.dot(act_ref[...], w_ref[...], preferred_element_type=F32) + bias_ref[...]
    inverse = lax.rsqrt(jnp.sum(z * z, 1, keepdims=True) + eps_unit)
    unit = (z * inverse).astype(BF16)
    z_ref[...] = z
    inverse_ref[...] = inverse
    unit_ref[...] = unit
    logits = jnp.dot(unit, table_ref[...], preferred_element_type=F32)
    logits_ref[...] = logits
    real = lax.broadcasted_iota(jnp.int32, (1, logits.shape[1]), 1) < protos
    batch = jnp.where(real, jnp.exp(logits / transport_epsilon), 0.0)
    batch_ref[...] = batch
    queued = jnp.dot(queue_ref[...], table_ref[...], preferred_element_type=F32)
    line = jnp.where(real, jnp.exp(queued / transport_epsilon), 0.0)
    line_ref[...] = line
    queue_sum = jnp.sum(line, axis=0, keepdims=True)
    for m in range(micro):
        at = slice(m * crops, (m + 1) * crops)
        sums_ref[m : m + 1, :] = jnp.sum(batch[at], axis=0, keepdims=True) + queue_sum


def embed_product(parts, members, protos, g, gain, shift, weight, bias, table, queue):
    lines = g.shape[0]
    micro = parts[0].shape[0]
    feat = weight.shape[1]
    wide = table.shape[1]
    outs = [
        shape(g.shape, BF16),
        shape((lines, feat)),
        shape((lines, 1)),
        shape((lines, feat), BF16),
        shape((lines, wide)),
        shape((lines, wide)),
        shape((queue.shape[0], wide)),
        shape((micro, wide)),
        shape((micro, 2, g.shape[1])),
    ]
    ins = [*parts, g, gain, shift, weight, bias, table, queue]
    return run(
        named("embed", embed_body, protos, len(parts), members),
        (1,),
        [whole(a) for a in ins],
        [whole(a) for a in outs],
        outs,
        flops=2 * lines * table.size,
        bytes_accessed=8 * lines * wide,
    )(*ins)


def sweep_body(protos, counts, refs):
    part_refs = refs[:counts]
    batch_ref, queue_ref, new_batch_ref, new_queue_ref, sums_ref = refs[counts:]
    micro, wide = sums_ref.shape
    crops = batch_ref.shape[0] // micro
    lines = new_queue_ref.shape[0] // micro
    shared = queue_ref.shape[0] == lines
    real = lax.broadcasted_iota(jnp.int32, (1, wide), 1) < protos
    for m in range(micro):
        column = jnp.where(real, tree([ref[m : m + 1, :] for ref in part_refs]), 1.0)
        at = slice(m * crops, (m + 1) * crops)
        batch = batch_ref[at, :] / column
        batch = batch / jnp.sum(batch, 1, keepdims=True)
        new_batch_ref[at, :] = batch
        own = slice(m * lines, (m + 1) * lines)
        queue = queue_ref[slice(0, lines) if shared else own, :] / column
        queue = queue / jnp.sum(queue, 1, keepdims=True)
        new_queue_ref[own, :] = queue
        sums_ref[m : m + 1, :] = jnp.sum(batch, axis=0, keepdims=True) + jnp.sum(
            queue, axis=0, keepdims=True
        )


def sweep(parts, protos, batch, queue, lines):
    micro, wide = parts[0].shape
    outs = [shape(batch.shape), shape((micro * lines, wide)), shape(parts[0].shape)]
    ins = [*parts, batch, queue]
    return run(
        named("sweep", sweep_body, protos, len(parts)),
        (1,),
        [whole(a) for a in ins],
        [whole(a) for a in outs],
        outs,
        flops=20 * batch.size,
        bytes_accessed=16 * batch.size,
    )(*ins)


def split_dot(dot, left, right, wide_left):
    value = left if wide_left else right
    high = value.astype(BF16)
    low = (value - high.astype(F32)).astype(BF16)
    if wide_left:
        return dot(high, right) + dot(low, right)
    return dot(left, high) + dot(left, low)


def pack_small(low, send_ref, keep_ref, protos, embed):
    shards, lines, width = send_ref.shape
    lines = lines // 2
    rows = protos.shape[0] // shards // 2
    half = protos.shape[1] // 2
    groups = half // width
    lane = embed.shape[1]
    below = lines - groups * rows

    def put(d, place, columns, one, two):
        keep_ref[d, place, columns] = jnp.where(low, one, two)
        send_ref[d, place, columns] = jnp.where(low, two, one)

    for d in range(shards):
        for y in range(2):
            first = (2 * d + y) * rows
            for q in range(groups):
                start = y * lines + q * rows
                one, two = [
                    protos[first : first + rows, c * half + q * width : c * half + (q + 1) * width]
                    for c in range(2)
                ]
                put(d, slice(start, start + rows), slice(None), one, two)
            for q in range(width // lane):
                one, two = [
                    embed[first : first + below]
                    for first in [
                        (((2 * d + c) * 2 + y) * (width // lane) + q) * below for c in range(2)
                    ]
                ]
                start = y * lines + groups * rows
                put(d, slice(start, start + below), slice(q * lane, (q + 1) * lane), one, two)


def unpack_small(halves, protos, embed):
    shards, lines, width = halves[0].shape
    lines = lines // 2
    packed = jnp.stack(halves).reshape(2, shards, 2, lines, width)
    rows = protos[0] // shards // 2
    groups = protos[1] // 2 // width
    lane = embed[1]
    above = packed[:, :, :, : groups * rows].reshape(2, shards, 2, groups, rows, width)
    below = packed[:, :, :, groups * rows :]
    below = below.reshape(2, shards, 2, lines - groups * rows, width // lane, lane)
    return (
        above.transpose(1, 2, 4, 0, 3, 5).reshape(protos),
        below.transpose(1, 0, 2, 4, 3, 5).reshape(embed),
    )


def packed_shape(protos, embed, shards):
    width = 512
    lines = protos[0] // shards // 2 * (protos[1] // 2 // width)
    return (shards, 2 * (lines + embed[0] * embed[1] // shards // 4 // width), width)


def loss_body(protos, scale, counts, refs):
    which_ref, part_refs = refs[0], refs[1 : 1 + counts]
    batch_ref, logits_ref, unit_ref, z_ref, inverse_ref, act_ref, g_ref, info_ref, gain_ref, shift_ref, w_ref, table_ref, send_ref, keep_ref, dy_ref, sums_ref = refs[1 + counts :]
    micro, wide = part_refs[0].shape
    lines = batch_ref.shape[0]
    crops = lines // micro
    real = lax.broadcasted_iota(jnp.int32, (1, wide), 1) < protos
    odd = lax.broadcasted_iota(jnp.int32, (crops, 1), 0) % 2 == 1
    parts = []
    loss = jnp.zeros((1, 1), F32)
    for m in range(micro):
        at = slice(m * crops, (m + 1) * crops)
        codes = batch_ref[at, :] / jnp.where(
            real, tree([ref[m : m + 1, :] for ref in part_refs]), 1.0
        )
        codes = codes / jnp.sum(codes, 1, keepdims=True)
        partner = jnp.where(odd, pltpu.roll(codes, 1, 0), pltpu.roll(codes, crops - 1, 0))
        sharp = logits_ref[at, :] / softmax_sharpness
        top = jnp.max(jnp.where(real, sharp, -jnp.inf), 1, keepdims=True)
        shifted = sharp - top
        mass = jnp.where(real, jnp.exp(shifted), 0.0)
        total = jnp.sum(mass, 1, keepdims=True)
        chance = shifted - jnp.log(total)
        loss += jnp.sum(jnp.sum(partner * chance, 1, keepdims=True), 0, keepdims=True)
        weight = jnp.sum(partner, 1, keepdims=True)
        parts.append((scale / softmax_sharpness) * (weight * (mass / total) - partner))
    d_scores = jnp.concatenate(parts, 0)
    unit = unit_ref[...]
    grad_protos = split_dot(tn_dot, unit, d_scores, False)
    d_unit = split_dot(nt_dot, d_scores, table_ref[...], True)
    z = z_ref[...]
    inverse = inverse_ref[...]
    dz = inverse * d_unit - z * (inverse * inverse * inverse) * jnp.sum(
        z * d_unit, 1, keepdims=True
    )
    grad_embed = split_dot(tn_dot, act_ref[...], dz, False)
    pack_small(which_ref[0] == 0, send_ref, keep_ref, grad_protos, grad_embed)
    d_act = split_dot(nt_dot, dz, w_ref[...], True)
    for m in range(micro):
        at = slice(m * crops, (m + 1) * crops)
        normal = (g_ref[at, :] - info_ref[m, 0:1, :]) * info_ref[m, 1:2, :]
        pre = normal * gain_ref[...] + shift_ref[...]
        dy = d_act[at] * slope_of(pre)
        dy_ref[at, :] = dy
        sums_ref[m : m + 1, : dy.shape[1]] = jnp.sum(dy, axis=0, keepdims=True)
        sums_ref[micro + m : micro + m + 1, : dy.shape[1]] = jnp.sum(
            dy * normal, axis=0, keepdims=True
        )
    feat = z.shape[1]
    wide = dy_ref.shape[1]
    extra = jnp.concatenate(
        [jnp.sum(dz, axis=0, keepdims=True), jnp.broadcast_to(-scale * loss, (1, feat))], 1
    )
    sums_ref[:, wide:] = jnp.broadcast_to(extra, (2 * micro, 2 * feat))


def loss_grads(which, parts, protos, scale, batch, logits, unit, z, inverse, act, g, info, gain, shift, weight, table, shards):
    ins = [*parts, batch, logits, unit, z, inverse, act, g, info, gain, shift, weight, table]
    micro = info.shape[0]
    outs = [
        shape(packed_shape(table.shape, weight.shape, shards)),
        shape(packed_shape(table.shape, weight.shape, shards)),
        shape(g.shape),
        shape((2 * micro, g.shape[1] + 2 * weight.shape[1])),
    ]
    return run(
        named("loss", loss_body, protos, scale, len(parts)),
        (1,),
        [whole(a) for a in ins],
        [whole(a) for a in outs],
        outs,
        flops=8 * table.size * batch.shape[0],
        bytes_accessed=16 * batch.size,
        prefetch=1,
    )(which, *ins)


def pick_block(rows, width, cell, *fixed):
    return pl.BlockSpec((1, rows, width), lambda g, w: cell(g, *fixed, w[0], w[1], w[2]) + (0,))


def sent_first(g, i, core, x, y):
    z, b = 2 * g + i // 2, i % 2
    return (2 * z + (1 - core) * (1 - x) + core * b, (1 - core) * b + core * (1 - y))


def kept_second(g, i, core, x, y):
    return (2 * (2 * g + i) + x, y)


def sent_second(g, i, core, x, y):
    z = 2 * g + i
    return (2 * z + (1 - core) * x + core * (1 - x), (1 - core) * (1 - y) + core * y)


def add_groups(refs, sizes, out_ref, index, extra=None):
    start = 0
    place = 0
    for count, rows in sizes:
        value = refs[place][0]
        for ref in refs[place + 1 : place + count]:
            value = value + ref[0]
        if extra is not None:
            value = value + extra[0, start : start + rows, :]
        out_ref[index, start : start + rows, :] = value
        place += count
        start += rows


def group_sizes(groups):
    return [(len(addends), addends[0].shape[1] // 2) for addends in groups]


def first_send(scalars, groups):
    sizes = group_sizes(groups)
    shards, _, width = groups[0][0].shape
    lines = sum(rows for _, rows in sizes)
    flat = [array for addends in groups for array in addends]
    specs = []
    for i in range(4):
        for array in flat:
            specs.append(pick_block(array.shape[1] // 2, width, sent_first, i))

    def body(refs):
        refs = refs[1:]
        for i in range(4):
            add_groups(refs[i * len(flat) : (i + 1) * len(flat)], sizes, refs[-1], i)

    return run(
        named("first_send", body),
        (shards // 4,),
        specs,
        pl.BlockSpec((4, lines, width), lambda g, w: (g, 0, 0)),
        shape((shards, lines, width)),
        bytes_accessed=4 * lines * width * shards * 3,
        prefetch=1,
    )(scalars, *(flat * 4))


def second_send(scalars, groups, came):
    sizes = group_sizes(groups)
    shards, _, width = groups[0][0].shape
    lines = sum(rows for _, rows in sizes)
    flat = [array for addends in groups for array in addends]
    specs = []
    for cell in (sent_second, kept_second):
        for i in range(2):
            for array in flat:
                specs.append(pick_block(array.shape[1] // 2, width, cell, i))

    def bit(w):
        return (1 - w[0]) * w[2] + w[0] * w[1]

    for flip in (1, 0):
        for i in range(2):
            specs.append(
                pl.BlockSpec(
                    (1, lines, width),
                    lambda g, w, i=i, flip=flip: (2 * (2 * g + i) + (1 - bit(w) if flip else bit(w)), 0, 0),
                )
            )
    out = pl.BlockSpec((2, lines, width), lambda g, w: (g, 0, 0))

    def body(refs):
        refs = refs[1:]
        count = len(flat)
        came_refs = refs[4 * count : 4 * count + 4]
        for side in range(2):
            for i in range(2):
                place = 2 * side + i
                add_groups(
                    refs[place * count : (place + 1) * count],
                    sizes,
                    refs[-2 + side],
                    i,
                    came_refs[place],
                )

    return run(
        named("second_send", body),
        (shards // 4,),
        specs,
        [out, out],
        [shape((shards // 2, lines, width))] * 2,
        bytes_accessed=4 * lines * width * shards * 4,
        prefetch=1,
    )(scalars, *(flat * 4), *([came] * 4))


def place_early_body(scalars_ref, mine_ref, far_ref, mine_core_ref, far_core_ref, out_ref, embed_ref, protos_ref, head_ref):
    lines = out_ref.shape[0]
    rows = protos_ref.shape[0] // 2
    wide = 512
    groups = protos_ref.shape[1] // 2 // wide
    lane = embed_ref.shape[1]
    below = embed_ref.shape[0] // 4 // (wide // lane)
    start = lines + groups * rows + below
    for c, y, ref in ((0, 0, mine_ref), (0, 1, far_ref), (1, 0, mine_core_ref), (1, 1, far_core_ref)):
        c = scalars_ref[0] if c == 0 else 1 - scalars_ref[0]
        y = scalars_ref[2] if y == 0 else 1 - scalars_ref[2]
        column = pl.multiple_of((2 * c + y) * wide, wide)
        out_ref[:, pl.ds(column, wide)] = ref[0:lines, :]
        head_ref[:, pl.ds(column, wide)] = ref[start:, :]
        at = pl.ds(pl.multiple_of(y * rows, rows), rows)
        for q in range(groups):
            column = pl.multiple_of((c * groups + q) * wide, wide)
            protos_ref[at, pl.ds(column, wide)] = ref[lines + q * rows : lines + (q + 1) * rows, :]
        for q in range(wide // lane):
            first = pl.multiple_of(((2 * c + y) * (wide // lane) + q) * below, below)
            embed_ref[pl.ds(first, below), :] = ref[
                lines + groups * rows : start, q * lane : (q + 1) * lane
            ]


def place_late_body(scalars_ref, mine_ref, far_ref, mine_core_ref, far_core_ref, *out_refs):
    for c, y, ref in ((0, 0, mine_ref), (0, 1, far_ref), (1, 0, mine_core_ref), (1, 1, far_core_ref)):
        c = scalars_ref[0] if c == 0 else 1 - scalars_ref[0]
        y = scalars_ref[2] if y == 0 else 1 - scalars_ref[2]
        start = 0
        for out_ref in out_refs:
            rows, width = out_ref.shape[0] // 2, out_ref.shape[1] // 2
            out_ref[
                pl.ds(pl.multiple_of(y * rows, rows), rows),
                pl.ds(pl.multiple_of(c * width, width), width),
            ] = ref[start : start + rows, :]
            start += rows


def placed_pieces(body, scalars, pieces, outs):
    return run(
        body,
        (1,),
        [whole(a) for a in pieces],
        [whole(a) for a in outs],
        outs,
        prefetch=1,
    )(scalars, *pieces)


def on_device(
    pixels,
    crop_map,
    queue_rows,
    conv_in,
    gain_one,
    shift_one,
    conv_mid,
    gain_two,
    shift_two,
    conv_out,
    gain_three,
    shift_three,
    head_weight,
    head_gain,
    head_shift,
    embed_weight,
    embed_bias,
    prototypes,
):
    micro, canvas, pixel_count, channels = pixels.shape
    devices = lax.axis_size("dp") * lax.axis_size("hst")
    crops = canvas * SLOTS
    total_crops = crops * devices * 1.0
    loss_scale = 1.0 / (micro * total_crops)
    x = pixels.reshape(micro * canvas * pixel_count, channels)
    valid = (crop_map < SLOTS).astype(F32).reshape(-1, 1)
    sizes = jnp.sum(
        (crop_map[:, :, None, :] == jnp.arange(SLOTS, dtype=jnp.int32)[:, None]).astype(F32), 3
    ).reshape(-1, 1)

    shards = lax.axis_size("dp")
    quick = shards == 8 and lax.axis_size("hst") == 4
    packs = 8
    protos = prototypes.shape[1]
    table = jnp.pad(prototypes, ((0, 0), (0, -protos % 1024)))

    def row(vector):
        return vector.reshape(1, -1)

    masks = dp_masks()
    near, far = masks[0], masks[1:]
    core = bit_of(1)
    side = bit_of(2)
    scalars = jnp.stack([core, bit_of(near), side]).astype(jnp.int32)
    keep_half = core.astype(jnp.int32).reshape(1)
    send_half = 1 - keep_half

    h1, stats = first_product(x, conv_in, valid, micro)
    members, counts = first_parts(stats)
    act_one, h2, stats, info_one = second_product(
        members, h1, valid, row(gain_one), row(shift_one), conv_mid, micro
    )
    parts = moment_parts(stats, counts)
    act_two, h3, stats, info_two = third_product(
        parts, members, h2, valid, row(gain_two), row(shift_two), conv_out, micro
    )
    parts = moment_parts(stats, counts)
    feat, info_three = pool(
        parts, members, h3, x, valid, row(gain_three), row(shift_three), sizes, micro
    )

    lines = feat.shape[0]
    if quick:
        by_bit = feat.reshape(lines, shards // 2, 2, -1)
        bit = bit_of(near)
        feat_keep = at(by_bit, bit, 2).reshape(lines, -1)
        feat_send = at(by_bit, 1 - bit, 2).reshape(lines, -1)
        feat_near = swap(feat_send, near)
    g, stats = head_product(feat, head_weight, micro)
    if quick:
        stats, feat_near = tie(stats, feat_near)

    crop_counts = []
    crop_members = []
    number = crops * 1.0
    for group in sync_groups():
        crop_members = [number] * (len(group) + 1)
        crop_counts.append(crop_members)
        number = number * (len(group) + 1)
    slopes = []

    def slope_filler(index):
        def fill(gate):
            source = tie(h3, gate)[0]
            slopes[:] = slope_part(
                source, x, valid, info_three, row(gain_three), row(shift_three), micro, index, slopes
            )
            return slopes

        return fill

    parts = moment_parts(stats, crop_counts, ((), (slope_filler(0),), (slope_filler(1),)))

    act_four, embedded, inverse, unit_rows, logits, batch, queue, column, info_four = embed_product(
        parts,
        crop_members,
        protos,
        g,
        row(head_gain),
        row(head_shift),
        embed_weight,
        row(embed_bias),
        table,
        queue_rows,
    )
    fillers = ((), (slope_filler(2),), (slope_filler(3),))
    for _ in range(SINK_ITERS - 1):
        parts = sum_parts(column, fillers)
        fillers = ()
        batch, queue, column = sweep(parts, protos, batch, queue, queue_rows.shape[0])
    parts = sum_parts(column, fillers)
    slope, slope_first, slope_second = slopes
    which = (1 - send_half) if quick else jnp.zeros((1,), jnp.int32)
    small_send, small_keep, dy_four, payload = loss_grads(
        which,
        parts,
        protos,
        loss_scale,
        batch,
        logits,
        unit_rows,
        embedded,
        inverse,
        act_four,
        g,
        info_four,
        row(head_gain),
        row(head_shift),
        embed_weight,
        table,
        packs,
    )
    parts = sum_parts(payload)
    payload = tree(list(parts))
    channel_sums = payload[:, : head_gain.shape[0]]
    first_four, second_four = channel_sums[:micro], channel_sums[micro:]
    extra = payload[0, head_gain.shape[0] :]
    grad_bias, total_loss = extra[: embed_bias.shape[0]], extra[embed_bias.shape[0]]

    if quick:
        feat_keep, feat_near, small_send, *parts = tie(feat_keep, feat_near, small_send, *parts)
        feat_near = jnp.concatenate([feat_keep, feat_near], 0)
        feat_far = swap(feat_near, 2)
        small_recv = swap(small_send, 1)
    dg, wide, sums = head_back(
        parts,
        dy_four,
        g,
        info_four,
        row(head_gain),
        head_weight,
        sizes,
        slope_first,
        slope_second,
        total_crops,
    )
    first_norm = (h1, valid, info_one, info_one, row(gain_one))
    second_norm = (h2, valid, info_two, info_one, row(gain_two))

    def from_third(which, parts):
        return third_back(
            which,
            parts,
            wide,
            slope,
            h3,
            valid,
            info_three,
            row(gain_three),
            info_one,
            conv_out,
            act_two,
            h2,
            info_two,
            row(gain_two),
            row(shift_two),
            micro,
            shards,
        )

    def from_second(d):
        return second_back(
            d, conv_mid, valid, h1, info_one, row(gain_one), row(shift_one), micro
        )

    if quick:
        sums, dg, feat_far, small_recv = tie(sums, dg, feat_far, small_recv)
        feat_both = jnp.concatenate([feat_near, feat_far], 0)
        split = dg.reshape(lines, 2, -1)
        dg_send = at(split, 1 - core, 1)

        def core_filler(gate):
            source, other = tie(dg_send, feat_both, gate)[:2]
            grads["dg"] = swap(source, 1)
            grads["feat"] = swap(other, 1)
            return [grads["dg"], grads["feat"]]

        grads = {}
        parts_three = sum_parts(sums, ((), (core_filler,)))
        feat_other = grads["feat"]
        split = jnp.concatenate([at(split, core, 1), grads["dg"]], 0).reshape(2 * lines, 2, -1)
        dg_here, dg_there = at(split, side, 1), at(split, 1 - side, 1)
        *parts_three, dg_here, dg_there = tie(*parts_three, dg_here, dg_there)
        dg_far, dg_near, dg_both = swap(dg_there, 2), swap(dg_here, near), swap(dg_there, 2 + near)
        dy, sums, out_send, out_keep = from_third(send_half, parts_three)
        sums, dy, out_send, dg_far, dg_near, dg_both = tie(
            sums, dy, out_send, dg_far, dg_near, dg_both
        )
        small = [small_keep, small_recv]

        def out_filler(gate):
            grads["out"] = swap(tie(out_send, gate)[0], 1)
            return [grads["out"]]

        def head_filler(gate):
            source = tie(dg_near, gate)[0]
            grads["head"] = factor_grad(feat_both, feat_other, dg_here, dg_far, source, dg_both)
            return [grads["head"]]

        def early_filler(gate):
            source = tie(grads["out"], gate)[0]
            grads["early"] = [[out_keep, source], small]
            grads["early_out"] = first_send(scalars, grads["early"])
            return [grads["early_out"]]

        parts_two = sum_parts(sums, ((), (out_filler,), (head_filler, early_filler)))

        early = grads["early"]
        *parts_two, early_out, partial = tie(*parts_two, grads["early_out"], grads["head"])
        early_came = core_swap(early_out, near, 2)
        partial = partial.reshape(2, 2, -1, partial.shape[1])
        head = dp_halves([partial], far[0], 1)
        d_two, mid_send = mid_grad(
            "mid_first",
            mid_first_body,
            send_half,
            [*parts_two, dy, *second_norm, act_one],
            act_one,
            True,
        )
        d_two, mid_send, early_came = tie(d_two, mid_send, early_came)
        mid_recv = swap(mid_send, 1)
        early_out, early_keep = second_send(scalars, early, early_came)
        early_came = core_swap(early_out, 2, near)
        mid_keep = mid_grad(
            "mid_second", mid_second_body, keep_half, [d_two, act_one], act_one, False
        )
        mid_keep, mid_recv, early_came, head[-1] = tie(mid_keep, mid_recv, early_came, head[-1])

        def sharded(array):
            return array.reshape(shards, -1, array.shape[-1])

        def by_bits(array):
            return array.reshape((2, 2) + array.shape[1:])

        late = [[sharded(mid_keep), sharded(mid_recv)]]
        mid_out = first_send(scalars, late)
        d_two, mid_out = tie(d_two, mid_out)
        mid_came = core_swap(mid_out, near, 2)
        head = dp_halves(head, far[1], 0)
        dy, sums = from_second(d_two)
        dy, sums, mid_came, head[-1], early_keep, early_came = tie(
            dy, sums, mid_came, head[-1], early_keep, early_came
        )
        early = [by_bits(early_keep), by_bits(early_came)]

        def early_z_filler(gate):
            grads["z"] = dp_halves(early, far[0], 1)
            return [grads["z"][-1]]

        def mid_filler(gate):
            source = tie(mid_came, gate)[0]
            grads["mid"] = second_send(scalars, late, source)
            return grads["mid"]

        parts_one = sum_parts(sums, ((), (early_z_filler,), (mid_filler,)))
        mid_out, mid_keep = grads["mid"]
        *parts_one, mid_out, early_came = tie(*parts_one, mid_out, grads["z"][-1])
        early = dp_halves(grads["z"][:-1] + [early_came], far[1], 0)
        mid_came = core_swap(mid_out, 2, near)
        d_one, in_send, in_keep = in_grad(send_half, parts_one, dy, *first_norm, x)
        d_one, in_send, in_keep, mid_came, early[-1] = tie(
            d_one, in_send, in_keep, mid_came, early[-1]
        )
        in_recv = swap(in_send, 1)
        inner = [[sharded(in_keep), sharded(in_recv)]]
        in_out = first_send(scalars, inner)
        mid = dp_halves([by_bits(mid_keep), by_bits(mid_came)], far[0], 1)
        early_mine = jnp.concatenate([sum(early), sum(head)], 0)
        d_one, in_out, early_mine = tie(d_one, in_out, early_mine)
        in_came = core_swap(in_out, near, 2)
        early_far = swap(early_mine, 2)
        early_core = swap(early_mine, 1)
        grad_x = pixels_grad(d_one, conv_in, wide, slope, micro)
        grad_x, in_came, mid[-1], early_core = tie(grad_x, in_came, mid[-1], early_core)
        in_out, in_keep = second_send(scalars, inner, in_came)
        in_came = core_swap(in_out, 2, near)
        mid = dp_halves(mid, far[1], 0)
        inner = dp_halves([by_bits(in_keep), by_bits(in_came)], far[0], 1)
        early_far = tie(early_far, inner[-1])[0]
        early_pieces = [early_mine, early_far, early_core, swap(early_far, 1)]
        inner = dp_halves(inner, far[1], 0)
        channel = channels // shards
        early_grads = placed_pieces(
            place_early_body,
            scalars,
            early_pieces,
            [
                shape((conv_out.shape[0] // shards, channels)),
                shape((embed_weight.shape[0] // shards, embed_weight.shape[1])),
                shape((table.shape[0] // shards, table.shape[1])),
                shape((channel, head_weight.shape[1])),
            ],
        )
        late_mine = jnp.concatenate([sum(mid), sum(inner)], 0)
        late_far = swap(late_mine, 2)
        late_core = swap(late_mine, 1)
        late_far, late_core, *early_grads = tie(late_far, late_core, *early_grads)
        grad_conv_out, grad_embed, grad_protos, grad_head = early_grads
        grad_protos = grad_protos[:, :protos]
        grad_conv_mid, grad_conv_in = placed_pieces(
            place_late_body,
            scalars,
            [late_mine, late_far, late_core, swap(late_far, 1)],
            [
                shape((conv_mid.shape[0] // shards, conv_mid.shape[1])),
                shape((channel, conv_in.shape[1])),
            ],
        )
    else:
        low, high = jnp.zeros((1,), jnp.int32), jnp.ones((1,), jnp.int32)

        def reduced(array):
            return lax.psum(lax.psum_scatter(array, "dp", scatter_dimension=0, tiled=True), "hst")

        parts_three = sum_parts(sums)
        dy, sums, out_low, out_high = from_third(low, parts_three)
        parts_two = sum_parts(sums)
        ins = [*parts_two, dy, *second_norm, act_one]
        d_two, mid_low = mid_grad("mid_first", mid_first_body, low, ins, act_one, True)
        mid_high = mid_grad("mid_second", mid_second_body, high, [d_two, act_one], act_one, False)
        dy, sums = from_second(d_two)
        parts_one = sum_parts(sums)
        d_one, in_low, in_high = in_grad(low, parts_one, dy, *first_norm, x)
        grad_x = pixels_grad(d_one, conv_in, wide, slope, micro)
        out = jnp.stack([out_low, out_high])
        out = out.reshape(2, shards, -1, conv_out.shape[0] // shards, out.shape[-1])
        small_protos, small_embed = unpack_small(
            [small_keep, small_send], table.shape, embed_weight.shape
        )
        grad_conv_out = reduced(out.transpose(1, 3, 0, 2, 4).reshape(conv_out.shape))
        grad_conv_mid = reduced(jnp.concatenate([mid_low, mid_high], 1))
        grad_conv_in = reduced(jnp.concatenate([in_low, in_high], 1))
        grad_head = reduced(
            jnp.dot(feat.astype(BF16).T, dg.astype(BF16), preferred_element_type=F32)
        )
        grad_embed = reduced(small_embed)
        grad_protos = reduced(small_protos)[:, :protos]

    def own_rows(vectors):
        sums = [jnp.sum(vector, 0) for vector in vectors]
        piece = sums[0].shape[0] // shards
        stacked = jnp.stack(sums)
        found = lax.dynamic_slice_in_dim(stacked, lax.axis_index("dp") * piece, piece, 1)
        return [found[i] for i in range(len(vectors))]

    def both_sums(parts):
        total = tree(list(parts))
        return [total[:, 1], total[:, 0]]

    small_ones = own_rows(both_sums(parts_one) + both_sums(parts_two))
    large_ones = own_rows(both_sums(parts_three) + [second_four, first_four])

    return (
        total_loss,
        grad_x.reshape(pixels.shape),
        grad_conv_in,
        small_ones[0],
        small_ones[1],
        grad_conv_mid,
        small_ones[2],
        small_ones[3],
        grad_conv_out,
        large_ones[0],
        large_ones[1],
        grad_head,
        large_ones[2],
        large_ones[3],
        grad_embed,
        lax.dynamic_slice_in_dim(
            grad_bias,
            lax.axis_index("dp") * (grad_bias.shape[0] // shards),
            grad_bias.shape[0] // shards,
            0,
        ),
        grad_protos,
    )


def solution(mesh):
    placed = (
        P(None, ("dp", "hst"), None, None),
        P(None, ("dp", "hst"), None),
        P(("dp", "hst"), None),
    ) + (P(),) * 15
    return jax.shard_map(
        on_device,
        mesh=mesh,
        in_specs=placed,
        out_specs=(
            P(),
            P(None, ("dp", "hst"), None, None),
            P("dp", None),
            P("dp"),
            P("dp"),
            P("dp", None),
            P("dp"),
            P("dp"),
            P("dp", None),
            P("dp"),
            P("dp"),
            P("dp", None),
            P("dp"),
            P("dp"),
            P("dp", None),
            P("dp"),
            P("dp", None),
        ),
        check_vma=False,
    )
```

```python
import functools

import jax
import jax.numpy as jnp
from jax import lax
from jax.experimental import pallas as pl
from jax.experimental.pallas import tpu as pltpu
from jax.sharding import PartitionSpec as P

ROWS = 8
COLS = 16
SLOTS = 4
CELL = COLS // SLOTS
PIX = ROWS * COLS
SINK_ITERS = 3
TAPS = 9

eps_norm = 1e-05
eps_unit = 1e-06
transport_epsilon = 0.05
softmax_sharpness = 0.1
highest = lax.Precision.HIGHEST
F32 = jnp.float32
BF16 = jnp.bfloat16
AXES = ("dp", "hst")
MIB = 1 << 20
LANES = 128


def swap(value, mask):
    count = lax.axis_size("dp") * lax.axis_size("hst")
    return lax.ppermute(value, AXES, [(i, i ^ mask) for i in range(count)])


def sync_groups():
    bits = (lax.axis_size("dp") * lax.axis_size("hst")).bit_length() - 1
    groups = [(1,)]
    bit = 1
    while bit < bits:
        if bit + 1 < bits:
            groups.append((1 << bit, 2 << bit, 3 << bit))
            bit += 2
        else:
            groups.append((1 << bit,))
            bit += 1
    return groups


def tree(parts):
    while len(parts) > 1:
        parts = [parts[i] + parts[i + 1] for i in range(0, len(parts), 2)]
    return parts[0]


def between(parts, gate, fillers):
    for filler in fillers:
        parts = list(tie(*parts, *filler(gate)))[: len(parts)]
    return parts


def pick(fillers, step):
    return fillers[step] if step < len(fillers) else ()


def sum_parts(value, fillers=()):
    groups = sync_groups()
    for step, group in enumerate(groups):
        parts = [value] + [swap(value, mask) for mask in group]
        parts = between(parts, value, pick(fillers, step))
        value = tree(parts)
    return parts


def merge(parts, members):
    whole = tree(list(members))
    mean = tree([n * part[:, 0] for n, part in zip(members, parts)]) / whole
    spread = tree(
        [part[:, 1] + n * (part[:, 0] - mean) ** 2 for n, part in zip(members, parts)]
    )
    return mean, spread, whole


def moment_parts(moments, counts, fillers=()):
    groups = sync_groups()
    for step, group in enumerate(groups):
        parts = [moments] + [swap(moments, mask) for mask in group]
        parts = between(parts, moments, pick(fillers, step))
        if step + 1 < len(groups):
            moments = jnp.stack(merge(parts, counts[step])[:2], 1)
    return parts


def first_parts(moments):
    groups = sync_groups()
    counts = []
    for step, group in enumerate(groups):
        parts = [moments] + [swap(moments, mask) for mask in group]
        if step + 1 < len(groups):
            members = [part[:, 2] for part in parts]
            moments = jnp.stack(merge(parts, members), 1)
            counts.append([n[:, :1] for n in members])
    return parts, counts


def bit_of(mask):
    index = lax.axis_index("dp") * lax.axis_size("hst") + lax.axis_index("hst")
    return (index // mask) % 2


def dp_masks():
    base = lax.axis_size("hst")
    return [base << j for j in range(lax.axis_size("dp").bit_length() - 1)]


def tie(first, *others):
    return lax.optimization_barrier((first,) + others)


def at(view, place, axis):
    return lax.dynamic_index_in_dim(view, place, axis, keepdims=False)


def core_swap(value, low, high):
    count = lax.axis_size("dp") * lax.axis_size("hst")
    pairs = [(i, i ^ (high if i % 2 else low)) for i in range(count)]
    return lax.ppermute(value, AXES, pairs)


def dp_halves(addends, mask, axis):
    bit = bit_of(mask)
    send = sum(at(array, 1 - bit, axis) for array in addends)
    return [at(array, bit, axis) for array in addends] + [swap(send, mask)]


def run(body, grid, in_specs, out_specs, out_shape, scratch=(), flops=0, bytes_accessed=0, prefetch=0, aliases=None):
    return pl.pallas_call(
        body,
        grid_spec=pltpu.PrefetchScalarGridSpec(
            num_scalar_prefetch=prefetch,
            grid=grid,
            in_specs=in_specs,
            out_specs=out_specs,
            scratch_shapes=list(scratch),
        ),
        out_shape=out_shape,
        name=body.__name__,
        input_output_aliases=aliases or {},
        compiler_params=pltpu.CompilerParams(
            vmem_limit_bytes=52 * MIB, dimension_semantics=("arbitrary",) * len(grid)
        ),
        cost_estimate=pl.CostEstimate(
            flops=flops, bytes_accessed=bytes_accessed, transcendentals=0
        ),
    )


def shape(dims, dtype=F32):
    return jax.ShapeDtypeStruct(tuple(dims), dtype)


def sigmoid(u):
    return 0.5 * jnp.tanh(0.5 * u) + 0.5


def norm_of(part_refs, members, m=0, lane=slice(None)):
    whole = tree(list(members))
    means = [ref[m, 0:1, lane] for ref in part_refs]
    mean = tree([n * one for n, one in zip(members, means)]) / whole
    spread = tree(
        [ref[m, 1:2, lane] + n * (one - mean) ** 2 for n, ref, one in zip(members, part_refs, means)]
    )
    return mean, lax.rsqrt(spread / whole + eps_norm)


def sums_of(part_refs, first, second, m=0):
    return (
        tree([ref[m, first : first + 1, :] for ref in part_refs]),
        tree([ref[m, second : second + 1, :] for ref in part_refs]),
    )


def counts_of(count_refs, m=0):
    return [ref[m, 2:3, 0:1] for ref in count_refs]


def whole(array):
    return pl.BlockSpec(array.shape, lambda *_: (0,) * len(array.shape))


def per_micro(array):
    return pl.BlockSpec((1,) + array.shape[1:], lambda m, *_: (m,) + (0,) * (array.ndim - 1))


def slope_of(u):
    s = sigmoid(u)
    return s * (1.0 + u * (1.0 - s))


def nt_dot(left, right):
    return lax.dot_general(left, right, (((1,), (1,)), ((), ())), preferred_element_type=F32)


def tn_dot(left, right):
    return lax.dot_general(left, right, (((0,), (0,)), ((), ())), preferred_element_type=F32)


def fold(y):
    return jnp.sum(y.reshape(y.shape[0] // 8, 8, y.shape[1]), 0)


def put_moments(stats_ref, h_ref, v_ref, with_count):
    rows, width = h_ref.shape
    chunk = 32
    lanes = 512
    v = v_ref[...]
    count = jnp.sum(v, axis=0, keepdims=True)
    first = jnp.sum(v[:PIX], axis=0, keepdims=True)
    for j in range(0, width, lanes):
        lane = slice(j, j + lanes)
        acc = jnp.zeros((8, lanes), F32)
        for i in range(0, PIX, chunk):
            acc += fold(h_ref[i : i + chunk, lane].astype(F32) * v_ref[i : i + chunk, :])
        pivot = jnp.sum(acc, axis=0, keepdims=True) / first
        line = jnp.zeros((8, lanes), F32)
        square = jnp.zeros((8, lanes), F32)
        for i in range(0, rows, chunk):
            off = (h_ref[i : i + chunk, lane].astype(F32) - pivot) * v_ref[i : i + chunk, :]
            line += fold(off)
            square += fold(off * off)
        total = jnp.sum(line, axis=0, keepdims=True)
        stats_ref[0, 0:1, lane] = pivot + total / count
        stats_ref[0, 1:2, lane] = (
            jnp.sum(square, axis=0, keepdims=True) - total * total / count
        )
        if with_count:
            stats_ref[0, 2:3, lane] = jnp.broadcast_to(count, (1, lanes))


def first_body(x_ref, w_ref, v_ref, h_ref, stats_ref):
    h_ref[...] = jnp.dot(x_ref[...], w_ref[...], preferred_element_type=F32)
    put_moments(stats_ref, h_ref, v_ref, True)


def first_product(x, weight, valid, micro):
    rows = x.shape[0] // micro
    depth, width = weight.shape
    return run(
        first_body,
        (micro,),
        [
            pl.BlockSpec((rows, depth), lambda m: (m, 0)),
            pl.BlockSpec((depth, width), lambda m: (0, 0)),
            pl.BlockSpec((rows, 1), lambda m: (m, 0)),
        ],
        [
            pl.BlockSpec((rows, width), lambda m: (m, 0)),
            pl.BlockSpec((1, 3, width), lambda m: (m, 0, 0)),
        ],
        [shape((micro * rows, width)), shape((micro, 3, width))],
        flops=2 * micro * rows * depth * width,
        bytes_accessed=2 * x.size,
    )(x, weight, valid)


def cell_column(rows):
    return lax.broadcasted_iota(jnp.int32, (rows, 1), 0) % CELL


def second_body(counts, refs):
    part_refs, (h_ref, v_ref, gain_ref, shift_ref, w_ref, a_ref, h2_ref, stats_ref, info_ref, cols_ref) = refs[:counts], refs[counts:]
    rows, width = h_ref.shape
    members = counts_of(part_refs)
    mean, scaled = norm_of(part_refs, members)
    info_ref[0, 0:1, :] = mean
    info_ref[0, 1:2, :] = scaled
    info_ref[0, 2:3, :] = jnp.broadcast_to(tree(list(members)), mean.shape)
    factor = scaled * gain_ref[...]
    shift = shift_ref[...]
    place = cell_column(COLS)
    has_left = (place >= 1).astype(F32)
    has_right = (place <= CELL - 2).astype(F32)
    blank = jnp.zeros((COLS, width), BF16)
    for i in range(0, rows, COLS):
        at = slice(i, i + COLS)
        pre = (h_ref[at, :] - mean) * factor + shift
        act = (pre * sigmoid(pre) * v_ref[at, :]).astype(BF16)
        a_ref[at, :] = act
        wide = act.astype(F32)
        sides = (
            (pltpu.roll(wide, 1, 0) * has_left).astype(BF16),
            act,
            (pltpu.roll(wide, COLS - 1, 0) * has_right).astype(BF16),
        )
        for c in range(3):
            cols_ref[at, (3 + c) * width : (4 + c) * width] = sides[c]
            if i % PIX < PIX - COLS:
                cols_ref[i + COLS : i + 2 * COLS, c * width : (c + 1) * width] = sides[c]
            else:
                cols_ref[at, (6 + c) * width : (7 + c) * width] = blank
            if i % PIX > 0:
                cols_ref[i - COLS : i, (6 + c) * width : (7 + c) * width] = sides[c]
            else:
                cols_ref[at, c * width : (c + 1) * width] = blank
    h2_ref[...] = jnp.dot(cols_ref[...], w_ref[...], preferred_element_type=F32)
    put_moments(stats_ref, h2_ref, v_ref, False)


def named(name, body, *fixed):
    def kernel(*refs):
        body(*fixed, refs)

    kernel.__name__ = name
    return kernel


def second_product(parts, h1, valid, gain, shift, weight, micro):
    rows, width = h1.shape[0] // micro, h1.shape[1]
    mid = pl.BlockSpec((rows, width), lambda m: (m, 0))
    return run(
        named("second_product", second_body, len(parts)),
        (micro,),
        [per_micro(part) for part in parts]
        + [
            mid,
            pl.BlockSpec((rows, 1), lambda m: (m, 0)),
            whole(gain),
            whole(shift),
            whole(weight),
        ],
        [
            mid,
            mid,
            pl.BlockSpec((1, 2, width), lambda m: (m, 0, 0)),
            pl.BlockSpec((1, 3, width), lambda m: (m, 0, 0)),
        ],
        [
            shape((micro * rows, width), BF16),
            shape((micro * rows, width)),
            shape((micro, 2, width)),
            shape((micro, 3, width)),
        ],
        [pltpu.VMEM((rows, weight.shape[0]), BF16)],
        flops=2 * micro * rows * weight.size,
        bytes_accessed=10 * h1.size,
    )(*parts, h1, valid, gain, shift, weight)


def third_body(counts, refs):
    part_refs, count_refs = refs[:counts], refs[counts : 2 * counts]
    h_ref, v_ref, gain_ref, shift_ref, w_ref, a_ref, h3_ref, stats_ref, info_ref, wide_ref = refs[2 * counts :]
    rows = h_ref.shape[0]
    mean, scaled = norm_of(part_refs, counts_of(count_refs))
    info_ref[0, 0:1, :] = mean
    info_ref[0, 1:2, :] = scaled
    factor = scaled * gain_ref[...]
    shift = shift_ref[...]
    for i in range(0, rows, 32):
        at = slice(i, i + 32)
        pre = (h_ref[at, :] - mean) * factor + shift
        a_ref[at, :] = (pre * sigmoid(pre) * v_ref[at, :]).astype(BF16)
    wide_ref[...] = jnp.dot(a_ref[...], w_ref[...], preferred_element_type=F32)
    h3_ref[...] = wide_ref[...].astype(BF16)
    put_moments(stats_ref, wide_ref, v_ref, False)


def third_product(parts, members, h2, valid, gain, shift, weight, micro):
    rows, depth = h2.shape[0] // micro, h2.shape[1]
    width = weight.shape[1]
    mid = pl.BlockSpec((rows, depth), lambda m: (m, 0))
    return run(
        named("third_product", third_body, len(parts)),
        (micro,),
        [per_micro(part) for part in parts + members]
        + [
            mid,
            pl.BlockSpec((rows, 1), lambda m: (m, 0)),
            whole(gain),
            whole(shift),
            whole(weight),
        ],
        [
            mid,
            pl.BlockSpec((rows, width), lambda m: (m, 0)),
            pl.BlockSpec((1, 2, width), lambda m: (m, 0, 0)),
            pl.BlockSpec((1, 2, depth), lambda m: (m, 0, 0)),
        ],
        [
            shape((micro * rows, depth), BF16),
            shape((micro * rows, width), BF16),
            shape((micro, 2, width)),
            shape((micro, 2, depth)),
        ],
        [pltpu.VMEM((rows, width), F32)],
        flops=2 * micro * rows * weight.size,
        bytes_accessed=4 * micro * rows * width,
    )(*parts, *members, h2, valid, gain, shift, weight)


def crop_sums(ref, *index):
    crops = ref.shape[-2] // CELL
    slabs = [
        tree([ref[(*index, j, pl.ds(i, crops, CELL), slice(None))] for i in range(CELL)])
        for j in range(ref.shape[-3])
    ]
    return jnp.concatenate(slabs, 1)


def put_lanes(ref, place, first, value, *index):
    for j in range(0, value.shape[1], LANES):
        ref[(*index, (first + j) // LANES, place, slice(None))] = value[:, j : j + LANES]


def pool_body(counts, split, refs):
    scalars_ref, part_refs, count_refs = refs[0], refs[1 : 1 + counts], refs[1 + counts : 1 + 2 * counts]
    h_ref, x_ref, v_ref, gain_ref, shift_ref, size_ref = refs[1 + 2 * counts : 7 + 2 * counts]
    feat_ref, info_ref, slope_ref, first_ref, second_ref = refs[7 + 2 * counts : 12 + 2 * counts]
    sums_ref = refs[-1]
    rows, width = h_ref.shape
    mean, scaled = norm_of(part_refs, counts_of(count_refs))
    info_ref[0, 0:1, :] = mean
    info_ref[0, 1:2, :] = scaled
    factor = scaled * gain_ref[...]
    shift = shift_ref[...]
    chunk = 256
    for j in range(0, width, chunk):
        lane = slice(j, j + chunk)
        for k in range(rows // PIX):
            acc = jnp.zeros((COLS, chunk), F32)
            acc_first = jnp.zeros((COLS, chunk), F32)
            acc_second = jnp.zeros((COLS, chunk), F32)
            for r in range(ROWS):
                at = pl.ds(k * PIX + r * COLS, COLS)
                centred = h_ref[at, lane].astype(F32) - mean[:, lane]
                resid = centred * factor[:, lane] + shift[:, lane] + x_ref[at, lane].astype(F32)
                sig = sigmoid(resid)
                kept = sig * v_ref[at, :]
                out = resid * kept
                acc += out.astype(BF16).astype(F32)
                slope = kept + out * (1.0 - sig)
                acc_first += slope
                acc_second += slope * centred
                slope_ref[at, lane] = slope.astype(BF16)
            place = pl.ds(k * COLS, COLS)
            put_lanes(sums_ref, place, j, acc, 0)
            put_lanes(sums_ref, place, j, acc_first, 1)
            put_lanes(sums_ref, place, j, acc_second * scaled[:, lane], 2)
    feat = (crop_sums(sums_ref, 0) / size_ref[...]).astype(BF16).astype(F32)
    feat_ref[...] = feat
    first_ref[...] = crop_sums(sums_ref, 1)
    second_ref[...] = crop_sums(sums_ref, 2)
    if split:
        keep_ref, send_ref = refs[12 + 2 * counts : 14 + 2 * counts]
        low = scalars_ref[1] == 0
        for i in range(0, width, 2 * split):
            one, two = feat[:, i : i + split], feat[:, i + split : i + 2 * split]
            place = slice(i // 2, i // 2 + split)
            keep_ref[:, place] = jnp.where(low, one, two)
            send_ref[:, place] = jnp.where(low, two, one)


def pool(scalars, parts, members, h3, x, valid, gain, shift, sizes, micro, split):
    rows, channels = h3.shape[0] // micro, h3.shape[1]
    crops = sizes.shape[0] // micro
    width = 1024
    tile = pl.BlockSpec((rows, width), lambda m, c, w: (m, c))
    line = pl.BlockSpec((1, width), lambda m, c, w: (0, c))
    pair = pl.BlockSpec((1, 2, width), lambda m, c, w: (m, 0, c))
    small = pl.BlockSpec((crops, width), lambda m, c, w: (m, c))
    part = pl.BlockSpec((crops, width // 2), lambda m, c, w: (m, c))
    lines = shape((micro * crops, channels))
    half = shape((micro * crops, channels // 2))
    return run(
        named("pool", pool_body, len(parts), split),
        (micro, channels // width),
        [pair] * len(parts)
        + [per_micro(part) for part in members]
        + [
            tile,
            tile,
            pl.BlockSpec((rows, 1), lambda m, c, w: (m, 0)),
            line,
            line,
            pl.BlockSpec((crops, 1), lambda m, c, w: (m, 0)),
        ],
        [small, pair, tile, small, small] + ([part, part] if split else []),
        [lines, shape((micro, 2, channels)), shape(h3.shape, BF16), lines, lines]
        + ([half, half] if split else []),
        [pltpu.VMEM((3, width // LANES, rows // ROWS, LANES), F32)],
        flops=20 * h3.size,
        bytes_accessed=4 * h3.size,
        prefetch=1,
    )(scalars, *parts, *members, h3, x, valid, gain, shift, sizes)


def head_body(feat_ref, w_ref, g_ref, stats_ref):
    g = jnp.dot(feat_ref[...].astype(BF16), w_ref[...], preferred_element_type=F32)
    g_ref[...] = g
    micro = stats_ref.shape[0]
    crops = g.shape[0] // micro
    for m in range(micro):
        part = g[m * crops : (m + 1) * crops]
        mean = jnp.sum(part, axis=0, keepdims=True) / crops
        stats_ref[m, 0:1, :] = mean
        stats_ref[m, 1:2, :] = jnp.sum((part - mean) ** 2, axis=0, keepdims=True)


def head_product(feat, weight, micro):
    lines = feat.shape[0]
    depth, width = weight.shape
    tile = 512
    return run(
        head_body,
        (width // tile,),
        [
            pl.BlockSpec((lines, depth), lambda c: (0, 0)),
            pl.BlockSpec((depth, tile), lambda c: (0, c)),
        ],
        [
            pl.BlockSpec((lines, tile), lambda c: (0, c)),
            pl.BlockSpec((micro, 2, tile), lambda c: (0, 0, c)),
        ],
        [shape((lines, width)), shape((micro, 2, width))],
        flops=2 * lines * weight.size,
        bytes_accessed=2 * weight.size,
    )(feat, weight)


def head_back_body(total_crops, counts, refs):
    which_ref, part_refs = refs[0], refs[1 : 1 + counts]
    dy_ref, g_ref, info_ref, gain_ref, w_ref, size_ref, first_ref, second_ref, send_ref, keep_ref, wide_ref, stats_ref, low_ref, spread_ref = refs[1 + counts :]
    micro = stats_ref.shape[0]
    lines, width = dy_ref.shape
    crops = lines // micro

    @pl.when(pl.program_id(0) == 0)
    def _():
        for m in range(micro):
            at = pl.ds(m * crops, crops)
            one = tree([ref[m : m + 1, :width] for ref in part_refs]) / total_crops
            two = tree([ref[micro + m : micro + m + 1, :width] for ref in part_refs]) / total_crops
            scaled = info_ref[m, 1:2, :]
            normal = (g_ref[at, :] - info_ref[m, 0:1, :]) * scaled
            dg = gain_ref[...] * scaled * (dy_ref[at, :] - (one + normal * two))
            low = dg.astype(BF16)
            low_ref[at, :] = low
            left, right = [low[:, i : i + width // 2].astype(F32) for i in (0, width // 2)]
            send_ref[at, :] = jnp.where(which_ref[0] == 0, right, left)
            keep_ref[at, :] = jnp.where(which_ref[0] == 0, left, right)

    per_crop = nt_dot(low_ref[...], w_ref[...]) / size_ref[...]
    for j in range(wide_ref.shape[1] // LANES):
        lane = slice(j * LANES, (j + 1) * LANES)
        for i in range(CELL):
            spread_ref[j, pl.ds(i, lines, CELL), :] = per_crop[:, lane]
        wide_ref[:, lane] = spread_ref[j]
    one = per_crop * first_ref[...]
    two = per_crop * second_ref[...]
    for m in range(micro):
        at = slice(m * crops, (m + 1) * crops)
        stats_ref[m, 0:1, :] = jnp.sum(one[at], axis=0, keepdims=True)
        stats_ref[m, 1:2, :] = jnp.sum(two[at], axis=0, keepdims=True)


def head_back(which, parts, dy, g, info, gain, weight, sizes, first, second, total_crops):
    lines, width = dy.shape
    channels = weight.shape[0]
    micro = info.shape[0]
    tile = 512
    part = pl.BlockSpec((lines, tile), lambda c, w: (0, c))
    half = shape((lines, width // 2))
    return run(
        named("head_back", head_back_body, total_crops, len(parts)),
        (channels // tile,),
        [whole(a) for a in parts]
        + [
            whole(dy),
            whole(g),
            whole(info),
            whole(gain),
            pl.BlockSpec((tile, width), lambda c, w: (c, 0)),
            whole(sizes),
            part,
            part,
        ],
        [
            whole(half),
            whole(half),
            pl.BlockSpec((lines * CELL, tile), lambda c, w: (0, c)),
            pl.BlockSpec((micro, 2, tile), lambda c, w: (0, 0, c)),
        ],
        [half, half, shape((lines * CELL, channels)), shape((micro, 2, channels))],
        [
            pltpu.VMEM((lines, width), BF16),
            pltpu.VMEM((tile // LANES, lines * CELL, LANES), F32),
        ],
        flops=2 * lines * weight.size,
        bytes_accessed=2 * weight.size,
        prefetch=1,
    )(which, *parts, dy, g, info, gain, weight, sizes, first, second)


def third_back_body(counts, refs):
    which_ref, part_refs = refs[0], refs[1 : 1 + counts]
    wide_ref, slope_ref, h3_ref, v_ref, info3_ref, gain3_ref, info1_ref, w_ref, act_ref, h2_ref, info2_ref, gain2_ref, shift2_ref, dy_ref, stats_ref, send_ref, keep_ref, d_ref, sum_ref = refs[1 + counts :]
    rows, channels = slope_ref.shape
    step = pl.program_id(0)
    number = info1_ref[0, 2:3, 0:1]
    first, second = sums_of(part_refs, 0, 1)
    mean = info3_ref[0, 0:1, :]
    scaled = info3_ref[0, 1:2, :]
    factor = gain3_ref[...] * scaled
    one = factor * first / number
    two = factor * scaled * second / number
    act = act_ref[...].T

    @pl.when(step == 0)
    def _():
        sum_ref[...] = jnp.zeros(sum_ref.shape, F32)

    tile = sum_ref.shape[2]
    for j in range(0, channels, tile):
        lane = slice(j, j + tile)
        for k in range(rows // PIX):
            wide = wide_ref[pl.ds(k * COLS, COLS), lane] * factor[:, lane]
            for r in range(ROWS):
                at = pl.ds(k * PIX + r * COLS, COLS)
                back = one[:, lane] + (h3_ref[at, lane].astype(F32) - mean[:, lane]) * two[:, lane]
                d = wide * slope_ref[at, lane].astype(F32) - v_ref[at, :] * back
                d_ref[at, lane] = d.astype(BF16)
        part = nt_dot(d_ref[:, lane], w_ref[:, lane])
        if j == 0:
            dy_ref[...] = part
        else:
            dy_ref[...] += part
        sum_ref[j // tile] += jnp.dot(act, d_ref[:, lane], preferred_element_type=F32)
    put_back(dy_ref, h2_ref, v_ref, info2_ref, gain2_ref, shift2_ref, stats_ref)

    @pl.when(step == pl.num_programs(0) - 1)
    def _():
        low = which_ref[0] == 0
        steps = sum_ref.shape[0] // 2
        lines = send_ref.shape[1] // steps
        for q in range(steps):
            place = slice(q * lines, (q + 1) * lines)
            left = sum_ref[q].reshape(-1, lines, tile)
            right = sum_ref[steps + q].reshape(-1, lines, tile)
            send_ref[:, place, :] = jnp.where(low, left, right)
            keep_ref[:, place, :] = jnp.where(low, right, left)


def put_back(dy_ref, h_ref, v_ref, info_ref, gain_ref, shift_ref, stats_ref):
    rows, width = dy_ref.shape
    first = jnp.zeros((8, width), F32)
    second = jnp.zeros((8, width), F32)
    for i in range(0, rows, 32):
        at = slice(i, i + 32)
        normal = (h_ref[at, :] - info_ref[0, 0:1, :]) * info_ref[0, 1:2, :]
        pre = normal * gain_ref[...] + shift_ref[...]
        dy = dy_ref[at, :] * v_ref[at, :] * slope_of(pre)
        dy_ref[at, :] = dy
        first += fold(dy)
        second += fold(dy * normal)
    stats_ref[0, 0:1, :] = jnp.sum(first, axis=0, keepdims=True)
    stats_ref[0, 1:2, :] = jnp.sum(second, axis=0, keepdims=True)


def third_back(which, parts, wide, slope, h3, valid, info3, gain3, info1, weight, act, h2, info2, gain2, shift2, micro, shards):
    rows, channels = slope.shape[0] // micro, slope.shape[1]
    middle = weight.shape[0]
    lines = wide.shape[0] // micro
    tile = 512
    big = pl.BlockSpec((rows, channels), lambda m, w: (m, 0))
    mid = pl.BlockSpec((rows, middle), lambda m, w: (m, 0))
    half = shape((shards, middle // shards * (channels // tile // 2), tile))
    return run(
        named("third_back", third_back_body, len(parts)),
        (micro,),
        [per_micro(part) for part in parts]
        + [
            pl.BlockSpec((lines, channels), lambda m, w: (m, 0)),
            big,
            big,
            pl.BlockSpec((rows, 1), lambda m, w: (m, 0)),
            per_micro(info3),
            whole(gain3),
            per_micro(info1),
            whole(weight),
            mid,
            mid,
            per_micro(info2),
            whole(gain2),
            whole(shift2),
        ],
        [
            mid,
            pl.BlockSpec((1, 2, middle), lambda m, w: (m, 0, 0)),
            whole(half),
            whole(half),
        ],
        [shape(h2.shape), shape((micro, 2, middle)), half, half],
        [
            pltpu.VMEM((rows, channels), BF16),
            pltpu.VMEM((channels // tile, middle, tile), F32),
        ],
        flops=4 * slope.shape[0] * weight.size,
        bytes_accessed=6 * slope.size,
        prefetch=1,
    )(which, *parts, wide, slope, h3, valid, info3, gain3, info1, weight, act, h2, info2, gain2, shift2)


def put_norm_back(part_refs, dy_ref, h_ref, v_ref, info_ref, number_ref, gain_ref, d_ref):
    micro = info_ref.shape[0]
    rows = dy_ref.shape[0] // micro
    for m in range(micro):
        number = number_ref[m, 2:3, 0:1]
        first, second = sums_of(part_refs, 0, 1, m)
        scaled = info_ref[m, 1:2, :]
        factor = gain_ref[...] * scaled
        one = factor * first / number
        two = factor * scaled * second / number
        mean = info_ref[m, 0:1, :]
        for i in range(m * rows, (m + 1) * rows, 32):
            at = slice(i, i + 32)
            back = one + (h_ref[at, :] - mean) * two
            d_ref[at, :] = (factor * dy_ref[at, :] - v_ref[at, :] * back).astype(BF16)


def put_sides(a_ref, sides_ref):
    rows, width = a_ref.shape
    blank = jnp.zeros((COLS, width), BF16)
    place = cell_column(COLS)
    has_left = (place >= 1).astype(F32)
    has_right = (place <= CELL - 2).astype(F32)
    for k in range(rows // PIX):
        for c in range(3):
            sides_ref[c, k, 0:COLS, :] = blank
            sides_ref[c, k, COLS + PIX :, :] = blank
        for r in range(ROWS):
            act = a_ref[k * PIX + r * COLS : k * PIX + (r + 1) * COLS, :]
            wide = act.astype(F32)
            at = slice((r + 1) * COLS, (r + 2) * COLS)
            sides_ref[0, k, at, :] = (pltpu.roll(wide, 1, 0) * has_left).astype(BF16)
            sides_ref[1, k, at, :] = act
            sides_ref[2, k, at, :] = (pltpu.roll(wide, COLS - 1, 0) * has_right).astype(BF16)


def put_tap(out_ref, sides_ref, half_ref):
    tap = pl.program_id(0)
    _, canvases, _, width = sides_ref.shape
    start = pl.multiple_of(tap // 3 * COLS, COLS)
    left = sides_ref[tap % 3, :, pl.ds(start, PIX), :].reshape(canvases * PIX, width)
    out_ref[...] = tn_dot(left, half_ref[...])


def half_of(which_ref, d_ref):
    half = d_ref.shape[1] // 2
    return d_ref[:, pl.ds(pl.multiple_of(which_ref[0] * half, half), half)]


def mid_first_body(counts, refs):
    which_ref, part_refs = refs[0], refs[1 : 1 + counts]
    dy_ref, h_ref, v_ref, info_ref, number_ref, gain_ref, a_ref, d_ref, out_ref, sides_ref, half_ref = refs[1 + counts :]

    @pl.when(pl.program_id(0) == 0)
    def _():
        put_norm_back(part_refs, dy_ref, h_ref, v_ref, info_ref, number_ref, gain_ref, d_ref)
        half_ref[...] = half_of(which_ref, d_ref)
        put_sides(a_ref, sides_ref)

    put_tap(out_ref, sides_ref, half_ref)


def mid_second_body(refs):
    which_ref, d_ref, a_ref, out_ref, sides_ref, half_ref = refs

    @pl.when(pl.program_id(0) == 0)
    def _():
        half_ref[...] = half_of(which_ref, d_ref)
        put_sides(a_ref, sides_ref)

    put_tap(out_ref, sides_ref, half_ref)


def mid_grad(name, body, which, ins, act, with_d):
    rows, width = act.shape
    half = width // 2
    grad = pl.BlockSpec((width, half), lambda t, w: (t, 0))
    return run(
        named(name, body, *([len(ins) - 7] if with_d else [])),
        (TAPS,),
        [whole(a) for a in ins],
        [whole(act), grad] if with_d else grad,
        [shape(act.shape, BF16), shape((TAPS * width, half))]
        if with_d
        else shape((TAPS * width, half)),
        [
            pltpu.VMEM((3, rows // PIX, PIX + 2 * COLS, width), BF16),
            pltpu.VMEM((rows, half), BF16),
        ],
        flops=2 * rows * TAPS * width * half,
        bytes_accessed=4 * TAPS * width * half,
        prefetch=1,
    )(which, *ins)


def in_grad_body(counts, refs):
    which_ref, part_refs = refs[0], refs[1 : 1 + counts]
    dy_ref, h_ref, v_ref, info_ref, number_ref, gain_ref, x_ref, d_ref, send_ref, keep_ref = refs[1 + counts :]

    @pl.when(pl.program_id(0) == 0)
    def _():
        put_norm_back(part_refs, dy_ref, h_ref, v_ref, info_ref, number_ref, gain_ref, d_ref)

    grad = tn_dot(x_ref[...], d_ref[...])
    half = grad.shape[1] // 2
    low = which_ref[0] == 0
    left, right = grad[:, :half], grad[:, half:]
    send_ref[...] = jnp.where(low, left, right)
    keep_ref[...] = jnp.where(low, right, left)


def in_grad(which, parts, dy, h, valid, info, number, gain, x):
    rows, width = dy.shape
    depth = x.shape[1]
    half = width // 2
    tile = 512
    ins = [*parts, dy, h, valid, info, number, gain]
    grad = pl.BlockSpec((tile, half), lambda c, w: (c, 0))
    return run(
        named("in_grad", in_grad_body, len(parts)),
        (depth // tile,),
        [whole(a) for a in ins] + [pl.BlockSpec((rows, tile), lambda c, w: (0, c))],
        [whole(dy), grad, grad],
        [shape(dy.shape, BF16), shape((depth, half)), shape((depth, half))],
        flops=2 * rows * depth * width,
        bytes_accessed=2 * x.size + 4 * depth * width + 10 * dy.size,
        prefetch=1,
    )(which, *ins, x)


def second_back_body(d_ref, w_ref, v_ref, h1_ref, info_ref, gain_ref, shift_ref, dy_ref, stats_ref, moved_ref, packed_ref):
    rows, width = d_ref.shape

    @pl.when(pl.program_id(0) == 0)
    def _():
        for r in range(3):
            for c in range(3):
                tap = 3 * r + c
                packed_ref[c, :, r * width : (r + 1) * width] = w_ref[
                    tap * width : (tap + 1) * width, :
                ]

    blank = jnp.zeros((COLS, width), BF16)
    for k in range(0, rows, PIX):
        moved_ref[k : k + PIX - COLS, 0:width] = d_ref[k + COLS : k + PIX, :]
        moved_ref[k + PIX - COLS : k + PIX, 0:width] = blank
        moved_ref[k : k + COLS, 2 * width :] = blank
        moved_ref[k + COLS : k + PIX, 2 * width :] = d_ref[k : k + PIX - COLS, :]
    moved_ref[:, width : 2 * width] = d_ref[...]
    parts = [nt_dot(moved_ref[...], packed_ref[c]) for c in range(3)]
    place = cell_column(rows)
    dy_ref[...] = (
        parts[1]
        + pltpu.roll(parts[2], 1, 0) * (place >= 1).astype(F32)
        + pltpu.roll(parts[0], rows - 1, 0) * (place <= CELL - 2).astype(F32)
    )
    put_back(dy_ref, h1_ref, v_ref, info_ref, gain_ref, shift_ref, stats_ref)


def second_back(d, weight, valid, h1, info, gain, shift, micro):
    rows, width = d.shape[0] // micro, d.shape[1]
    mid = pl.BlockSpec((rows, width), lambda m: (m, 0))
    return run(
        second_back_body,
        (micro,),
        [
            mid,
            whole(weight),
            pl.BlockSpec((rows, 1), lambda m: (m, 0)),
            mid,
            per_micro(info),
            whole(gain),
            whole(shift),
        ],
        [mid, pl.BlockSpec((1, 2, width), lambda m: (m, 0, 0))],
        [shape(d.shape), shape((micro, 2, width))],
        [pltpu.VMEM((rows, 3 * width), BF16), pltpu.VMEM((3, width, 3 * width), BF16)],
        flops=2 * micro * rows * weight.size,
        bytes_accessed=10 * d.size,
    )(d, weight, valid, h1, info, gain, shift)


def pixels_body(d_ref, w_ref, wide_ref, slope_ref, out_ref):
    rows, channels = out_ref.shape
    width = 512
    for j in range(0, channels, width):
        lane = pl.ds(j, width)
        grad = nt_dot(d_ref[...], w_ref[lane, :])
        for k in range(rows // PIX):
            wide = wide_ref[pl.ds(k * COLS, COLS), lane]
            for r in range(ROWS):
                first = k * PIX + r * COLS
                at = pl.ds(first, COLS)
                out_ref[at, lane] = (
                    grad[first : first + COLS] + wide * slope_ref[at, lane].astype(F32)
                ).astype(BF16)


def pixels_grad(d, weight, wide, slope, micro):
    rows, channels = slope.shape[0] // micro, slope.shape[1]
    lines = wide.shape[0] // micro
    big = pl.BlockSpec((rows, channels), lambda m: (m, 0))
    return run(
        pixels_body,
        (micro,),
        [
            pl.BlockSpec((rows, d.shape[1]), lambda m: (m, 0)),
            pl.BlockSpec(weight.shape, lambda m: (0, 0)),
            pl.BlockSpec((lines, channels), lambda m: (m, 0)),
            big,
        ],
        big,
        shape(slope.shape, BF16),
        flops=2 * slope.shape[0] * weight.size,
        bytes_accessed=4 * slope.size,
    )(d, weight, wide, slope)


def factor_body(feat_ref, other_feat_ref, dg_ref, far_ref, near_ref, both_ref, out_ref):
    left = jnp.concatenate([feat_ref[...], other_feat_ref[...]], 0).astype(BF16)
    lines = dg_ref.shape[0] // 2
    right = jnp.concatenate(
        [
            ref[c * lines : (c + 1) * lines, :]
            for c in range(2)
            for ref in (dg_ref, near_ref, far_ref, both_ref)
        ],
        0,
    ).astype(BF16)
    out_ref[...] = tn_dot(left, right)


def factor_grad(feat, other_feat, dg, far, near, both):
    lines, depth = feat.shape
    width = dg.shape[1]
    tile = 512
    left = pl.BlockSpec((lines, tile), lambda c: (0, c))
    return run(
        factor_body,
        (depth // tile,),
        [left, left] + [whole(dg)] * 4,
        pl.BlockSpec((tile, width), lambda c: (c, 0)),
        shape((depth, width)),
        flops=4 * lines * depth * width,
        bytes_accessed=4 * depth * width,
    )(feat, other_feat, dg, far, near, both)


def embed_body(protos, counts, members, refs):
    part_refs = refs[:counts]
    g_ref, gain_ref, shift_ref, w_ref, bias_ref, table_ref, queue_ref, act_ref, z_ref, inverse_ref, unit_ref, logits_ref, batch_ref, line_ref, sums_ref, info_ref = refs[counts:]
    micro = info_ref.shape[0]
    crops = g_ref.shape[0] // micro
    for m in range(micro):
        at = slice(m * crops, (m + 1) * crops)
        mean, scaled = norm_of(part_refs, members, m)
        info_ref[m, 0:1, :] = mean
        info_ref[m, 1:2, :] = scaled
        pre = (g_ref[at, :] - mean) * scaled * gain_ref[...] + shift_ref[...]
        act_ref[at, :] = (pre * sigmoid(pre)).astype(BF16)
    z = jnp.dot(act_ref[...], w_ref[...], preferred_element_type=F32) + bias_ref[...]
    inverse = lax.rsqrt(jnp.sum(z * z, 1, keepdims=True) + eps_unit)
    unit = (z * inverse).astype(BF16)
    z_ref[...] = z
    inverse_ref[...] = inverse
    unit_ref[...] = unit
    logits = jnp.dot(unit, table_ref[...], preferred_element_type=F32)
    logits_ref[...] = logits
    real = lax.broadcasted_iota(jnp.int32, (1, logits.shape[1]), 1) < protos
    batch = jnp.where(real, jnp.exp(logits / transport_epsilon), 0.0)
    batch_ref[...] = batch
    queued = jnp.dot(queue_ref[...], table_ref[...], preferred_element_type=F32)
    line = jnp.where(real, jnp.exp(queued / transport_epsilon), 0.0)
    line_ref[...] = line
    queue_sum = jnp.sum(line, axis=0, keepdims=True)
    for m in range(micro):
        at = slice(m * crops, (m + 1) * crops)
        sums_ref[m : m + 1, :] = jnp.sum(batch[at], axis=0, keepdims=True) + queue_sum


def embed_product(parts, members, protos, g, gain, shift, weight, bias, table, queue):
    lines = g.shape[0]
    micro = parts[0].shape[0]
    feat = weight.shape[1]
    wide = table.shape[1]
    outs = [
        shape(g.shape, BF16),
        shape((lines, feat)),
        shape((lines, 1)),
        shape((lines, feat), BF16),
        shape((lines, wide)),
        shape((lines, wide)),
        shape((queue.shape[0], wide)),
        shape((micro, wide)),
        shape((micro, 2, g.shape[1])),
    ]
    ins = [*parts, g, gain, shift, weight, bias, table, queue]
    return run(
        named("embed", embed_body, protos, len(parts), members),
        (1,),
        [whole(a) for a in ins],
        [whole(a) for a in outs],
        outs,
        flops=2 * lines * table.size,
        bytes_accessed=8 * lines * wide,
    )(*ins)


def sweep_body(protos, counts, refs):
    part_refs = refs[:counts]
    batch_ref, queue_ref, new_batch_ref, new_queue_ref, sums_ref = refs[counts:]
    micro, wide = sums_ref.shape
    crops = batch_ref.shape[0] // micro
    lines = new_queue_ref.shape[0] // micro
    shared = queue_ref.shape[0] == lines
    real = lax.broadcasted_iota(jnp.int32, (1, wide), 1) < protos
    for m in range(micro):
        column = jnp.where(real, tree([ref[m : m + 1, :] for ref in part_refs]), 1.0)
        at = slice(m * crops, (m + 1) * crops)
        batch = batch_ref[at, :] / column
        batch = batch / jnp.sum(batch, 1, keepdims=True)
        new_batch_ref[at, :] = batch
        own = slice(m * lines, (m + 1) * lines)
        queue = queue_ref[slice(0, lines) if shared else own, :] / column
        queue = queue / jnp.sum(queue, 1, keepdims=True)
        new_queue_ref[own, :] = queue
        sums_ref[m : m + 1, :] = jnp.sum(batch, axis=0, keepdims=True) + jnp.sum(
            queue, axis=0, keepdims=True
        )


def sweep(parts, protos, batch, queue, lines):
    micro, wide = parts[0].shape
    outs = [shape(batch.shape), shape((micro * lines, wide)), shape(parts[0].shape)]
    ins = [*parts, batch, queue]
    return run(
        named("sweep", sweep_body, protos, len(parts)),
        (1,),
        [whole(a) for a in ins],
        [whole(a) for a in outs],
        outs,
        flops=20 * batch.size,
        bytes_accessed=16 * batch.size,
    )(*ins)


def split_dot(dot, left, right, wide_left):
    value = left if wide_left else right
    high = value.astype(BF16)
    low = (value - high.astype(F32)).astype(BF16)
    if wide_left:
        return dot(high, right) + dot(low, right)
    return dot(left, high) + dot(left, low)


def pack_small(low, send_ref, keep_ref, protos, embed):
    shards, lines, width = send_ref.shape
    lines = lines // 2
    rows = protos.shape[0] // shards // 2
    half = protos.shape[1] // 2
    groups = half // width
    lane = embed.shape[1]
    below = lines - groups * rows

    def put(d, place, columns, one, two):
        keep_ref[d, place, columns] = jnp.where(low, one, two)
        send_ref[d, place, columns] = jnp.where(low, two, one)

    for d in range(shards):
        for y in range(2):
            first = (2 * d + y) * rows
            for q in range(groups):
                start = y * lines + q * rows
                one, two = [
                    protos[first : first + rows, c * half + q * width : c * half + (q + 1) * width]
                    for c in range(2)
                ]
                put(d, slice(start, start + rows), slice(None), one, two)
            for q in range(width // lane):
                one, two = [
                    embed[first : first + below]
                    for first in [
                        (((2 * d + c) * 2 + y) * (width // lane) + q) * below for c in range(2)
                    ]
                ]
                start = y * lines + groups * rows
                put(d, slice(start, start + below), slice(q * lane, (q + 1) * lane), one, two)


def unpack_small(halves, protos, embed):
    shards, lines, width = halves[0].shape
    lines = lines // 2
    packed = jnp.stack(halves).reshape(2, shards, 2, lines, width)
    rows = protos[0] // shards // 2
    groups = protos[1] // 2 // width
    lane = embed[1]
    above = packed[:, :, :, : groups * rows].reshape(2, shards, 2, groups, rows, width)
    below = packed[:, :, :, groups * rows :]
    below = below.reshape(2, shards, 2, lines - groups * rows, width // lane, lane)
    return (
        above.transpose(1, 2, 4, 0, 3, 5).reshape(protos),
        below.transpose(1, 0, 2, 4, 3, 5).reshape(embed),
    )


def packed_shape(protos, embed, shards):
    width = 512
    lines = protos[0] // shards // 2 * (protos[1] // 2 // width)
    return (shards, 2 * (lines + embed[0] * embed[1] // shards // 4 // width), width)


def loss_body(protos, scale, counts, refs):
    which_ref, part_refs = refs[0], refs[1 : 1 + counts]
    batch_ref, logits_ref, unit_ref, z_ref, inverse_ref, act_ref, g_ref, info_ref, gain_ref, shift_ref, w_ref, table_ref, send_ref, keep_ref, dy_ref, sums_ref = refs[1 + counts :]
    micro, wide = part_refs[0].shape
    lines = batch_ref.shape[0]
    crops = lines // micro
    real = lax.broadcasted_iota(jnp.int32, (1, wide), 1) < protos
    odd = lax.broadcasted_iota(jnp.int32, (crops, 1), 0) % 2 == 1
    parts = []
    loss = jnp.zeros((1, 1), F32)
    for m in range(micro):
        at = slice(m * crops, (m + 1) * crops)
        codes = batch_ref[at, :] / jnp.where(
            real, tree([ref[m : m + 1, :] for ref in part_refs]), 1.0
        )
        codes = codes / jnp.sum(codes, 1, keepdims=True)
        partner = jnp.where(odd, pltpu.roll(codes, 1, 0), pltpu.roll(codes, crops - 1, 0))
        sharp = logits_ref[at, :] / softmax_sharpness
        top = jnp.max(jnp.where(real, sharp, -jnp.inf), 1, keepdims=True)
        shifted = sharp - top
        mass = jnp.where(real, jnp.exp(shifted), 0.0)
        total = jnp.sum(mass, 1, keepdims=True)
        chance = shifted - jnp.log(total)
        loss += jnp.sum(jnp.sum(partner * chance, 1, keepdims=True), 0, keepdims=True)
        weight = jnp.sum(partner, 1, keepdims=True)
        parts.append((scale / softmax_sharpness) * (weight * (mass / total) - partner))
    d_scores = jnp.concatenate(parts, 0)
    unit = unit_ref[...]
    grad_protos = split_dot(tn_dot, unit, d_scores, False)
    d_unit = split_dot(nt_dot, d_scores, table_ref[...], True)
    z = z_ref[...]
    inverse = inverse_ref[...]
    dz = inverse * d_unit - z * (inverse * inverse * inverse) * jnp.sum(
        z * d_unit, 1, keepdims=True
    )
    grad_embed = split_dot(tn_dot, act_ref[...], dz, False)
    pack_small(which_ref[0] == 0, send_ref, keep_ref, grad_protos, grad_embed)
    d_act = split_dot(nt_dot, dz, w_ref[...], True)
    for m in range(micro):
        at = slice(m * crops, (m + 1) * crops)
        normal = (g_ref[at, :] - info_ref[m, 0:1, :]) * info_ref[m, 1:2, :]
        pre = normal * gain_ref[...] + shift_ref[...]
        dy = d_act[at] * slope_of(pre)
        dy_ref[at, :] = dy
        sums_ref[m : m + 1, : dy.shape[1]] = jnp.sum(dy, axis=0, keepdims=True)
        sums_ref[micro + m : micro + m + 1, : dy.shape[1]] = jnp.sum(
            dy * normal, axis=0, keepdims=True
        )
    feat = z.shape[1]
    wide = dy_ref.shape[1]
    extra = jnp.concatenate(
        [jnp.sum(dz, axis=0, keepdims=True), jnp.broadcast_to(-scale * loss, (1, feat))], 1
    )
    sums_ref[:, wide:] = jnp.broadcast_to(extra, (2 * micro, 2 * feat))


def loss_grads(which, parts, protos, scale, batch, logits, unit, z, inverse, act, g, info, gain, shift, weight, table, shards):
    ins = [*parts, batch, logits, unit, z, inverse, act, g, info, gain, shift, weight, table]
    micro = info.shape[0]
    outs = [
        shape(packed_shape(table.shape, weight.shape, shards)),
        shape(packed_shape(table.shape, weight.shape, shards)),
        shape(g.shape),
        shape((2 * micro, g.shape[1] + 2 * weight.shape[1])),
    ]
    return run(
        named("loss", loss_body, protos, scale, len(parts)),
        (1,),
        [whole(a) for a in ins],
        [whole(a) for a in outs],
        outs,
        flops=8 * table.size * batch.shape[0],
        bytes_accessed=16 * batch.size,
        prefetch=1,
    )(which, *ins)


def pick_block(rows, width, cell, *fixed):
    return pl.BlockSpec((1, rows, width), lambda g, w: cell(g, *fixed, w[0], w[1], w[2]) + (0,))


def sent_first(g, i, core, x, y):
    z, b = 2 * g + i // 2, i % 2
    return (2 * z + (1 - core) * (1 - x) + core * b, (1 - core) * b + core * (1 - y))


def kept_second(g, i, core, x, y):
    return (2 * (2 * g + i) + x, y)


def sent_second(g, i, core, x, y):
    z = 2 * g + i
    return (2 * z + (1 - core) * x + core * (1 - x), (1 - core) * (1 - y) + core * y)


def add_groups(refs, sizes, out_ref, index, extra=None):
    start = 0
    place = 0
    for count, rows in sizes:
        value = refs[place][0]
        for ref in refs[place + 1 : place + count]:
            value = value + ref[0]
        if extra is not None:
            value = value + extra[0, start : start + rows, :]
        out_ref[index, start : start + rows, :] = value
        place += count
        start += rows


def group_sizes(groups):
    return [(len(addends), addends[0].shape[1] // 2) for addends in groups]


def first_send(scalars, groups):
    sizes = group_sizes(groups)
    shards, _, width = groups[0][0].shape
    lines = sum(rows for _, rows in sizes)
    flat = [array for addends in groups for array in addends]
    specs = []
    for i in range(4):
        for array in flat:
            specs.append(pick_block(array.shape[1] // 2, width, sent_first, i))

    def body(refs):
        refs = refs[1:]
        for i in range(4):
            add_groups(refs[i * len(flat) : (i + 1) * len(flat)], sizes, refs[-1], i)

    return run(
        named("first_send", body),
        (shards // 4,),
        specs,
        pl.BlockSpec((4, lines, width), lambda g, w: (g, 0, 0)),
        shape((shards, lines, width)),
        bytes_accessed=4 * lines * width * shards * 3,
        prefetch=1,
    )(scalars, *(flat * 4))


def second_send(scalars, groups, came):
    sizes = group_sizes(groups)
    shards, _, width = groups[0][0].shape
    lines = sum(rows for _, rows in sizes)
    flat = [array for addends in groups for array in addends]
    specs = []
    for cell in (sent_second, kept_second):
        for i in range(2):
            for array in flat:
                specs.append(pick_block(array.shape[1] // 2, width, cell, i))

    def bit(w):
        return (1 - w[0]) * w[2] + w[0] * w[1]

    for flip in (1, 0):
        for i in range(2):
            specs.append(
                pl.BlockSpec(
                    (1, lines, width),
                    lambda g, w, i=i, flip=flip: (2 * (2 * g + i) + (1 - bit(w) if flip else bit(w)), 0, 0),
                )
            )
    out = pl.BlockSpec((2, lines, width), lambda g, w: (g, 0, 0))

    def body(refs):
        refs = refs[1:]
        count = len(flat)
        came_refs = refs[4 * count : 4 * count + 4]
        for side in range(2):
            for i in range(2):
                place = 2 * side + i
                add_groups(
                    refs[place * count : (place + 1) * count],
                    sizes,
                    refs[-2 + side],
                    i,
                    came_refs[place],
                )

    return run(
        named("second_send", body),
        (shards // 4,),
        specs,
        [out, out],
        [shape((shards // 2, lines, width))] * 2,
        bytes_accessed=4 * lines * width * shards * 4,
        prefetch=1,
    )(scalars, *(flat * 4), *([came] * 4))


def place_early_body(scalars_ref, mine_ref, far_ref, mine_core_ref, far_core_ref, out_ref, embed_ref, protos_ref, head_ref):
    lines = out_ref.shape[0]
    rows = protos_ref.shape[0] // 2
    wide = 512
    groups = protos_ref.shape[1] // 2 // wide
    lane = embed_ref.shape[1]
    below = embed_ref.shape[0] // 4 // (wide // lane)
    start = lines + groups * rows + below
    for c, y, ref in ((0, 0, mine_ref), (0, 1, far_ref), (1, 0, mine_core_ref), (1, 1, far_core_ref)):
        c = scalars_ref[0] if c == 0 else 1 - scalars_ref[0]
        y = scalars_ref[2] if y == 0 else 1 - scalars_ref[2]
        column = pl.multiple_of((2 * c + y) * wide, wide)
        out_ref[:, pl.ds(column, wide)] = ref[0:lines, :]
        head_ref[:, pl.ds(column, wide)] = ref[start:, :]
        at = pl.ds(pl.multiple_of(y * rows, rows), rows)
        for q in range(groups):
            column = pl.multiple_of((c * groups + q) * wide, wide)
            protos_ref[at, pl.ds(column, wide)] = ref[lines + q * rows : lines + (q + 1) * rows, :]
        for q in range(wide // lane):
            first = pl.multiple_of(((2 * c + y) * (wide // lane) + q) * below, below)
            embed_ref[pl.ds(first, below), :] = ref[
                lines + groups * rows : start, q * lane : (q + 1) * lane
            ]


def place_late_body(scalars_ref, mine_ref, far_ref, mine_core_ref, far_core_ref, *out_refs):
    for c, y, ref in ((0, 0, mine_ref), (0, 1, far_ref), (1, 0, mine_core_ref), (1, 1, far_core_ref)):
        c = scalars_ref[0] if c == 0 else 1 - scalars_ref[0]
        y = scalars_ref[2] if y == 0 else 1 - scalars_ref[2]
        start = 0
        for out_ref in out_refs:
            rows, width = out_ref.shape[0] // 2, out_ref.shape[1] // 2
            out_ref[
                pl.ds(pl.multiple_of(y * rows, rows), rows),
                pl.ds(pl.multiple_of(c * width, width), width),
            ] = ref[start : start + rows, :]
            start += rows


def placed_pieces(body, scalars, pieces, outs):
    return run(
        body,
        (1,),
        [whole(a) for a in pieces],
        [whole(a) for a in outs],
        outs,
        prefetch=1,
    )(scalars, *pieces)


def on_device(
    pixels,
    crop_map,
    queue_rows,
    conv_in,
    gain_one,
    shift_one,
    conv_mid,
    gain_two,
    shift_two,
    conv_out,
    gain_three,
    shift_three,
    head_weight,
    head_gain,
    head_shift,
    embed_weight,
    embed_bias,
    prototypes,
):
    micro, canvas, pixel_count, channels = pixels.shape
    devices = lax.axis_size("dp") * lax.axis_size("hst")
    crops = canvas * SLOTS
    total_crops = crops * devices * 1.0
    loss_scale = 1.0 / (micro * total_crops)
    x = pixels.reshape(micro * canvas * pixel_count, channels)
    valid = (crop_map < SLOTS).astype(F32).reshape(-1, 1)
    sizes = jnp.sum(
        (crop_map[:, :, None, :] == jnp.arange(SLOTS, dtype=jnp.int32)[:, None]).astype(F32), 3
    ).reshape(-1, 1)

    shards = lax.axis_size("dp")
    quick = shards == 8 and lax.axis_size("hst") == 4
    packs = 8
    protos = prototypes.shape[1]
    table = jnp.pad(prototypes, ((0, 0), (0, -protos % 1024)))

    def row(vector):
        return vector.reshape(1, -1)

    masks = dp_masks()
    near, far = masks[0], masks[1:]
    core = bit_of(1)
    side = bit_of(2)
    scalars = jnp.stack([core, bit_of(near), side]).astype(jnp.int32)
    keep_half = core.astype(jnp.int32).reshape(1)
    send_half = 1 - keep_half

    h1, stats = first_product(x, conv_in, valid, micro)
    members, counts = first_parts(stats)
    act_one, h2, stats, info_one = second_product(
        members, h1, valid, row(gain_one), row(shift_one), conv_mid, micro
    )
    parts = moment_parts(stats, counts)
    act_two, h3, stats, info_two = third_product(
        parts, members, h2, valid, row(gain_two), row(shift_two), conv_out, micro
    )
    parts = moment_parts(stats, counts)
    feat, info_three, slope, slope_first, slope_second, *feat_halves = pool(
        scalars,
        parts,
        members,
        h3,
        x,
        valid,
        row(gain_three),
        row(shift_three),
        sizes,
        micro,
        channels // shards if quick else 0,
    )

    lines = feat.shape[0]
    if quick:
        feat_keep, feat_send = feat_halves
        feat_near, feat_far = swap(feat_send, near), swap(feat_keep, 2)
    g, stats = head_product(feat, head_weight, micro)
    if quick:
        stats, feat_near, feat_far = tie(stats, feat_near, feat_far)

    crop_counts = []
    crop_members = []
    number = crops * 1.0
    for group in sync_groups():
        crop_members = [number] * (len(group) + 1)
        crop_counts.append(crop_members)
        number = number * (len(group) + 1)
    parts = moment_parts(stats, crop_counts)

    act_four, embedded, inverse, unit_rows, logits, batch, queue, column, info_four = embed_product(
        parts,
        crop_members,
        protos,
        g,
        row(head_gain),
        row(head_shift),
        embed_weight,
        row(embed_bias),
        table,
        queue_rows,
    )
    for _ in range(SINK_ITERS - 1):
        parts = sum_parts(column)
        batch, queue, column = sweep(parts, protos, batch, queue, queue_rows.shape[0])
    parts = sum_parts(column)
    which = (1 - send_half) if quick else jnp.zeros((1,), jnp.int32)
    small_send, small_keep, dy_four, payload = loss_grads(
        which,
        parts,
        protos,
        loss_scale,
        batch,
        logits,
        unit_rows,
        embedded,
        inverse,
        act_four,
        g,
        info_four,
        row(head_gain),
        row(head_shift),
        embed_weight,
        table,
        packs,
    )
    parts = sum_parts(payload)
    payload = tree(list(parts))
    channel_sums = payload[:, : head_gain.shape[0]]
    first_four, second_four = channel_sums[:micro], channel_sums[micro:]
    extra = payload[0, head_gain.shape[0] :]
    grad_bias, total_loss = extra[: embed_bias.shape[0]], extra[embed_bias.shape[0]]

    if quick:
        feat_near, small_send, *parts = tie(feat_near, small_send, *parts)
        feat_both = swap(feat_near, 2)
        small_recv = swap(small_send, 1)
    dg_send, dg_keep, wide, sums = head_back(
        which,
        parts,
        dy_four,
        g,
        info_four,
        row(head_gain),
        head_weight,
        sizes,
        slope_first,
        slope_second,
        total_crops,
    )
    first_norm = (h1, valid, info_one, info_one, row(gain_one))
    second_norm = (h2, valid, info_two, info_one, row(gain_two))

    def from_third(which, parts):
        return third_back(
            which,
            parts,
            wide,
            slope,
            h3,
            valid,
            info_three,
            row(gain_three),
            info_one,
            conv_out,
            act_two,
            h2,
            info_two,
            row(gain_two),
            row(shift_two),
            micro,
            shards,
        )

    def from_second(d):
        return second_back(
            d, conv_mid, valid, h1, info_one, row(gain_one), row(shift_one), micro
        )

    if quick:
        sums, dg_send, feat_both, small_recv = tie(sums, dg_send, feat_both, small_recv)
        feat_both = jnp.concatenate([feat_keep, feat_near, feat_far, feat_both], 0)

        def core_filler(gate):
            source, other = tie(dg_send, feat_both, gate)[:2]
            grads["dg"] = swap(source, 1)
            grads["feat"] = swap(other, 1)
            return [grads["dg"], grads["feat"]]

        grads = {}
        parts_three = sum_parts(sums, ((), (core_filler,)))
        feat_other = grads["feat"]
        quarter = dg_keep.shape[1] // 2

        def quarter_of(place):
            return jnp.concatenate(
                [
                    lax.dynamic_slice_in_dim(array, place * quarter, quarter, 1)
                    for array in (dg_keep, grads["dg"])
                ],
                0,
            )

        dg_here, dg_there = quarter_of(side), quarter_of(1 - side)
        *parts_three, dg_here, dg_there = tie(*parts_three, dg_here, dg_there)
        dg_far, dg_near, dg_both = swap(dg_there, 2), swap(dg_here, near), swap(dg_there, 2 + near)
        dy, sums, out_send, out_keep = from_third(send_half, parts_three)
        sums, dy, out_send, dg_far, dg_near, dg_both = tie(
            sums, dy, out_send, dg_far, dg_near, dg_both
        )
        small = [small_keep, small_recv]

        def out_filler(gate):
            grads["out"] = swap(tie(out_send, gate)[0], 1)
            return [grads["out"]]

        def head_filler(gate):
            source = tie(dg_near, gate)[0]
            grads["head"] = factor_grad(feat_both, feat_other, dg_here, dg_far, source, dg_both)
            return [grads["head"]]

        def early_filler(gate):
            source = tie(grads["out"], gate)[0]
            grads["early"] = [[out_keep, source], small]
            grads["early_out"] = first_send(scalars, grads["early"])
            return [grads["early_out"]]

        parts_two = sum_parts(sums, ((), (out_filler,), (head_filler, early_filler)))

        early = grads["early"]
        *parts_two, early_out, partial = tie(*parts_two, grads["early_out"], grads["head"])
        early_came = core_swap(early_out, near, 2)
        partial = partial.reshape(2, 2, 2, -1, partial.shape[1])
        heads = [dp_halves([partial[:, :, 0]], far[0], 1)]
        d_two, mid_send = mid_grad(
            "mid_first",
            mid_first_body,
            send_half,
            [*parts_two, dy, *second_norm, act_one],
            act_one,
            True,
        )
        d_two, mid_send, early_came, heads[0][-1] = tie(
            d_two, mid_send, early_came, heads[0][-1]
        )
        heads.append(dp_halves([partial[:, :, 1]], far[0], 1))
        mid_recv = swap(mid_send, 1)
        early_out, early_keep = second_send(scalars, early, early_came)
        early_came = core_swap(early_out, 2, near)
        mid_keep = mid_grad(
            "mid_second", mid_second_body, keep_half, [d_two, act_one], act_one, False
        )
        mid_keep, mid_recv, early_came, heads[1][-1] = tie(
            mid_keep, mid_recv, early_came, heads[1][-1]
        )

        def sharded(array):
            return array.reshape(shards, -1, array.shape[-1])

        def by_bits(array):
            return array.reshape((2, 2) + array.shape[1:])

        late = [[sharded(mid_keep), sharded(mid_recv)]]
        mid_out = first_send(scalars, late)
        d_two, mid_out = tie(d_two, mid_out)
        mid_came = core_swap(mid_out, near, 2)
        heads = [dp_halves(head, far[1], 0) for head in heads]
        dy, sums = from_second(d_two)
        dy, sums, mid_came, heads[0][-1], heads[1][-1], early_keep, early_came = tie(
            dy, sums, mid_came, heads[0][-1], heads[1][-1], early_keep, early_came
        )
        early = [by_bits(early_keep), by_bits(early_came)]

        def early_z_filler(gate):
            grads["z"] = dp_halves(early, far[0], 1)
            return [grads["z"][-1]]

        def mid_filler(gate):
            source = tie(mid_came, gate)[0]
            grads["mid"] = second_send(scalars, late, source)
            return grads["mid"]

        parts_one = sum_parts(sums, ((), (early_z_filler,), (mid_filler,)))
        mid_out, mid_keep = grads["mid"]
        *parts_one, mid_out, early_came = tie(*parts_one, mid_out, grads["z"][-1])
        early = dp_halves(grads["z"][:-1] + [early_came], far[1], 0)
        mid_came = core_swap(mid_out, 2, near)
        d_one, in_send, in_keep = in_grad(send_half, parts_one, dy, *first_norm, x)
        d_one, in_send, in_keep, mid_came, early[-1] = tie(
            d_one, in_send, in_keep, mid_came, early[-1]
        )
        in_recv = swap(in_send, 1)
        inner = [[sharded(in_keep), sharded(in_recv)]]
        in_out = first_send(scalars, inner)
        mid = dp_halves([by_bits(mid_keep), by_bits(mid_came)], far[0], 1)
        early_mine = jnp.concatenate([sum(early), sum(heads[0]), sum(heads[1])], 0)
        d_one, in_out, early_mine = tie(d_one, in_out, early_mine)
        in_came = core_swap(in_out, near, 2)
        early_core = swap(early_mine, 1)
        grad_x = pixels_grad(d_one, conv_in, wide, slope, micro)
        grad_x, in_came, mid[-1], early_core = tie(grad_x, in_came, mid[-1], early_core)
        mid = dp_halves(mid, far[1], 0)
        in_out, in_keep = second_send(scalars, inner, in_came)
        in_came = core_swap(in_out, 2, near)
        in_came, mid[-1], early_mine = tie(in_came, mid[-1], early_mine)
        inner = dp_halves([by_bits(in_keep), by_bits(in_came)], far[0], 1)
        early_far = swap(early_mine, 2)
        inner = dp_halves(inner, far[1], 0)
        early_far, inner[-1] = tie(early_far, inner[-1])
        early_pieces = [early_mine, early_far, early_core, swap(early_far, 1)]
        channel = channels // shards
        early_grads = placed_pieces(
            place_early_body,
            scalars,
            early_pieces,
            [
                shape((conv_out.shape[0] // shards, channels)),
                shape((embed_weight.shape[0] // shards, embed_weight.shape[1])),
                shape((table.shape[0] // shards, table.shape[1])),
                shape((channel, head_weight.shape[1])),
            ],
        )
        late_mine = jnp.concatenate([sum(mid), sum(inner)], 0)
        late_far = swap(late_mine, 2)
        late_core = swap(late_mine, 1)
        late_far, late_core, *early_grads = tie(late_far, late_core, *early_grads)
        grad_conv_out, grad_embed, grad_protos, grad_head = early_grads
        grad_protos = grad_protos[:, :protos]
        grad_conv_mid, grad_conv_in = placed_pieces(
            place_late_body,
            scalars,
            [late_mine, late_far, late_core, swap(late_far, 1)],
            [
                shape((conv_mid.shape[0] // shards, conv_mid.shape[1])),
                shape((channel, conv_in.shape[1])),
            ],
        )
    else:
        low, high = jnp.zeros((1,), jnp.int32), jnp.ones((1,), jnp.int32)

        def reduced(array):
            return lax.psum(lax.psum_scatter(array, "dp", scatter_dimension=0, tiled=True), "hst")

        parts_three = sum_parts(sums)
        dy, sums, out_low, out_high = from_third(low, parts_three)
        parts_two = sum_parts(sums)
        ins = [*parts_two, dy, *second_norm, act_one]
        d_two, mid_low = mid_grad("mid_first", mid_first_body, low, ins, act_one, True)
        mid_high = mid_grad("mid_second", mid_second_body, high, [d_two, act_one], act_one, False)
        dy, sums = from_second(d_two)
        parts_one = sum_parts(sums)
        d_one, in_low, in_high = in_grad(low, parts_one, dy, *first_norm, x)
        grad_x = pixels_grad(d_one, conv_in, wide, slope, micro)
        out = jnp.stack([out_low, out_high])
        out = out.reshape(2, shards, -1, conv_out.shape[0] // shards, out.shape[-1])
        small_protos, small_embed = unpack_small(
            [small_keep, small_send], table.shape, embed_weight.shape
        )
        grad_conv_out = reduced(out.transpose(1, 3, 0, 2, 4).reshape(conv_out.shape))
        grad_conv_mid = reduced(jnp.concatenate([mid_low, mid_high], 1))
        grad_conv_in = reduced(jnp.concatenate([in_low, in_high], 1))
        dg = jnp.concatenate([dg_keep, dg_send], 1).astype(BF16)
        grad_head = reduced(jnp.dot(feat.astype(BF16).T, dg, preferred_element_type=F32))
        grad_embed = reduced(small_embed)
        grad_protos = reduced(small_protos)[:, :protos]

    def own_rows(vectors):
        sums = [jnp.sum(vector, 0) for vector in vectors]
        piece = sums[0].shape[0] // shards
        stacked = jnp.stack(sums)
        found = lax.dynamic_slice_in_dim(stacked, lax.axis_index("dp") * piece, piece, 1)
        return [found[i] for i in range(len(vectors))]

    def both_sums(parts):
        total = tree(list(parts))
        return [total[:, 1], total[:, 0]]

    small_ones = own_rows(both_sums(parts_one) + both_sums(parts_two))
    large_ones = own_rows(both_sums(parts_three) + [second_four, first_four])

    return (
        total_loss,
        grad_x.reshape(pixels.shape),
        grad_conv_in,
        small_ones[0],
        small_ones[1],
        grad_conv_mid,
        small_ones[2],
        small_ones[3],
        grad_conv_out,
        large_ones[0],
        large_ones[1],
        grad_head,
        large_ones[2],
        large_ones[3],
        grad_embed,
        lax.dynamic_slice_in_dim(
            grad_bias,
            lax.axis_index("dp") * (grad_bias.shape[0] // shards),
            grad_bias.shape[0] // shards,
            0,
        ),
        grad_protos,
    )


def solution(mesh):
    placed = (
        P(None, ("dp", "hst"), None, None),
        P(None, ("dp", "hst"), None),
        P(("dp", "hst"), None),
    ) + (P(),) * 15
    return jax.shard_map(
        on_device,
        mesh=mesh,
        in_specs=placed,
        out_specs=(
            P(),
            P(None, ("dp", "hst"), None, None),
            P("dp", None),
            P("dp"),
            P("dp"),
            P("dp", None),
            P("dp"),
            P("dp"),
            P("dp", None),
            P("dp"),
            P("dp"),
            P("dp", None),
            P("dp"),
            P("dp"),
            P("dp", None),
            P("dp"),
            P("dp", None),
        ),
        check_vma=False,
    )
```

```python
import functools

import jax
import jax.numpy as jnp
from jax import lax
from jax.experimental import pallas as pl
from jax.experimental.pallas import tpu as pltpu
from jax.sharding import PartitionSpec as P

ROWS = 8
COLS = 16
SLOTS = 4
CELL = COLS // SLOTS
PIX = ROWS * COLS
SINK_ITERS = 3
TAPS = 9

eps_norm = 1e-05
eps_unit = 1e-06
transport_epsilon = 0.05
softmax_sharpness = 0.1
highest = lax.Precision.HIGHEST
F32 = jnp.float32
BF16 = jnp.bfloat16
AXES = ("dp", "hst")
MIB = 1 << 20
LANES = 128


def swap(value, mask):
    count = lax.axis_size("dp") * lax.axis_size("hst")
    return lax.ppermute(value, AXES, [(i, i ^ mask) for i in range(count)])


def sync_groups():
    bits = (lax.axis_size("dp") * lax.axis_size("hst")).bit_length() - 1
    groups = [(1,)]
    bit = 1
    while bit < bits:
        if bit + 1 < bits:
            groups.append((1 << bit, 2 << bit, 3 << bit))
            bit += 2
        else:
            groups.append((1 << bit,))
            bit += 1
    return groups


def tree(parts):
    while len(parts) > 1:
        parts = [parts[i] + parts[i + 1] for i in range(0, len(parts), 2)]
    return parts[0]


def between(parts, gate, fillers):
    for filler in fillers:
        parts = list(tie(*parts, *filler(gate)))[: len(parts)]
    return parts


def pick(fillers, step):
    return fillers[step] if step < len(fillers) else ()


def sum_parts(value, fillers=()):
    groups = sync_groups()
    for step, group in enumerate(groups):
        parts = [value] + [swap(value, mask) for mask in group]
        parts = between(parts, value, pick(fillers, step))
        value = tree(parts)
    return parts


def merge(parts, members):
    whole = tree(list(members))
    mean = tree([n * part[:, 0] for n, part in zip(members, parts)]) / whole
    spread = tree(
        [part[:, 1] + n * (part[:, 0] - mean) ** 2 for n, part in zip(members, parts)]
    )
    return mean, spread, whole


def moment_parts(moments, counts, fillers=()):
    groups = sync_groups()
    for step, group in enumerate(groups):
        parts = [moments] + [swap(moments, mask) for mask in group]
        parts = between(parts, moments, pick(fillers, step))
        if step + 1 < len(groups):
            moments = jnp.stack(merge(parts, counts[step])[:2], 1)
    return parts


def first_parts(moments):
    groups = sync_groups()
    counts = []
    for step, group in enumerate(groups):
        parts = [moments] + [swap(moments, mask) for mask in group]
        if step + 1 < len(groups):
            members = [part[:, 2] for part in parts]
            moments = jnp.stack(merge(parts, members), 1)
            counts.append([n[:, :1] for n in members])
    return parts, counts


def bit_of(mask):
    index = lax.axis_index("dp") * lax.axis_size("hst") + lax.axis_index("hst")
    return (index // mask) % 2


def dp_masks():
    base = lax.axis_size("hst")
    return [base << j for j in range(lax.axis_size("dp").bit_length() - 1)]


def tie(first, *others):
    return lax.optimization_barrier((first,) + others)


def at(view, place, axis):
    return lax.dynamic_index_in_dim(view, place, axis, keepdims=False)


def core_swap(value, low, high):
    count = lax.axis_size("dp") * lax.axis_size("hst")
    pairs = [(i, i ^ (high if i % 2 else low)) for i in range(count)]
    return lax.ppermute(value, AXES, pairs)


def dp_split(addends, mask, axis):
    bit = bit_of(mask)
    send = sum(at(array, 1 - bit, axis) for array in addends)
    return [at(array, bit, axis) for array in addends], send


def dp_halves(addends, mask, axis):
    keep, send = dp_split(addends, mask, axis)
    return keep + [swap(send, mask)]


VMEM_MIB = {
    "third_back": 58,
    "second_back_body": 58,
}


def run(body, grid, in_specs, out_specs, out_shape, scratch=(), flops=0, bytes_accessed=0, prefetch=0, aliases=None):
    return pl.pallas_call(
        body,
        grid_spec=pltpu.PrefetchScalarGridSpec(
            num_scalar_prefetch=prefetch,
            grid=grid,
            in_specs=in_specs,
            out_specs=out_specs,
            scratch_shapes=list(scratch),
        ),
        out_shape=out_shape,
        name=body.__name__,
        input_output_aliases=aliases or {},
        compiler_params=pltpu.CompilerParams(
            vmem_limit_bytes=VMEM_MIB.get(body.__name__, 44) * MIB, dimension_semantics=("arbitrary",) * len(grid)
        ),
        cost_estimate=pl.CostEstimate(
            flops=flops, bytes_accessed=bytes_accessed, transcendentals=0
        ),
    )


def shape(dims, dtype=F32):
    return jax.ShapeDtypeStruct(tuple(dims), dtype)


def sigmoid(u):
    return 0.5 * jnp.tanh(0.5 * u) + 0.5


def norm_of(part_refs, members, m=0, lane=slice(None)):
    whole = tree(list(members))
    means = [ref[m, 0:1, lane] for ref in part_refs]
    mean = tree([n * one for n, one in zip(members, means)]) / whole
    spread = tree(
        [ref[m, 1:2, lane] + n * (one - mean) ** 2 for n, ref, one in zip(members, part_refs, means)]
    )
    return mean, lax.rsqrt(spread / whole + eps_norm)


def sums_of(part_refs, first, second, m=0):
    return (
        tree([ref[m, first : first + 1, :] for ref in part_refs]),
        tree([ref[m, second : second + 1, :] for ref in part_refs]),
    )


def counts_of(count_refs, m=0):
    return [ref[m, 2:3, 0:1] for ref in count_refs]


def whole(array):
    return pl.BlockSpec(array.shape, lambda *_: (0,) * len(array.shape))


def per_micro(array):
    return pl.BlockSpec((1,) + array.shape[1:], lambda m, *_: (m,) + (0,) * (array.ndim - 1))


def slope_of(u):
    s = sigmoid(u)
    return s * (1.0 + u * (1.0 - s))


def nt_dot(left, right):
    return lax.dot_general(left, right, (((1,), (1,)), ((), ())), preferred_element_type=F32)


def tn_dot(left, right):
    return lax.dot_general(left, right, (((0,), (0,)), ((), ())), preferred_element_type=F32)


def fold(y):
    return jnp.sum(y.reshape(y.shape[0] // 8, 8, y.shape[1]), 0)


def put_moments(stats_ref, h_ref, v_ref, with_count):
    rows, width = h_ref.shape
    chunk = 32
    lanes = 512
    v = v_ref[...]
    count = jnp.sum(v, axis=0, keepdims=True)
    first = jnp.sum(v[:PIX], axis=0, keepdims=True)
    for j in range(0, width, lanes):
        lane = slice(j, j + lanes)
        acc = jnp.zeros((8, lanes), F32)
        for i in range(0, PIX, chunk):
            acc += fold(h_ref[i : i + chunk, lane].astype(F32) * v_ref[i : i + chunk, :])
        pivot = jnp.sum(acc, axis=0, keepdims=True) / first
        line = jnp.zeros((8, lanes), F32)
        square = jnp.zeros((8, lanes), F32)
        for i in range(0, rows, chunk):
            off = (h_ref[i : i + chunk, lane].astype(F32) - pivot) * v_ref[i : i + chunk, :]
            line += fold(off)
            square += fold(off * off)
        total = jnp.sum(line, axis=0, keepdims=True)
        stats_ref[0, 0:1, lane] = pivot + total / count
        stats_ref[0, 1:2, lane] = (
            jnp.sum(square, axis=0, keepdims=True) - total * total / count
        )
        if with_count:
            stats_ref[0, 2:3, lane] = jnp.broadcast_to(count, (1, lanes))


def first_body(x_ref, w_ref, v_ref, h_ref, stats_ref):
    h_ref[...] = jnp.dot(x_ref[...], w_ref[...], preferred_element_type=F32)
    put_moments(stats_ref, h_ref, v_ref, True)


def first_product(x, weight, valid, micro):
    rows = x.shape[0] // micro
    depth, width = weight.shape
    return run(
        first_body,
        (micro,),
        [
            pl.BlockSpec((rows, depth), lambda m: (m, 0)),
            pl.BlockSpec((depth, width), lambda m: (0, 0)),
            pl.BlockSpec((rows, 1), lambda m: (m, 0)),
        ],
        [
            pl.BlockSpec((rows, width), lambda m: (m, 0)),
            pl.BlockSpec((1, 3, width), lambda m: (m, 0, 0)),
        ],
        [shape((micro * rows, width)), shape((micro, 3, width))],
        flops=2 * micro * rows * depth * width,
        bytes_accessed=2 * x.size,
    )(x, weight, valid)


def cell_column(rows):
    return lax.broadcasted_iota(jnp.int32, (rows, 1), 0) % CELL


def second_body(counts, refs):
    part_refs, (h_ref, v_ref, gain_ref, shift_ref, w_ref, a_ref, h2_ref, stats_ref, info_ref, cols_ref) = refs[:counts], refs[counts:]
    rows, width = h_ref.shape
    members = counts_of(part_refs)
    mean, scaled = norm_of(part_refs, members)
    info_ref[0, 0:1, :] = mean
    info_ref[0, 1:2, :] = scaled
    info_ref[0, 2:3, :] = jnp.broadcast_to(tree(list(members)), mean.shape)
    factor = scaled * gain_ref[...]
    shift = shift_ref[...]
    place = cell_column(COLS)
    has_left = (place >= 1).astype(F32)
    has_right = (place <= CELL - 2).astype(F32)
    blank = jnp.zeros((COLS, width), BF16)
    for i in range(0, rows, COLS):
        at = slice(i, i + COLS)
        pre = (h_ref[at, :] - mean) * factor + shift
        act = (pre * sigmoid(pre) * v_ref[at, :]).astype(BF16)
        a_ref[at, :] = act
        wide = act.astype(F32)
        sides = (
            (pltpu.roll(wide, 1, 0) * has_left).astype(BF16),
            act,
            (pltpu.roll(wide, COLS - 1, 0) * has_right).astype(BF16),
        )
        for c in range(3):
            cols_ref[at, (3 + c) * width : (4 + c) * width] = sides[c]
            if i % PIX < PIX - COLS:
                cols_ref[i + COLS : i + 2 * COLS, c * width : (c + 1) * width] = sides[c]
            else:
                cols_ref[at, (6 + c) * width : (7 + c) * width] = blank
            if i % PIX > 0:
                cols_ref[i - COLS : i, (6 + c) * width : (7 + c) * width] = sides[c]
            else:
                cols_ref[at, c * width : (c + 1) * width] = blank
    h2_ref[...] = jnp.dot(cols_ref[...], w_ref[...], preferred_element_type=F32)
    put_moments(stats_ref, h2_ref, v_ref, False)


def named(name, body, *fixed):
    def kernel(*refs):
        body(*fixed, refs)

    kernel.__name__ = name
    return kernel


def second_product(parts, h1, valid, gain, shift, weight, micro):
    rows, width = h1.shape[0] // micro, h1.shape[1]
    mid = pl.BlockSpec((rows, width), lambda m: (m, 0))
    return run(
        named("second_product", second_body, len(parts)),
        (micro,),
        [per_micro(part) for part in parts]
        + [
            mid,
            pl.BlockSpec((rows, 1), lambda m: (m, 0)),
            whole(gain),
            whole(shift),
            whole(weight),
        ],
        [
            mid,
            mid,
            pl.BlockSpec((1, 2, width), lambda m: (m, 0, 0)),
            pl.BlockSpec((1, 3, width), lambda m: (m, 0, 0)),
        ],
        [
            shape((micro * rows, width), BF16),
            shape((micro * rows, width)),
            shape((micro, 2, width)),
            shape((micro, 3, width)),
        ],
        [pltpu.VMEM((rows, weight.shape[0]), BF16)],
        flops=2 * micro * rows * weight.size,
        bytes_accessed=10 * h1.size,
    )(*parts, h1, valid, gain, shift, weight)


def third_body(counts, refs):
    part_refs, count_refs = refs[:counts], refs[counts : 2 * counts]
    h_ref, v_ref, gain_ref, shift_ref, w_ref, a_ref, h3_ref, stats_ref, info_ref, wide_ref = refs[2 * counts :]
    rows = h_ref.shape[0]
    mean, scaled = norm_of(part_refs, counts_of(count_refs))
    info_ref[0, 0:1, :] = mean
    info_ref[0, 1:2, :] = scaled
    factor = scaled * gain_ref[...]
    shift = shift_ref[...]
    for i in range(0, rows, 32):
        at = slice(i, i + 32)
        pre = (h_ref[at, :] - mean) * factor + shift
        a_ref[at, :] = (pre * sigmoid(pre) * v_ref[at, :]).astype(BF16)
    wide_ref[...] = jnp.dot(a_ref[...], w_ref[...], preferred_element_type=F32)
    put_moments(stats_ref, wide_ref, v_ref, False)
    for i in range(0, rows, 32):
        at = slice(i, i + 32)
        h3_ref[at, :] = (wide_ref[at, :] - stats_ref[0, 0:1, :]).astype(BF16)


def third_product(parts, members, h2, valid, gain, shift, weight, micro):
    rows, depth = h2.shape[0] // micro, h2.shape[1]
    width = weight.shape[1]
    mid = pl.BlockSpec((rows, depth), lambda m: (m, 0))
    return run(
        named("third_product", third_body, len(parts)),
        (micro,),
        [per_micro(part) for part in parts + members]
        + [
            mid,
            pl.BlockSpec((rows, 1), lambda m: (m, 0)),
            whole(gain),
            whole(shift),
            whole(weight),
        ],
        [
            mid,
            pl.BlockSpec((rows, width), lambda m: (m, 0)),
            pl.BlockSpec((1, 2, width), lambda m: (m, 0, 0)),
            pl.BlockSpec((1, 2, depth), lambda m: (m, 0, 0)),
        ],
        [
            shape((micro * rows, depth), BF16),
            shape((micro * rows, width), BF16),
            shape((micro, 2, width)),
            shape((micro, 2, depth)),
        ],
        [pltpu.VMEM((rows, width), F32)],
        flops=2 * micro * rows * weight.size,
        bytes_accessed=4 * micro * rows * width,
    )(*parts, *members, h2, valid, gain, shift, weight)


def crop_sums(ref, *index):
    crops = ref.shape[-2] // CELL
    slabs = [
        tree([ref[(*index, j, pl.ds(i, crops, CELL), slice(None))] for i in range(CELL)])
        for j in range(ref.shape[-3])
    ]
    return jnp.concatenate(slabs, 1)


def put_lanes(ref, place, first, value, *index):
    for j in range(0, value.shape[1], LANES):
        ref[(*index, (first + j) // LANES, place, slice(None))] = value[:, j : j + LANES]


def pool_body(counts, split, refs):
    scalars_ref, part_refs, count_refs = refs[0], refs[1 : 1 + counts], refs[1 + counts : 1 + 2 * counts]
    base_ref, h_ref, x_ref, v_ref, gain_ref, shift_ref, size_ref = refs[1 + 2 * counts : 8 + 2 * counts]
    feat_ref, info_ref, slope_ref, first_ref, second_ref = refs[8 + 2 * counts : 13 + 2 * counts]
    sums_ref = refs[-1]
    rows, width = h_ref.shape
    mean, scaled = norm_of(part_refs, counts_of(count_refs))
    mean = mean - base_ref[0, 0:1, :]
    info_ref[0, 0:1, :] = mean
    info_ref[0, 1:2, :] = scaled
    factor = scaled * gain_ref[...]
    shift = shift_ref[...]
    chunk = 256
    for j in range(0, width, chunk):
        lane = slice(j, j + chunk)
        for k in range(rows // PIX):
            acc = jnp.zeros((COLS, chunk), F32)
            acc_first = jnp.zeros((COLS, chunk), F32)
            acc_second = jnp.zeros((COLS, chunk), F32)
            for r in range(ROWS):
                at = pl.ds(k * PIX + r * COLS, COLS)
                centred = h_ref[at, lane].astype(F32) - mean[:, lane]
                resid = centred * factor[:, lane] + shift[:, lane] + x_ref[at, lane].astype(F32)
                sig = sigmoid(resid)
                kept = sig * v_ref[at, :]
                out = resid * kept
                acc += out.astype(BF16).astype(F32)
                slope = kept + out * (1.0 - sig)
                acc_first += slope
                acc_second += slope * centred
                slope_ref[at, lane] = slope.astype(BF16)
            place = pl.ds(k * COLS, COLS)
            put_lanes(sums_ref, place, j, acc, 0)
            put_lanes(sums_ref, place, j, acc_first, 1)
            put_lanes(sums_ref, place, j, acc_second * scaled[:, lane], 2)
    feat = (crop_sums(sums_ref, 0) / size_ref[...]).astype(BF16).astype(F32)
    feat_ref[...] = feat
    first_ref[...] = crop_sums(sums_ref, 1)
    second_ref[...] = crop_sums(sums_ref, 2)
    if split:
        keep_ref, send_ref = refs[13 + 2 * counts : 15 + 2 * counts]
        low = scalars_ref[1] == 0
        for i in range(0, width, 2 * split):
            one, two = feat[:, i : i + split], feat[:, i + split : i + 2 * split]
            place = slice(i // 2, i // 2 + split)
            keep_ref[:, place] = jnp.where(low, one, two)
            send_ref[:, place] = jnp.where(low, two, one)


def pool(scalars, parts, members, base, h3, x, valid, gain, shift, sizes, micro, split):
    rows, channels = h3.shape[0] // micro, h3.shape[1]
    crops = sizes.shape[0] // micro
    width = 1024
    tile = pl.BlockSpec((rows, width), lambda m, c, w: (m, c))
    line = pl.BlockSpec((1, width), lambda m, c, w: (0, c))
    pair = pl.BlockSpec((1, 2, width), lambda m, c, w: (m, 0, c))
    small = pl.BlockSpec((crops, width), lambda m, c, w: (m, c))
    part = pl.BlockSpec((crops, width // 2), lambda m, c, w: (m, c))
    lines = shape((micro * crops, channels))
    half = shape((micro * crops, channels // 2))
    return run(
        named("pool", pool_body, len(parts), split),
        (micro, channels // width),
        [pair] * len(parts)
        + [per_micro(part) for part in members]
        + [
            pair,
            tile,
            tile,
            pl.BlockSpec((rows, 1), lambda m, c, w: (m, 0)),
            line,
            line,
            pl.BlockSpec((crops, 1), lambda m, c, w: (m, 0)),
        ],
        [small, pair, tile, small, small] + ([part, part] if split else []),
        [lines, shape((micro, 2, channels)), shape(h3.shape, BF16), lines, lines]
        + ([half, half] if split else []),
        [pltpu.VMEM((3, width // LANES, rows // ROWS, LANES), F32)],
        flops=20 * h3.size,
        bytes_accessed=4 * h3.size,
        prefetch=1,
    )(scalars, *parts, *members, base, h3, x, valid, gain, shift, sizes)


def head_body(feat_ref, w_ref, g_ref, stats_ref):
    g = jnp.dot(feat_ref[...].astype(BF16), w_ref[...], preferred_element_type=F32)
    g_ref[...] = g
    micro = stats_ref.shape[0]
    crops = g.shape[0] // micro
    for m in range(micro):
        part = g[m * crops : (m + 1) * crops]
        mean = jnp.sum(part, axis=0, keepdims=True) / crops
        stats_ref[m, 0:1, :] = mean
        stats_ref[m, 1:2, :] = jnp.sum((part - mean) ** 2, axis=0, keepdims=True)


def head_product(feat, weight, micro):
    lines = feat.shape[0]
    depth, width = weight.shape
    tile = 512
    return run(
        head_body,
        (width // tile,),
        [
            pl.BlockSpec((lines, depth), lambda c: (0, 0)),
            pl.BlockSpec((depth, tile), lambda c: (0, c)),
        ],
        [
            pl.BlockSpec((lines, tile), lambda c: (0, c)),
            pl.BlockSpec((micro, 2, tile), lambda c: (0, 0, c)),
        ],
        [shape((lines, width)), shape((micro, 2, width))],
        flops=2 * lines * weight.size,
        bytes_accessed=2 * weight.size,
    )(feat, weight)


def head_back_body(total_crops, counts, refs):
    which_ref, part_refs = refs[0], refs[1 : 1 + counts]
    dy_ref, g_ref, info_ref, gain_ref, w_ref, size_ref, first_ref, second_ref, send_ref, keep_ref, wide_ref, stats_ref, low_ref, spread_ref = refs[1 + counts :]
    micro = stats_ref.shape[0]
    lines, width = dy_ref.shape
    crops = lines // micro

    @pl.when(pl.program_id(0) == 0)
    def _():
        for m in range(micro):
            at = pl.ds(m * crops, crops)
            one = tree([ref[m : m + 1, :width] for ref in part_refs]) / total_crops
            two = tree([ref[micro + m : micro + m + 1, :width] for ref in part_refs]) / total_crops
            scaled = info_ref[m, 1:2, :]
            normal = (g_ref[at, :] - info_ref[m, 0:1, :]) * scaled
            dg = gain_ref[...] * scaled * (dy_ref[at, :] - (one + normal * two))
            low = dg.astype(BF16)
            low_ref[at, :] = low
            left, right = [low[:, i : i + width // 2].astype(F32) for i in (0, width // 2)]
            send_ref[at, :] = jnp.where(which_ref[0] == 0, right, left)
            keep_ref[at, :] = jnp.where(which_ref[0] == 0, left, right)

    per_crop = nt_dot(low_ref[...], w_ref[...]) / size_ref[...]
    for j in range(wide_ref.shape[1] // LANES):
        lane = slice(j * LANES, (j + 1) * LANES)
        for i in range(CELL):
            spread_ref[j, pl.ds(i, lines, CELL), :] = per_crop[:, lane]
        wide_ref[:, lane] = spread_ref[j]
    one = per_crop * first_ref[...]
    two = per_crop * second_ref[...]
    for m in range(micro):
        at = slice(m * crops, (m + 1) * crops)
        stats_ref[m, 0:1, :] = jnp.sum(one[at], axis=0, keepdims=True)
        stats_ref[m, 1:2, :] = jnp.sum(two[at], axis=0, keepdims=True)


def head_back(which, parts, dy, g, info, gain, weight, sizes, first, second, total_crops):
    lines, width = dy.shape
    channels = weight.shape[0]
    micro = info.shape[0]
    tile = 512
    part = pl.BlockSpec((lines, tile), lambda c, w: (0, c))
    half = shape((lines, width // 2))
    return run(
        named("head_back", head_back_body, total_crops, len(parts)),
        (channels // tile,),
        [whole(a) for a in parts]
        + [
            whole(dy),
            whole(g),
            whole(info),
            whole(gain),
            pl.BlockSpec((tile, width), lambda c, w: (c, 0)),
            whole(sizes),
            part,
            part,
        ],
        [
            whole(half),
            whole(half),
            pl.BlockSpec((lines * CELL, tile), lambda c, w: (0, c)),
            pl.BlockSpec((micro, 2, tile), lambda c, w: (0, 0, c)),
        ],
        [half, half, shape((lines * CELL, channels)), shape((micro, 2, channels))],
        [
            pltpu.VMEM((lines, width), BF16),
            pltpu.VMEM((tile // LANES, lines * CELL, LANES), F32),
        ],
        flops=2 * lines * weight.size,
        bytes_accessed=2 * weight.size,
        prefetch=1,
    )(which, *parts, dy, g, info, gain, weight, sizes, first, second)


def third_back_body(counts, refs):
    which_ref, part_refs = refs[0], refs[1 : 1 + counts]
    wide_ref, slope_ref, h3_ref, v_ref, info3_ref, gain3_ref, info1_ref, w_ref, act_ref, h2_ref, info2_ref, gain2_ref, shift2_ref, dy_ref, stats_ref, send_ref, keep_ref, d_ref, sum_ref = refs[1 + counts :]
    rows, channels = slope_ref.shape
    step = pl.program_id(0)
    number = info1_ref[0, 2:3, 0:1]
    first, second = sums_of(part_refs, 0, 1)
    mean = info3_ref[0, 0:1, :]
    scaled = info3_ref[0, 1:2, :]
    factor = gain3_ref[...] * scaled
    one = factor * first / number
    two = factor * scaled * second / number
    act = act_ref[...].T

    @pl.when(step == 0)
    def _():
        sum_ref[...] = jnp.zeros(sum_ref.shape, F32)

    tile = sum_ref.shape[2]
    for j in range(0, channels, tile):
        lane = slice(j, j + tile)
        for k in range(rows // PIX):
            wide = wide_ref[pl.ds(k * COLS, COLS), lane] * factor[:, lane]
            for r in range(ROWS):
                at = pl.ds(k * PIX + r * COLS, COLS)
                back = one[:, lane] + (h3_ref[at, lane].astype(F32) - mean[:, lane]) * two[:, lane]
                d = wide * slope_ref[at, lane].astype(F32) - v_ref[at, :] * back
                d_ref[at, lane] = d.astype(BF16)
        part = nt_dot(d_ref[:, lane], w_ref[:, lane])
        if j == 0:
            dy_ref[...] = part
        else:
            dy_ref[...] += part
        sum_ref[j // tile] += jnp.dot(act, d_ref[:, lane], preferred_element_type=F32)
    put_back(dy_ref, h2_ref, v_ref, info2_ref, gain2_ref, shift2_ref, stats_ref)

    @pl.when(step == pl.num_programs(0) - 1)
    def _():
        low = which_ref[0] == 0
        steps = sum_ref.shape[0] // 2
        lines = send_ref.shape[1] // steps
        for q in range(steps):
            place = slice(q * lines, (q + 1) * lines)
            left = sum_ref[q].reshape(-1, lines, tile)
            right = sum_ref[steps + q].reshape(-1, lines, tile)
            send_ref[:, place, :] = jnp.where(low, left, right)
            keep_ref[:, place, :] = jnp.where(low, right, left)


def put_back(dy_ref, h_ref, v_ref, info_ref, gain_ref, shift_ref, stats_ref):
    rows, width = dy_ref.shape
    first = jnp.zeros((8, width), F32)
    second = jnp.zeros((8, width), F32)
    for i in range(0, rows, 32):
        at = slice(i, i + 32)
        normal = (h_ref[at, :] - info_ref[0, 0:1, :]) * info_ref[0, 1:2, :]
        pre = normal * gain_ref[...] + shift_ref[...]
        dy = dy_ref[at, :] * v_ref[at, :] * slope_of(pre)
        dy_ref[at, :] = dy
        first += fold(dy)
        second += fold(dy * normal)
    stats_ref[0, 0:1, :] = jnp.sum(first, axis=0, keepdims=True)
    stats_ref[0, 1:2, :] = jnp.sum(second, axis=0, keepdims=True)


def third_back(which, parts, wide, slope, h3, valid, info3, gain3, info1, weight, act, h2, info2, gain2, shift2, micro, shards):
    rows, channels = slope.shape[0] // micro, slope.shape[1]
    middle = weight.shape[0]
    lines = wide.shape[0] // micro
    tile = 512
    big = pl.BlockSpec((rows, channels), lambda m, w: (m, 0))
    mid = pl.BlockSpec((rows, middle), lambda m, w: (m, 0))
    half = shape((shards, middle // shards * (channels // tile // 2), tile))
    return run(
        named("third_back", third_back_body, len(parts)),
        (micro,),
        [per_micro(part) for part in parts]
        + [
            pl.BlockSpec((lines, channels), lambda m, w: (m, 0)),
            big,
            big,
            pl.BlockSpec((rows, 1), lambda m, w: (m, 0)),
            per_micro(info3),
            whole(gain3),
            per_micro(info1),
            whole(weight),
            mid,
            mid,
            per_micro(info2),
            whole(gain2),
            whole(shift2),
        ],
        [
            mid,
            pl.BlockSpec((1, 2, middle), lambda m, w: (m, 0, 0)),
            whole(half),
            whole(half),
        ],
        [shape(h2.shape), shape((micro, 2, middle)), half, half],
        [
            pltpu.VMEM((rows, channels), BF16),
            pltpu.VMEM((channels // tile, middle, tile), F32),
        ],
        flops=4 * slope.shape[0] * weight.size,
        bytes_accessed=6 * slope.size,
        prefetch=1,
    )(which, *parts, wide, slope, h3, valid, info3, gain3, info1, weight, act, h2, info2, gain2, shift2)


def put_norm_back(part_refs, dy_ref, h_ref, v_ref, info_ref, number_ref, gain_ref, d_ref):
    micro = info_ref.shape[0]
    rows = dy_ref.shape[0] // micro
    for m in range(micro):
        number = number_ref[m, 2:3, 0:1]
        first, second = sums_of(part_refs, 0, 1, m)
        scaled = info_ref[m, 1:2, :]
        factor = gain_ref[...] * scaled
        one = factor * first / number
        two = factor * scaled * second / number
        mean = info_ref[m, 0:1, :]
        for i in range(m * rows, (m + 1) * rows, 32):
            at = slice(i, i + 32)
            back = one + (h_ref[at, :] - mean) * two
            d_ref[at, :] = (factor * dy_ref[at, :] - v_ref[at, :] * back).astype(BF16)


def put_sides(a_ref, sides_ref):
    rows, width = a_ref.shape
    blank = jnp.zeros((COLS, width), BF16)
    place = cell_column(COLS)
    has_left = (place >= 1).astype(F32)
    has_right = (place <= CELL - 2).astype(F32)
    for k in range(rows // PIX):
        for c in range(3):
            sides_ref[c, k, 0:COLS, :] = blank
            sides_ref[c, k, COLS + PIX :, :] = blank
        for r in range(ROWS):
            act = a_ref[k * PIX + r * COLS : k * PIX + (r + 1) * COLS, :]
            wide = act.astype(F32)
            at = slice((r + 1) * COLS, (r + 2) * COLS)
            sides_ref[0, k, at, :] = (pltpu.roll(wide, 1, 0) * has_left).astype(BF16)
            sides_ref[1, k, at, :] = act
            sides_ref[2, k, at, :] = (pltpu.roll(wide, COLS - 1, 0) * has_right).astype(BF16)


def put_tap(out_ref, sides_ref, half_ref):
    tap = pl.program_id(0)
    _, canvases, _, width = sides_ref.shape
    start = pl.multiple_of(tap // 3 * COLS, COLS)
    left = sides_ref[tap % 3, :, pl.ds(start, PIX), :].reshape(canvases * PIX, width)
    out_ref[...] = tn_dot(left, half_ref[...])


def half_of(which_ref, d_ref):
    half = d_ref.shape[1] // 2
    return d_ref[:, pl.ds(pl.multiple_of(which_ref[0] * half, half), half)]


def mid_first_body(counts, refs):
    which_ref, part_refs = refs[0], refs[1 : 1 + counts]
    dy_ref, h_ref, v_ref, info_ref, number_ref, gain_ref, a_ref, d_ref, out_ref, sides_ref, half_ref = refs[1 + counts :]

    @pl.when(pl.program_id(0) == 0)
    def _():
        put_norm_back(part_refs, dy_ref, h_ref, v_ref, info_ref, number_ref, gain_ref, d_ref)
        half_ref[...] = half_of(which_ref, d_ref)
        put_sides(a_ref, sides_ref)

    put_tap(out_ref, sides_ref, half_ref)


def mid_second_body(refs):
    which_ref, d_ref, a_ref, out_ref, sides_ref, half_ref = refs

    @pl.when(pl.program_id(0) == 0)
    def _():
        half_ref[...] = half_of(which_ref, d_ref)
        put_sides(a_ref, sides_ref)

    put_tap(out_ref, sides_ref, half_ref)


def mid_grad(name, body, which, ins, act, with_d):
    rows, width = act.shape
    half = width // 2
    grad = pl.BlockSpec((width, half), lambda t, w: (t, 0))
    return run(
        named(name, body, *([len(ins) - 7] if with_d else [])),
        (TAPS,),
        [whole(a) for a in ins],
        [whole(act), grad] if with_d else grad,
        [shape(act.shape, BF16), shape((TAPS * width, half))]
        if with_d
        else shape((TAPS * width, half)),
        [
            pltpu.VMEM((3, rows // PIX, PIX + 2 * COLS, width), BF16),
            pltpu.VMEM((rows, half), BF16),
        ],
        flops=2 * rows * TAPS * width * half,
        bytes_accessed=4 * TAPS * width * half,
        prefetch=1,
    )(which, *ins)


def in_grad_body(counts, refs):
    which_ref, part_refs = refs[0], refs[1 : 1 + counts]
    dy_ref, h_ref, v_ref, info_ref, number_ref, gain_ref, x_ref, d_ref, send_ref, keep_ref = refs[1 + counts :]

    @pl.when(pl.program_id(0) == 0)
    def _():
        put_norm_back(part_refs, dy_ref, h_ref, v_ref, info_ref, number_ref, gain_ref, d_ref)

    grad = tn_dot(x_ref[...], d_ref[...])
    half = grad.shape[1] // 2
    low = which_ref[0] == 0
    left, right = grad[:, :half], grad[:, half:]
    send_ref[...] = jnp.where(low, left, right)
    keep_ref[...] = jnp.where(low, right, left)


def in_grad(which, parts, dy, h, valid, info, number, gain, x):
    rows, width = dy.shape
    depth = x.shape[1]
    half = width // 2
    tile = 512
    ins = [*parts, dy, h, valid, info, number, gain]
    grad = pl.BlockSpec((tile, half), lambda c, w: (c, 0))
    return run(
        named("in_grad", in_grad_body, len(parts)),
        (depth // tile,),
        [whole(a) for a in ins] + [pl.BlockSpec((rows, tile), lambda c, w: (0, c))],
        [whole(dy), grad, grad],
        [shape(dy.shape, BF16), shape((depth, half)), shape((depth, half))],
        flops=2 * rows * depth * width,
        bytes_accessed=2 * x.size + 4 * depth * width + 10 * dy.size,
        prefetch=1,
    )(which, *ins, x)


def second_back_body(d_ref, w_ref, v_ref, h1_ref, info_ref, gain_ref, shift_ref, dy_ref, stats_ref, moved_ref, packed_ref):
    rows, width = d_ref.shape

    @pl.when(pl.program_id(0) == 0)
    def _():
        for r in range(3):
            for c in range(3):
                tap = 3 * r + c
                packed_ref[c, :, r * width : (r + 1) * width] = w_ref[
                    tap * width : (tap + 1) * width, :
                ]

    blank = jnp.zeros((COLS, width), BF16)
    for k in range(0, rows, PIX):
        moved_ref[k : k + PIX - COLS, 0:width] = d_ref[k + COLS : k + PIX, :]
        moved_ref[k + PIX - COLS : k + PIX, 0:width] = blank
        moved_ref[k : k + COLS, 2 * width :] = blank
        moved_ref[k + COLS : k + PIX, 2 * width :] = d_ref[k : k + PIX - COLS, :]
    moved_ref[:, width : 2 * width] = d_ref[...]
    parts = [nt_dot(moved_ref[...], packed_ref[c]) for c in range(3)]
    place = cell_column(rows)
    dy_ref[...] = (
        parts[1]
        + pltpu.roll(parts[2], 1, 0) * (place >= 1).astype(F32)
        + pltpu.roll(parts[0], rows - 1, 0) * (place <= CELL - 2).astype(F32)
    )
    put_back(dy_ref, h1_ref, v_ref, info_ref, gain_ref, shift_ref, stats_ref)


def second_back(d, weight, valid, h1, info, gain, shift, micro):
    rows, width = d.shape[0] // micro, d.shape[1]
    mid = pl.BlockSpec((rows, width), lambda m: (m, 0))
    return run(
        second_back_body,
        (micro,),
        [
            mid,
            whole(weight),
            pl.BlockSpec((rows, 1), lambda m: (m, 0)),
            mid,
            per_micro(info),
            whole(gain),
            whole(shift),
        ],
        [mid, pl.BlockSpec((1, 2, width), lambda m: (m, 0, 0))],
        [shape(d.shape), shape((micro, 2, width))],
        [pltpu.VMEM((rows, 3 * width), BF16), pltpu.VMEM((3, width, 3 * width), BF16)],
        flops=2 * micro * rows * weight.size,
        bytes_accessed=10 * d.size,
    )(d, weight, valid, h1, info, gain, shift)


def pixels_body(d_ref, w_ref, wide_ref, slope_ref, out_ref):
    rows, channels = out_ref.shape
    width = 512
    for j in range(0, channels, width):
        lane = pl.ds(j, width)
        grad = nt_dot(d_ref[...], w_ref[lane, :])
        for k in range(rows // PIX):
            wide = wide_ref[pl.ds(k * COLS, COLS), lane]
            for r in range(ROWS):
                first = k * PIX + r * COLS
                at = pl.ds(first, COLS)
                out_ref[at, lane] = (
                    grad[first : first + COLS] + wide * slope_ref[at, lane].astype(F32)
                ).astype(BF16)


def pixels_grad(d, weight, wide, slope, micro):
    rows, channels = slope.shape[0] // micro, slope.shape[1]
    lines = wide.shape[0] // micro
    big = pl.BlockSpec((rows, channels), lambda m: (m, 0))
    return run(
        pixels_body,
        (micro,),
        [
            pl.BlockSpec((rows, d.shape[1]), lambda m: (m, 0)),
            pl.BlockSpec(weight.shape, lambda m: (0, 0)),
            pl.BlockSpec((lines, channels), lambda m: (m, 0)),
            big,
        ],
        big,
        shape(slope.shape, BF16),
        flops=2 * slope.shape[0] * weight.size,
        bytes_accessed=4 * slope.size,
    )(d, weight, wide, slope)


def factor_body(feat_ref, other_feat_ref, dg_ref, far_ref, near_ref, both_ref, out_ref):
    left = jnp.concatenate([feat_ref[...], other_feat_ref[...]], 0).astype(BF16)
    lines = dg_ref.shape[0] // 2
    right = jnp.concatenate(
        [
            ref[c * lines : (c + 1) * lines, :]
            for c in range(2)
            for ref in (dg_ref, near_ref, far_ref, both_ref)
        ],
        0,
    ).astype(BF16)
    out_ref[...] = tn_dot(left, right)


def factor_grad(feat, other_feat, dg, far, near, both):
    lines, depth = feat.shape
    width = dg.shape[1]
    tile = 512
    left = pl.BlockSpec((lines, tile), lambda c: (0, c))
    return run(
        factor_body,
        (depth // tile,),
        [left, left] + [whole(dg)] * 4,
        pl.BlockSpec((tile, width), lambda c: (c, 0)),
        shape((depth, width)),
        flops=4 * lines * depth * width,
        bytes_accessed=4 * depth * width,
    )(feat, other_feat, dg, far, near, both)


def embed_body(protos, counts, members, refs):
    part_refs = refs[:counts]
    g_ref, gain_ref, shift_ref, w_ref, bias_ref, table_ref, queue_ref, act_ref, z_ref, inverse_ref, unit_ref, logits_ref, batch_ref, line_ref, sums_ref, info_ref = refs[counts:]
    micro = info_ref.shape[0]
    crops = g_ref.shape[0] // micro
    for m in range(micro):
        at = slice(m * crops, (m + 1) * crops)
        mean, scaled = norm_of(part_refs, members, m)
        info_ref[m, 0:1, :] = mean
        info_ref[m, 1:2, :] = scaled
        pre = (g_ref[at, :] - mean) * scaled * gain_ref[...] + shift_ref[...]
        act_ref[at, :] = (pre * sigmoid(pre)).astype(BF16)
    z = jnp.dot(act_ref[...], w_ref[...], preferred_element_type=F32) + bias_ref[...]
    inverse = lax.rsqrt(jnp.sum(z * z, 1, keepdims=True) + eps_unit)
    unit = (z * inverse).astype(BF16)
    z_ref[...] = z
    inverse_ref[...] = inverse
    unit_ref[...] = unit
    logits = jnp.dot(unit, table_ref[...], preferred_element_type=F32)
    logits_ref[...] = logits
    real = lax.broadcasted_iota(jnp.int32, (1, logits.shape[1]), 1) < protos
    batch = jnp.where(real, jnp.exp(logits / transport_epsilon), 0.0)
    batch_ref[...] = batch
    queued = jnp.dot(queue_ref[...], table_ref[...], preferred_element_type=F32)
    line = jnp.where(real, jnp.exp(queued / transport_epsilon), 0.0)
    line_ref[...] = line
    queue_sum = jnp.sum(line, axis=0, keepdims=True)
    for m in range(micro):
        at = slice(m * crops, (m + 1) * crops)
        sums_ref[m : m + 1, :] = jnp.sum(batch[at], axis=0, keepdims=True) + queue_sum


def embed_product(parts, members, protos, g, gain, shift, weight, bias, table, queue):
    lines = g.shape[0]
    micro = parts[0].shape[0]
    feat = weight.shape[1]
    wide = table.shape[1]
    outs = [
        shape(g.shape, BF16),
        shape((lines, feat)),
        shape((lines, 1)),
        shape((lines, feat), BF16),
        shape((lines, wide)),
        shape((lines, wide)),
        shape((queue.shape[0], wide)),
        shape((micro, wide)),
        shape((micro, 2, g.shape[1])),
    ]
    ins = [*parts, g, gain, shift, weight, bias, table, queue]
    return run(
        named("embed", embed_body, protos, len(parts), members),
        (1,),
        [whole(a) for a in ins],
        [whole(a) for a in outs],
        outs,
        flops=2 * lines * table.size,
        bytes_accessed=8 * lines * wide,
    )(*ins)


def sweep_body(protos, counts, refs):
    part_refs = refs[:counts]
    batch_ref, queue_ref, new_batch_ref, new_queue_ref, sums_ref = refs[counts:]
    micro, wide = sums_ref.shape
    crops = batch_ref.shape[0] // micro
    lines = new_queue_ref.shape[0] // micro
    shared = queue_ref.shape[0] == lines
    real = lax.broadcasted_iota(jnp.int32, (1, wide), 1) < protos
    for m in range(micro):
        column = jnp.where(real, tree([ref[m : m + 1, :] for ref in part_refs]), 1.0)
        at = slice(m * crops, (m + 1) * crops)
        batch = batch_ref[at, :] / column
        batch = batch / jnp.sum(batch, 1, keepdims=True)
        new_batch_ref[at, :] = batch
        own = slice(m * lines, (m + 1) * lines)
        queue = queue_ref[slice(0, lines) if shared else own, :] / column
        queue = queue / jnp.sum(queue, 1, keepdims=True)
        new_queue_ref[own, :] = queue
        sums_ref[m : m + 1, :] = jnp.sum(batch, axis=0, keepdims=True) + jnp.sum(
            queue, axis=0, keepdims=True
        )


def sweep(parts, protos, batch, queue, lines):
    micro, wide = parts[0].shape
    outs = [shape(batch.shape), shape((micro * lines, wide)), shape(parts[0].shape)]
    ins = [*parts, batch, queue]
    return run(
        named("sweep", sweep_body, protos, len(parts)),
        (1,),
        [whole(a) for a in ins],
        [whole(a) for a in outs],
        outs,
        flops=20 * batch.size,
        bytes_accessed=16 * batch.size,
    )(*ins)


def split_dot(dot, left, right, wide_left):
    value = left if wide_left else right
    high = value.astype(BF16)
    low = (value - high.astype(F32)).astype(BF16)
    if wide_left:
        return dot(high, right) + dot(low, right)
    return dot(left, high) + dot(left, low)


def pack_small(low, send_ref, keep_ref, protos, embed):
    shards, lines, width = send_ref.shape
    lines = lines // 2
    rows = protos.shape[0] // shards // 2
    half = protos.shape[1] // 2
    groups = half // width
    lane = embed.shape[1]
    below = lines - groups * rows

    def put(d, place, columns, one, two):
        keep_ref[d, place, columns] = jnp.where(low, one, two)
        send_ref[d, place, columns] = jnp.where(low, two, one)

    for d in range(shards):
        for y in range(2):
            first = (2 * d + y) * rows
            for q in range(groups):
                start = y * lines + q * rows
                one, two = [
                    protos[first : first + rows, c * half + q * width : c * half + (q + 1) * width]
                    for c in range(2)
                ]
                put(d, slice(start, start + rows), slice(None), one, two)
            for q in range(width // lane):
                one, two = [
                    embed[first : first + below]
                    for first in [
                        (((2 * d + c) * 2 + y) * (width // lane) + q) * below for c in range(2)
                    ]
                ]
                start = y * lines + groups * rows
                put(d, slice(start, start + below), slice(q * lane, (q + 1) * lane), one, two)


def unpack_small(halves, protos, embed):
    shards, lines, width = halves[0].shape
    lines = lines // 2
    packed = jnp.stack(halves).reshape(2, shards, 2, lines, width)
    rows = protos[0] // shards // 2
    groups = protos[1] // 2 // width
    lane = embed[1]
    above = packed[:, :, :, : groups * rows].reshape(2, shards, 2, groups, rows, width)
    below = packed[:, :, :, groups * rows :]
    below = below.reshape(2, shards, 2, lines - groups * rows, width // lane, lane)
    return (
        above.transpose(1, 2, 4, 0, 3, 5).reshape(protos),
        below.transpose(1, 0, 2, 4, 3, 5).reshape(embed),
    )


def packed_shape(protos, embed, shards):
    width = 512
    lines = protos[0] // shards // 2 * (protos[1] // 2 // width)
    return (shards, 2 * (lines + embed[0] * embed[1] // shards // 4 // width), width)


def loss_body(protos, scale, counts, refs):
    which_ref, part_refs = refs[0], refs[1 : 1 + counts]
    batch_ref, logits_ref, unit_ref, z_ref, inverse_ref, act_ref, g_ref, info_ref, gain_ref, shift_ref, w_ref, table_ref, send_ref, keep_ref, dy_ref, sums_ref = refs[1 + counts :]
    micro, wide = part_refs[0].shape
    lines = batch_ref.shape[0]
    crops = lines // micro
    real = lax.broadcasted_iota(jnp.int32, (1, wide), 1) < protos
    odd = lax.broadcasted_iota(jnp.int32, (crops, 1), 0) % 2 == 1
    parts = []
    loss = jnp.zeros((1, 1), F32)
    for m in range(micro):
        at = slice(m * crops, (m + 1) * crops)
        codes = batch_ref[at, :] / jnp.where(
            real, tree([ref[m : m + 1, :] for ref in part_refs]), 1.0
        )
        codes = codes / jnp.sum(codes, 1, keepdims=True)
        partner = jnp.where(odd, pltpu.roll(codes, 1, 0), pltpu.roll(codes, crops - 1, 0))
        sharp = logits_ref[at, :] / softmax_sharpness
        top = jnp.max(jnp.where(real, sharp, -jnp.inf), 1, keepdims=True)
        shifted = sharp - top
        mass = jnp.where(real, jnp.exp(shifted), 0.0)
        total = jnp.sum(mass, 1, keepdims=True)
        chance = shifted - jnp.log(total)
        loss += jnp.sum(jnp.sum(partner * chance, 1, keepdims=True), 0, keepdims=True)
        weight = jnp.sum(partner, 1, keepdims=True)
        parts.append((scale / softmax_sharpness) * (weight * (mass / total) - partner))
    d_scores = jnp.concatenate(parts, 0)
    unit = unit_ref[...]
    grad_protos = split_dot(tn_dot, unit, d_scores, False)
    d_unit = split_dot(nt_dot, d_scores, table_ref[...], True)
    z = z_ref[...]
    inverse = inverse_ref[...]
    dz = inverse * d_unit - z * (inverse * inverse * inverse) * jnp.sum(
        z * d_unit, 1, keepdims=True
    )
    grad_embed = split_dot(tn_dot, act_ref[...], dz, False)
    pack_small(which_ref[0] == 0, send_ref, keep_ref, grad_protos, grad_embed)
    d_act = split_dot(nt_dot, dz, w_ref[...], True)
    for m in range(micro):
        at = slice(m * crops, (m + 1) * crops)
        normal = (g_ref[at, :] - info_ref[m, 0:1, :]) * info_ref[m, 1:2, :]
        pre = normal * gain_ref[...] + shift_ref[...]
        dy = d_act[at] * slope_of(pre)
        dy_ref[at, :] = dy
        sums_ref[m : m + 1, : dy.shape[1]] = jnp.sum(dy, axis=0, keepdims=True)
        sums_ref[micro + m : micro + m + 1, : dy.shape[1]] = jnp.sum(
            dy * normal, axis=0, keepdims=True
        )
    feat = z.shape[1]
    wide = dy_ref.shape[1]
    extra = jnp.concatenate(
        [jnp.sum(dz, axis=0, keepdims=True), jnp.broadcast_to(-scale * loss, (1, feat))], 1
    )
    sums_ref[:, wide:] = jnp.broadcast_to(extra, (2 * micro, 2 * feat))


def loss_grads(which, parts, protos, scale, batch, logits, unit, z, inverse, act, g, info, gain, shift, weight, table, shards):
    ins = [*parts, batch, logits, unit, z, inverse, act, g, info, gain, shift, weight, table]
    micro = info.shape[0]
    outs = [
        shape(packed_shape(table.shape, weight.shape, shards)),
        shape(packed_shape(table.shape, weight.shape, shards)),
        shape(g.shape),
        shape((2 * micro, g.shape[1] + 2 * weight.shape[1])),
    ]
    return run(
        named("loss", loss_body, protos, scale, len(parts)),
        (1,),
        [whole(a) for a in ins],
        [whole(a) for a in outs],
        outs,
        flops=8 * table.size * batch.shape[0],
        bytes_accessed=16 * batch.size,
        prefetch=1,
    )(which, *ins)


def pick_block(rows, width, cell, *fixed):
    return pl.BlockSpec((1, rows, width), lambda g, w: cell(g, *fixed, w[0], w[1], w[2]) + (0,))


def sent_first(g, i, core, x, y):
    z, b = 2 * g + i // 2, i % 2
    return (2 * z + (1 - core) * (1 - x) + core * b, (1 - core) * b + core * (1 - y))


def kept_second(g, i, core, x, y):
    return (2 * (2 * g + i) + x, y)


def sent_second(g, i, core, x, y):
    z = 2 * g + i
    return (2 * z + (1 - core) * x + core * (1 - x), (1 - core) * (1 - y) + core * y)


def add_groups(refs, sizes, out_ref, index, extra=None):
    start = 0
    place = 0
    for count, rows in sizes:
        value = refs[place][0]
        for ref in refs[place + 1 : place + count]:
            value = value + ref[0]
        if extra is not None:
            value = value + extra[0, start : start + rows, :]
        out_ref[index, start : start + rows, :] = value
        place += count
        start += rows


def group_sizes(groups):
    return [(len(addends), addends[0].shape[1] // 2) for addends in groups]


def first_send(scalars, groups):
    sizes = group_sizes(groups)
    shards, _, width = groups[0][0].shape
    lines = sum(rows for _, rows in sizes)
    flat = [array for addends in groups for array in addends]
    specs = []
    for i in range(4):
        for array in flat:
            specs.append(pick_block(array.shape[1] // 2, width, sent_first, i))

    def body(refs):
        refs = refs[1:]
        for i in range(4):
            add_groups(refs[i * len(flat) : (i + 1) * len(flat)], sizes, refs[-1], i)

    return run(
        named("first_send", body),
        (shards // 4,),
        specs,
        pl.BlockSpec((4, lines, width), lambda g, w: (g, 0, 0)),
        shape((shards, lines, width)),
        bytes_accessed=4 * lines * width * shards * 3,
        prefetch=1,
    )(scalars, *(flat * 4))


def second_send(scalars, groups, came):
    sizes = group_sizes(groups)
    shards, _, width = groups[0][0].shape
    lines = sum(rows for _, rows in sizes)
    flat = [array for addends in groups for array in addends]
    specs = []
    for cell in (sent_second, kept_second):
        for i in range(2):
            for array in flat:
                specs.append(pick_block(array.shape[1] // 2, width, cell, i))

    def bit(w):
        return (1 - w[0]) * w[2] + w[0] * w[1]

    for flip in (1, 0):
        for i in range(2):
            specs.append(
                pl.BlockSpec(
                    (1, lines, width),
                    lambda g, w, i=i, flip=flip: (2 * (2 * g + i) + (1 - bit(w) if flip else bit(w)), 0, 0),
                )
            )
    out = pl.BlockSpec((2, lines, width), lambda g, w: (g, 0, 0))

    def body(refs):
        refs = refs[1:]
        count = len(flat)
        came_refs = refs[4 * count : 4 * count + 4]
        for side in range(2):
            for i in range(2):
                place = 2 * side + i
                add_groups(
                    refs[place * count : (place + 1) * count],
                    sizes,
                    refs[-2 + side],
                    i,
                    came_refs[place],
                )

    return run(
        named("second_send", body),
        (shards // 4,),
        specs,
        [out, out],
        [shape((shards // 2, lines, width))] * 2,
        bytes_accessed=4 * lines * width * shards * 4,
        prefetch=1,
    )(scalars, *(flat * 4), *([came] * 4))


def four_places(scalars_ref, refs):
    core, side = scalars_ref[0], scalars_ref[2]
    return [
        (core, side, refs[0]),
        (core, 1 - side, refs[1]),
        (1 - core, side, refs[2]),
        (1 - core, 1 - side, refs[3]),
    ]


def place_early_body(scalars_ref, *refs):
    out_ref, embed_ref, protos_ref, head_ref = refs[8:]
    lines = out_ref.shape[0]
    rows = protos_ref.shape[0] // 2
    wide = 512
    groups = protos_ref.shape[1] // 2 // wide
    lane = embed_ref.shape[1]
    below = embed_ref.shape[0] // 4 // (wide // lane)
    start = lines + groups * rows
    for c, y, ref in four_places(scalars_ref, refs[:4]):
        out_ref[:, pl.ds(pl.multiple_of((2 * c + y) * wide, wide), wide)] = ref[0:lines, :]
        at = pl.ds(pl.multiple_of(y * rows, rows), rows)
        for q in range(groups):
            column = pl.multiple_of((c * groups + q) * wide, wide)
            protos_ref[at, pl.ds(column, wide)] = ref[lines + q * rows : lines + (q + 1) * rows, :]
        for q in range(wide // lane):
            first = pl.multiple_of(((2 * c + y) * (wide // lane) + q) * below, below)
            embed_ref[pl.ds(first, below), :] = ref[start:, q * lane : (q + 1) * lane]
    for c, y, ref in four_places(scalars_ref, refs[4:8]):
        head_ref[:, pl.ds(pl.multiple_of((2 * c + y) * wide, wide), wide)] = ref[...]


def place_late_body(scalars_ref, *refs):
    outs = refs[8:]
    for out_ref, pieces in zip(outs, (refs[:4], refs[4:8])):
        rows, width = out_ref.shape[0] // 2, out_ref.shape[1] // 2
        for c, y, ref in four_places(scalars_ref, pieces):
            out_ref[
                pl.ds(pl.multiple_of(y * rows, rows), rows),
                pl.ds(pl.multiple_of(c * width, width), width),
            ] = ref[...]


def placed_pieces(body, scalars, pieces, outs):
    return run(
        body,
        (1,),
        [whole(a) for a in pieces],
        [whole(a) for a in outs],
        outs,
        prefetch=1,
    )(scalars, *pieces)


def on_device(
    pixels,
    crop_map,
    queue_rows,
    conv_in,
    gain_one,
    shift_one,
    conv_mid,
    gain_two,
    shift_two,
    conv_out,
    gain_three,
    shift_three,
    head_weight,
    head_gain,
    head_shift,
    embed_weight,
    embed_bias,
    prototypes,
):
    micro, canvas, pixel_count, channels = pixels.shape
    devices = lax.axis_size("dp") * lax.axis_size("hst")
    crops = canvas * SLOTS
    total_crops = crops * devices * 1.0
    loss_scale = 1.0 / (micro * total_crops)
    x = pixels.reshape(micro * canvas * pixel_count, channels)
    valid = (crop_map < SLOTS).astype(F32).reshape(-1, 1)
    sizes = jnp.sum(
        (crop_map[:, :, None, :] == jnp.arange(SLOTS, dtype=jnp.int32)[:, None]).astype(F32), 3
    ).reshape(-1, 1)

    shards = lax.axis_size("dp")
    quick = shards == 8 and lax.axis_size("hst") == 4
    packs = 8
    protos = prototypes.shape[1]
    table = jnp.pad(prototypes, ((0, 0), (0, -protos % 1024)))

    def row(vector):
        return vector.reshape(1, -1)

    masks = dp_masks()
    near, far = masks[0], masks[1:]
    core = bit_of(1)
    side = bit_of(2)
    scalars = jnp.stack([core, bit_of(near), side]).astype(jnp.int32)
    keep_half = core.astype(jnp.int32).reshape(1)
    send_half = 1 - keep_half

    h1, stats = first_product(x, conv_in, valid, micro)
    members, counts = first_parts(stats)
    act_one, h2, stats, info_one = second_product(
        members, h1, valid, row(gain_one), row(shift_one), conv_mid, micro
    )
    parts = moment_parts(stats, counts)
    act_two, h3, stats, info_two = third_product(
        parts, members, h2, valid, row(gain_two), row(shift_two), conv_out, micro
    )
    base = stats
    parts = moment_parts(stats, counts)
    feat, info_three, slope, slope_first, slope_second, *feat_halves = pool(
        scalars,
        parts,
        members,
        base,
        h3,
        x,
        valid,
        row(gain_three),
        row(shift_three),
        sizes,
        micro,
        channels // shards if quick else 0,
    )

    lines = feat.shape[0]
    if quick:
        feat_keep, feat_send = feat_halves
        feat_near, feat_far = swap(feat_send, near), swap(feat_keep, 2)
    g, stats = head_product(feat, head_weight, micro)
    if quick:
        stats, feat_near, feat_far = tie(stats, feat_near, feat_far)

    crop_counts = []
    crop_members = []
    number = crops * 1.0
    for group in sync_groups():
        crop_members = [number] * (len(group) + 1)
        crop_counts.append(crop_members)
        number = number * (len(group) + 1)
    parts = moment_parts(stats, crop_counts)

    act_four, embedded, inverse, unit_rows, logits, batch, queue, column, info_four = embed_product(
        parts,
        crop_members,
        protos,
        g,
        row(head_gain),
        row(head_shift),
        embed_weight,
        row(embed_bias),
        table,
        queue_rows,
    )
    for _ in range(SINK_ITERS - 1):
        parts = sum_parts(column)
        batch, queue, column = sweep(parts, protos, batch, queue, queue_rows.shape[0])
    parts = sum_parts(column)
    which = (1 - send_half) if quick else jnp.zeros((1,), jnp.int32)
    small_send, small_keep, dy_four, payload = loss_grads(
        which,
        parts,
        protos,
        loss_scale,
        batch,
        logits,
        unit_rows,
        embedded,
        inverse,
        act_four,
        g,
        info_four,
        row(head_gain),
        row(head_shift),
        embed_weight,
        table,
        packs,
    )
    parts = sum_parts(payload)
    payload = tree(list(parts))
    channel_sums = payload[:, : head_gain.shape[0]]
    first_four, second_four = channel_sums[:micro], channel_sums[micro:]
    extra = payload[0, head_gain.shape[0] :]
    grad_bias, total_loss = extra[: embed_bias.shape[0]], extra[embed_bias.shape[0]]

    if quick:
        feat_near, small_send, *parts = tie(feat_near, small_send, *parts)
        feat_both = swap(feat_near, 2)
        small_recv = swap(small_send, 1)
    dg_send, dg_keep, wide, sums = head_back(
        which,
        parts,
        dy_four,
        g,
        info_four,
        row(head_gain),
        head_weight,
        sizes,
        slope_first,
        slope_second,
        total_crops,
    )
    first_norm = (h1, valid, info_one, info_one, row(gain_one))
    second_norm = (h2, valid, info_two, info_one, row(gain_two))

    def from_third(which, parts):
        return third_back(
            which,
            parts,
            wide,
            slope,
            h3,
            valid,
            info_three,
            row(gain_three),
            info_one,
            conv_out,
            act_two,
            h2,
            info_two,
            row(gain_two),
            row(shift_two),
            micro,
            shards,
        )

    def from_second(d):
        return second_back(
            d, conv_mid, valid, h1, info_one, row(gain_one), row(shift_one), micro
        )

    if quick:
        sums, dg_send, feat_both, small_recv = tie(sums, dg_send, feat_both, small_recv)
        feat_both = jnp.concatenate([feat_keep, feat_near, feat_far, feat_both], 0)

        def core_filler(gate):
            source, other = tie(dg_send, feat_both, gate)[:2]
            grads["dg"] = swap(source, 1)
            grads["feat"] = swap(other, 1)
            return [grads["dg"], grads["feat"]]

        grads = {}
        parts_three = sum_parts(sums, ((), (core_filler,)))
        feat_other = grads["feat"]
        quarter = dg_keep.shape[1] // 2

        def quarter_of(place):
            return jnp.concatenate(
                [
                    lax.dynamic_slice_in_dim(array, place * quarter, quarter, 1)
                    for array in (dg_keep, grads["dg"])
                ],
                0,
            )

        dg_here, dg_there = quarter_of(side), quarter_of(1 - side)
        *parts_three, dg_here, dg_there = tie(*parts_three, dg_here, dg_there)
        dg_far, dg_near, dg_both = swap(dg_there, 2), swap(dg_here, near), swap(dg_there, 2 + near)
        dy, sums, out_send, out_keep = from_third(send_half, parts_three)
        sums, dy, out_send, dg_far, dg_near, dg_both = tie(
            sums, dy, out_send, dg_far, dg_near, dg_both
        )
        small = [small_keep, small_recv]

        def out_filler(gate):
            grads["out"] = swap(tie(out_send, gate)[0], 1)
            return [grads["out"]]

        def head_filler(gate):
            source = tie(dg_near, gate)[0]
            grads["head"] = factor_grad(feat_both, feat_other, dg_here, dg_far, source, dg_both)
            return [grads["head"]]

        def early_filler(gate):
            source = tie(grads["out"], gate)[0]
            grads["early"] = [[out_keep, source], small]
            grads["early_out"] = first_send(scalars, grads["early"])
            return [grads["early_out"]]

        parts_two = sum_parts(sums, ((), (out_filler,), (head_filler, early_filler)))

        early = grads["early"]
        *parts_two, early_out, partial = tie(*parts_two, grads["early_out"], grads["head"])
        early_came = core_swap(early_out, near, 2)
        partial = partial.reshape(2, 2, 2, -1, partial.shape[1])
        heads = [dp_halves([partial[:, :, 0]], far[0], 1)]
        d_two, mid_send = mid_grad(
            "mid_first",
            mid_first_body,
            send_half,
            [*parts_two, dy, *second_norm, act_one],
            act_one,
            True,
        )
        d_two, mid_send, early_came, heads[0][-1] = tie(
            d_two, mid_send, early_came, heads[0][-1]
        )
        heads.append(dp_halves([partial[:, :, 1]], far[0], 1))
        mid_recv = swap(mid_send, 1)
        early_out, early_keep = second_send(scalars, early, early_came)
        early_came = core_swap(early_out, 2, near)
        mid_keep = mid_grad(
            "mid_second", mid_second_body, keep_half, [d_two, act_one], act_one, False
        )
        mid_keep, mid_recv, early_came, heads[1][-1] = tie(
            mid_keep, mid_recv, early_came, heads[1][-1]
        )

        def sharded(array):
            return array.reshape(shards, -1, array.shape[-1])

        def by_bits(array):
            return array.reshape((2, 2) + array.shape[1:])

        late = [[sharded(mid_keep), sharded(mid_recv)]]
        mid_out = first_send(scalars, late)
        d_two, mid_out = tie(d_two, mid_out)
        mid_came = core_swap(mid_out, near, 2)
        halves = [dp_split(head, far[1], 0) for head in heads]
        head_came = swap(jnp.concatenate([send for _, send in halves], 0), far[1])
        dy, sums = from_second(d_two)
        dy, sums, mid_came, head_came, early_keep, early_came = tie(
            dy, sums, mid_came, head_came, early_keep, early_came
        )
        early = [by_bits(early_keep), by_bits(early_came)]

        def early_z_filler(gate):
            grads["z"] = dp_halves(early, far[0], 1)
            return [grads["z"][-1]]

        def mid_filler(gate):
            source = tie(mid_came, gate)[0]
            grads["mid"] = second_send(scalars, late, source)
            return grads["mid"]

        parts_one = sum_parts(sums, ((), (early_z_filler,), (mid_filler,)))
        mid_out, mid_keep = grads["mid"]
        *parts_one, mid_out, early_came = tie(*parts_one, mid_out, grads["z"][-1])
        early = dp_halves(grads["z"][:-1] + [early_came], far[1], 0)
        mid_came = core_swap(mid_out, 2, near)
        d_one, in_send, in_keep = in_grad(send_half, parts_one, dy, *first_norm, x)
        d_one, in_send, in_keep, mid_came, early[-1] = tie(
            d_one, in_send, in_keep, mid_came, early[-1]
        )
        in_recv = swap(in_send, 1)
        inner = [[sharded(in_keep), sharded(in_recv)]]
        in_out = first_send(scalars, inner)
        mid = dp_halves([by_bits(mid_keep), by_bits(mid_came)], far[0], 1)
        d_one, in_out = tie(d_one, in_out)
        in_came = core_swap(in_out, near, 2)
        early_mine, head_mine = sum(early), jnp.concatenate([sum(keep) for keep, _ in halves], 0) + head_came
        early_core, head_core = swap(early_mine, 1), swap(head_mine, 1)
        grad_x = pixels_grad(d_one, conv_in, wide, slope, micro)
        grad_x, in_came, mid[-1], early_mine, early_core, head_mine, head_core = tie(
            grad_x, in_came, mid[-1], early_mine, early_core, head_mine, head_core
        )
        mid_keep, mid_out = dp_split(mid, far[1], 0)
        in_came, mid_out = tie(in_came, mid_out)
        mid_came = swap(mid_out, far[1])
        in_out, in_keep = second_send(scalars, inner, in_came)
        in_came = core_swap(in_out, 2, near)
        head_far = swap(head_mine, 2)
        in_came, mid_came, head_far = tie(in_came, mid_came, head_far)
        inner = dp_halves([by_bits(in_keep), by_bits(in_came)], far[0], 1)
        mid_mine = sum(mid_keep) + mid_came
        early_far, mid_core, head_both = swap(early_mine, 2), swap(mid_mine, 1), swap(head_far, 1)
        inner[-1], early_far, mid_mine, mid_core, head_both = tie(
            inner[-1], early_far, mid_mine, mid_core, head_both
        )
        inner = dp_halves(inner, far[1], 0)
        mid_far, early_both = swap(mid_mine, 2), swap(early_far, 1)
        channel = channels // shards
        early_grads = placed_pieces(
            place_early_body,
            scalars,
            [early_mine, early_far, early_core, early_both]
            + [head_mine, head_far, head_core, head_both],
            [
                shape((conv_out.shape[0] // shards, channels)),
                shape((embed_weight.shape[0] // shards, embed_weight.shape[1])),
                shape((table.shape[0] // shards, table.shape[1])),
                shape((channel, head_weight.shape[1])),
            ],
        )
        inner[-1], mid_far, *early_grads = tie(inner[-1], mid_far, *early_grads)
        in_mine = sum(inner)
        in_far, in_core, mid_both = swap(in_mine, 2), swap(in_mine, 1), swap(mid_far, 1)
        grad_conv_out, grad_embed, grad_protos, grad_head = early_grads
        grad_protos = grad_protos[:, :protos]
        grad_conv_mid, grad_conv_in = placed_pieces(
            place_late_body,
            scalars,
            [mid_mine, mid_far, mid_core, mid_both, in_mine, in_far, in_core, swap(in_far, 1)],
            [
                shape((conv_mid.shape[0] // shards, conv_mid.shape[1])),
                shape((channel, conv_in.shape[1])),
            ],
        )
    else:
        low, high = jnp.zeros((1,), jnp.int32), jnp.ones((1,), jnp.int32)

        def reduced(array):
            return lax.psum(lax.psum_scatter(array, "dp", scatter_dimension=0, tiled=True), "hst")

        parts_three = sum_parts(sums)
        dy, sums, out_low, out_high = from_third(low, parts_three)
        parts_two = sum_parts(sums)
        ins = [*parts_two, dy, *second_norm, act_one]
        d_two, mid_low = mid_grad("mid_first", mid_first_body, low, ins, act_one, True)
        mid_high = mid_grad("mid_second", mid_second_body, high, [d_two, act_one], act_one, False)
        dy, sums = from_second(d_two)
        parts_one = sum_parts(sums)
        d_one, in_low, in_high = in_grad(low, parts_one, dy, *first_norm, x)
        grad_x = pixels_grad(d_one, conv_in, wide, slope, micro)
        out = jnp.stack([out_low, out_high])
        out = out.reshape(2, shards, -1, conv_out.shape[0] // shards, out.shape[-1])
        small_protos, small_embed = unpack_small(
            [small_keep, small_send], table.shape, embed_weight.shape
        )
        grad_conv_out = reduced(out.transpose(1, 3, 0, 2, 4).reshape(conv_out.shape))
        grad_conv_mid = reduced(jnp.concatenate([mid_low, mid_high], 1))
        grad_conv_in = reduced(jnp.concatenate([in_low, in_high], 1))
        dg = jnp.concatenate([dg_keep, dg_send], 1).astype(BF16)
        grad_head = reduced(jnp.dot(feat.astype(BF16).T, dg, preferred_element_type=F32))
        grad_embed = reduced(small_embed)
        grad_protos = reduced(small_protos)[:, :protos]

    def own_rows(vectors):
        sums = [jnp.sum(vector, 0) for vector in vectors]
        piece = sums[0].shape[0] // shards
        stacked = jnp.stack(sums)
        found = lax.dynamic_slice_in_dim(stacked, lax.axis_index("dp") * piece, piece, 1)
        return [found[i] for i in range(len(vectors))]

    def both_sums(parts):
        total = tree(list(parts))
        return [total[:, 1], total[:, 0]]

    small_ones = own_rows(both_sums(parts_one) + both_sums(parts_two))
    large_ones = own_rows(both_sums(parts_three) + [second_four, first_four])

    return (
        total_loss,
        grad_x.reshape(pixels.shape),
        grad_conv_in,
        small_ones[0],
        small_ones[1],
        grad_conv_mid,
        small_ones[2],
        small_ones[3],
        grad_conv_out,
        large_ones[0],
        large_ones[1],
        grad_head,
        large_ones[2],
        large_ones[3],
        grad_embed,
        lax.dynamic_slice_in_dim(
            grad_bias,
            lax.axis_index("dp") * (grad_bias.shape[0] // shards),
            grad_bias.shape[0] // shards,
            0,
        ),
        grad_protos,
    )


def solution(mesh):
    placed = (
        P(None, ("dp", "hst"), None, None),
        P(None, ("dp", "hst"), None),
        P(("dp", "hst"), None),
    ) + (P(),) * 15
    return jax.shard_map(
        on_device,
        mesh=mesh,
        in_specs=placed,
        out_specs=(
            P(),
            P(None, ("dp", "hst"), None, None),
            P("dp", None),
            P("dp"),
            P("dp"),
            P("dp", None),
            P("dp"),
            P("dp"),
            P("dp", None),
            P("dp"),
            P("dp"),
            P("dp", None),
            P("dp"),
            P("dp"),
            P("dp", None),
            P("dp"),
            P("dp", None),
        ),
        check_vma=False,
    )
```

```python
import functools

import jax
import jax.numpy as jnp
from jax import lax
from jax.experimental import pallas as pl
from jax.experimental.pallas import tpu as pltpu
from jax.sharding import PartitionSpec as P

ROWS = 8
COLS = 16
SLOTS = 4
CELL = COLS // SLOTS
PIX = ROWS * COLS
SINK_ITERS = 3
TAPS = 9

eps_norm = 1e-05
eps_unit = 1e-06
transport_epsilon = 0.05
softmax_sharpness = 0.1
highest = lax.Precision.HIGHEST
F32 = jnp.float32
BF16 = jnp.bfloat16
AXES = ("dp", "hst")
MIB = 1 << 20
LANES = 128


def swap(value, mask):
    count = lax.axis_size("dp") * lax.axis_size("hst")
    return lax.ppermute(value, AXES, [(i, i ^ mask) for i in range(count)])


def sync_groups():
    bits = (lax.axis_size("dp") * lax.axis_size("hst")).bit_length() - 1
    groups = [(1,)]
    bit = 1
    while bit < bits:
        if bit + 1 < bits:
            groups.append((1 << bit, 2 << bit, 3 << bit))
            bit += 2
        else:
            groups.append((1 << bit,))
            bit += 1
    return groups


def tree(parts):
    while len(parts) > 1:
        parts = [parts[i] + parts[i + 1] for i in range(0, len(parts), 2)]
    return parts[0]


def between(parts, gate, fillers):
    for filler in fillers:
        parts = list(tie(*parts, *filler(gate)))[: len(parts)]
    return parts


def pick(fillers, step):
    return fillers[step] if step < len(fillers) else ()


def sum_parts(value, fillers=()):
    groups = sync_groups()
    for step, group in enumerate(groups):
        parts = [value] + [swap(value, mask) for mask in group]
        parts = between(parts, value, pick(fillers, step))
        value = tree(parts)
    return parts


def merge(parts, members):
    whole = tree(list(members))
    mean = tree([n * part[:, 0] for n, part in zip(members, parts)]) / whole
    spread = tree(
        [part[:, 1] + n * (part[:, 0] - mean) ** 2 for n, part in zip(members, parts)]
    )
    return mean, spread, whole


def moment_parts(moments, counts, fillers=()):
    groups = sync_groups()
    for step, group in enumerate(groups):
        parts = [moments] + [swap(moments, mask) for mask in group]
        parts = between(parts, moments, pick(fillers, step))
        if step + 1 < len(groups):
            moments = jnp.stack(merge(parts, counts[step])[:2], 1)
    return parts


def first_parts(moments):
    groups = sync_groups()
    counts = []
    for step, group in enumerate(groups):
        parts = [moments] + [swap(moments, mask) for mask in group]
        if step + 1 < len(groups):
            members = [part[:, 2] for part in parts]
            moments = jnp.stack(merge(parts, members), 1)
            counts.append([n[:, :1] for n in members])
    return parts, counts


def bit_of(mask):
    index = lax.axis_index("dp") * lax.axis_size("hst") + lax.axis_index("hst")
    return (index // mask) % 2


def dp_masks():
    base = lax.axis_size("hst")
    return [base << j for j in range(lax.axis_size("dp").bit_length() - 1)]


def tie(first, *others):
    return lax.optimization_barrier((first,) + others)


def at(view, place, axis):
    return lax.dynamic_index_in_dim(view, place, axis, keepdims=False)


def core_swap(value, low, high):
    count = lax.axis_size("dp") * lax.axis_size("hst")
    pairs = [(i, i ^ (high if i % 2 else low)) for i in range(count)]
    return lax.ppermute(value, AXES, pairs)


def dp_split(addends, mask, axis):
    bit = bit_of(mask)
    send = sum(at(array, 1 - bit, axis) for array in addends)
    return [at(array, bit, axis) for array in addends], send


def dp_halves(addends, mask, axis):
    keep, send = dp_split(addends, mask, axis)
    return keep + [swap(send, mask)]


VMEM_MIB = {
    "third_back": 58,
    "second_back_body": 58,
}


def run(body, grid, in_specs, out_specs, out_shape, scratch=(), flops=0, bytes_accessed=0, prefetch=0, aliases=None):
    return pl.pallas_call(
        body,
        grid_spec=pltpu.PrefetchScalarGridSpec(
            num_scalar_prefetch=prefetch,
            grid=grid,
            in_specs=in_specs,
            out_specs=out_specs,
            scratch_shapes=list(scratch),
        ),
        out_shape=out_shape,
        name=body.__name__,
        input_output_aliases=aliases or {},
        compiler_params=pltpu.CompilerParams(
            vmem_limit_bytes=VMEM_MIB.get(body.__name__, 44) * MIB, dimension_semantics=("arbitrary",) * len(grid)
        ),
        cost_estimate=pl.CostEstimate(
            flops=flops, bytes_accessed=bytes_accessed, transcendentals=0
        ),
    )


def shape(dims, dtype=F32):
    return jax.ShapeDtypeStruct(tuple(dims), dtype)


def sigmoid(u):
    return 0.5 * jnp.tanh(0.5 * u) + 0.5


def norm_of(part_refs, members, m=0, lane=slice(None)):
    whole = tree(list(members))
    means = [ref[m, 0:1, lane] for ref in part_refs]
    mean = tree([n * one for n, one in zip(members, means)]) / whole
    spread = tree(
        [ref[m, 1:2, lane] + n * (one - mean) ** 2 for n, ref, one in zip(members, part_refs, means)]
    )
    return mean, lax.rsqrt(spread / whole + eps_norm)


def sums_of(part_refs, first, second, m=0):
    return (
        tree([ref[m, first : first + 1, :] for ref in part_refs]),
        tree([ref[m, second : second + 1, :] for ref in part_refs]),
    )


def counts_of(count_refs, m=0):
    return [ref[m, 2:3, 0:1] for ref in count_refs]


def whole(array):
    return pl.BlockSpec(array.shape, lambda *_: (0,) * len(array.shape))


def per_micro(array):
    return pl.BlockSpec((1,) + array.shape[1:], lambda m, *_: (m,) + (0,) * (array.ndim - 1))


def slope_of(u):
    s = sigmoid(u)
    return s * (1.0 + u * (1.0 - s))


def nt_dot(left, right):
    return lax.dot_general(left, right, (((1,), (1,)), ((), ())), preferred_element_type=F32)


def tn_dot(left, right):
    return lax.dot_general(left, right, (((0,), (0,)), ((), ())), preferred_element_type=F32)


def fold(y):
    return jnp.sum(y.reshape(y.shape[0] // 8, 8, y.shape[1]), 0)


def put_moments(stats_ref, h_ref, v_ref, with_count):
    rows, width = h_ref.shape
    chunk = 32
    lanes = 512
    v = v_ref[...]
    count = jnp.sum(v, axis=0, keepdims=True)
    first = jnp.sum(v[:PIX], axis=0, keepdims=True)
    for j in range(0, width, lanes):
        lane = slice(j, j + lanes)
        acc = jnp.zeros((8, lanes), F32)
        for i in range(0, PIX, chunk):
            acc += fold(h_ref[i : i + chunk, lane].astype(F32) * v_ref[i : i + chunk, :])
        pivot = jnp.sum(acc, axis=0, keepdims=True) / first
        line = jnp.zeros((8, lanes), F32)
        square = jnp.zeros((8, lanes), F32)
        for i in range(0, rows, chunk):
            off = (h_ref[i : i + chunk, lane].astype(F32) - pivot) * v_ref[i : i + chunk, :]
            line += fold(off)
            square += fold(off * off)
        total = jnp.sum(line, axis=0, keepdims=True)
        stats_ref[0, 0:1, lane] = pivot + total / count
        stats_ref[0, 1:2, lane] = (
            jnp.sum(square, axis=0, keepdims=True) - total * total / count
        )
        if with_count:
            stats_ref[0, 2:3, lane] = jnp.broadcast_to(count, (1, lanes))


def first_body(x_ref, w_ref, v_ref, h_ref, stats_ref):
    h_ref[...] = jnp.dot(x_ref[...], w_ref[...], preferred_element_type=F32)
    put_moments(stats_ref, h_ref, v_ref, True)


def first_product(x, weight, valid, micro):
    rows = x.shape[0] // micro
    depth, width = weight.shape
    return run(
        first_body,
        (micro,),
        [
            pl.BlockSpec((rows, depth), lambda m: (m, 0)),
            pl.BlockSpec((depth, width), lambda m: (0, 0)),
            pl.BlockSpec((rows, 1), lambda m: (m, 0)),
        ],
        [
            pl.BlockSpec((rows, width), lambda m: (m, 0)),
            pl.BlockSpec((1, 3, width), lambda m: (m, 0, 0)),
        ],
        [shape((micro * rows, width)), shape((micro, 3, width))],
        flops=2 * micro * rows * depth * width,
        bytes_accessed=2 * x.size,
    )(x, weight, valid)


def cell_column(rows):
    return lax.broadcasted_iota(jnp.int32, (rows, 1), 0) % CELL


def second_body(counts, refs):
    part_refs, (h_ref, v_ref, gain_ref, shift_ref, w_ref, a_ref, h2_ref, stats_ref, info_ref, cols_ref) = refs[:counts], refs[counts:]
    rows, width = h_ref.shape
    members = counts_of(part_refs)
    mean, scaled = norm_of(part_refs, members)
    info_ref[0, 0:1, :] = mean
    info_ref[0, 1:2, :] = scaled
    info_ref[0, 2:3, :] = jnp.broadcast_to(tree(list(members)), mean.shape)
    factor = scaled * gain_ref[...]
    shift = shift_ref[...]
    place = cell_column(COLS)
    has_left = (place >= 1).astype(F32)
    has_right = (place <= CELL - 2).astype(F32)
    blank = jnp.zeros((COLS, width), BF16)
    for i in range(0, rows, COLS):
        at = slice(i, i + COLS)
        pre = (h_ref[at, :] - mean) * factor + shift
        act = (pre * sigmoid(pre) * v_ref[at, :]).astype(BF16)
        a_ref[at, :] = act
        wide = act.astype(F32)
        sides = (
            (pltpu.roll(wide, 1, 0) * has_left).astype(BF16),
            act,
            (pltpu.roll(wide, COLS - 1, 0) * has_right).astype(BF16),
        )
        for c in range(3):
            cols_ref[at, (3 + c) * width : (4 + c) * width] = sides[c]
            if i % PIX < PIX - COLS:
                cols_ref[i + COLS : i + 2 * COLS, c * width : (c + 1) * width] = sides[c]
            else:
                cols_ref[at, (6 + c) * width : (7 + c) * width] = blank
            if i % PIX > 0:
                cols_ref[i - COLS : i, (6 + c) * width : (7 + c) * width] = sides[c]
            else:
                cols_ref[at, c * width : (c + 1) * width] = blank
    h2_ref[...] = jnp.dot(cols_ref[...], w_ref[...], preferred_element_type=F32)
    put_moments(stats_ref, h2_ref, v_ref, False)


def named(name, body, *fixed):
    def kernel(*refs):
        body(*fixed, refs)

    kernel.__name__ = name
    return kernel


def second_product(parts, h1, valid, gain, shift, weight, micro):
    rows, width = h1.shape[0] // micro, h1.shape[1]
    mid = pl.BlockSpec((rows, width), lambda m: (m, 0))
    return run(
        named("second_product", second_body, len(parts)),
        (micro,),
        [per_micro(part) for part in parts]
        + [
            mid,
            pl.BlockSpec((rows, 1), lambda m: (m, 0)),
            whole(gain),
            whole(shift),
            whole(weight),
        ],
        [
            mid,
            mid,
            pl.BlockSpec((1, 2, width), lambda m: (m, 0, 0)),
            pl.BlockSpec((1, 3, width), lambda m: (m, 0, 0)),
        ],
        [
            shape((micro * rows, width), BF16),
            shape((micro * rows, width)),
            shape((micro, 2, width)),
            shape((micro, 3, width)),
        ],
        [pltpu.VMEM((rows, weight.shape[0]), BF16)],
        flops=2 * micro * rows * weight.size,
        bytes_accessed=10 * h1.size,
    )(*parts, h1, valid, gain, shift, weight)


def third_body(counts, refs):
    part_refs, count_refs = refs[:counts], refs[counts : 2 * counts]
    h_ref, v_ref, gain_ref, shift_ref, w_ref, a_ref, h3_ref, stats_ref, info_ref, wide_ref = refs[2 * counts :]
    rows = h_ref.shape[0]
    mean, scaled = norm_of(part_refs, counts_of(count_refs))
    info_ref[0, 0:1, :] = mean
    info_ref[0, 1:2, :] = scaled
    factor = scaled * gain_ref[...]
    shift = shift_ref[...]
    for i in range(0, rows, 32):
        at = slice(i, i + 32)
        pre = (h_ref[at, :] - mean) * factor + shift
        a_ref[at, :] = (pre * sigmoid(pre) * v_ref[at, :]).astype(BF16)
    wide_ref[...] = jnp.dot(a_ref[...], w_ref[...], preferred_element_type=F32)
    put_moments(stats_ref, wide_ref, v_ref, False)
    for i in range(0, rows, 32):
        at = slice(i, i + 32)
        h3_ref[at, :] = (wide_ref[at, :] - stats_ref[0, 0:1, :]).astype(BF16)


def third_product(parts, members, h2, valid, gain, shift, weight, micro):
    rows, depth = h2.shape[0] // micro, h2.shape[1]
    width = weight.shape[1]
    mid = pl.BlockSpec((rows, depth), lambda m: (m, 0))
    return run(
        named("third_product", third_body, len(parts)),
        (micro,),
        [per_micro(part) for part in parts + members]
        + [
            mid,
            pl.BlockSpec((rows, 1), lambda m: (m, 0)),
            whole(gain),
            whole(shift),
            whole(weight),
        ],
        [
            mid,
            pl.BlockSpec((rows, width), lambda m: (m, 0)),
            pl.BlockSpec((1, 2, width), lambda m: (m, 0, 0)),
            pl.BlockSpec((1, 2, depth), lambda m: (m, 0, 0)),
        ],
        [
            shape((micro * rows, depth), BF16),
            shape((micro * rows, width), BF16),
            shape((micro, 2, width)),
            shape((micro, 2, depth)),
        ],
        [pltpu.VMEM((rows, width), F32)],
        flops=2 * micro * rows * weight.size,
        bytes_accessed=4 * micro * rows * width,
    )(*parts, *members, h2, valid, gain, shift, weight)


def crop_sums(ref, *index):
    crops = ref.shape[-2] // CELL
    slabs = [
        tree([ref[(*index, j, pl.ds(i, crops, CELL), slice(None))] for i in range(CELL)])
        for j in range(ref.shape[-3])
    ]
    return jnp.concatenate(slabs, 1)


def put_lanes(ref, place, first, value, *index):
    for j in range(0, value.shape[1], LANES):
        ref[(*index, (first + j) // LANES, place, slice(None))] = value[:, j : j + LANES]


def pool_body(counts, split, refs):
    scalars_ref, part_refs, count_refs = refs[0], refs[1 : 1 + counts], refs[1 + counts : 1 + 2 * counts]
    base_ref, h_ref, x_ref, v_ref, gain_ref, shift_ref, size_ref = refs[1 + 2 * counts : 8 + 2 * counts]
    feat_ref, info_ref, slope_ref, first_ref, second_ref = refs[8 + 2 * counts : 13 + 2 * counts]
    sums_ref = refs[-1]
    rows, width = h_ref.shape
    mean, scaled = norm_of(part_refs, counts_of(count_refs))
    mean = mean - base_ref[0, 0:1, :]
    info_ref[0, 0:1, :] = mean
    info_ref[0, 1:2, :] = scaled
    factor = scaled * gain_ref[...]
    shift = shift_ref[...]
    chunk = 256
    for j in range(0, width, chunk):
        lane = slice(j, j + chunk)
        for k in range(rows // PIX):
            acc = jnp.zeros((COLS, chunk), F32)
            acc_first = jnp.zeros((COLS, chunk), F32)
            acc_second = jnp.zeros((COLS, chunk), F32)
            for r in range(ROWS):
                at = pl.ds(k * PIX + r * COLS, COLS)
                centred = h_ref[at, lane].astype(F32) - mean[:, lane]
                resid = centred * factor[:, lane] + shift[:, lane] + x_ref[at, lane].astype(F32)
                sig = sigmoid(resid)
                kept = sig * v_ref[at, :]
                out = resid * kept
                acc += out.astype(BF16).astype(F32)
                slope = kept + out * (1.0 - sig)
                acc_first += slope
                acc_second += slope * centred
                slope_ref[at, lane] = slope.astype(BF16)
            place = pl.ds(k * COLS, COLS)
            put_lanes(sums_ref, place, j, acc, 0)
            put_lanes(sums_ref, place, j, acc_first, 1)
            put_lanes(sums_ref, place, j, acc_second * scaled[:, lane], 2)
    feat = (crop_sums(sums_ref, 0) / size_ref[...]).astype(BF16).astype(F32)
    feat_ref[...] = feat
    first_ref[...] = crop_sums(sums_ref, 1)
    second_ref[...] = crop_sums(sums_ref, 2)
    if split:
        keep_ref, send_ref = refs[13 + 2 * counts : 15 + 2 * counts]
        low = scalars_ref[1] == 0
        for i in range(0, width, 2 * split):
            one, two = feat[:, i : i + split], feat[:, i + split : i + 2 * split]
            place = slice(i // 2, i // 2 + split)
            keep_ref[:, place] = jnp.where(low, one, two)
            send_ref[:, place] = jnp.where(low, two, one)


def pool(scalars, parts, members, base, h3, x, valid, gain, shift, sizes, micro, split):
    rows, channels = h3.shape[0] // micro, h3.shape[1]
    crops = sizes.shape[0] // micro
    width = 1024
    tile = pl.BlockSpec((rows, width), lambda m, c, w: (m, c))
    line = pl.BlockSpec((1, width), lambda m, c, w: (0, c))
    pair = pl.BlockSpec((1, 2, width), lambda m, c, w: (m, 0, c))
    small = pl.BlockSpec((crops, width), lambda m, c, w: (m, c))
    part = pl.BlockSpec((crops, width // 2), lambda m, c, w: (m, c))
    lines = shape((micro * crops, channels))
    half = shape((micro * crops, channels // 2))
    return run(
        named("pool", pool_body, len(parts), split),
        (micro, channels // width),
        [pair] * len(parts)
        + [per_micro(part) for part in members]
        + [
            pair,
            tile,
            tile,
            pl.BlockSpec((rows, 1), lambda m, c, w: (m, 0)),
            line,
            line,
            pl.BlockSpec((crops, 1), lambda m, c, w: (m, 0)),
        ],
        [small, pair, tile, small, small] + ([part, part] if split else []),
        [lines, shape((micro, 2, channels)), shape(h3.shape, BF16), lines, lines]
        + ([half, half] if split else []),
        [pltpu.VMEM((3, width // LANES, rows // ROWS, LANES), F32)],
        flops=20 * h3.size,
        bytes_accessed=4 * h3.size,
        prefetch=1,
    )(scalars, *parts, *members, base, h3, x, valid, gain, shift, sizes)


def head_body(feat_ref, w_ref, g_ref, stats_ref):
    g = jnp.dot(feat_ref[...].astype(BF16), w_ref[...], preferred_element_type=F32)
    g_ref[...] = g
    micro = stats_ref.shape[0]
    crops = g.shape[0] // micro
    for m in range(micro):
        part = g[m * crops : (m + 1) * crops]
        mean = jnp.sum(part, axis=0, keepdims=True) / crops
        stats_ref[m, 0:1, :] = mean
        stats_ref[m, 1:2, :] = jnp.sum((part - mean) ** 2, axis=0, keepdims=True)


def head_product(feat, weight, micro):
    lines = feat.shape[0]
    depth, width = weight.shape
    tile = 512
    return run(
        head_body,
        (width // tile,),
        [
            pl.BlockSpec((lines, depth), lambda c: (0, 0)),
            pl.BlockSpec((depth, tile), lambda c: (0, c)),
        ],
        [
            pl.BlockSpec((lines, tile), lambda c: (0, c)),
            pl.BlockSpec((micro, 2, tile), lambda c: (0, 0, c)),
        ],
        [shape((lines, width)), shape((micro, 2, width))],
        flops=2 * lines * weight.size,
        bytes_accessed=2 * weight.size,
    )(feat, weight)


def head_back_body(total_crops, counts, refs):
    which_ref, part_refs = refs[0], refs[1 : 1 + counts]
    dy_ref, g_ref, info_ref, gain_ref, w_ref, size_ref, first_ref, second_ref, send_ref, keep_ref, wide_ref, stats_ref, low_ref, spread_ref = refs[1 + counts :]
    micro = stats_ref.shape[0]
    lines, width = dy_ref.shape
    crops = lines // micro

    @pl.when(pl.program_id(0) == 0)
    def _():
        for m in range(micro):
            at = pl.ds(m * crops, crops)
            one = tree([ref[m : m + 1, :width] for ref in part_refs]) / total_crops
            two = tree([ref[micro + m : micro + m + 1, :width] for ref in part_refs]) / total_crops
            scaled = info_ref[m, 1:2, :]
            normal = (g_ref[at, :] - info_ref[m, 0:1, :]) * scaled
            dg = gain_ref[...] * scaled * (dy_ref[at, :] - (one + normal * two))
            low = dg.astype(BF16)
            low_ref[at, :] = low
            left, right = [low[:, i : i + width // 2].astype(F32) for i in (0, width // 2)]
            send_ref[at, :] = jnp.where(which_ref[0] == 0, right, left)
            keep_ref[at, :] = jnp.where(which_ref[0] == 0, left, right)

    per_crop = nt_dot(low_ref[...], w_ref[...]) / size_ref[...]
    for j in range(wide_ref.shape[1] // LANES):
        lane = slice(j * LANES, (j + 1) * LANES)
        for i in range(CELL):
            spread_ref[j, pl.ds(i, lines, CELL), :] = per_crop[:, lane]
        wide_ref[:, lane] = spread_ref[j]
    one = per_crop * first_ref[...]
    two = per_crop * second_ref[...]
    for m in range(micro):
        at = slice(m * crops, (m + 1) * crops)
        stats_ref[m, 0:1, :] = jnp.sum(one[at], axis=0, keepdims=True)
        stats_ref[m, 1:2, :] = jnp.sum(two[at], axis=0, keepdims=True)


def head_back(which, parts, dy, g, info, gain, weight, sizes, first, second, total_crops):
    lines, width = dy.shape
    channels = weight.shape[0]
    micro = info.shape[0]
    tile = 512
    part = pl.BlockSpec((lines, tile), lambda c, w: (0, c))
    half = shape((lines, width // 2))
    return run(
        named("head_back", head_back_body, total_crops, len(parts)),
        (channels // tile,),
        [whole(a) for a in parts]
        + [
            whole(dy),
            whole(g),
            whole(info),
            whole(gain),
            pl.BlockSpec((tile, width), lambda c, w: (c, 0)),
            whole(sizes),
            part,
            part,
        ],
        [
            whole(half),
            whole(half),
            pl.BlockSpec((lines * CELL, tile), lambda c, w: (0, c)),
            pl.BlockSpec((micro, 2, tile), lambda c, w: (0, 0, c)),
        ],
        [half, half, shape((lines * CELL, channels)), shape((micro, 2, channels))],
        [
            pltpu.VMEM((lines, width), BF16),
            pltpu.VMEM((tile // LANES, lines * CELL, LANES), F32),
        ],
        flops=2 * lines * weight.size,
        bytes_accessed=2 * weight.size,
        prefetch=1,
    )(which, *parts, dy, g, info, gain, weight, sizes, first, second)


def third_back_body(counts, refs):
    which_ref, part_refs = refs[0], refs[1 : 1 + counts]
    wide_ref, slope_ref, h3_ref, v_ref, info3_ref, gain3_ref, info1_ref, w_ref, act_ref, h2_ref, info2_ref, gain2_ref, shift2_ref, dy_ref, stats_ref, send_ref, keep_ref, d_ref, sum_ref = refs[1 + counts :]
    rows, channels = slope_ref.shape
    step = pl.program_id(0)
    number = info1_ref[0, 2:3, 0:1]
    first, second = sums_of(part_refs, 0, 1)
    mean = info3_ref[0, 0:1, :]
    scaled = info3_ref[0, 1:2, :]
    factor = gain3_ref[...] * scaled
    one = factor * first / number
    two = factor * scaled * second / number
    act = act_ref[...].T

    @pl.when(step == 0)
    def _():
        sum_ref[...] = jnp.zeros(sum_ref.shape, F32)

    tile = sum_ref.shape[2]
    for j in range(0, channels, tile):
        lane = slice(j, j + tile)
        for k in range(rows // PIX):
            wide = wide_ref[pl.ds(k * COLS, COLS), lane] * factor[:, lane]
            for r in range(ROWS):
                at = pl.ds(k * PIX + r * COLS, COLS)
                back = one[:, lane] + (h3_ref[at, lane].astype(F32) - mean[:, lane]) * two[:, lane]
                d = wide * slope_ref[at, lane].astype(F32) - v_ref[at, :] * back
                d_ref[at, lane] = d.astype(BF16)
        part = nt_dot(d_ref[:, lane], w_ref[:, lane])
        if j == 0:
            dy_ref[...] = part
        else:
            dy_ref[...] += part
        sum_ref[j // tile] += jnp.dot(act, d_ref[:, lane], preferred_element_type=F32)
    put_back(dy_ref, h2_ref, v_ref, info2_ref, gain2_ref, shift2_ref, stats_ref)

    @pl.when(step == pl.num_programs(0) - 1)
    def _():
        low = which_ref[0] == 0
        steps = sum_ref.shape[0] // 2
        lines = send_ref.shape[1] // steps
        for q in range(steps):
            place = slice(q * lines, (q + 1) * lines)
            left = sum_ref[q].reshape(-1, lines, tile)
            right = sum_ref[steps + q].reshape(-1, lines, tile)
            send_ref[:, place, :] = jnp.where(low, left, right)
            keep_ref[:, place, :] = jnp.where(low, right, left)


def put_back(dy_ref, h_ref, v_ref, info_ref, gain_ref, shift_ref, stats_ref):
    rows, width = dy_ref.shape
    first = jnp.zeros((8, width), F32)
    second = jnp.zeros((8, width), F32)
    for i in range(0, rows, 32):
        at = slice(i, i + 32)
        normal = (h_ref[at, :] - info_ref[0, 0:1, :]) * info_ref[0, 1:2, :]
        pre = normal * gain_ref[...] + shift_ref[...]
        dy = dy_ref[at, :] * v_ref[at, :] * slope_of(pre)
        dy_ref[at, :] = dy
        first += fold(dy)
        second += fold(dy * normal)
    stats_ref[0, 0:1, :] = jnp.sum(first, axis=0, keepdims=True)
    stats_ref[0, 1:2, :] = jnp.sum(second, axis=0, keepdims=True)


def third_back(which, parts, wide, slope, h3, valid, info3, gain3, info1, weight, act, h2, info2, gain2, shift2, micro, shards):
    rows, channels = slope.shape[0] // micro, slope.shape[1]
    middle = weight.shape[0]
    lines = wide.shape[0] // micro
    tile = 512
    big = pl.BlockSpec((rows, channels), lambda m, w: (m, 0))
    mid = pl.BlockSpec((rows, middle), lambda m, w: (m, 0))
    half = shape((shards, middle // shards * (channels // tile // 2), tile))
    return run(
        named("third_back", third_back_body, len(parts)),
        (micro,),
        [per_micro(part) for part in parts]
        + [
            pl.BlockSpec((lines, channels), lambda m, w: (m, 0)),
            big,
            big,
            pl.BlockSpec((rows, 1), lambda m, w: (m, 0)),
            per_micro(info3),
            whole(gain3),
            per_micro(info1),
            whole(weight),
            mid,
            mid,
            per_micro(info2),
            whole(gain2),
            whole(shift2),
        ],
        [
            mid,
            pl.BlockSpec((1, 2, middle), lambda m, w: (m, 0, 0)),
            whole(half),
            whole(half),
        ],
        [shape(h2.shape), shape((micro, 2, middle)), half, half],
        [
            pltpu.VMEM((rows, channels), BF16),
            pltpu.VMEM((channels // tile, middle, tile), F32),
        ],
        flops=4 * slope.shape[0] * weight.size,
        bytes_accessed=6 * slope.size,
        prefetch=1,
    )(which, *parts, wide, slope, h3, valid, info3, gain3, info1, weight, act, h2, info2, gain2, shift2)


def put_norm_back(part_refs, dy_ref, h_ref, v_ref, info_ref, number_ref, gain_ref, d_ref):
    micro = info_ref.shape[0]
    rows = dy_ref.shape[0] // micro
    for m in range(micro):
        number = number_ref[m, 2:3, 0:1]
        first, second = sums_of(part_refs, 0, 1, m)
        scaled = info_ref[m, 1:2, :]
        factor = gain_ref[...] * scaled
        one = factor * first / number
        two = factor * scaled * second / number
        mean = info_ref[m, 0:1, :]
        for i in range(m * rows, (m + 1) * rows, 32):
            at = slice(i, i + 32)
            back = one + (h_ref[at, :] - mean) * two
            d_ref[at, :] = (factor * dy_ref[at, :] - v_ref[at, :] * back).astype(BF16)


def put_sides(a_ref, sides_ref):
    rows, width = a_ref.shape
    blank = jnp.zeros((COLS, width), BF16)
    place = cell_column(COLS)
    has_left = (place >= 1).astype(F32)
    has_right = (place <= CELL - 2).astype(F32)
    for k in range(rows // PIX):
        for c in range(3):
            sides_ref[c, k, 0:COLS, :] = blank
            sides_ref[c, k, COLS + PIX :, :] = blank
        for r in range(ROWS):
            act = a_ref[k * PIX + r * COLS : k * PIX + (r + 1) * COLS, :]
            wide = act.astype(F32)
            at = slice((r + 1) * COLS, (r + 2) * COLS)
            sides_ref[0, k, at, :] = (pltpu.roll(wide, 1, 0) * has_left).astype(BF16)
            sides_ref[1, k, at, :] = act
            sides_ref[2, k, at, :] = (pltpu.roll(wide, COLS - 1, 0) * has_right).astype(BF16)


def put_tap(out_ref, sides_ref, half_ref):
    tap = pl.program_id(0)
    _, canvases, _, width = sides_ref.shape
    start = pl.multiple_of(tap // 3 * COLS, COLS)
    left = sides_ref[tap % 3, :, pl.ds(start, PIX), :].reshape(canvases * PIX, width)
    out_ref[...] = tn_dot(left, half_ref[...])


def half_of(which_ref, d_ref):
    half = d_ref.shape[1] // 2
    return d_ref[:, pl.ds(pl.multiple_of(which_ref[0] * half, half), half)]


def mid_first_body(counts, refs):
    which_ref, part_refs = refs[0], refs[1 : 1 + counts]
    dy_ref, h_ref, v_ref, info_ref, number_ref, gain_ref, a_ref, d_ref, out_ref, sides_ref, half_ref = refs[1 + counts :]

    @pl.when(pl.program_id(0) == 0)
    def _():
        put_norm_back(part_refs, dy_ref, h_ref, v_ref, info_ref, number_ref, gain_ref, d_ref)
        half_ref[...] = half_of(which_ref, d_ref)
        put_sides(a_ref, sides_ref)

    put_tap(out_ref, sides_ref, half_ref)


def mid_second_body(refs):
    which_ref, d_ref, a_ref, out_ref, sides_ref, half_ref = refs

    @pl.when(pl.program_id(0) == 0)
    def _():
        half_ref[...] = half_of(which_ref, d_ref)
        put_sides(a_ref, sides_ref)

    put_tap(out_ref, sides_ref, half_ref)


def mid_grad(name, body, which, ins, act, with_d):
    rows, width = act.shape
    half = width // 2
    grad = pl.BlockSpec((width, half), lambda t, w: (t, 0))
    return run(
        named(name, body, *([len(ins) - 7] if with_d else [])),
        (TAPS,),
        [whole(a) for a in ins],
        [whole(act), grad] if with_d else grad,
        [shape(act.shape, BF16), shape((TAPS * width, half))]
        if with_d
        else shape((TAPS * width, half)),
        [
            pltpu.VMEM((3, rows // PIX, PIX + 2 * COLS, width), BF16),
            pltpu.VMEM((rows, half), BF16),
        ],
        flops=2 * rows * TAPS * width * half,
        bytes_accessed=4 * TAPS * width * half,
        prefetch=1,
    )(which, *ins)


def in_grad_body(counts, refs):
    which_ref, part_refs = refs[0], refs[1 : 1 + counts]
    dy_ref, h_ref, v_ref, info_ref, number_ref, gain_ref, x_ref, d_ref, send_ref, keep_ref = refs[1 + counts :]

    @pl.when(pl.program_id(0) == 0)
    def _():
        put_norm_back(part_refs, dy_ref, h_ref, v_ref, info_ref, number_ref, gain_ref, d_ref)

    grad = tn_dot(x_ref[...], d_ref[...])
    half = grad.shape[1] // 2
    low = which_ref[0] == 0
    left, right = grad[:, :half], grad[:, half:]
    send_ref[...] = jnp.where(low, left, right)
    keep_ref[...] = jnp.where(low, right, left)


def in_grad(which, parts, dy, h, valid, info, number, gain, x):
    rows, width = dy.shape
    depth = x.shape[1]
    half = width // 2
    tile = 512
    ins = [*parts, dy, h, valid, info, number, gain]
    grad = pl.BlockSpec((tile, half), lambda c, w: (c, 0))
    return run(
        named("in_grad", in_grad_body, len(parts)),
        (depth // tile,),
        [whole(a) for a in ins] + [pl.BlockSpec((rows, tile), lambda c, w: (0, c))],
        [whole(dy), grad, grad],
        [shape(dy.shape, BF16), shape((depth, half)), shape((depth, half))],
        flops=2 * rows * depth * width,
        bytes_accessed=2 * x.size + 4 * depth * width + 10 * dy.size,
        prefetch=1,
    )(which, *ins, x)


def second_back_body(d_ref, w_ref, v_ref, h1_ref, info_ref, gain_ref, shift_ref, dy_ref, stats_ref, moved_ref, packed_ref):
    rows, width = d_ref.shape

    @pl.when(pl.program_id(0) == 0)
    def _():
        for r in range(3):
            for c in range(3):
                tap = 3 * r + c
                packed_ref[c, :, r * width : (r + 1) * width] = w_ref[
                    tap * width : (tap + 1) * width, :
                ]

    blank = jnp.zeros((COLS, width), BF16)
    for k in range(0, rows, PIX):
        moved_ref[k : k + PIX - COLS, 0:width] = d_ref[k + COLS : k + PIX, :]
        moved_ref[k + PIX - COLS : k + PIX, 0:width] = blank
        moved_ref[k : k + COLS, 2 * width :] = blank
        moved_ref[k + COLS : k + PIX, 2 * width :] = d_ref[k : k + PIX - COLS, :]
    moved_ref[:, width : 2 * width] = d_ref[...]
    parts = [nt_dot(moved_ref[...], packed_ref[c]) for c in range(3)]
    place = cell_column(rows)
    dy_ref[...] = (
        parts[1]
        + pltpu.roll(parts[2], 1, 0) * (place >= 1).astype(F32)
        + pltpu.roll(parts[0], rows - 1, 0) * (place <= CELL - 2).astype(F32)
    )
    put_back(dy_ref, h1_ref, v_ref, info_ref, gain_ref, shift_ref, stats_ref)


def second_back(d, weight, valid, h1, info, gain, shift, micro):
    rows, width = d.shape[0] // micro, d.shape[1]
    mid = pl.BlockSpec((rows, width), lambda m: (m, 0))
    return run(
        second_back_body,
        (micro,),
        [
            mid,
            whole(weight),
            pl.BlockSpec((rows, 1), lambda m: (m, 0)),
            mid,
            per_micro(info),
            whole(gain),
            whole(shift),
        ],
        [mid, pl.BlockSpec((1, 2, width), lambda m: (m, 0, 0))],
        [shape(d.shape), shape((micro, 2, width))],
        [pltpu.VMEM((rows, 3 * width), BF16), pltpu.VMEM((3, width, 3 * width), BF16)],
        flops=2 * micro * rows * weight.size,
        bytes_accessed=10 * d.size,
    )(d, weight, valid, h1, info, gain, shift)


def pixels_body(d_ref, w_ref, wide_ref, slope_ref, out_ref):
    rows, channels = out_ref.shape
    width = 512
    for j in range(0, channels, width):
        lane = pl.ds(j, width)
        grad = nt_dot(d_ref[...], w_ref[lane, :])
        for k in range(rows // PIX):
            wide = wide_ref[pl.ds(k * COLS, COLS), lane]
            for r in range(ROWS):
                first = k * PIX + r * COLS
                at = pl.ds(first, COLS)
                out_ref[at, lane] = (
                    grad[first : first + COLS] + wide * slope_ref[at, lane].astype(F32)
                ).astype(BF16)


def pixels_grad(d, weight, wide, slope, micro):
    rows, channels = slope.shape[0] // micro, slope.shape[1]
    lines = wide.shape[0] // micro
    big = pl.BlockSpec((rows, channels), lambda m: (m, 0))
    return run(
        pixels_body,
        (micro,),
        [
            pl.BlockSpec((rows, d.shape[1]), lambda m: (m, 0)),
            pl.BlockSpec(weight.shape, lambda m: (0, 0)),
            pl.BlockSpec((lines, channels), lambda m: (m, 0)),
            big,
        ],
        big,
        shape(slope.shape, BF16),
        flops=2 * slope.shape[0] * weight.size,
        bytes_accessed=4 * slope.size,
    )(d, weight, wide, slope)


def factor_body(feat_ref, other_feat_ref, dg_ref, far_ref, near_ref, both_ref, out_ref):
    left = jnp.concatenate([feat_ref[...], other_feat_ref[...]], 0).astype(BF16)
    lines = dg_ref.shape[0] // 2
    right = jnp.concatenate(
        [
            ref[c * lines : (c + 1) * lines, :]
            for c in range(2)
            for ref in (dg_ref, near_ref, far_ref, both_ref)
        ],
        0,
    ).astype(BF16)
    out_ref[...] = tn_dot(left, right)


def factor_grad(feat, other_feat, dg, far, near, both):
    lines, depth = feat.shape
    width = dg.shape[1]
    tile = 512
    left = pl.BlockSpec((lines, tile), lambda c: (0, c))
    return run(
        factor_body,
        (depth // tile,),
        [left, left] + [whole(dg)] * 4,
        pl.BlockSpec((tile, width), lambda c: (c, 0)),
        shape((depth, width)),
        flops=4 * lines * depth * width,
        bytes_accessed=4 * depth * width,
    )(feat, other_feat, dg, far, near, both)


def embed_body(protos, counts, members, refs):
    part_refs = refs[:counts]
    g_ref, gain_ref, shift_ref, w_ref, bias_ref, table_ref, queue_ref, act_ref, z_ref, inverse_ref, unit_ref, logits_ref, batch_ref, line_ref, sums_ref, info_ref = refs[counts:]
    micro = info_ref.shape[0]
    crops = g_ref.shape[0] // micro
    for m in range(micro):
        at = slice(m * crops, (m + 1) * crops)
        mean, scaled = norm_of(part_refs, members, m)
        info_ref[m, 0:1, :] = mean
        info_ref[m, 1:2, :] = scaled
        pre = (g_ref[at, :] - mean) * scaled * gain_ref[...] + shift_ref[...]
        act_ref[at, :] = (pre * sigmoid(pre)).astype(BF16)
    z = jnp.dot(act_ref[...], w_ref[...], preferred_element_type=F32) + bias_ref[...]
    inverse = lax.rsqrt(jnp.sum(z * z, 1, keepdims=True) + eps_unit)
    unit = (z * inverse).astype(BF16)
    z_ref[...] = z
    inverse_ref[...] = inverse
    unit_ref[...] = unit
    logits = jnp.dot(unit, table_ref[...], preferred_element_type=F32)
    logits_ref[...] = logits
    real = lax.broadcasted_iota(jnp.int32, (1, logits.shape[1]), 1) < protos
    batch = jnp.where(real, jnp.exp(logits / transport_epsilon), 0.0)
    batch_ref[...] = batch
    queued = jnp.dot(queue_ref[...], table_ref[...], preferred_element_type=F32)
    line = jnp.where(real, jnp.exp(queued / transport_epsilon), 0.0)
    line_ref[...] = line
    queue_sum = jnp.sum(line, axis=0, keepdims=True)
    for m in range(micro):
        at = slice(m * crops, (m + 1) * crops)
        sums_ref[m : m + 1, :] = jnp.sum(batch[at], axis=0, keepdims=True) + queue_sum


def embed_product(parts, members, protos, g, gain, shift, weight, bias, table, queue):
    lines = g.shape[0]
    micro = parts[0].shape[0]
    feat = weight.shape[1]
    wide = table.shape[1]
    outs = [
        shape(g.shape, BF16),
        shape((lines, feat)),
        shape((lines, 1)),
        shape((lines, feat), BF16),
        shape((lines, wide)),
        shape((lines, wide)),
        shape((queue.shape[0], wide)),
        shape((micro, wide)),
        shape((micro, 2, g.shape[1])),
    ]
    ins = [*parts, g, gain, shift, weight, bias, table, queue]
    return run(
        named("embed", embed_body, protos, len(parts), members),
        (1,),
        [whole(a) for a in ins],
        [whole(a) for a in outs],
        outs,
        flops=2 * lines * table.size,
        bytes_accessed=8 * lines * wide,
    )(*ins)


def sweep_body(protos, counts, refs):
    part_refs = refs[:counts]
    batch_ref, queue_ref, new_batch_ref, new_queue_ref, sums_ref = refs[counts:]
    micro, wide = sums_ref.shape
    crops = batch_ref.shape[0] // micro
    lines = new_queue_ref.shape[0] // micro
    shared = queue_ref.shape[0] == lines
    real = lax.broadcasted_iota(jnp.int32, (1, wide), 1) < protos
    for m in range(micro):
        column = jnp.where(real, tree([ref[m : m + 1, :] for ref in part_refs]), 1.0)
        at = slice(m * crops, (m + 1) * crops)
        batch = batch_ref[at, :] / column
        batch = batch / jnp.sum(batch, 1, keepdims=True)
        new_batch_ref[at, :] = batch
        own = slice(m * lines, (m + 1) * lines)
        queue = queue_ref[slice(0, lines) if shared else own, :] / column
        queue = queue / jnp.sum(queue, 1, keepdims=True)
        new_queue_ref[own, :] = queue
        sums_ref[m : m + 1, :] = jnp.sum(batch, axis=0, keepdims=True) + jnp.sum(
            queue, axis=0, keepdims=True
        )


def sweep(parts, protos, batch, queue, lines):
    micro, wide = parts[0].shape
    outs = [shape(batch.shape), shape((micro * lines, wide)), shape(parts[0].shape)]
    ins = [*parts, batch, queue]
    return run(
        named("sweep", sweep_body, protos, len(parts)),
        (1,),
        [whole(a) for a in ins],
        [whole(a) for a in outs],
        outs,
        flops=20 * batch.size,
        bytes_accessed=16 * batch.size,
    )(*ins)


def split_dot(dot, left, right, wide_left):
    value = left if wide_left else right
    high = value.astype(BF16)
    low = (value - high.astype(F32)).astype(BF16)
    if wide_left:
        return dot(high, right) + dot(low, right)
    return dot(left, high) + dot(left, low)


def pack_small(low, send_ref, keep_ref, protos, embed):
    shards, lines, width = send_ref.shape
    lines = lines // 2
    rows = protos.shape[0] // shards // 2
    half = protos.shape[1] // 2
    groups = half // width
    lane = embed.shape[1]
    below = lines - groups * rows

    def put(d, place, columns, one, two):
        keep_ref[d, place, columns] = jnp.where(low, one, two)
        send_ref[d, place, columns] = jnp.where(low, two, one)

    for d in range(shards):
        for y in range(2):
            first = (2 * d + y) * rows
            for q in range(groups):
                start = y * lines + q * rows
                one, two = [
                    protos[first : first + rows, c * half + q * width : c * half + (q + 1) * width]
                    for c in range(2)
                ]
                put(d, slice(start, start + rows), slice(None), one, two)
            for q in range(width // lane):
                one, two = [
                    embed[first : first + below]
                    for first in [
                        (((2 * d + c) * 2 + y) * (width // lane) + q) * below for c in range(2)
                    ]
                ]
                start = y * lines + groups * rows
                put(d, slice(start, start + below), slice(q * lane, (q + 1) * lane), one, two)


def unpack_small(halves, protos, embed):
    shards, lines, width = halves[0].shape
    lines = lines // 2
    packed = jnp.stack(halves).reshape(2, shards, 2, lines, width)
    rows = protos[0] // shards // 2
    groups = protos[1] // 2 // width
    lane = embed[1]
    above = packed[:, :, :, : groups * rows].reshape(2, shards, 2, groups, rows, width)
    below = packed[:, :, :, groups * rows :]
    below = below.reshape(2, shards, 2, lines - groups * rows, width // lane, lane)
    return (
        above.transpose(1, 2, 4, 0, 3, 5).reshape(protos),
        below.transpose(1, 0, 2, 4, 3, 5).reshape(embed),
    )


def packed_shape(protos, embed, shards):
    width = 512
    lines = protos[0] // shards // 2 * (protos[1] // 2 // width)
    return (shards, 2 * (lines + embed[0] * embed[1] // shards // 4 // width), width)


def loss_body(protos, scale, counts, refs):
    which_ref, part_refs = refs[0], refs[1 : 1 + counts]
    batch_ref, logits_ref, unit_ref, z_ref, inverse_ref, act_ref, g_ref, info_ref, gain_ref, shift_ref, w_ref, table_ref, send_ref, keep_ref, dy_ref, sums_ref = refs[1 + counts :]
    micro, wide = part_refs[0].shape
    lines = batch_ref.shape[0]
    crops = lines // micro
    real = lax.broadcasted_iota(jnp.int32, (1, wide), 1) < protos
    odd = lax.broadcasted_iota(jnp.int32, (crops, 1), 0) % 2 == 1
    parts = []
    loss = jnp.zeros((1, 1), F32)
    for m in range(micro):
        at = slice(m * crops, (m + 1) * crops)
        codes = batch_ref[at, :] / jnp.where(
            real, tree([ref[m : m + 1, :] for ref in part_refs]), 1.0
        )
        codes = codes / jnp.sum(codes, 1, keepdims=True)
        partner = jnp.where(odd, pltpu.roll(codes, 1, 0), pltpu.roll(codes, crops - 1, 0))
        sharp = logits_ref[at, :] / softmax_sharpness
        top = jnp.max(jnp.where(real, sharp, -jnp.inf), 1, keepdims=True)
        shifted = sharp - top
        mass = jnp.where(real, jnp.exp(shifted), 0.0)
        total = jnp.sum(mass, 1, keepdims=True)
        chance = shifted - jnp.log(total)
        loss += jnp.sum(jnp.sum(partner * chance, 1, keepdims=True), 0, keepdims=True)
        weight = jnp.sum(partner, 1, keepdims=True)
        parts.append((scale / softmax_sharpness) * (weight * (mass / total) - partner))
    d_scores = jnp.concatenate(parts, 0)
    unit = unit_ref[...]
    grad_protos = split_dot(tn_dot, unit, d_scores, False)
    d_unit = split_dot(nt_dot, d_scores, table_ref[...], True)
    z = z_ref[...]
    inverse = inverse_ref[...]
    dz = inverse * d_unit - z * (inverse * inverse * inverse) * jnp.sum(
        z * d_unit, 1, keepdims=True
    )
    grad_embed = split_dot(tn_dot, act_ref[...], dz, False)
    pack_small(which_ref[0] == 0, send_ref, keep_ref, grad_protos, grad_embed)
    d_act = split_dot(nt_dot, dz, w_ref[...], True)
    for m in range(micro):
        at = slice(m * crops, (m + 1) * crops)
        normal = (g_ref[at, :] - info_ref[m, 0:1, :]) * info_ref[m, 1:2, :]
        pre = normal * gain_ref[...] + shift_ref[...]
        dy = d_act[at] * slope_of(pre)
        dy_ref[at, :] = dy
        sums_ref[m : m + 1, : dy.shape[1]] = jnp.sum(dy, axis=0, keepdims=True)
        sums_ref[micro + m : micro + m + 1, : dy.shape[1]] = jnp.sum(
            dy * normal, axis=0, keepdims=True
        )
    feat = z.shape[1]
    wide = dy_ref.shape[1]
    extra = jnp.concatenate(
        [jnp.sum(dz, axis=0, keepdims=True), jnp.broadcast_to(-scale * loss, (1, feat))], 1
    )
    sums_ref[:, wide:] = jnp.broadcast_to(extra, (2 * micro, 2 * feat))


def loss_grads(which, parts, protos, scale, batch, logits, unit, z, inverse, act, g, info, gain, shift, weight, table, shards):
    ins = [*parts, batch, logits, unit, z, inverse, act, g, info, gain, shift, weight, table]
    micro = info.shape[0]
    outs = [
        shape(packed_shape(table.shape, weight.shape, shards)),
        shape(packed_shape(table.shape, weight.shape, shards)),
        shape(g.shape),
        shape((2 * micro, g.shape[1] + 2 * weight.shape[1])),
    ]
    return run(
        named("loss", loss_body, protos, scale, len(parts)),
        (1,),
        [whole(a) for a in ins],
        [whole(a) for a in outs],
        outs,
        flops=8 * table.size * batch.shape[0],
        bytes_accessed=16 * batch.size,
        prefetch=1,
    )(which, *ins)


def pick_block(rows, width, cell, *fixed):
    return pl.BlockSpec((1, rows, width), lambda g, w: cell(g, *fixed, w[0], w[1], w[2]) + (0,))


def sent_first(g, i, core, x, y):
    z, b = 2 * g + i // 2, i % 2
    return (2 * z + (1 - core) * (1 - x) + core * b, (1 - core) * b + core * (1 - y))


def kept_second(g, i, core, x, y):
    return (2 * (2 * g + i) + x, y)


def sent_second(g, i, core, x, y):
    z = 2 * g + i
    return (2 * z + (1 - core) * x + core * (1 - x), (1 - core) * (1 - y) + core * y)


def add_groups(refs, sizes, out_ref, index, extra=None):
    start = 0
    place = 0
    for count, rows in sizes:
        value = refs[place][0]
        for ref in refs[place + 1 : place + count]:
            value = value + ref[0]
        if extra is not None:
            value = value + extra[0, start : start + rows, :]
        out_ref[index, start : start + rows, :] = value
        place += count
        start += rows


def group_sizes(groups):
    return [(len(addends), addends[0].shape[1] // 2) for addends in groups]


def first_send(scalars, groups):
    sizes = group_sizes(groups)
    shards, _, width = groups[0][0].shape
    lines = sum(rows for _, rows in sizes)
    flat = [array for addends in groups for array in addends]
    specs = []
    for i in range(4):
        for array in flat:
            specs.append(pick_block(array.shape[1] // 2, width, sent_first, i))

    def body(refs):
        refs = refs[1:]
        for i in range(4):
            add_groups(refs[i * len(flat) : (i + 1) * len(flat)], sizes, refs[-1], i)

    return run(
        named("first_send", body),
        (shards // 4,),
        specs,
        pl.BlockSpec((4, lines, width), lambda g, w: (g, 0, 0)),
        shape((shards, lines, width)),
        bytes_accessed=4 * lines * width * shards * 3,
        prefetch=1,
    )(scalars, *(flat * 4))


def second_send(scalars, groups, came):
    sizes = group_sizes(groups)
    shards, _, width = groups[0][0].shape
    lines = sum(rows for _, rows in sizes)
    flat = [array for addends in groups for array in addends]
    specs = []
    for cell in (sent_second, kept_second):
        for i in range(2):
            for array in flat:
                specs.append(pick_block(array.shape[1] // 2, width, cell, i))

    def bit(w):
        return (1 - w[0]) * w[2] + w[0] * w[1]

    for flip in (1, 0):
        for i in range(2):
            specs.append(
                pl.BlockSpec(
                    (1, lines, width),
                    lambda g, w, i=i, flip=flip: (2 * (2 * g + i) + (1 - bit(w) if flip else bit(w)), 0, 0),
                )
            )
    out = pl.BlockSpec((2, lines, width), lambda g, w: (g, 0, 0))

    def body(refs):
        refs = refs[1:]
        count = len(flat)
        came_refs = refs[4 * count : 4 * count + 4]
        for side in range(2):
            for i in range(2):
                place = 2 * side + i
                add_groups(
                    refs[place * count : (place + 1) * count],
                    sizes,
                    refs[-2 + side],
                    i,
                    came_refs[place],
                )

    return run(
        named("second_send", body),
        (shards // 4,),
        specs,
        [out, out],
        [shape((shards // 2, lines, width))] * 2,
        bytes_accessed=4 * lines * width * shards * 4,
        prefetch=1,
    )(scalars, *(flat * 4), *([came] * 4))


def four_places(scalars_ref, refs):
    core, side = scalars_ref[0], scalars_ref[2]
    return [
        (core, side, refs[0]),
        (core, 1 - side, refs[1]),
        (1 - core, side, refs[2]),
        (1 - core, 1 - side, refs[3]),
    ]


def place_early_body(scalars_ref, *refs):
    out_ref, embed_ref, protos_ref, head_ref = refs[8:]
    lines = out_ref.shape[0]
    rows = protos_ref.shape[0] // 2
    wide = 512
    groups = protos_ref.shape[1] // 2 // wide
    lane = embed_ref.shape[1]
    below = embed_ref.shape[0] // 4 // (wide // lane)
    start = lines + groups * rows
    for c, y, ref in four_places(scalars_ref, refs[:4]):
        out_ref[:, pl.ds(pl.multiple_of((2 * c + y) * wide, wide), wide)] = ref[0:lines, :]
        at = pl.ds(pl.multiple_of(y * rows, rows), rows)
        for q in range(groups):
            column = pl.multiple_of((c * groups + q) * wide, wide)
            protos_ref[at, pl.ds(column, wide)] = ref[lines + q * rows : lines + (q + 1) * rows, :]
        for q in range(wide // lane):
            first = pl.multiple_of(((2 * c + y) * (wide // lane) + q) * below, below)
            embed_ref[pl.ds(first, below), :] = ref[start:, q * lane : (q + 1) * lane]
    for c, y, ref in four_places(scalars_ref, refs[4:8]):
        head_ref[:, pl.ds(pl.multiple_of((2 * c + y) * wide, wide), wide)] = ref[...]


def place_late_body(scalars_ref, *refs):
    outs = refs[8:]
    for out_ref, pieces in zip(outs, (refs[:4], refs[4:8])):
        rows, width = out_ref.shape[0] // 2, out_ref.shape[1] // 2
        for c, y, ref in four_places(scalars_ref, pieces):
            out_ref[
                pl.ds(pl.multiple_of(y * rows, rows), rows),
                pl.ds(pl.multiple_of(c * width, width), width),
            ] = ref[...]


def placed_pieces(body, scalars, pieces, outs):
    return run(
        body,
        (1,),
        [whole(a) for a in pieces],
        [whole(a) for a in outs],
        outs,
        prefetch=1,
    )(scalars, *pieces)


def on_device(
    pixels,
    crop_map,
    queue_rows,
    conv_in,
    gain_one,
    shift_one,
    conv_mid,
    gain_two,
    shift_two,
    conv_out,
    gain_three,
    shift_three,
    head_weight,
    head_gain,
    head_shift,
    embed_weight,
    embed_bias,
    prototypes,
):
    micro, canvas, pixel_count, channels = pixels.shape
    devices = lax.axis_size("dp") * lax.axis_size("hst")
    crops = canvas * SLOTS
    total_crops = crops * devices * 1.0
    loss_scale = 1.0 / (micro * total_crops)
    x = pixels.reshape(micro * canvas * pixel_count, channels)
    valid = (crop_map < SLOTS).astype(F32).reshape(-1, 1)
    sizes = jnp.sum(
        (crop_map[:, :, None, :] == jnp.arange(SLOTS, dtype=jnp.int32)[:, None]).astype(F32), 3
    ).reshape(-1, 1)

    shards = lax.axis_size("dp")
    quick = shards == 8 and lax.axis_size("hst") == 4
    packs = 8
    protos = prototypes.shape[1]
    table = jnp.pad(prototypes, ((0, 0), (0, -protos % 1024)))

    def row(vector):
        return vector.reshape(1, -1)

    masks = dp_masks()
    near, far = masks[0], masks[1:]
    core = bit_of(1)
    side = bit_of(2)
    scalars = jnp.stack([core, bit_of(near), side]).astype(jnp.int32)
    keep_half = core.astype(jnp.int32).reshape(1)
    send_half = 1 - keep_half

    h1, stats = first_product(x, conv_in, valid, micro)
    members, counts = first_parts(stats)
    act_one, h2, stats, info_one = second_product(
        members, h1, valid, row(gain_one), row(shift_one), conv_mid, micro
    )
    parts = moment_parts(stats, counts)
    act_two, h3, stats, info_two = third_product(
        parts, members, h2, valid, row(gain_two), row(shift_two), conv_out, micro
    )
    base = stats
    parts = moment_parts(stats, counts)
    feat, info_three, slope, slope_first, slope_second, *feat_halves = pool(
        scalars,
        parts,
        members,
        base,
        h3,
        x,
        valid,
        row(gain_three),
        row(shift_three),
        sizes,
        micro,
        channels // shards if quick else 0,
    )

    lines = feat.shape[0]
    if quick:
        feat_keep, feat_send = feat_halves
        feat_near, feat_far = swap(feat_send, near), swap(feat_keep, 2)
    g, stats = head_product(feat, head_weight, micro)
    if quick:
        stats, feat_near, feat_far = tie(stats, feat_near, feat_far)

    crop_counts = []
    crop_members = []
    number = crops * 1.0
    for group in sync_groups():
        crop_members = [number] * (len(group) + 1)
        crop_counts.append(crop_members)
        number = number * (len(group) + 1)
    parts = moment_parts(stats, crop_counts)

    act_four, embedded, inverse, unit_rows, logits, batch, queue, column, info_four = embed_product(
        parts,
        crop_members,
        protos,
        g,
        row(head_gain),
        row(head_shift),
        embed_weight,
        row(embed_bias),
        table,
        queue_rows,
    )
    for _ in range(SINK_ITERS - 1):
        parts = sum_parts(column)
        batch, queue, column = sweep(parts, protos, batch, queue, queue_rows.shape[0])
    parts = sum_parts(column)
    which = (1 - send_half) if quick else jnp.zeros((1,), jnp.int32)
    small_send, small_keep, dy_four, payload = loss_grads(
        which,
        parts,
        protos,
        loss_scale,
        batch,
        logits,
        unit_rows,
        embedded,
        inverse,
        act_four,
        g,
        info_four,
        row(head_gain),
        row(head_shift),
        embed_weight,
        table,
        packs,
    )
    parts = sum_parts(payload)
    payload = tree(list(parts))
    channel_sums = payload[:, : head_gain.shape[0]]
    first_four, second_four = channel_sums[:micro], channel_sums[micro:]
    extra = payload[0, head_gain.shape[0] :]
    grad_bias, total_loss = extra[: embed_bias.shape[0]], extra[embed_bias.shape[0]]

    if quick:
        feat_near, small_send, *parts = tie(feat_near, small_send, *parts)
        feat_both = swap(feat_near, 2)
        small_recv = swap(small_send, 1)
    dg_send, dg_keep, wide, sums = head_back(
        which,
        parts,
        dy_four,
        g,
        info_four,
        row(head_gain),
        head_weight,
        sizes,
        slope_first,
        slope_second,
        total_crops,
    )
    first_norm = (h1, valid, info_one, info_one, row(gain_one))
    second_norm = (h2, valid, info_two, info_one, row(gain_two))

    def from_third(which, parts):
        return third_back(
            which,
            parts,
            wide,
            slope,
            h3,
            valid,
            info_three,
            row(gain_three),
            info_one,
            conv_out,
            act_two,
            h2,
            info_two,
            row(gain_two),
            row(shift_two),
            micro,
            shards,
        )

    def from_second(d):
        return second_back(
            d, conv_mid, valid, h1, info_one, row(gain_one), row(shift_one), micro
        )

    if quick:
        sums, dg_send, feat_both, small_recv = tie(sums, dg_send, feat_both, small_recv)
        feat_both = jnp.concatenate([feat_keep, feat_near, feat_far, feat_both], 0)

        def core_filler(gate):
            source, other = tie(dg_send, feat_both, gate)[:2]
            grads["dg"] = swap(source, 1)
            grads["feat"] = swap(other, 1)
            return [grads["dg"], grads["feat"]]

        grads = {}
        parts_three = sum_parts(sums, ((), (core_filler,)))
        feat_other = grads["feat"]
        quarter = dg_keep.shape[1] // 2

        def quarter_of(place):
            return jnp.concatenate(
                [
                    lax.dynamic_slice_in_dim(array, place * quarter, quarter, 1)
                    for array in (dg_keep, grads["dg"])
                ],
                0,
            )

        dg_here, dg_there = quarter_of(side), quarter_of(1 - side)
        *parts_three, dg_here, dg_there = tie(*parts_three, dg_here, dg_there)
        dg_far, dg_near, dg_both = swap(dg_there, 2), swap(dg_here, near), swap(dg_there, 2 + near)
        dy, sums, out_send, out_keep = from_third(send_half, parts_three)
        sums, dy, out_send, dg_far, dg_near, dg_both = tie(
            sums, dy, out_send, dg_far, dg_near, dg_both
        )
        small = [small_keep, small_recv]

        def out_filler(gate):
            grads["out"] = swap(tie(out_send, gate)[0], 1)
            return [grads["out"]]

        def head_filler(gate):
            source = tie(dg_near, gate)[0]
            grads["head"] = factor_grad(feat_both, feat_other, dg_here, dg_far, source, dg_both)
            return [grads["head"]]

        def early_filler(gate):
            source = tie(grads["out"], gate)[0]
            grads["early"] = [[out_keep, source], small]
            grads["early_out"] = first_send(scalars, grads["early"])
            return [grads["early_out"]]

        parts_two = sum_parts(sums, ((), (out_filler,), (head_filler, early_filler)))

        early = grads["early"]
        *parts_two, early_out, partial = tie(*parts_two, grads["early_out"], grads["head"])
        early_came = core_swap(early_out, near, 2)
        partial = partial.reshape(2, 2, -1, partial.shape[1])
        most = partial.shape[2] * 3 // 4
        heads = [dp_halves([partial[:, :, :most]], far[0], 1)]
        d_two, mid_send = mid_grad(
            "mid_first",
            mid_first_body,
            send_half,
            [*parts_two, dy, *second_norm, act_one],
            act_one,
            True,
        )
        d_two, mid_send, early_came, heads[0][-1] = tie(
            d_two, mid_send, early_came, heads[0][-1]
        )
        heads.append(dp_halves([partial[:, :, most:]], far[0], 1))
        mid_recv = swap(mid_send, 1)
        early_out, early_keep = second_send(scalars, early, early_came)
        early_came = core_swap(early_out, 2, near)
        mid_keep = mid_grad(
            "mid_second", mid_second_body, keep_half, [d_two, act_one], act_one, False
        )
        mid_keep, mid_recv, early_came, heads[1][-1] = tie(
            mid_keep, mid_recv, early_came, heads[1][-1]
        )

        def sharded(array):
            return array.reshape(shards, -1, array.shape[-1])

        def by_bits(array):
            return array.reshape((2, 2) + array.shape[1:])

        late = [[sharded(mid_keep), sharded(mid_recv)]]
        mid_out = first_send(scalars, late)
        d_two, mid_out = tie(d_two, mid_out)
        mid_came = core_swap(mid_out, near, 2)
        halves = [dp_split(head, far[1], 0) for head in heads]
        head_came = swap(jnp.concatenate([send for _, send in halves], 0), far[1])
        dy, sums = from_second(d_two)
        dy, sums, mid_came, head_came, early_keep, early_came = tie(
            dy, sums, mid_came, head_came, early_keep, early_came
        )
        early = [by_bits(early_keep), by_bits(early_came)]

        def early_z_filler(gate):
            grads["z"] = dp_halves(early, far[0], 1)
            return [grads["z"][-1]]

        def mid_filler(gate):
            source = tie(mid_came, gate)[0]
            grads["mid"] = second_send(scalars, late, source)
            return grads["mid"]

        parts_one = sum_parts(sums, ((), (early_z_filler,), (mid_filler,)))
        mid_out, mid_keep = grads["mid"]
        *parts_one, mid_out, early_came = tie(*parts_one, mid_out, grads["z"][-1])
        early = dp_halves(grads["z"][:-1] + [early_came], far[1], 0)
        mid_came = core_swap(mid_out, 2, near)
        d_one, in_send, in_keep = in_grad(send_half, parts_one, dy, *first_norm, x)
        d_one, in_send, in_keep, mid_came, early[-1] = tie(
            d_one, in_send, in_keep, mid_came, early[-1]
        )
        in_recv = swap(in_send, 1)
        inner = [[sharded(in_keep), sharded(in_recv)]]
        in_out = first_send(scalars, inner)
        mid = dp_halves([by_bits(mid_keep), by_bits(mid_came)], far[0], 1)
        d_one, in_out = tie(d_one, in_out)
        in_came = core_swap(in_out, near, 2)
        grad_x = pixels_grad(d_one, conv_in, wide, slope, micro)
        grad_x, in_came, mid[-1], early[-1], head_came = tie(
            grad_x, in_came, mid[-1], early[-1], head_came
        )
        head_mine = jnp.concatenate([sum(keep) for keep, _ in halves], 0) + head_came
        mid_keep, mid_out = dp_split(mid, far[1], 0)
        in_came, mid_out = tie(in_came, mid_out)
        mid_came = swap(mid_out, far[1])
        in_out, in_keep = second_send(scalars, inner, in_came)
        in_came = core_swap(in_out, 2, near)
        head_far, head_core = swap(head_mine, 2), swap(head_mine, 1)
        early_mine = sum(early)
        in_came, mid_came, head_far, head_core, early_mine = tie(
            in_came, mid_came, head_far, head_core, early_mine
        )
        inner = dp_halves([by_bits(in_keep), by_bits(in_came)], far[0], 1)
        mid_mine = sum(mid_keep) + mid_came
        early_far, early_core = swap(early_mine, 2), swap(early_mine, 1)
        mid_core, head_both = swap(mid_mine, 1), swap(head_far, 1)
        inner[-1], early_far, early_core, mid_mine, mid_core, head_both = tie(
            inner[-1], early_far, early_core, mid_mine, mid_core, head_both
        )
        inner = dp_halves(inner, far[1], 0)
        mid_far, early_both = swap(mid_mine, 2), swap(early_far, 1)
        channel = channels // shards
        early_grads = placed_pieces(
            place_early_body,
            scalars,
            [early_mine, early_far, early_core, early_both]
            + [head_mine, head_far, head_core, head_both],
            [
                shape((conv_out.shape[0] // shards, channels)),
                shape((embed_weight.shape[0] // shards, embed_weight.shape[1])),
                shape((table.shape[0] // shards, table.shape[1])),
                shape((channel, head_weight.shape[1])),
            ],
        )
        inner[-1], mid_far, *early_grads = tie(inner[-1], mid_far, *early_grads)
        in_mine = sum(inner)
        in_far, in_core, mid_both = swap(in_mine, 2), swap(in_mine, 1), swap(mid_far, 1)
        grad_conv_out, grad_embed, grad_protos, grad_head = early_grads
        grad_protos = grad_protos[:, :protos]
        grad_conv_mid, grad_conv_in = placed_pieces(
            place_late_body,
            scalars,
            [mid_mine, mid_far, mid_core, mid_both, in_mine, in_far, in_core, swap(in_far, 1)],
            [
                shape((conv_mid.shape[0] // shards, conv_mid.shape[1])),
                shape((channel, conv_in.shape[1])),
            ],
        )
    else:
        low, high = jnp.zeros((1,), jnp.int32), jnp.ones((1,), jnp.int32)

        def reduced(array):
            return lax.psum(lax.psum_scatter(array, "dp", scatter_dimension=0, tiled=True), "hst")

        parts_three = sum_parts(sums)
        dy, sums, out_low, out_high = from_third(low, parts_three)
        parts_two = sum_parts(sums)
        ins = [*parts_two, dy, *second_norm, act_one]
        d_two, mid_low = mid_grad("mid_first", mid_first_body, low, ins, act_one, True)
        mid_high = mid_grad("mid_second", mid_second_body, high, [d_two, act_one], act_one, False)
        dy, sums = from_second(d_two)
        parts_one = sum_parts(sums)
        d_one, in_low, in_high = in_grad(low, parts_one, dy, *first_norm, x)
        grad_x = pixels_grad(d_one, conv_in, wide, slope, micro)
        out = jnp.stack([out_low, out_high])
        out = out.reshape(2, shards, -1, conv_out.shape[0] // shards, out.shape[-1])
        small_protos, small_embed = unpack_small(
            [small_keep, small_send], table.shape, embed_weight.shape
        )
        grad_conv_out = reduced(out.transpose(1, 3, 0, 2, 4).reshape(conv_out.shape))
        grad_conv_mid = reduced(jnp.concatenate([mid_low, mid_high], 1))
        grad_conv_in = reduced(jnp.concatenate([in_low, in_high], 1))
        dg = jnp.concatenate([dg_keep, dg_send], 1).astype(BF16)
        grad_head = reduced(jnp.dot(feat.astype(BF16).T, dg, preferred_element_type=F32))
        grad_embed = reduced(small_embed)
        grad_protos = reduced(small_protos)[:, :protos]

    def own_rows(vectors):
        sums = [jnp.sum(vector, 0) for vector in vectors]
        piece = sums[0].shape[0] // shards
        stacked = jnp.stack(sums)
        found = lax.dynamic_slice_in_dim(stacked, lax.axis_index("dp") * piece, piece, 1)
        return [found[i] for i in range(len(vectors))]

    def both_sums(parts):
        total = tree(list(parts))
        return [total[:, 1], total[:, 0]]

    small_ones = own_rows(both_sums(parts_one) + both_sums(parts_two))
    large_ones = own_rows(both_sums(parts_three) + [second_four, first_four])

    return (
        total_loss,
        grad_x.reshape(pixels.shape),
        grad_conv_in,
        small_ones[0],
        small_ones[1],
        grad_conv_mid,
        small_ones[2],
        small_ones[3],
        grad_conv_out,
        large_ones[0],
        large_ones[1],
        grad_head,
        large_ones[2],
        large_ones[3],
        grad_embed,
        lax.dynamic_slice_in_dim(
            grad_bias,
            lax.axis_index("dp") * (grad_bias.shape[0] // shards),
            grad_bias.shape[0] // shards,
            0,
        ),
        grad_protos,
    )


def solution(mesh):
    placed = (
        P(None, ("dp", "hst"), None, None),
        P(None, ("dp", "hst"), None),
        P(("dp", "hst"), None),
    ) + (P(),) * 15
    return jax.shard_map(
        on_device,
        mesh=mesh,
        in_specs=placed,
        out_specs=(
            P(),
            P(None, ("dp", "hst"), None, None),
            P("dp", None),
            P("dp"),
            P("dp"),
            P("dp", None),
            P("dp"),
            P("dp"),
            P("dp", None),
            P("dp"),
            P("dp"),
            P("dp", None),
            P("dp"),
            P("dp"),
            P("dp", None),
            P("dp"),
            P("dp", None),
        ),
        check_vma=False,
    )
```

```python
import functools

import jax
import jax.numpy as jnp
from jax import lax
from jax.experimental import pallas as pl
from jax.experimental.pallas import tpu as pltpu
from jax.sharding import PartitionSpec as P

ROWS = 8
COLS = 16
SLOTS = 4
CELL = COLS // SLOTS
PIX = ROWS * COLS
SINK_ITERS = 3
TAPS = 9

eps_norm = 1e-05
eps_unit = 1e-06
transport_epsilon = 0.05
softmax_sharpness = 0.1
highest = lax.Precision.HIGHEST
F32 = jnp.float32
BF16 = jnp.bfloat16
AXES = ("dp", "hst")
MIB = 1 << 20
LANES = 128


def swap(value, mask):
    count = lax.axis_size("dp") * lax.axis_size("hst")
    return lax.ppermute(value, AXES, [(i, i ^ mask) for i in range(count)])


def sync_groups():
    bits = (lax.axis_size("dp") * lax.axis_size("hst")).bit_length() - 1
    groups = [(1,)]
    bit = 1
    while bit < bits:
        if bit + 1 < bits:
            groups.append((1 << bit, 2 << bit, 3 << bit))
            bit += 2
        else:
            groups.append((1 << bit,))
            bit += 1
    return groups


def tree(parts):
    while len(parts) > 1:
        parts = [parts[i] + parts[i + 1] for i in range(0, len(parts), 2)]
    return parts[0]


def between(parts, gate, fillers):
    for filler in fillers:
        parts = list(tie(*parts, *filler(gate)))[: len(parts)]
    return parts


def pick(fillers, step):
    return fillers[step] if step < len(fillers) else ()


def sum_parts(value, fillers=()):
    groups = sync_groups()
    for step, group in enumerate(groups):
        parts = [value] + [swap(value, mask) for mask in group]
        parts = between(parts, value, pick(fillers, step))
        value = tree(parts)
    return parts


def merge(parts, members):
    whole = tree(list(members))
    mean = tree([n * part[:, 0] for n, part in zip(members, parts)]) / whole
    spread = tree(
        [part[:, 1] + n * (part[:, 0] - mean) ** 2 for n, part in zip(members, parts)]
    )
    return mean, spread, whole


def moment_parts(moments, counts, fillers=()):
    groups = sync_groups()
    for step, group in enumerate(groups):
        parts = [moments] + [swap(moments, mask) for mask in group]
        parts = between(parts, moments, pick(fillers, step))
        if step + 1 < len(groups):
            moments = jnp.stack(merge(parts, counts[step])[:2], 1)
    return parts


def first_parts(moments):
    groups = sync_groups()
    counts = []
    for step, group in enumerate(groups):
        parts = [moments] + [swap(moments, mask) for mask in group]
        if step + 1 < len(groups):
            members = [part[:, 2] for part in parts]
            moments = jnp.stack(merge(parts, members), 1)
            counts.append([n[:, :1] for n in members])
    return parts, counts


def bit_of(mask):
    index = lax.axis_index("dp") * lax.axis_size("hst") + lax.axis_index("hst")
    return (index // mask) % 2


def dp_masks():
    base = lax.axis_size("hst")
    return [base << j for j in range(lax.axis_size("dp").bit_length() - 1)]


def tie(first, *others):
    return lax.optimization_barrier((first,) + others)


def at(view, place, axis):
    return lax.dynamic_index_in_dim(view, place, axis, keepdims=False)


def core_swap(value, low, high):
    count = lax.axis_size("dp") * lax.axis_size("hst")
    pairs = [(i, i ^ (high if i % 2 else low)) for i in range(count)]
    return lax.ppermute(value, AXES, pairs)


def dp_split(addends, mask, axis):
    bit = bit_of(mask)
    send = sum(at(array, 1 - bit, axis) for array in addends)
    return [at(array, bit, axis) for array in addends], send


def dp_halves(addends, mask, axis):
    keep, send = dp_split(addends, mask, axis)
    return keep + [swap(send, mask)]


VMEM_MIB = {
    "third_back": 58,
    "second_back_body": 58,
}


def run(body, grid, in_specs, out_specs, out_shape, scratch=(), flops=0, bytes_accessed=0, prefetch=0, aliases=None):
    return pl.pallas_call(
        body,
        grid_spec=pltpu.PrefetchScalarGridSpec(
            num_scalar_prefetch=prefetch,
            grid=grid,
            in_specs=in_specs,
            out_specs=out_specs,
            scratch_shapes=list(scratch),
        ),
        out_shape=out_shape,
        name=body.__name__,
        input_output_aliases=aliases or {},
        compiler_params=pltpu.CompilerParams(
            vmem_limit_bytes=VMEM_MIB.get(body.__name__, 44) * MIB, dimension_semantics=("arbitrary",) * len(grid)
        ),
        cost_estimate=pl.CostEstimate(
            flops=flops, bytes_accessed=bytes_accessed, transcendentals=0
        ),
    )


def shape(dims, dtype=F32):
    return jax.ShapeDtypeStruct(tuple(dims), dtype)


def sigmoid(u):
    return 0.5 * jnp.tanh(0.5 * u) + 0.5


def norm_of(part_refs, members, m=0, lane=slice(None)):
    whole = tree(list(members))
    means = [ref[m, 0:1, lane] for ref in part_refs]
    mean = tree([n * one for n, one in zip(members, means)]) / whole
    spread = tree(
        [ref[m, 1:2, lane] + n * (one - mean) ** 2 for n, ref, one in zip(members, part_refs, means)]
    )
    return mean, lax.rsqrt(spread / whole + eps_norm)


def sums_of(part_refs, first, second, m=0):
    return (
        tree([ref[m, first : first + 1, :] for ref in part_refs]),
        tree([ref[m, second : second + 1, :] for ref in part_refs]),
    )


def counts_of(count_refs, m=0):
    return [ref[m, 2:3, 0:1] for ref in count_refs]


def whole(array):
    return pl.BlockSpec(array.shape, lambda *_: (0,) * len(array.shape))


def per_micro(array):
    return pl.BlockSpec((1,) + array.shape[1:], lambda m, *_: (m,) + (0,) * (array.ndim - 1))


def slope_of(u):
    s = sigmoid(u)
    return s * (1.0 + u * (1.0 - s))


def nt_dot(left, right):
    return lax.dot_general(left, right, (((1,), (1,)), ((), ())), preferred_element_type=F32)


def tn_dot(left, right):
    return lax.dot_general(left, right, (((0,), (0,)), ((), ())), preferred_element_type=F32)


def fold(y):
    return jnp.sum(y.reshape(y.shape[0] // 8, 8, y.shape[1]), 0)


def put_moments(stats_ref, h_ref, v_ref, with_count):
    rows, width = h_ref.shape
    chunk = 32
    lanes = 512
    v = v_ref[...]
    count = jnp.sum(v, axis=0, keepdims=True)
    first = jnp.sum(v[:PIX], axis=0, keepdims=True)
    for j in range(0, width, lanes):
        lane = slice(j, j + lanes)
        acc = jnp.zeros((8, lanes), F32)
        for i in range(0, PIX, chunk):
            acc += fold(h_ref[i : i + chunk, lane].astype(F32) * v_ref[i : i + chunk, :])
        pivot = jnp.sum(acc, axis=0, keepdims=True) / first
        line = jnp.zeros((8, lanes), F32)
        square = jnp.zeros((8, lanes), F32)
        for i in range(0, rows, chunk):
            off = (h_ref[i : i + chunk, lane].astype(F32) - pivot) * v_ref[i : i + chunk, :]
            line += fold(off)
            square += fold(off * off)
        total = jnp.sum(line, axis=0, keepdims=True)
        stats_ref[0, 0:1, lane] = pivot + total / count
        stats_ref[0, 1:2, lane] = (
            jnp.sum(square, axis=0, keepdims=True) - total * total / count
        )
        if with_count:
            stats_ref[0, 2:3, lane] = jnp.broadcast_to(count, (1, lanes))


def first_body(x_ref, w_ref, v_ref, h_ref, stats_ref):
    h_ref[...] = jnp.dot(x_ref[...], w_ref[...], preferred_element_type=F32)
    put_moments(stats_ref, h_ref, v_ref, True)


def first_product(x, weight, valid, micro):
    rows = x.shape[0] // micro
    depth, width = weight.shape
    return run(
        first_body,
        (micro,),
        [
            pl.BlockSpec((rows, depth), lambda m: (m, 0)),
            pl.BlockSpec((depth, width), lambda m: (0, 0)),
            pl.BlockSpec((rows, 1), lambda m: (m, 0)),
        ],
        [
            pl.BlockSpec((rows, width), lambda m: (m, 0)),
            pl.BlockSpec((1, 3, width), lambda m: (m, 0, 0)),
        ],
        [shape((micro * rows, width)), shape((micro, 3, width))],
        flops=2 * micro * rows * depth * width,
        bytes_accessed=2 * x.size,
    )(x, weight, valid)


def cell_column(rows):
    return lax.broadcasted_iota(jnp.int32, (rows, 1), 0) % CELL


def second_body(counts, refs):
    part_refs, (h_ref, v_ref, gain_ref, shift_ref, w_ref, a_ref, h2_ref, stats_ref, info_ref, cols_ref) = refs[:counts], refs[counts:]
    rows, width = h_ref.shape
    members = counts_of(part_refs)
    mean, scaled = norm_of(part_refs, members)
    info_ref[0, 0:1, :] = mean
    info_ref[0, 1:2, :] = scaled
    info_ref[0, 2:3, :] = jnp.broadcast_to(tree(list(members)), mean.shape)
    factor = scaled * gain_ref[...]
    shift = shift_ref[...]
    place = cell_column(COLS)
    has_left = (place >= 1).astype(F32)
    has_right = (place <= CELL - 2).astype(F32)
    blank = jnp.zeros((COLS, width), BF16)
    for i in range(0, rows, COLS):
        at = slice(i, i + COLS)
        pre = (h_ref[at, :] - mean) * factor + shift
        act = (pre * sigmoid(pre) * v_ref[at, :]).astype(BF16)
        a_ref[at, :] = act
        wide = act.astype(F32)
        sides = (
            (pltpu.roll(wide, 1, 0) * has_left).astype(BF16),
            act,
            (pltpu.roll(wide, COLS - 1, 0) * has_right).astype(BF16),
        )
        for c in range(3):
            cols_ref[at, (3 + c) * width : (4 + c) * width] = sides[c]
            if i % PIX < PIX - COLS:
                cols_ref[i + COLS : i + 2 * COLS, c * width : (c + 1) * width] = sides[c]
            else:
                cols_ref[at, (6 + c) * width : (7 + c) * width] = blank
            if i % PIX > 0:
                cols_ref[i - COLS : i, (6 + c) * width : (7 + c) * width] = sides[c]
            else:
                cols_ref[at, c * width : (c + 1) * width] = blank
    h2_ref[...] = jnp.dot(cols_ref[...], w_ref[...], preferred_element_type=F32)
    put_moments(stats_ref, h2_ref, v_ref, False)


def named(name, body, *fixed):
    def kernel(*refs):
        body(*fixed, refs)

    kernel.__name__ = name
    return kernel


def second_product(parts, h1, valid, gain, shift, weight, micro):
    rows, width = h1.shape[0] // micro, h1.shape[1]
    mid = pl.BlockSpec((rows, width), lambda m: (m, 0))
    return run(
        named("second_product", second_body, len(parts)),
        (micro,),
        [per_micro(part) for part in parts]
        + [
            mid,
            pl.BlockSpec((rows, 1), lambda m: (m, 0)),
            whole(gain),
            whole(shift),
            whole(weight),
        ],
        [
            mid,
            mid,
            pl.BlockSpec((1, 2, width), lambda m: (m, 0, 0)),
            pl.BlockSpec((1, 3, width), lambda m: (m, 0, 0)),
        ],
        [
            shape((micro * rows, width), BF16),
            shape((micro * rows, width)),
            shape((micro, 2, width)),
            shape((micro, 3, width)),
        ],
        [pltpu.VMEM((rows, weight.shape[0]), BF16)],
        flops=2 * micro * rows * weight.size,
        bytes_accessed=10 * h1.size,
    )(*parts, h1, valid, gain, shift, weight)


def third_body(counts, refs):
    part_refs, count_refs = refs[:counts], refs[counts : 2 * counts]
    h_ref, v_ref, gain_ref, shift_ref, w_ref, a_ref, h3_ref, stats_ref, info_ref, wide_ref = refs[2 * counts :]
    rows = h_ref.shape[0]
    mean, scaled = norm_of(part_refs, counts_of(count_refs))
    info_ref[0, 0:1, :] = mean
    info_ref[0, 1:2, :] = scaled
    factor = scaled * gain_ref[...]
    shift = shift_ref[...]
    for i in range(0, rows, 32):
        at = slice(i, i + 32)
        pre = (h_ref[at, :] - mean) * factor + shift
        a_ref[at, :] = (pre * sigmoid(pre) * v_ref[at, :]).astype(BF16)
    wide_ref[...] = jnp.dot(a_ref[...], w_ref[...], preferred_element_type=F32)
    put_moments(stats_ref, wide_ref, v_ref, False)
    for i in range(0, rows, 32):
        at = slice(i, i + 32)
        h3_ref[at, :] = (wide_ref[at, :] - stats_ref[0, 0:1, :]).astype(BF16)


def third_product(parts, members, h2, valid, gain, shift, weight, micro):
    rows, depth = h2.shape[0] // micro, h2.shape[1]
    width = weight.shape[1]
    mid = pl.BlockSpec((rows, depth), lambda m: (m, 0))
    return run(
        named("third_product", third_body, len(parts)),
        (micro,),
        [per_micro(part) for part in parts + members]
        + [
            mid,
            pl.BlockSpec((rows, 1), lambda m: (m, 0)),
            whole(gain),
            whole(shift),
            whole(weight),
        ],
        [
            mid,
            pl.BlockSpec((rows, width), lambda m: (m, 0)),
            pl.BlockSpec((1, 2, width), lambda m: (m, 0, 0)),
            pl.BlockSpec((1, 2, depth), lambda m: (m, 0, 0)),
        ],
        [
            shape((micro * rows, depth), BF16),
            shape((micro * rows, width), BF16),
            shape((micro, 2, width)),
            shape((micro, 2, depth)),
        ],
        [pltpu.VMEM((rows, width), F32)],
        flops=2 * micro * rows * weight.size,
        bytes_accessed=4 * micro * rows * width,
    )(*parts, *members, h2, valid, gain, shift, weight)


def crop_sums(ref, *index):
    crops = ref.shape[-2] // CELL
    slabs = [
        tree([ref[(*index, j, pl.ds(i, crops, CELL), slice(None))] for i in range(CELL)])
        for j in range(ref.shape[-3])
    ]
    return jnp.concatenate(slabs, 1)


def put_lanes(ref, place, first, value, *index):
    for j in range(0, value.shape[1], LANES):
        ref[(*index, (first + j) // LANES, place, slice(None))] = value[:, j : j + LANES]


def pool_body(counts, split, refs):
    scalars_ref, part_refs, count_refs = refs[0], refs[1 : 1 + counts], refs[1 + counts : 1 + 2 * counts]
    base_ref, h_ref, x_ref, v_ref, gain_ref, shift_ref, size_ref = refs[1 + 2 * counts : 8 + 2 * counts]
    feat_ref, info_ref, slope_ref, first_ref, second_ref = refs[8 + 2 * counts : 13 + 2 * counts]
    sums_ref = refs[-1]
    rows, width = h_ref.shape
    mean, scaled = norm_of(part_refs, counts_of(count_refs))
    mean = mean - base_ref[0, 0:1, :]
    info_ref[0, 0:1, :] = mean
    info_ref[0, 1:2, :] = scaled
    factor = scaled * gain_ref[...]
    shift = shift_ref[...]
    chunk = 256
    for j in range(0, width, chunk):
        lane = slice(j, j + chunk)
        for k in range(rows // PIX):
            acc = jnp.zeros((COLS, chunk), F32)
            acc_first = jnp.zeros((COLS, chunk), F32)
            acc_second = jnp.zeros((COLS, chunk), F32)
            for r in range(ROWS):
                at = pl.ds(k * PIX + r * COLS, COLS)
                centred = h_ref[at, lane].astype(F32) - mean[:, lane]
                resid = centred * factor[:, lane] + shift[:, lane] + x_ref[at, lane].astype(F32)
                sig = sigmoid(resid)
                kept = sig * v_ref[at, :]
                out = resid * kept
                acc += out.astype(BF16).astype(F32)
                slope = kept + out * (1.0 - sig)
                acc_first += slope
                acc_second += slope * centred
                slope_ref[at, lane] = slope.astype(BF16)
            place = pl.ds(k * COLS, COLS)
            put_lanes(sums_ref, place, j, acc, 0)
            put_lanes(sums_ref, place, j, acc_first, 1)
            put_lanes(sums_ref, place, j, acc_second * scaled[:, lane], 2)
    feat = (crop_sums(sums_ref, 0) / size_ref[...]).astype(BF16).astype(F32)
    feat_ref[...] = feat
    first_ref[...] = crop_sums(sums_ref, 1)
    second_ref[...] = crop_sums(sums_ref, 2)
    if split:
        keep_ref, send_ref = refs[13 + 2 * counts : 15 + 2 * counts]
        low = scalars_ref[1] == 0
        for i in range(0, width, 2 * split):
            one, two = feat[:, i : i + split], feat[:, i + split : i + 2 * split]
            place = slice(i // 2, i // 2 + split)
            keep_ref[:, place] = jnp.where(low, one, two)
            send_ref[:, place] = jnp.where(low, two, one)


def pool(scalars, parts, members, base, h3, x, valid, gain, shift, sizes, micro, split):
    rows, channels = h3.shape[0] // micro, h3.shape[1]
    crops = sizes.shape[0] // micro
    width = 1024
    tile = pl.BlockSpec((rows, width), lambda m, c, w: (m, c))
    line = pl.BlockSpec((1, width), lambda m, c, w: (0, c))
    pair = pl.BlockSpec((1, 2, width), lambda m, c, w: (m, 0, c))
    small = pl.BlockSpec((crops, width), lambda m, c, w: (m, c))
    part = pl.BlockSpec((crops, width // 2), lambda m, c, w: (m, c))
    lines = shape((micro * crops, channels))
    half = shape((micro * crops, channels // 2))
    return run(
        named("pool", pool_body, len(parts), split),
        (micro, channels // width),
        [pair] * len(parts)
        + [per_micro(part) for part in members]
        + [
            pair,
            tile,
            tile,
            pl.BlockSpec((rows, 1), lambda m, c, w: (m, 0)),
            line,
            line,
            pl.BlockSpec((crops, 1), lambda m, c, w: (m, 0)),
        ],
        [small, pair, tile, small, small] + ([part, part] if split else []),
        [lines, shape((micro, 2, channels)), shape(h3.shape, BF16), lines, lines]
        + ([half, half] if split else []),
        [pltpu.VMEM((3, width // LANES, rows // ROWS, LANES), F32)],
        flops=20 * h3.size,
        bytes_accessed=4 * h3.size,
        prefetch=1,
    )(scalars, *parts, *members, base, h3, x, valid, gain, shift, sizes)


def head_body(feat_ref, w_ref, g_ref, stats_ref):
    g = jnp.dot(feat_ref[...].astype(BF16), w_ref[...], preferred_element_type=F32)
    g_ref[...] = g
    micro = stats_ref.shape[0]
    crops = g.shape[0] // micro
    for m in range(micro):
        part = g[m * crops : (m + 1) * crops]
        mean = jnp.sum(part, axis=0, keepdims=True) / crops
        stats_ref[m, 0:1, :] = mean
        stats_ref[m, 1:2, :] = jnp.sum((part - mean) ** 2, axis=0, keepdims=True)


def head_product(feat, weight, micro):
    lines = feat.shape[0]
    depth, width = weight.shape
    tile = 512
    return run(
        head_body,
        (width // tile,),
        [
            pl.BlockSpec((lines, depth), lambda c: (0, 0)),
            pl.BlockSpec((depth, tile), lambda c: (0, c)),
        ],
        [
            pl.BlockSpec((lines, tile), lambda c: (0, c)),
            pl.BlockSpec((micro, 2, tile), lambda c: (0, 0, c)),
        ],
        [shape((lines, width)), shape((micro, 2, width))],
        flops=2 * lines * weight.size,
        bytes_accessed=2 * weight.size,
    )(feat, weight)


def head_back_body(total_crops, counts, refs):
    which_ref, part_refs = refs[0], refs[1 : 1 + counts]
    dy_ref, g_ref, info_ref, gain_ref, w_ref, size_ref, first_ref, second_ref, send_ref, keep_ref, wide_ref, stats_ref, low_ref, spread_ref = refs[1 + counts :]
    micro = stats_ref.shape[0]
    lines, width = dy_ref.shape
    crops = lines // micro

    @pl.when(pl.program_id(0) == 0)
    def _():
        for m in range(micro):
            at = pl.ds(m * crops, crops)
            one = tree([ref[m : m + 1, :width] for ref in part_refs]) / total_crops
            two = tree([ref[micro + m : micro + m + 1, :width] for ref in part_refs]) / total_crops
            scaled = info_ref[m, 1:2, :]
            normal = (g_ref[at, :] - info_ref[m, 0:1, :]) * scaled
            dg = gain_ref[...] * scaled * (dy_ref[at, :] - (one + normal * two))
            low = dg.astype(BF16)
            low_ref[at, :] = low
            left, right = [low[:, i : i + width // 2].astype(F32) for i in (0, width // 2)]
            send_ref[at, :] = jnp.where(which_ref[0] == 0, right, left)
            keep_ref[at, :] = jnp.where(which_ref[0] == 0, left, right)

    per_crop = nt_dot(low_ref[...], w_ref[...]) / size_ref[...]
    for j in range(wide_ref.shape[1] // LANES):
        lane = slice(j * LANES, (j + 1) * LANES)
        for i in range(CELL):
            spread_ref[j, pl.ds(i, lines, CELL), :] = per_crop[:, lane]
        wide_ref[:, lane] = spread_ref[j]
    one = per_crop * first_ref[...]
    two = per_crop * second_ref[...]
    for m in range(micro):
        at = slice(m * crops, (m + 1) * crops)
        stats_ref[m, 0:1, :] = jnp.sum(one[at], axis=0, keepdims=True)
        stats_ref[m, 1:2, :] = jnp.sum(two[at], axis=0, keepdims=True)


def head_back(which, parts, dy, g, info, gain, weight, sizes, first, second, total_crops):
    lines, width = dy.shape
    channels = weight.shape[0]
    micro = info.shape[0]
    tile = 512
    part = pl.BlockSpec((lines, tile), lambda c, w: (0, c))
    half = shape((lines, width // 2))
    return run(
        named("head_back", head_back_body, total_crops, len(parts)),
        (channels // tile,),
        [whole(a) for a in parts]
        + [
            whole(dy),
            whole(g),
            whole(info),
            whole(gain),
            pl.BlockSpec((tile, width), lambda c, w: (c, 0)),
            whole(sizes),
            part,
            part,
        ],
        [
            whole(half),
            whole(half),
            pl.BlockSpec((lines * CELL, tile), lambda c, w: (0, c)),
            pl.BlockSpec((micro, 2, tile), lambda c, w: (0, 0, c)),
        ],
        [half, half, shape((lines * CELL, channels)), shape((micro, 2, channels))],
        [
            pltpu.VMEM((lines, width), BF16),
            pltpu.VMEM((tile // LANES, lines * CELL, LANES), F32),
        ],
        flops=2 * lines * weight.size,
        bytes_accessed=2 * weight.size,
        prefetch=1,
    )(which, *parts, dy, g, info, gain, weight, sizes, first, second)


def third_back_body(counts, refs):
    which_ref, part_refs = refs[0], refs[1 : 1 + counts]
    wide_ref, slope_ref, h3_ref, v_ref, info3_ref, gain3_ref, info1_ref, w_ref, act_ref, h2_ref, info2_ref, gain2_ref, shift2_ref, dy_ref, stats_ref, send_ref, keep_ref, d_ref, sum_ref = refs[1 + counts :]
    rows, channels = slope_ref.shape
    step = pl.program_id(0)
    number = info1_ref[0, 2:3, 0:1]
    first, second = sums_of(part_refs, 0, 1)
    mean = info3_ref[0, 0:1, :]
    scaled = info3_ref[0, 1:2, :]
    factor = gain3_ref[...] * scaled
    one = factor * first / number
    two = factor * scaled * second / number
    act = act_ref[...].T

    @pl.when(step == 0)
    def _():
        sum_ref[...] = jnp.zeros(sum_ref.shape, F32)

    tile = sum_ref.shape[2]
    for j in range(0, channels, tile):
        lane = slice(j, j + tile)
        for k in range(rows // PIX):
            wide = wide_ref[pl.ds(k * COLS, COLS), lane] * factor[:, lane]
            for r in range(ROWS):
                at = pl.ds(k * PIX + r * COLS, COLS)
                back = one[:, lane] + (h3_ref[at, lane].astype(F32) - mean[:, lane]) * two[:, lane]
                d = wide * slope_ref[at, lane].astype(F32) - v_ref[at, :] * back
                d_ref[at, lane] = d.astype(BF16)
        part = nt_dot(d_ref[:, lane], w_ref[:, lane])
        if j == 0:
            dy_ref[...] = part
        else:
            dy_ref[...] += part
        sum_ref[j // tile] += jnp.dot(act, d_ref[:, lane], preferred_element_type=F32)
    put_back(dy_ref, h2_ref, v_ref, info2_ref, gain2_ref, shift2_ref, stats_ref)

    @pl.when(step == pl.num_programs(0) - 1)
    def _():
        low = which_ref[0] == 0
        steps = sum_ref.shape[0] // 2
        lines = send_ref.shape[1] // steps
        for q in range(steps):
            place = slice(q * lines, (q + 1) * lines)
            left = sum_ref[q].reshape(-1, lines, tile)
            right = sum_ref[steps + q].reshape(-1, lines, tile)
            send_ref[:, place, :] = jnp.where(low, left, right)
            keep_ref[:, place, :] = jnp.where(low, right, left)


def put_back(dy_ref, h_ref, v_ref, info_ref, gain_ref, shift_ref, stats_ref):
    rows, width = dy_ref.shape
    first = jnp.zeros((8, width), F32)
    second = jnp.zeros((8, width), F32)
    for i in range(0, rows, 32):
        at = slice(i, i + 32)
        normal = (h_ref[at, :] - info_ref[0, 0:1, :]) * info_ref[0, 1:2, :]
        pre = normal * gain_ref[...] + shift_ref[...]
        dy = dy_ref[at, :] * v_ref[at, :] * slope_of(pre)
        dy_ref[at, :] = dy
        first += fold(dy)
        second += fold(dy * normal)
    stats_ref[0, 0:1, :] = jnp.sum(first, axis=0, keepdims=True)
    stats_ref[0, 1:2, :] = jnp.sum(second, axis=0, keepdims=True)


def third_back(which, parts, wide, slope, h3, valid, info3, gain3, info1, weight, act, h2, info2, gain2, shift2, micro, shards):
    rows, channels = slope.shape[0] // micro, slope.shape[1]
    middle = weight.shape[0]
    lines = wide.shape[0] // micro
    tile = 512
    big = pl.BlockSpec((rows, channels), lambda m, w: (m, 0))
    mid = pl.BlockSpec((rows, middle), lambda m, w: (m, 0))
    half = shape((shards, middle // shards * (channels // tile // 2), tile))
    return run(
        named("third_back", third_back_body, len(parts)),
        (micro,),
        [per_micro(part) for part in parts]
        + [
            pl.BlockSpec((lines, channels), lambda m, w: (m, 0)),
            big,
            big,
            pl.BlockSpec((rows, 1), lambda m, w: (m, 0)),
            per_micro(info3),
            whole(gain3),
            per_micro(info1),
            whole(weight),
            mid,
            mid,
            per_micro(info2),
            whole(gain2),
            whole(shift2),
        ],
        [
            mid,
            pl.BlockSpec((1, 2, middle), lambda m, w: (m, 0, 0)),
            whole(half),
            whole(half),
        ],
        [shape(h2.shape), shape((micro, 2, middle)), half, half],
        [
            pltpu.VMEM((rows, channels), BF16),
            pltpu.VMEM((channels // tile, middle, tile), F32),
        ],
        flops=4 * slope.shape[0] * weight.size,
        bytes_accessed=6 * slope.size,
        prefetch=1,
    )(which, *parts, wide, slope, h3, valid, info3, gain3, info1, weight, act, h2, info2, gain2, shift2)


def put_norm_back(part_refs, dy_ref, h_ref, v_ref, info_ref, number_ref, gain_ref, d_ref):
    micro = info_ref.shape[0]
    rows = dy_ref.shape[0] // micro
    for m in range(micro):
        number = number_ref[m, 2:3, 0:1]
        first, second = sums_of(part_refs, 0, 1, m)
        scaled = info_ref[m, 1:2, :]
        factor = gain_ref[...] * scaled
        one = factor * first / number
        two = factor * scaled * second / number
        mean = info_ref[m, 0:1, :]
        for i in range(m * rows, (m + 1) * rows, 32):
            at = slice(i, i + 32)
            back = one + (h_ref[at, :] - mean) * two
            d_ref[at, :] = (factor * dy_ref[at, :] - v_ref[at, :] * back).astype(BF16)


def put_sides(a_ref, sides_ref):
    rows, width = a_ref.shape
    blank = jnp.zeros((COLS, width), BF16)
    place = cell_column(COLS)
    has_left = (place >= 1).astype(F32)
    has_right = (place <= CELL - 2).astype(F32)
    for k in range(rows // PIX):
        for c in range(3):
            sides_ref[c, k, 0:COLS, :] = blank
            sides_ref[c, k, COLS + PIX :, :] = blank
        for r in range(ROWS):
            act = a_ref[k * PIX + r * COLS : k * PIX + (r + 1) * COLS, :]
            wide = act.astype(F32)
            at = slice((r + 1) * COLS, (r + 2) * COLS)
            sides_ref[0, k, at, :] = (pltpu.roll(wide, 1, 0) * has_left).astype(BF16)
            sides_ref[1, k, at, :] = act
            sides_ref[2, k, at, :] = (pltpu.roll(wide, COLS - 1, 0) * has_right).astype(BF16)


def put_tap(out_ref, sides_ref, half_ref):
    tap = pl.program_id(0)
    _, canvases, _, width = sides_ref.shape
    start = pl.multiple_of(tap // 3 * COLS, COLS)
    left = sides_ref[tap % 3, :, pl.ds(start, PIX), :].reshape(canvases * PIX, width)
    out_ref[...] = tn_dot(left, half_ref[...])


def half_of(which_ref, d_ref):
    half = d_ref.shape[1] // 2
    return d_ref[:, pl.ds(pl.multiple_of(which_ref[0] * half, half), half)]


def mid_first_body(counts, refs):
    which_ref, part_refs = refs[0], refs[1 : 1 + counts]
    dy_ref, h_ref, v_ref, info_ref, number_ref, gain_ref, a_ref, d_ref, out_ref, sides_ref, half_ref = refs[1 + counts :]

    @pl.when(pl.program_id(0) == 0)
    def _():
        put_norm_back(part_refs, dy_ref, h_ref, v_ref, info_ref, number_ref, gain_ref, d_ref)
        half_ref[...] = half_of(which_ref, d_ref)
        put_sides(a_ref, sides_ref)

    put_tap(out_ref, sides_ref, half_ref)


def mid_second_body(refs):
    which_ref, d_ref, a_ref, out_ref, sides_ref, half_ref = refs

    @pl.when(pl.program_id(0) == 0)
    def _():
        half_ref[...] = half_of(which_ref, d_ref)
        put_sides(a_ref, sides_ref)

    put_tap(out_ref, sides_ref, half_ref)


def mid_grad(name, body, which, ins, act, with_d):
    rows, width = act.shape
    half = width // 2
    grad = pl.BlockSpec((width, half), lambda t, w: (t, 0))
    return run(
        named(name, body, *([len(ins) - 7] if with_d else [])),
        (TAPS,),
        [whole(a) for a in ins],
        [whole(act), grad] if with_d else grad,
        [shape(act.shape, BF16), shape((TAPS * width, half))]
        if with_d
        else shape((TAPS * width, half)),
        [
            pltpu.VMEM((3, rows // PIX, PIX + 2 * COLS, width), BF16),
            pltpu.VMEM((rows, half), BF16),
        ],
        flops=2 * rows * TAPS * width * half,
        bytes_accessed=4 * TAPS * width * half,
        prefetch=1,
    )(which, *ins)


def in_grad_body(counts, refs):
    which_ref, part_refs = refs[0], refs[1 : 1 + counts]
    dy_ref, h_ref, v_ref, info_ref, number_ref, gain_ref, x_ref, d_ref, send_ref, keep_ref = refs[1 + counts :]

    @pl.when(pl.program_id(0) == 0)
    def _():
        put_norm_back(part_refs, dy_ref, h_ref, v_ref, info_ref, number_ref, gain_ref, d_ref)

    grad = tn_dot(x_ref[...], d_ref[...])
    half = grad.shape[1] // 2
    low = which_ref[0] == 0
    left, right = grad[:, :half], grad[:, half:]
    send_ref[...] = jnp.where(low, left, right)
    keep_ref[...] = jnp.where(low, right, left)


def in_grad(which, parts, dy, h, valid, info, number, gain, x):
    rows, width = dy.shape
    depth = x.shape[1]
    half = width // 2
    tile = 512
    ins = [*parts, dy, h, valid, info, number, gain]
    grad = pl.BlockSpec((tile, half), lambda c, w: (c, 0))
    return run(
        named("in_grad", in_grad_body, len(parts)),
        (depth // tile,),
        [whole(a) for a in ins] + [pl.BlockSpec((rows, tile), lambda c, w: (0, c))],
        [whole(dy), grad, grad],
        [shape(dy.shape, BF16), shape((depth, half)), shape((depth, half))],
        flops=2 * rows * depth * width,
        bytes_accessed=2 * x.size + 4 * depth * width + 10 * dy.size,
        prefetch=1,
    )(which, *ins, x)


def second_back_body(d_ref, w_ref, v_ref, h1_ref, info_ref, gain_ref, shift_ref, dy_ref, stats_ref, moved_ref, packed_ref):
    rows, width = d_ref.shape

    @pl.when(pl.program_id(0) == 0)
    def _():
        for r in range(3):
            for c in range(3):
                tap = 3 * r + c
                packed_ref[c, :, r * width : (r + 1) * width] = w_ref[
                    tap * width : (tap + 1) * width, :
                ]

    blank = jnp.zeros((COLS, width), BF16)
    for k in range(0, rows, PIX):
        moved_ref[k : k + PIX - COLS, 0:width] = d_ref[k + COLS : k + PIX, :]
        moved_ref[k + PIX - COLS : k + PIX, 0:width] = blank
        moved_ref[k : k + COLS, 2 * width :] = blank
        moved_ref[k + COLS : k + PIX, 2 * width :] = d_ref[k : k + PIX - COLS, :]
    moved_ref[:, width : 2 * width] = d_ref[...]
    parts = [nt_dot(moved_ref[...], packed_ref[c]) for c in range(3)]
    place = cell_column(rows)
    dy_ref[...] = (
        parts[1]
        + pltpu.roll(parts[2], 1, 0) * (place >= 1).astype(F32)
        + pltpu.roll(parts[0], rows - 1, 0) * (place <= CELL - 2).astype(F32)
    )
    put_back(dy_ref, h1_ref, v_ref, info_ref, gain_ref, shift_ref, stats_ref)


def second_back(d, weight, valid, h1, info, gain, shift, micro):
    rows, width = d.shape[0] // micro, d.shape[1]
    mid = pl.BlockSpec((rows, width), lambda m: (m, 0))
    return run(
        second_back_body,
        (micro,),
        [
            mid,
            whole(weight),
            pl.BlockSpec((rows, 1), lambda m: (m, 0)),
            mid,
            per_micro(info),
            whole(gain),
            whole(shift),
        ],
        [mid, pl.BlockSpec((1, 2, width), lambda m: (m, 0, 0))],
        [shape(d.shape), shape((micro, 2, width))],
        [pltpu.VMEM((rows, 3 * width), BF16), pltpu.VMEM((3, width, 3 * width), BF16)],
        flops=2 * micro * rows * weight.size,
        bytes_accessed=10 * d.size,
    )(d, weight, valid, h1, info, gain, shift)


def pixels_body(d_ref, w_ref, wide_ref, slope_ref, out_ref):
    rows, channels = out_ref.shape
    width = 512
    for j in range(0, channels, width):
        lane = pl.ds(j, width)
        grad = nt_dot(d_ref[...], w_ref[lane, :])
        for k in range(rows // PIX):
            wide = wide_ref[pl.ds(k * COLS, COLS), lane]
            for r in range(ROWS):
                first = k * PIX + r * COLS
                at = pl.ds(first, COLS)
                out_ref[at, lane] = (
                    grad[first : first + COLS] + wide * slope_ref[at, lane].astype(F32)
                ).astype(BF16)


def pixels_grad(d, weight, wide, slope, micro):
    rows, channels = slope.shape[0] // micro, slope.shape[1]
    lines = wide.shape[0] // micro
    big = pl.BlockSpec((rows, channels), lambda m: (m, 0))
    return run(
        pixels_body,
        (micro,),
        [
            pl.BlockSpec((rows, d.shape[1]), lambda m: (m, 0)),
            pl.BlockSpec(weight.shape, lambda m: (0, 0)),
            pl.BlockSpec((lines, channels), lambda m: (m, 0)),
            big,
        ],
        big,
        shape(slope.shape, BF16),
        flops=2 * slope.shape[0] * weight.size,
        bytes_accessed=4 * slope.size,
    )(d, weight, wide, slope)


def factor_body(feat_ref, other_feat_ref, dg_ref, far_ref, near_ref, both_ref, out_ref):
    left = jnp.concatenate([feat_ref[...], other_feat_ref[...]], 0).astype(BF16)
    lines = dg_ref.shape[0] // 2
    right = jnp.concatenate(
        [
            ref[c * lines : (c + 1) * lines, :]
            for c in range(2)
            for ref in (dg_ref, near_ref, far_ref, both_ref)
        ],
        0,
    ).astype(BF16)
    out_ref[...] = tn_dot(left, right)


def factor_grad(feat, other_feat, dg, far, near, both):
    lines, depth = feat.shape
    width = dg.shape[1]
    tile = 512
    left = pl.BlockSpec((lines, tile), lambda c: (0, c))
    return run(
        factor_body,
        (depth // tile,),
        [left, left] + [whole(dg)] * 4,
        pl.BlockSpec((tile, width), lambda c: (c, 0)),
        shape((depth, width)),
        flops=4 * lines * depth * width,
        bytes_accessed=4 * depth * width,
    )(feat, other_feat, dg, far, near, both)


def embed_body(protos, counts, members, refs):
    part_refs = refs[:counts]
    g_ref, gain_ref, shift_ref, w_ref, bias_ref, table_ref, queue_ref, act_ref, z_ref, inverse_ref, unit_ref, logits_ref, batch_ref, line_ref, sums_ref, info_ref = refs[counts:]
    micro = info_ref.shape[0]
    crops = g_ref.shape[0] // micro
    for m in range(micro):
        at = slice(m * crops, (m + 1) * crops)
        mean, scaled = norm_of(part_refs, members, m)
        info_ref[m, 0:1, :] = mean
        info_ref[m, 1:2, :] = scaled
        pre = (g_ref[at, :] - mean) * scaled * gain_ref[...] + shift_ref[...]
        act_ref[at, :] = (pre * sigmoid(pre)).astype(BF16)
    z = jnp.dot(act_ref[...], w_ref[...], preferred_element_type=F32) + bias_ref[...]
    inverse = lax.rsqrt(jnp.sum(z * z, 1, keepdims=True) + eps_unit)
    unit = (z * inverse).astype(BF16)
    z_ref[...] = z
    inverse_ref[...] = inverse
    unit_ref[...] = unit
    logits = jnp.dot(unit, table_ref[...], preferred_element_type=F32)
    logits_ref[...] = logits
    real = lax.broadcasted_iota(jnp.int32, (1, logits.shape[1]), 1) < protos
    batch = jnp.where(real, jnp.exp(logits / transport_epsilon), 0.0)
    batch_ref[...] = batch
    queued = jnp.dot(queue_ref[...], table_ref[...], preferred_element_type=F32)
    line = jnp.where(real, jnp.exp(queued / transport_epsilon), 0.0)
    line_ref[...] = line
    queue_sum = jnp.sum(line, axis=0, keepdims=True)
    for m in range(micro):
        at = slice(m * crops, (m + 1) * crops)
        sums_ref[m : m + 1, :] = jnp.sum(batch[at], axis=0, keepdims=True) + queue_sum


def embed_product(parts, members, protos, g, gain, shift, weight, bias, table, queue):
    lines = g.shape[0]
    micro = parts[0].shape[0]
    feat = weight.shape[1]
    wide = table.shape[1]
    outs = [
        shape(g.shape, BF16),
        shape((lines, feat)),
        shape((lines, 1)),
        shape((lines, feat), BF16),
        shape((lines, wide)),
        shape((lines, wide)),
        shape((queue.shape[0], wide)),
        shape((micro, wide)),
        shape((micro, 2, g.shape[1])),
    ]
    ins = [*parts, g, gain, shift, weight, bias, table, queue]
    return run(
        named("embed", embed_body, protos, len(parts), members),
        (1,),
        [whole(a) for a in ins],
        [whole(a) for a in outs],
        outs,
        flops=2 * lines * table.size,
        bytes_accessed=8 * lines * wide,
    )(*ins)


def sweep_body(protos, counts, refs):
    part_refs = refs[:counts]
    batch_ref, queue_ref, new_batch_ref, new_queue_ref, sums_ref = refs[counts:]
    micro, wide = sums_ref.shape
    crops = batch_ref.shape[0] // micro
    lines = new_queue_ref.shape[0] // micro
    shared = queue_ref.shape[0] == lines
    real = lax.broadcasted_iota(jnp.int32, (1, wide), 1) < protos
    for m in range(micro):
        column = jnp.where(real, tree([ref[m : m + 1, :] for ref in part_refs]), 1.0)
        at = slice(m * crops, (m + 1) * crops)
        batch = batch_ref[at, :] / column
        batch = batch / jnp.sum(batch, 1, keepdims=True)
        new_batch_ref[at, :] = batch
        own = slice(m * lines, (m + 1) * lines)
        queue = queue_ref[slice(0, lines) if shared else own, :] / column
        queue = queue / jnp.sum(queue, 1, keepdims=True)
        new_queue_ref[own, :] = queue
        sums_ref[m : m + 1, :] = jnp.sum(batch, axis=0, keepdims=True) + jnp.sum(
            queue, axis=0, keepdims=True
        )


def sweep(parts, protos, batch, queue, lines):
    micro, wide = parts[0].shape
    outs = [shape(batch.shape), shape((micro * lines, wide)), shape(parts[0].shape)]
    ins = [*parts, batch, queue]
    return run(
        named("sweep", sweep_body, protos, len(parts)),
        (1,),
        [whole(a) for a in ins],
        [whole(a) for a in outs],
        outs,
        flops=20 * batch.size,
        bytes_accessed=16 * batch.size,
    )(*ins)


def split_dot(dot, left, right, wide_left):
    value = left if wide_left else right
    high = value.astype(BF16)
    low = (value - high.astype(F32)).astype(BF16)
    if wide_left:
        return dot(high, right) + dot(low, right)
    return dot(left, high) + dot(left, low)


def pack_small(low, send_ref, keep_ref, protos, embed):
    shards, lines, width = send_ref.shape
    lines = lines // 2
    rows = protos.shape[0] // shards // 2
    half = protos.shape[1] // 2
    groups = half // width
    lane = embed.shape[1]
    below = lines - groups * rows

    def put(d, place, columns, one, two):
        keep_ref[d, place, columns] = jnp.where(low, one, two)
        send_ref[d, place, columns] = jnp.where(low, two, one)

    for d in range(shards):
        for y in range(2):
            first = (2 * d + y) * rows
            for q in range(groups):
                start = y * lines + q * rows
                one, two = [
                    protos[first : first + rows, c * half + q * width : c * half + (q + 1) * width]
                    for c in range(2)
                ]
                put(d, slice(start, start + rows), slice(None), one, two)
            for q in range(width // lane):
                one, two = [
                    embed[first : first + below]
                    for first in [
                        (((2 * d + c) * 2 + y) * (width // lane) + q) * below for c in range(2)
                    ]
                ]
                start = y * lines + groups * rows
                put(d, slice(start, start + below), slice(q * lane, (q + 1) * lane), one, two)


def unpack_small(halves, protos, embed):
    shards, lines, width = halves[0].shape
    lines = lines // 2
    packed = jnp.stack(halves).reshape(2, shards, 2, lines, width)
    rows = protos[0] // shards // 2
    groups = protos[1] // 2 // width
    lane = embed[1]
    above = packed[:, :, :, : groups * rows].reshape(2, shards, 2, groups, rows, width)
    below = packed[:, :, :, groups * rows :]
    below = below.reshape(2, shards, 2, lines - groups * rows, width // lane, lane)
    return (
        above.transpose(1, 2, 4, 0, 3, 5).reshape(protos),
        below.transpose(1, 0, 2, 4, 3, 5).reshape(embed),
    )


def packed_shape(protos, embed, shards):
    width = 512
    lines = protos[0] // shards // 2 * (protos[1] // 2 // width)
    return (shards, 2 * (lines + embed[0] * embed[1] // shards // 4 // width), width)


def loss_body(protos, scale, counts, refs):
    which_ref, part_refs = refs[0], refs[1 : 1 + counts]
    batch_ref, logits_ref, unit_ref, z_ref, inverse_ref, act_ref, g_ref, info_ref, gain_ref, shift_ref, w_ref, table_ref, send_ref, keep_ref, dy_ref, sums_ref = refs[1 + counts :]
    micro, wide = part_refs[0].shape
    lines = batch_ref.shape[0]
    crops = lines // micro
    real = lax.broadcasted_iota(jnp.int32, (1, wide), 1) < protos
    odd = lax.broadcasted_iota(jnp.int32, (crops, 1), 0) % 2 == 1
    parts = []
    loss = jnp.zeros((1, 1), F32)
    for m in range(micro):
        at = slice(m * crops, (m + 1) * crops)
        codes = batch_ref[at, :] / jnp.where(
            real, tree([ref[m : m + 1, :] for ref in part_refs]), 1.0
        )
        codes = codes / jnp.sum(codes, 1, keepdims=True)
        partner = jnp.where(odd, pltpu.roll(codes, 1, 0), pltpu.roll(codes, crops - 1, 0))
        sharp = logits_ref[at, :] / softmax_sharpness
        top = jnp.max(jnp.where(real, sharp, -jnp.inf), 1, keepdims=True)
        shifted = sharp - top
        mass = jnp.where(real, jnp.exp(shifted), 0.0)
        total = jnp.sum(mass, 1, keepdims=True)
        chance = shifted - jnp.log(total)
        loss += jnp.sum(jnp.sum(partner * chance, 1, keepdims=True), 0, keepdims=True)
        weight = jnp.sum(partner, 1, keepdims=True)
        parts.append((scale / softmax_sharpness) * (weight * (mass / total) - partner))
    d_scores = jnp.concatenate(parts, 0)
    unit = unit_ref[...]
    grad_protos = split_dot(tn_dot, unit, d_scores, False)
    d_unit = split_dot(nt_dot, d_scores, table_ref[...], True)
    z = z_ref[...]
    inverse = inverse_ref[...]
    dz = inverse * d_unit - z * (inverse * inverse * inverse) * jnp.sum(
        z * d_unit, 1, keepdims=True
    )
    grad_embed = split_dot(tn_dot, act_ref[...], dz, False)
    pack_small(which_ref[0] == 0, send_ref, keep_ref, grad_protos, grad_embed)
    d_act = split_dot(nt_dot, dz, w_ref[...], True)
    for m in range(micro):
        at = slice(m * crops, (m + 1) * crops)
        normal = (g_ref[at, :] - info_ref[m, 0:1, :]) * info_ref[m, 1:2, :]
        pre = normal * gain_ref[...] + shift_ref[...]
        dy = d_act[at] * slope_of(pre)
        dy_ref[at, :] = dy
        sums_ref[m : m + 1, : dy.shape[1]] = jnp.sum(dy, axis=0, keepdims=True)
        sums_ref[micro + m : micro + m + 1, : dy.shape[1]] = jnp.sum(
            dy * normal, axis=0, keepdims=True
        )
    feat = z.shape[1]
    wide = dy_ref.shape[1]
    extra = jnp.concatenate(
        [jnp.sum(dz, axis=0, keepdims=True), jnp.broadcast_to(-scale * loss, (1, feat))], 1
    )
    sums_ref[:, wide:] = jnp.broadcast_to(extra, (2 * micro, 2 * feat))


def loss_grads(which, parts, protos, scale, batch, logits, unit, z, inverse, act, g, info, gain, shift, weight, table, shards):
    ins = [*parts, batch, logits, unit, z, inverse, act, g, info, gain, shift, weight, table]
    micro = info.shape[0]
    outs = [
        shape(packed_shape(table.shape, weight.shape, shards)),
        shape(packed_shape(table.shape, weight.shape, shards)),
        shape(g.shape),
        shape((2 * micro, g.shape[1] + 2 * weight.shape[1])),
    ]
    return run(
        named("loss", loss_body, protos, scale, len(parts)),
        (1,),
        [whole(a) for a in ins],
        [whole(a) for a in outs],
        outs,
        flops=8 * table.size * batch.shape[0],
        bytes_accessed=16 * batch.size,
        prefetch=1,
    )(which, *ins)


def pick_block(rows, width, cell, *fixed):
    return pl.BlockSpec((1, rows, width), lambda g, w: cell(g, *fixed, w[0], w[1], w[2]) + (0,))


def sent_first(g, i, core, x, y):
    z, b = 2 * g + i // 2, i % 2
    return (2 * z + (1 - core) * (1 - x) + core * b, (1 - core) * b + core * (1 - y))


def kept_second(g, i, core, x, y):
    return (2 * (2 * g + i) + x, y)


def sent_second(g, i, core, x, y):
    z = 2 * g + i
    return (2 * z + (1 - core) * x + core * (1 - x), (1 - core) * (1 - y) + core * y)


def add_groups(refs, sizes, out_ref, index, extra=None):
    start = 0
    place = 0
    for count, rows in sizes:
        value = refs[place][0]
        for ref in refs[place + 1 : place + count]:
            value = value + ref[0]
        if extra is not None:
            value = value + extra[0, start : start + rows, :]
        out_ref[index, start : start + rows, :] = value
        place += count
        start += rows


def group_sizes(groups):
    return [(len(addends), addends[0].shape[1] // 2) for addends in groups]


def first_send(scalars, groups):
    sizes = group_sizes(groups)
    shards, _, width = groups[0][0].shape
    lines = sum(rows for _, rows in sizes)
    flat = [array for addends in groups for array in addends]
    specs = []
    for i in range(4):
        for array in flat:
            specs.append(pick_block(array.shape[1] // 2, width, sent_first, i))

    def body(refs):
        refs = refs[1:]
        for i in range(4):
            add_groups(refs[i * len(flat) : (i + 1) * len(flat)], sizes, refs[-1], i)

    return run(
        named("first_send", body),
        (shards // 4,),
        specs,
        pl.BlockSpec((4, lines, width), lambda g, w: (g, 0, 0)),
        shape((shards, lines, width)),
        bytes_accessed=4 * lines * width * shards * 3,
        prefetch=1,
    )(scalars, *(flat * 4))


def second_send(scalars, groups, came):
    sizes = group_sizes(groups)
    shards, _, width = groups[0][0].shape
    lines = sum(rows for _, rows in sizes)
    flat = [array for addends in groups for array in addends]
    specs = []
    for cell in (sent_second, kept_second):
        for i in range(2):
            for array in flat:
                specs.append(pick_block(array.shape[1] // 2, width, cell, i))

    def bit(w):
        return (1 - w[0]) * w[2] + w[0] * w[1]

    for flip in (1, 0):
        for i in range(2):
            specs.append(
                pl.BlockSpec(
                    (1, lines, width),
                    lambda g, w, i=i, flip=flip: (2 * (2 * g + i) + (1 - bit(w) if flip else bit(w)), 0, 0),
                )
            )
    out = pl.BlockSpec((2, lines, width), lambda g, w: (g, 0, 0))

    def body(refs):
        refs = refs[1:]
        count = len(flat)
        came_refs = refs[4 * count : 4 * count + 4]
        for side in range(2):
            for i in range(2):
                place = 2 * side + i
                add_groups(
                    refs[place * count : (place + 1) * count],
                    sizes,
                    refs[-2 + side],
                    i,
                    came_refs[place],
                )

    return run(
        named("second_send", body),
        (shards // 4,),
        specs,
        [out, out],
        [shape((shards // 2, lines, width))] * 2,
        bytes_accessed=4 * lines * width * shards * 4,
        prefetch=1,
    )(scalars, *(flat * 4), *([came] * 4))


def four_places(scalars_ref, refs):
    core, side = scalars_ref[0], scalars_ref[2]
    return [
        (core, side, refs[0]),
        (core, 1 - side, refs[1]),
        (1 - core, side, refs[2]),
        (1 - core, 1 - side, refs[3]),
    ]


def place_early_body(scalars_ref, *refs):
    out_ref, embed_ref, protos_ref, head_ref = refs[8:]
    lines = out_ref.shape[0]
    rows = protos_ref.shape[0] // 2
    wide = 512
    groups = protos_ref.shape[1] // 2 // wide
    lane = embed_ref.shape[1]
    below = embed_ref.shape[0] // 4 // (wide // lane)
    start = lines + groups * rows
    for c, y, ref in four_places(scalars_ref, refs[:4]):
        out_ref[:, pl.ds(pl.multiple_of((2 * c + y) * wide, wide), wide)] = ref[0:lines, :]
        at = pl.ds(pl.multiple_of(y * rows, rows), rows)
        for q in range(groups):
            column = pl.multiple_of((c * groups + q) * wide, wide)
            protos_ref[at, pl.ds(column, wide)] = ref[lines + q * rows : lines + (q + 1) * rows, :]
        for q in range(wide // lane):
            first = pl.multiple_of(((2 * c + y) * (wide // lane) + q) * below, below)
            embed_ref[pl.ds(first, below), :] = ref[start:, q * lane : (q + 1) * lane]
    for c, y, ref in four_places(scalars_ref, refs[4:8]):
        head_ref[:, pl.ds(pl.multiple_of((2 * c + y) * wide, wide), wide)] = ref[...]


def place_late_body(scalars_ref, *refs):
    outs = refs[8:]
    for out_ref, pieces in zip(outs, (refs[:4], refs[4:8])):
        rows, width = out_ref.shape[0] // 2, out_ref.shape[1] // 2
        for c, y, ref in four_places(scalars_ref, pieces):
            out_ref[
                pl.ds(pl.multiple_of(y * rows, rows), rows),
                pl.ds(pl.multiple_of(c * width, width), width),
            ] = ref[...]


def placed_pieces(body, scalars, pieces, outs):
    return run(
        body,
        (1,),
        [whole(a) for a in pieces],
        [whole(a) for a in outs],
        outs,
        prefetch=1,
    )(scalars, *pieces)


def on_device(
    pixels,
    crop_map,
    queue_rows,
    conv_in,
    gain_one,
    shift_one,
    conv_mid,
    gain_two,
    shift_two,
    conv_out,
    gain_three,
    shift_three,
    head_weight,
    head_gain,
    head_shift,
    embed_weight,
    embed_bias,
    prototypes,
):
    micro, canvas, pixel_count, channels = pixels.shape
    devices = lax.axis_size("dp") * lax.axis_size("hst")
    crops = canvas * SLOTS
    total_crops = crops * devices * 1.0
    loss_scale = 1.0 / (micro * total_crops)
    x = pixels.reshape(micro * canvas * pixel_count, channels)
    valid = (crop_map < SLOTS).astype(F32).reshape(-1, 1)
    sizes = jnp.sum(
        (crop_map[:, :, None, :] == jnp.arange(SLOTS, dtype=jnp.int32)[:, None]).astype(F32), 3
    ).reshape(-1, 1)

    shards = lax.axis_size("dp")
    quick = shards == 8 and lax.axis_size("hst") == 4
    packs = 8
    protos = prototypes.shape[1]
    table = jnp.pad(prototypes, ((0, 0), (0, -protos % 1024)))

    def row(vector):
        return vector.reshape(1, -1)

    masks = dp_masks()
    near, far = masks[0], masks[1:]
    core = bit_of(1)
    side = bit_of(2)
    scalars = jnp.stack([core, bit_of(near), side]).astype(jnp.int32)
    keep_half = core.astype(jnp.int32).reshape(1)
    send_half = 1 - keep_half

    h1, stats = first_product(x, conv_in, valid, micro)
    members, counts = first_parts(stats)
    act_one, h2, stats, info_one = second_product(
        members, h1, valid, row(gain_one), row(shift_one), conv_mid, micro
    )
    parts = moment_parts(stats, counts)
    act_two, h3, stats, info_two = third_product(
        parts, members, h2, valid, row(gain_two), row(shift_two), conv_out, micro
    )
    base = stats
    parts = moment_parts(stats, counts)
    feat, info_three, slope, slope_first, slope_second, *feat_halves = pool(
        scalars,
        parts,
        members,
        base,
        h3,
        x,
        valid,
        row(gain_three),
        row(shift_three),
        sizes,
        micro,
        channels // shards if quick else 0,
    )

    lines = feat.shape[0]
    if quick:
        feat_keep, feat_send = feat_halves
        feat_near, feat_far = swap(feat_send, near), swap(feat_keep, 2)
    g, stats = head_product(feat, head_weight, micro)
    if quick:
        stats, feat_near, feat_far = tie(stats, feat_near, feat_far)

    crop_counts = []
    crop_members = []
    number = crops * 1.0
    for group in sync_groups():
        crop_members = [number] * (len(group) + 1)
        crop_counts.append(crop_members)
        number = number * (len(group) + 1)
    parts = moment_parts(stats, crop_counts)

    act_four, embedded, inverse, unit_rows, logits, batch, queue, column, info_four = embed_product(
        parts,
        crop_members,
        protos,
        g,
        row(head_gain),
        row(head_shift),
        embed_weight,
        row(embed_bias),
        table,
        queue_rows,
    )
    for _ in range(SINK_ITERS - 1):
        parts = sum_parts(column)
        batch, queue, column = sweep(parts, protos, batch, queue, queue_rows.shape[0])
    parts = sum_parts(column)
    which = (1 - send_half) if quick else jnp.zeros((1,), jnp.int32)
    small_send, small_keep, dy_four, payload = loss_grads(
        which,
        parts,
        protos,
        loss_scale,
        batch,
        logits,
        unit_rows,
        embedded,
        inverse,
        act_four,
        g,
        info_four,
        row(head_gain),
        row(head_shift),
        embed_weight,
        table,
        packs,
    )
    parts = sum_parts(payload)
    payload = tree(list(parts))
    channel_sums = payload[:, : head_gain.shape[0]]
    first_four, second_four = channel_sums[:micro], channel_sums[micro:]
    extra = payload[0, head_gain.shape[0] :]
    grad_bias, total_loss = extra[: embed_bias.shape[0]], extra[embed_bias.shape[0]]

    if quick:
        feat_near, small_send, *parts = tie(feat_near, small_send, *parts)
        feat_both = swap(feat_near, 2)
        small_recv = swap(small_send, 1)
    dg_send, dg_keep, wide, sums = head_back(
        which,
        parts,
        dy_four,
        g,
        info_four,
        row(head_gain),
        head_weight,
        sizes,
        slope_first,
        slope_second,
        total_crops,
    )
    first_norm = (h1, valid, info_one, info_one, row(gain_one))
    second_norm = (h2, valid, info_two, info_one, row(gain_two))

    def from_third(which, parts):
        return third_back(
            which,
            parts,
            wide,
            slope,
            h3,
            valid,
            info_three,
            row(gain_three),
            info_one,
            conv_out,
            act_two,
            h2,
            info_two,
            row(gain_two),
            row(shift_two),
            micro,
            shards,
        )

    def from_second(d):
        return second_back(
            d, conv_mid, valid, h1, info_one, row(gain_one), row(shift_one), micro
        )

    if quick:
        sums, dg_send, feat_both, small_recv = tie(sums, dg_send, feat_both, small_recv)
        feat_both = jnp.concatenate([feat_keep, feat_near, feat_far, feat_both], 0)

        def core_filler(gate):
            source, other = tie(dg_send, feat_both, gate)[:2]
            grads["dg"] = swap(source, 1)
            grads["feat"] = swap(other, 1)
            return [grads["dg"], grads["feat"]]

        grads = {}
        parts_three = sum_parts(sums, ((), (core_filler,)))
        feat_other = grads["feat"]
        quarter = dg_keep.shape[1] // 2

        def quarter_of(place):
            return jnp.concatenate(
                [
                    lax.dynamic_slice_in_dim(array, place * quarter, quarter, 1)
                    for array in (dg_keep, grads["dg"])
                ],
                0,
            )

        dg_here, dg_there = quarter_of(side), quarter_of(1 - side)
        *parts_three, dg_here, dg_there = tie(*parts_three, dg_here, dg_there)
        dg_far, dg_near, dg_both = swap(dg_there, 2), swap(dg_here, near), swap(dg_there, 2 + near)
        dy, sums, out_send, out_keep = from_third(send_half, parts_three)
        sums, dy, out_send, dg_far, dg_near, dg_both = tie(
            sums, dy, out_send, dg_far, dg_near, dg_both
        )
        small = [small_keep, small_recv]

        def out_filler(gate):
            grads["out"] = swap(tie(out_send, gate)[0], 1)
            return [grads["out"]]

        def head_filler(gate):
            source = tie(dg_near, gate)[0]
            grads["head"] = factor_grad(feat_both, feat_other, dg_here, dg_far, source, dg_both)
            return [grads["head"]]

        def early_filler(gate):
            source = tie(grads["out"], gate)[0]
            grads["early"] = [[out_keep, source], small]
            grads["early_out"] = first_send(scalars, grads["early"])
            return [grads["early_out"]]

        parts_two = sum_parts(sums, ((), (out_filler,), (head_filler, early_filler)))

        early = grads["early"]
        *parts_two, early_out, partial = tie(*parts_two, grads["early_out"], grads["head"])
        early_came = core_swap(early_out, near, 2)
        partial = partial.reshape(2, 2, -1, partial.shape[1])
        most = partial.shape[2] * 3 // 4
        heads = [dp_halves([partial[:, :, :most]], far[0], 1)]
        d_two, mid_send = mid_grad(
            "mid_first",
            mid_first_body,
            send_half,
            [*parts_two, dy, *second_norm, act_one],
            act_one,
            True,
        )
        d_two, mid_send, early_came, heads[0][-1] = tie(
            d_two, mid_send, early_came, heads[0][-1]
        )
        heads.append(dp_halves([partial[:, :, most:]], far[0], 1))
        mid_recv = swap(mid_send, 1)
        early_out, early_keep = second_send(scalars, early, early_came)
        early_came = core_swap(early_out, 2, near)
        mid_keep = mid_grad(
            "mid_second", mid_second_body, keep_half, [d_two, act_one], act_one, False
        )
        mid_keep, mid_recv, early_came, heads[1][-1] = tie(
            mid_keep, mid_recv, early_came, heads[1][-1]
        )

        def sharded(array):
            return array.reshape(shards, -1, array.shape[-1])

        def by_bits(array):
            return array.reshape((2, 2) + array.shape[1:])

        late = [[sharded(mid_keep), sharded(mid_recv)]]
        mid_out = first_send(scalars, late)
        d_two, mid_out = tie(d_two, mid_out)
        mid_came = core_swap(mid_out, near, 2)
        halves = [dp_split(head, far[1], 0) for head in heads]
        head_came = swap(jnp.concatenate([send for _, send in halves], 0), far[1])
        dy, sums = from_second(d_two)
        dy, sums, mid_came, head_came, early_keep, early_came = tie(
            dy, sums, mid_came, head_came, early_keep, early_came
        )
        early = [by_bits(early_keep), by_bits(early_came)]

        def early_z_filler(gate):
            grads["z"] = dp_halves(early, far[0], 1)
            return [grads["z"][-1]]

        def mid_filler(gate):
            source = tie(mid_came, gate)[0]
            grads["mid"] = second_send(scalars, late, source)
            return grads["mid"]

        parts_one = sum_parts(sums, ((), (early_z_filler,), (mid_filler,)))
        mid_out, mid_keep = grads["mid"]
        *parts_one, mid_out, early_came = tie(*parts_one, mid_out, grads["z"][-1])
        early = dp_halves(grads["z"][:-1] + [early_came], far[1], 0)
        mid_came = core_swap(mid_out, 2, near)
        d_one, in_send, in_keep = in_grad(send_half, parts_one, dy, *first_norm, x)
        d_one, in_send, in_keep, mid_came, early[-1] = tie(
            d_one, in_send, in_keep, mid_came, early[-1]
        )
        in_recv = swap(in_send, 1)
        inner = [[sharded(in_keep), sharded(in_recv)]]
        in_out = first_send(scalars, inner)
        mid = dp_halves([by_bits(mid_keep), by_bits(mid_came)], far[0], 1)
        d_one, in_out = tie(d_one, in_out)
        in_came = core_swap(in_out, near, 2)
        grad_x = pixels_grad(d_one, conv_in, wide, slope, micro)
        grad_x, in_came, mid[-1], early[-1], head_came = tie(
            grad_x, in_came, mid[-1], early[-1], head_came
        )
        head_mine = jnp.concatenate([sum(keep) for keep, _ in halves], 0) + head_came
        in_came, *later = tie(
            in_came, *parts_one, *parts_two, *parts_three, first_four, second_four
        )
        steps = len(parts_one)
        parts_one, parts_two, parts_three = [later[i * steps : (i + 1) * steps] for i in range(3)]
        first_four, second_four = later[3 * steps :]
        mid_keep, mid_out = dp_split(mid, far[1], 0)
        in_came, mid_out = tie(in_came, mid_out)
        mid_came = swap(mid_out, far[1])
        in_out, in_keep = second_send(scalars, inner, in_came)
        in_came = core_swap(in_out, 2, near)
        head_far, head_core = swap(head_mine, 2), swap(head_mine, 1)
        early_mine = sum(early)
        in_came, mid_came, head_far, head_core, early_mine = tie(
            in_came, mid_came, head_far, head_core, early_mine
        )
        inner = dp_halves([by_bits(in_keep), by_bits(in_came)], far[0], 1)
        mid_mine = sum(mid_keep) + mid_came
        early_far, early_core = swap(early_mine, 2), swap(early_mine, 1)
        mid_core, head_both = swap(mid_mine, 1), swap(head_far, 1)
        inner[-1], early_far, early_core, mid_mine, mid_core, head_both = tie(
            inner[-1], early_far, early_core, mid_mine, mid_core, head_both
        )
        inner = dp_halves(inner, far[1], 0)
        mid_far, early_both = swap(mid_mine, 2), swap(early_far, 1)
        channel = channels // shards
        early_grads = placed_pieces(
            place_early_body,
            scalars,
            [early_mine, early_far, early_core, early_both]
            + [head_mine, head_far, head_core, head_both],
            [
                shape((conv_out.shape[0] // shards, channels)),
                shape((embed_weight.shape[0] // shards, embed_weight.shape[1])),
                shape((table.shape[0] // shards, table.shape[1])),
                shape((channel, head_weight.shape[1])),
            ],
        )
        inner[-1], mid_far, *early_grads = tie(inner[-1], mid_far, *early_grads)
        in_mine = sum(inner)
        in_far, in_core, mid_both = swap(in_mine, 2), swap(in_mine, 1), swap(mid_far, 1)
        grad_conv_out, grad_embed, grad_protos, grad_head = early_grads
        grad_protos = grad_protos[:, :protos]
        grad_conv_mid, grad_conv_in = placed_pieces(
            place_late_body,
            scalars,
            [mid_mine, mid_far, mid_core, mid_both, in_mine, in_far, in_core, swap(in_far, 1)],
            [
                shape((conv_mid.shape[0] // shards, conv_mid.shape[1])),
                shape((channel, conv_in.shape[1])),
            ],
        )
    else:
        low, high = jnp.zeros((1,), jnp.int32), jnp.ones((1,), jnp.int32)

        def reduced(array):
            return lax.psum(lax.psum_scatter(array, "dp", scatter_dimension=0, tiled=True), "hst")

        parts_three = sum_parts(sums)
        dy, sums, out_low, out_high = from_third(low, parts_three)
        parts_two = sum_parts(sums)
        ins = [*parts_two, dy, *second_norm, act_one]
        d_two, mid_low = mid_grad("mid_first", mid_first_body, low, ins, act_one, True)
        mid_high = mid_grad("mid_second", mid_second_body, high, [d_two, act_one], act_one, False)
        dy, sums = from_second(d_two)
        parts_one = sum_parts(sums)
        d_one, in_low, in_high = in_grad(low, parts_one, dy, *first_norm, x)
        grad_x = pixels_grad(d_one, conv_in, wide, slope, micro)
        out = jnp.stack([out_low, out_high])
        out = out.reshape(2, shards, -1, conv_out.shape[0] // shards, out.shape[-1])
        small_protos, small_embed = unpack_small(
            [small_keep, small_send], table.shape, embed_weight.shape
        )
        grad_conv_out = reduced(out.transpose(1, 3, 0, 2, 4).reshape(conv_out.shape))
        grad_conv_mid = reduced(jnp.concatenate([mid_low, mid_high], 1))
        grad_conv_in = reduced(jnp.concatenate([in_low, in_high], 1))
        dg = jnp.concatenate([dg_keep, dg_send], 1).astype(BF16)
        grad_head = reduced(jnp.dot(feat.astype(BF16).T, dg, preferred_element_type=F32))
        grad_embed = reduced(small_embed)
        grad_protos = reduced(small_protos)[:, :protos]

    def own_rows(vectors):
        sums = [jnp.sum(vector, 0) for vector in vectors]
        piece = sums[0].shape[0] // shards
        stacked = jnp.stack(sums)
        found = lax.dynamic_slice_in_dim(stacked, lax.axis_index("dp") * piece, piece, 1)
        return [found[i] for i in range(len(vectors))]

    def both_sums(parts):
        total = tree(list(parts))
        return [total[:, 1], total[:, 0]]

    small_ones = own_rows(both_sums(parts_one) + both_sums(parts_two))
    large_ones = own_rows(both_sums(parts_three) + [second_four, first_four])

    return (
        total_loss,
        grad_x.reshape(pixels.shape),
        grad_conv_in,
        small_ones[0],
        small_ones[1],
        grad_conv_mid,
        small_ones[2],
        small_ones[3],
        grad_conv_out,
        large_ones[0],
        large_ones[1],
        grad_head,
        large_ones[2],
        large_ones[3],
        grad_embed,
        lax.dynamic_slice_in_dim(
            grad_bias,
            lax.axis_index("dp") * (grad_bias.shape[0] // shards),
            grad_bias.shape[0] // shards,
            0,
        ),
        grad_protos,
    )


def solution(mesh):
    placed = (
        P(None, ("dp", "hst"), None, None),
        P(None, ("dp", "hst"), None),
        P(("dp", "hst"), None),
    ) + (P(),) * 15
    return jax.shard_map(
        on_device,
        mesh=mesh,
        in_specs=placed,
        out_specs=(
            P(),
            P(None, ("dp", "hst"), None, None),
            P("dp", None),
            P("dp"),
            P("dp"),
            P("dp", None),
            P("dp"),
            P("dp"),
            P("dp", None),
            P("dp"),
            P("dp"),
            P("dp", None),
            P("dp"),
            P("dp"),
            P("dp", None),
            P("dp"),
            P("dp", None),
        ),
        check_vma=False,
    )
```
